32 devices in a mesh: comp: 2 (over core), tile: 16 (over z, y, x).
Axes of the slice: x: 2, y: 2, z: 4, core: 2. Of those that a mesh axis runs over, the one named last changes fastest.
Arguments:
- fields: float32 [2, 8, 131072], P('comp', None, 'tile'), may hold values from -6 to 6
- level_rate: float32 [2, 8], P('comp'), may hold values from 0.1 to 0.9
- edge_weight: float32 [2, 3, 131072], P('comp', None, 'tile'), may hold values from 0.5 to 2
- fine_diagonal: float32 [2, 131072], P('comp', 'tile'), may hold values from 0.1 to 1
- fine_table: int32 [2, 3, 131072], P('comp', None, 'tile'), may hold values from 0 to 8447, as said below
- old_height: float32 [2, 131072], P('comp', 'tile'), may hold values from -6 to 6
- level_weight: float32 [2, 8], P('comp'), may hold values from 0.1 to 0.6
- flux_weight: float32 [2, 4], P('comp'), may hold values from 0.2 to 1
- fine_owner: int32 [2, 131072], P('comp', 'tile'), may hold values from 0 to 1023, as said below
- coarse_table: int32 [2, 3, 16384], P('comp', None, 'tile'), may hold values from 0 to 1055, as said below
- coarse_edge: float32 [2, 3, 16384], P('comp', None, 'tile'), may hold values from 2 to 8
- coarse_diagonal: float32 [2, 16384], P('comp', 'tile'), may hold values from 0.5 to 5
- coarse_owner: int32 [2, 16384], P('comp', 'tile'), may hold values from 0 to 15, as said below
- coarse_inverse: float32 [2, 256, 256], P('comp', 'tile'), may hold values from -0.05 to 0.05, as said below
- surface_out: bfloat16 [2, 4, 131072], P('comp', None, 'tile'), may hold values from -6 to 6
- send_blocks: int32 [2, 16, 160], P('comp', 'tile'), may hold values from 0 to 64, as said below
- entry_slot: int32 [2, 16, 160], P('comp', 'tile'), may hold values from 0 to 159, as said below
- entry_block: int32 [2, 16, 160], P('comp', 'tile'), may hold values from 0 to 63, as said below
- remap_tiles: bfloat16 [2, 16, 160, 128, 128], P('comp', 'tile'), may hold values from 0 to 0.17675781
Outputs:
- new_fields: float32 [2, 8, 131072], P('comp', None, 'tile')
- received: float32 [2, 4, 131072], P('comp', None, 'tile')
- height: float32 [2, 131072], P('comp', 'tile')
The draws below stay inside these ranges and needn't reach their ends.
Inputs may be any that keep to these rules, and one draw needn't show every extreme that they name: A position in the cells of the cell's own device, extended by 128 cells on each side (the loop of tiles closes), lying within 128 cells of the cell itself: fine_table[g, k, c] - 128 - (c mod 8192) is between -128 and 128. A position in the first-level cells of the cell's own device, extended by 16 cells on each side (the loop of tiles closes), lying within 16 cells of the cell itself: coarse_table[g, k, a] - 16 - (a mod 1024) is between -16 and 16. `fine_owner`: nondecreasing within each device's cells; every aggregate of a device owns at least one cell. `coarse_owner`: nondecreasing within each device's first-level cells; every aggregate owns at least one cell. `coarse_inverse`: exactly symmetric. `send_blocks`: for each offset j, the used slots come first and at least one is used; 64 marks an unused slot; on some offset of every device all 32 slots are used. `entry_slot`: names a used slot of the receiving device; every used slot is named by some entry. `entry_block`: nondecreasing along the entries of a device; every block is named.
All inputs are finite; a program needn't handle non-finite values.
Results may differ from the reference program's by a relative error of at most 0.0003.
Values may be sent and summed in bfloat16 or wider, within the bound.
No kernel may reach another device: no remote copies, remote signals or barrier semaphores. Data moves between devices by JAX's collectives and lax.ppermute only.
A program may use at most 128 MiB of HBM per device.

```python
import math
import jax
import jax.numpy as jnp
from jax import lax

LEV = 8
NF = 4
TILE_W = 128
HALO = 128
CD = 8192
CELLS = 131072
CDB = 64
SLOT = 32
RB = 160
C1 = 1024
C2 = 16
HALO1 = 16
L1CELLS = 16384
NC2 = 256
N_TILE = 16


def neighbour_table(base_key, cells_dev, cell_total, halo_width):
    first_key, second_key, third_key = jax.random.split(base_key, 3)
    table_shape = (2, cell_total)
    upward = jax.random.randint(first_key, table_shape, 1, 5)
    downward = -jax.random.randint(second_key, table_shape, 1, 5)
    distant = jax.random.randint(third_key, table_shape, -halo_width, halo_width + 1)
    local_cell = jnp.arange(cell_total, dtype=jnp.int32) % cells_dev
    distant = jnp.where(local_cell == 0, -halo_width, distant)
    distant = jnp.where(local_cell == cells_dev - 1, halo_width, distant)
    offsets = jnp.stack([upward, downward, distant], axis=1)
    return (local_cell[None, None, :] + halo_width + offsets).astype(jnp.int32)


def owner_table(base_key, cells_dev, owners_dev, cell_total):
    row_count = 2 * cell_total // cells_dev
    extra_ids = jax.random.randint(base_key, (row_count, cells_dev - owners_dev), 0, owners_dev)
    every_id = jnp.broadcast_to(jnp.arange(owners_dev, dtype=jnp.int32), (row_count, owners_dev))
    joined = jnp.sort(jnp.concatenate([every_id, extra_ids.astype(jnp.int32)], axis=1), axis=1)
    return joined.reshape(2, cell_total)


def send_layout(base_key):
    tile_total = CELLS // CD
    block_key, count_key, full_key = jax.random.split(jax.random.fold_in(base_key, 17), 3)
    counts = jax.random.randint(count_key, (2, tile_total, 5), 1, SLOT + 1)
    full_offset = jax.random.randint(full_key, (2, tile_total), 0, 5)
    full_offset = full_offset.at[:, 0].set(4)
    counts = jnp.where(jnp.arange(5)[None, None, :] == full_offset[:, :, None], SLOT, counts)
    chosen = jax.random.randint(block_key, (2, tile_total, 5, SLOT), 0, CDB)
    used = jnp.arange(SLOT)[None, None, None, :] < counts[:, :, :, None]
    blocks = jnp.where(used, chosen, CDB).astype(jnp.int32)
    return (blocks.reshape(2, tile_total, 5 * SLOT), used.reshape(2, tile_total, 5 * SLOT))


def entry_layout(base_key):
    tile_total = CELLS // CD
    blocks, used = send_layout(base_key)
    slot_column = jnp.arange(5 * SLOT, dtype=jnp.int32)
    source_tile = (jnp.arange(tile_total, dtype=jnp.int32)[:, None] + slot_column[None, :] // SLOT - 2) % tile_total
    live_slot = used[::-1][:, source_tile, slot_column[None, :]].astype(jnp.int32)
    live_count = jnp.sum(live_slot, axis=-1)
    running = jnp.cumsum(live_slot, axis=-1)
    pick_key, order_key, block_key = jax.random.split(jax.random.fold_in(base_key, 29), 3)
    entry_number = jnp.arange(RB, dtype=jnp.int32)
    random_pick = jax.random.randint(pick_key, (2, tile_total, RB), 0, live_count[:, :, None])
    slot_rank = jnp.where(entry_number[None, None, :] < live_count[:, :, None], entry_number[None, None, :], random_pick)
    slot_rank = slot_rank[:, :, jax.random.permutation(order_key, RB)]
    slot_choice = jnp.sum(running[:, :, None, :] <= slot_rank[:, :, :, None], axis=-1).astype(jnp.int32)
    extra_ids = jax.random.randint(block_key, (2, tile_total, RB - CDB), 0, CDB)
    every_id = jnp.broadcast_to(jnp.arange(CDB, dtype=jnp.int32), (2, tile_total, CDB))
    owners = jnp.sort(jnp.concatenate([every_id, extra_ids.astype(jnp.int32)], axis=-1), axis=-1)
    return (slot_choice, owners)


def draw_fine_table(key, part):
    return neighbour_table(jax.random.fold_in(key, 3), CD, CELLS, HALO)


def draw_coarse_table(key, part):
    return neighbour_table(jax.random.fold_in(key, 5), C1, L1CELLS, HALO1)


def draw_fine_owner(key, part):
    return owner_table(jax.random.fold_in(key, 7), CD, C1, CELLS)


def draw_coarse_owner(key, part):
    return owner_table(jax.random.fold_in(key, 9), C1, C2, L1CELLS)


def draw_send_blocks(key, part):
    return send_layout(key)[0]


def draw_entry_slot(key, part):
    return entry_layout(key)[0]


def draw_entry_block(key, part):
    return entry_layout(key)[1]


def draw_coarse_inverse(key, part):
    diag_key, noise_key = jax.random.split(jax.random.fold_in(key, 41))
    diagonal = jnp.exp(jax.random.uniform(diag_key, (2, NC2), jnp.float32, jnp.log(0.002), jnp.log(0.02)))
    raw_noise = jax.random.normal(noise_key, (2, NC2, NC2), jnp.float32)
    symmetric = (raw_noise + jnp.swapaxes(raw_noise, 1, 2)) * (0.35 / NC2 ** 0.5)
    scale_pair = jnp.sqrt(diagonal[:, :, None] * diagonal[:, None, :])
    return symmetric * scale_pair + diagonal[:, :, None] * jnp.eye(NC2, dtype=jnp.float32)[None]


def block_levels(key, dims, pieces, least, high):
    def one(axis_at, parts):
        draws = jax.random.uniform(jax.random.fold_in(jax.random.fold_in(key, 6), axis_at), (parts,), jnp.float32, least / len(pieces), high / len(pieces))
        return jnp.repeat(jnp.exp(draws), dims[axis_at] // parts).reshape((-1,) + (1,) * (len(dims) - axis_at - 1))

    level = one(*pieces[0])
    for cut in pieces[1:]:
        level = level * one(*cut)
    return level


def normal_values(stream_key, dims, deviation, most, cuts=(), held_as=jnp.bfloat16):
    values = jax.random.normal(stream_key, dims, jnp.float32) * deviation
    if len(cuts) > 0:
        values = block_levels(stream_key, dims, cuts, -0.22, 0.18) * values
    return jnp.clip(values, min=-most, max=most).astype(held_as)


def setup_inputs(seed: int = 0) -> dict:
    splits = jax.random.split(jax.random.key(seed), 20)
    fields = normal_values(splits[0], (2, LEV, CELLS), 1.0, 6.0, ((0, 2), (2, 16)), jnp.float32)
    level_rate = jnp.clip(jnp.exp(math.log(0.9) - 2.1972245 * jax.random.uniform(splits[1], (2, LEV), jnp.float32) ** block_levels(splits[1], (2, LEV), ((0, 2),), -0.2, 0.2)), 0.1, 0.9)
    edge_weight = jnp.clip(jnp.exp(math.log(2.0) - 1.3862944 * jax.random.uniform(splits[2], (2, 3, CELLS), jnp.float32) ** block_levels(splits[2], (2, 3, CELLS), ((0, 2), (2, 16)), -0.2, 0.2)), 0.5, 2.0)
    fine_diagonal = jnp.clip(jnp.exp(math.log(1.0) - 2.3025851 * jax.random.uniform(splits[3], (2, CELLS), jnp.float32) ** block_levels(splits[3], (2, CELLS), ((0, 2), (1, 16)), -0.2, 0.2)), 0.1, 1.0)
    fine_table = draw_fine_table(jax.random.fold_in(splits[19], 71), 0)
    old_height = normal_values(splits[5], (2, CELLS), 1.0, 6.0, ((0, 2), (1, 16)), jnp.float32)
    level_weight = jnp.clip(0.1 + 0.5 * jax.random.uniform(splits[6], (2, LEV), jnp.float32) ** block_levels(splits[6], (2, LEV), ((0, 2),), -0.2, 0.2), 0.1, 0.6)
    flux_weight = jnp.clip(0.2 + 0.8 * jax.random.uniform(splits[7], (2, NF), jnp.float32) ** block_levels(splits[7], (2, NF), ((0, 2),), -0.2, 0.2), 0.2, 1.0)
    fine_owner = draw_fine_owner(jax.random.fold_in(splits[19], 71), 0)
    coarse_table = draw_coarse_table(jax.random.fold_in(splits[19], 71), 0)
    coarse_edge = jnp.clip(jnp.exp(math.log(8.0) - 1.3862944 * jax.random.uniform(splits[10], (2, 3, L1CELLS), jnp.float32) ** block_levels(splits[10], (2, 3, L1CELLS), ((0, 2), (2, 16)), -0.2, 0.2)), 2.0, 8.0)
    coarse_diagonal = jnp.clip(jnp.exp(math.log(5.0) - 2.3025851 * jax.random.uniform(splits[11], (2, L1CELLS), jnp.float32) ** block_levels(splits[11], (2, L1CELLS), ((0, 2), (1, 16)), -0.2, 0.2)), 0.5, 5.0)
    coarse_owner = draw_coarse_owner(jax.random.fold_in(splits[19], 71), 0)
    coarse_inverse = draw_coarse_inverse(jax.random.fold_in(splits[19], 71), 0)
    surface_out = normal_values(splits[14], (2, NF, CELLS), 1.0, 6.0, ((0, 2), (2, 16)))
    send_blocks = draw_send_blocks(jax.random.fold_in(splits[19], 71), 0)
    entry_slot = draw_entry_slot(jax.random.fold_in(splits[19], 71), 0)
    entry_block = draw_entry_block(jax.random.fold_in(splits[19], 71), 0)
    remap_tiles = jnp.clip(0.17675781 * jax.random.uniform(splits[18], (2, N_TILE, RB, TILE_W, TILE_W), jnp.float32) ** block_levels(splits[18], (2, N_TILE, RB, TILE_W, TILE_W), ((0, 2), (1, 16)), -0.2, 0.2), 0.0, 0.17675781).astype(jnp.bfloat16)
    return dict(fields=fields, level_rate=level_rate, edge_weight=edge_weight, fine_diagonal=fine_diagonal, fine_table=fine_table, old_height=old_height, level_weight=level_weight, flux_weight=flux_weight, fine_owner=fine_owner, coarse_table=coarse_table, coarse_edge=coarse_edge, coarse_diagonal=coarse_diagonal, coarse_owner=coarse_owner, coarse_inverse=coarse_inverse, surface_out=surface_out, send_blocks=send_blocks, entry_slot=entry_slot, entry_block=entry_block, remap_tiles=remap_tiles)


RELAXATION = 0.8


def neighbour_index(local_table, cells_dev, halo_width, cell_total):
    position = jnp.arange(cell_total, dtype=jnp.int32)
    first_cell = (position // cells_dev) * cells_dev
    return (first_cell[None, :] + local_table.astype(jnp.int32) - halo_width) % cell_total


def owner_index(local_owner, cells_dev, owners_dev):
    position = jnp.arange(local_owner.shape[0], dtype=jnp.int32)
    return (position // cells_dev) * owners_dev + local_owner.astype(jnp.int32)


def apply_operator(values, neighbours, weights, diagonal):
    return (diagonal + jnp.sum(weights, axis=0)) * values - jnp.sum(weights * values[neighbours], axis=0)


def remap_member(member, surface_out, send_blocks, entry_slot, entry_block, remap_tiles):
    partner = 1 - member
    source = surface_out[partner].reshape(NF, N_TILE, CDB, TILE_W).transpose(1, 2, 0, 3)
    source = jnp.concatenate([source, jnp.zeros((N_TILE, 1, NF, TILE_W), source.dtype)], axis=1)
    sender = send_blocks[partner]
    slot_offset = jnp.repeat(jnp.arange(5, dtype=jnp.int32), SLOT)
    slot_column = jnp.arange(5 * SLOT, dtype=jnp.int32)

    def one_tile(tile_number):
        source_tile = (tile_number + slot_offset - 2) % N_TILE
        chosen = sender[source_tile, slot_column]
        slot_data = source[source_tile, chosen]
        picked = slot_data[entry_slot[member, tile_number]].astype(jnp.float32)
        tiles_now = remap_tiles[member, tile_number].astype(jnp.float32)
        products = jnp.einsum("efs,eds->efd", picked, tiles_now)
        return jax.ops.segment_sum(products, entry_block[member, tile_number], num_segments=CDB)

    blocks = lax.map(one_tile, jnp.arange(N_TILE, dtype=jnp.int32))
    return blocks.transpose(2, 0, 1, 3).reshape(NF, CELLS)


def reference(fields, level_rate, edge_weight, fine_diagonal, fine_table, old_height, level_weight, flux_weight, fine_owner, coarse_table, coarse_edge, coarse_diagonal, coarse_owner, coarse_inverse, surface_out, send_blocks, entry_slot, entry_block, remap_tiles):
    new_list = []
    received_list = []
    height_list = []
    for member in range(2):
        fine_links = neighbour_index(fine_table[member], CD, HALO, CELLS)
        coarse_links = neighbour_index(coarse_table[member], C1, HALO1, L1CELLS)
        fine_owners = owner_index(fine_owner[member], CD, C1)
        coarse_owners = owner_index(coarse_owner[member], C1, C2)
        weights = edge_weight[member]
        weight_sum = jnp.sum(weights, axis=0)
        current = fields[member]
        beside_all = jnp.sum(weights[None] * current[:, fine_links], axis=1)
        advanced = current + level_rate[member][:, None] * (beside_all - weight_sum * current) / weight_sum
        received = remap_member(member, surface_out, send_blocks, entry_slot, entry_block, remap_tiles)
        forcing = jnp.sum(level_weight[member][:, None] * advanced, axis=0) + jnp.sum(flux_weight[member][:, None] * received, axis=0)
        fine_total = fine_diagonal[member] + weight_sum
        previous = old_height[member]
        smoothed = previous + RELAXATION * (forcing - apply_operator(previous, fine_links, weights, fine_diagonal[member])) / fine_total
        fine_residual = forcing - apply_operator(smoothed, fine_links, weights, fine_diagonal[member])
        coarse_source = jax.ops.segment_sum(fine_residual, fine_owners, num_segments=L1CELLS)
        coarse_weights = coarse_edge[member]
        coarse_total = coarse_diagonal[member] + jnp.sum(coarse_weights, axis=0)
        coarse_first = RELAXATION * coarse_source / coarse_total
        coarse_residual = coarse_source - apply_operator(coarse_first, coarse_links, coarse_weights, coarse_diagonal[member])
        bottom_source = jax.ops.segment_sum(coarse_residual, coarse_owners, num_segments=NC2)
        bottom_value = jnp.dot(coarse_inverse[member], bottom_source, precision=lax.Precision.HIGHEST)
        coarse_second = coarse_first + bottom_value[coarse_owners]
        coarse_third = coarse_second + RELAXATION * (coarse_source - apply_operator(coarse_second, coarse_links, coarse_weights, coarse_diagonal[member])) / coarse_total
        corrected = smoothed + coarse_third[fine_owners]
        height = corrected + RELAXATION * (forcing - apply_operator(corrected, fine_links, weights, fine_diagonal[member])) / fine_total
        new_list.append(advanced)
        received_list.append(received)
        height_list.append(height)
    return (jnp.stack(new_list), jnp.stack(received_list), jnp.stack(height_list))
```

```python
import functools

import jax
import jax.numpy as jnp
from jax import lax
from jax.experimental import pallas as pl
from jax.experimental.pallas import tpu as pltpu
from jax.sharding import PartitionSpec as P

LANES = 128
RELAXATION = 0.8
F32 = jnp.float32
BF16 = jnp.bfloat16
I32 = jnp.int32

FIELD_HI, FIELD_LO = 0, 8
EDGE_HI, EDGE_LO, OLD_HI, OLD_LO = 16, 19, 22, 23
OFFSET, OWNER = 24, 27
CEDGE_HI, CEDGE_LO, CDIAG_HI, CDIAG_LO = 32, 38, 44, 46
COFFSET, COWNER = 48, 54
INVERSE = 56

FRAME, OWN = 32, 8


def gather_lanes(table, index):
    return jnp.take_along_axis(table, index, axis=1)


def wide(row, count=8):
    return jnp.broadcast_to(row, (count, row.shape[1]))


def split3(x):
    high = x.astype(BF16)
    rest = x - high.astype(F32)
    middle = rest.astype(BF16)
    low = (rest - middle.astype(F32)).astype(BF16)
    return high, middle, low


def dot_nt(a, b):
    return lax.dot_general(a, b, (((1,), (1,)), ((), ())), preferred_element_type=F32)


def dot_tn(a, b):
    return lax.dot_general(a, b, (((0,), (0,)), ((), ())), preferred_element_type=F32)


def column_of(scalars, offset, count):
    sublane = lax.broadcasted_iota(I32, (8, LANES), 0)
    value = jnp.zeros((8, LANES), F32)
    for level in range(count):
        value = jnp.where(sublane == level, scalars[0, level], value)
    return value


def pick_base(inverse_blocks):
    return -(-(INVERSE + 32 * inverse_blocks) // 16) * 16


def pack_kernel(
    surface, sends, fields, old, edge, table, owner, ctable, cedge, cdiag, cowner, cinverse,
    near1, far1, near2, far2, here, chunks, left_rows, right_rows,
):
    tile = lax.axis_index("tile")
    even = lax.rem(tile, 2) == 0
    low = lax.rem(tile, 4) < 2
    cells = fields.shape[1]
    blocks = cells // LANES
    firsts = ctable.shape[1]
    frows = firsts // LANES
    base = pick_base(cinverse.shape[1] // LANES)
    lane = lax.broadcasted_iota(I32, (1, LANES), 1)

    for rows, at_left in ((right_rows, False), (left_rows, True)):
        start = 0 if at_left else cells - LANES
        part = pl.ds(start, LANES)

        def both(high, low_row, value):
            count = value.shape[0]
            rows[pl.ds(high, count), :] = value
            rows[pl.ds(low_row, count), :] = value - value.astype(BF16).astype(F32)

        rows[pl.ds(24, 8), :] = jnp.zeros((8, LANES), F32)
        both(FIELD_HI, FIELD_LO, fields[:, part])
        both(EDGE_HI, EDGE_LO, edge[:, part])
        block = 0 if at_left else blocks - 1
        both(OLD_HI, OLD_LO, old[pl.ds(block, 1), :])
        rows[pl.ds(OFFSET, 3), :] = (table[:, part] - (LANES + start) - lane).astype(F32)
        shift = 0 if at_left else firsts - LANES
        rows[pl.ds(OWNER, 1), :] = (owner[pl.ds(block, 1), :] - shift).astype(F32)
        first = 0 if at_left else frows - 2
        reach = LANES // 8
        for step in range(2):
            cpart = pl.ds((first + step) * LANES, LANES)
            both(CEDGE_HI + 3 * step, CEDGE_LO + 3 * step, cedge[:, cpart])
            rows[pl.ds(COFFSET + 3 * step, 3), :] = (
                ctable[:, cpart] - (reach + (first + step) * LANES) - lane
            ).astype(F32)
            both(CDIAG_HI + step, CDIAG_LO + step, cdiag[pl.ds(first + step, 1), :])
            rows[pl.ds(COWNER + step, 1), :] = cowner[pl.ds(first + step, 1), :].astype(F32)
        halves = cinverse.shape[1] // LANES
        for half in range(halves):
            both(
                INVERSE + 16 * half,
                INVERSE + 16 * (halves + half),
                cinverse[:, pl.ds(half * LANES, LANES)],
            )
        end = INVERSE + 32 * halves
        if base > end:
            rows[pl.ds(end, base - end), :] = jnp.zeros((base - end, LANES), F32)

    for block in range(blocks):
        chunks[pl.ds(4 * block, 4), :] = surface[:, pl.ds(block * LANES, LANES)].astype(F32)
    slots = sends.shape[1]
    hot = jnp.where(
        lax.broadcasted_iota(I32, (blocks, slots), 0) == sends[...], 1.0, 0.0
    ).astype(BF16)
    picks = []
    for channel in range(4):
        source = chunks[pl.ds(channel, blocks, stride=4), :].astype(BF16)
        picks.append(dot_tn(hot, source).astype(BF16))
    count = slots // 5

    def chosen(j):
        return jnp.concatenate([p[j * count : (j + 1) * count] for p in picks], axis=0)

    to_right, to_left = chosen(1), chosen(3)
    far_right, far_left = chosen(0), chosen(4)
    here[...] = chosen(2)
    rim_right = right_rows[...].astype(BF16)
    rim_left = left_rows[...].astype(BF16)
    near1[pl.ds(0, base), :] = jnp.where(even, rim_right, rim_left)
    far1[pl.ds(0, base), :] = jnp.where(even, rim_left, rim_right)
    near1[pl.ds(base, 4 * count), :] = jnp.where(even, to_right, to_left)
    far1[pl.ds(base, 4 * count), :] = jnp.where(even, to_left, to_right)
    near2[...] = jnp.where(low, far_right, far_left)
    far2[...] = jnp.where(low, far_left, far_right)


def stencil_kernel(
    rate, level_weight, fields, edge, table, old, owner,
    fresh, force, beside_old, edges, window, ends_row, ends_lane, oldpad,
):
    blocks = old.shape[0]
    speed = column_of(rate, 0, fields.shape[0])
    share = column_of(level_weight, 0, fields.shape[0])

    def one(block, before, here, after):
        part = pl.ds(pl.multiple_of(block * LANES, LANES), LANES)
        weights = edge[:, part]
        place = table[:, part] - block * LANES
        for link in range(3):
            edges[link, pl.ds(block, 1), :] = weights[link : link + 1]
            window[link, pl.ds(block, 1), :] = place[link : link + 1]
        total = weights[0:1] + weights[1:2] + weights[2:3]
        inverse = 1.0 / total
        lanes = lax.bitwise_and(place, LANES - 1)
        which = lax.shift_right_logical(place, 7)
        beside = jnp.zeros((8, LANES), F32)
        for link in range(3):
            index = wide(lanes[link : link + 1])
            row = wide(which[link : link + 1])
            value = jnp.where(
                row == 1,
                gather_lanes(here, index),
                jnp.where(row == 0, gather_lanes(before, index), gather_lanes(after, index)),
            )
            beside = beside + wide(weights[link : link + 1]) * value
        result = here + speed * (beside - wide(total) * here) * wide(inverse)
        fresh[:, part] = result
        force[pl.ds(block, 1), :] = jnp.sum(result * share, axis=0, keepdims=True)

    blank = jnp.zeros((8, LANES), F32)

    def chunk(block):
        return fields[:, pl.ds(pl.multiple_of(block * LANES, LANES), LANES)]

    one(0, blank, chunk(0), chunk(1))

    def step(block, carry):
        one(block, chunk(block - 1), chunk(block), chunk(block + 1))
        return carry

    lax.fori_loop(1, blocks - 1, step, 0, unroll=2)
    one(blocks - 1, chunk(blocks - 2), chunk(blocks - 1), blank)

    oldpad[pl.ds(0, 8), :] = blank
    oldpad[pl.ds(8 + blocks, 8), :] = blank
    oldpad[pl.ds(8, blocks), :] = old[...]
    beside_old[...] = neighbour_sum(oldpad, edges, window, blocks)

    firsts = ends_row.shape[0] * LANES
    ident = lax.broadcasted_iota(I32, ends_row.shape, 0) * LANES + lax.broadcasted_iota(
        I32, ends_row.shape, 1
    )
    count = ends_row.shape[0]
    rows = jnp.zeros(ends_row.shape, I32)
    for block in range(blocks):
        last = jnp.broadcast_to(owner[pl.ds(block, 1), LANES - 1 : LANES], ends_row.shape)
        rows = rows + jnp.where(last <= ident, 1, 0)
    lanes = jnp.zeros(ends_row.shape, I32)
    for bit in (64, 32, 16, 8, 4, 2, 1):
        probe = lanes + (bit - 1)
        value = jnp.full(ends_row.shape, firsts, I32)
        for block in range(blocks):
            value = jnp.where(
                rows == block, gather_lanes(wide(owner[pl.ds(block, 1), :], count), probe), value
            )
        lanes = jnp.where(value <= ident, lanes + bit, lanes)
    ends_row[...] = rows
    ends_lane[...] = lanes


def neighbour_sum(padded, edges, window, blocks):
    before = padded[pl.ds(7, blocks), :]
    here = padded[pl.ds(8, blocks), :]
    after = padded[pl.ds(9, blocks), :]
    result = jnp.zeros((blocks, LANES), F32)
    for link in range(3):
        place = window[link]
        index = lax.bitwise_and(place, LANES - 1)
        row = lax.shift_right_logical(place, 7)
        value = jnp.where(
            row == 1,
            gather_lanes(here, index),
            jnp.where(row == 0, gather_lanes(before, index), gather_lanes(after, index)),
        )
        result = result + edges[link] * value
    return result


def first_level_sum(values, frame):
    before = pltpu.roll(values, 1, axis=0)
    after = pltpu.roll(values, FRAME - 1, axis=0)
    lane = lax.broadcasted_iota(I32, (FRAME, LANES), 1)
    result = jnp.zeros((FRAME, LANES), F32)
    for link in range(3):
        place = lane + frame[pl.ds(link * FRAME, FRAME), :].astype(I32)
        index = lax.bitwise_and(place, LANES - 1)
        value = jnp.where(
            place < 0,
            gather_lanes(before, index),
            jnp.where(place >= LANES, gather_lanes(after, index), gather_lanes(values, index)),
        )
        result = result + frame[pl.ds((3 + link) * FRAME, FRAME), :] * value
    return result


def previous_one(values):
    rolled = pltpu.roll(values, 1, axis=1)
    above = pltpu.roll(rolled, 1, axis=0)
    lane = lax.broadcasted_iota(I32, values.shape, 1)
    row = lax.broadcasted_iota(I32, values.shape, 0)
    return jnp.where(lane > 0, rolled, jnp.where(row > 0, above, 0.0))


def triangle():
    return jnp.where(
        lax.broadcasted_iota(I32, (LANES, LANES), 0) < lax.broadcasted_iota(I32, (LANES, LANES), 1),
        1.0,
        0.0,
    ).astype(BF16)


def prefix(values):
    ones = jnp.ones((LANES, LANES), BF16)
    right = jnp.concatenate([triangle(), ones], axis=1)
    count = values.shape[0]
    out = jnp.dot(
        jnp.concatenate(split3(values), axis=0), right, preferred_element_type=F32
    )
    out = out[:count] + out[count : 2 * count] + out[2 * count :]
    return out[:, :LANES], out[:, LANES:]


def forward_kernel(
    entry_block, rate, level_weight, flux_weight,
    tiles, near1, far1, near2, far2, here, slots, fields, edges, window, old, diagonal,
    force_part, beside_old, ends_row, ends_lane, fresh_ends,
    ctable, cedge, cdiag, cowner,
    summed, force_out, smooth_out, source_out, frame, ends_out, message,
    tile_buffer, picked, padded, prefixed, totals, arrivals, sems,
):
    tile = lax.axis_index("tile")
    tile_count = lax.axis_size("tile")
    even = lax.rem(tile, 2) == 0
    low = lax.rem(tile, 4) < 2
    entries = tiles.shape[0]
    blocks = old.shape[0]
    parts = sems.shape[0]
    step = entries // parts

    def load(part):
        return pltpu.make_async_copy(
            tiles.at[pl.ds(part * step, step)],
            tile_buffer.at[pl.ds(part * step, step)],
            sems.at[part],
        )

    for part in range(parts):
        load(part).start()

    base = near1.shape[0] - near2.shape[0]
    near, far = near1[...], far1[...]
    from_left = jnp.where(even, far, near)
    from_right = jnp.where(even, near, far)
    two_near, two_far = near2[...], far2[...]
    j0 = jnp.where(low, two_far, two_near)
    j4 = jnp.where(low, two_near, two_far)
    j1, j3, j2 = from_left[base:], from_right[base:], here[...]
    slot_count = slots.shape[1]
    each = j0.shape[0] // 4
    hot = jnp.where(
        lax.broadcasted_iota(I32, (slot_count, entries), 0) == slots[...], 1.0, 0.0
    ).astype(BF16)
    for channel in range(4):
        span = slice(channel * each, (channel + 1) * each)
        source = jnp.concatenate([j[span] for j in (j0, j1, j2, j3, j4)], axis=0)
        picked[pl.ds(channel, entries, stride=4), :] = dot_tn(hot, source)

    arrivals[0] = from_left[:base].astype(F32)
    arrivals[1] = from_right[:base].astype(F32)

    summed[...] = jnp.zeros(summed.shape, F32)
    for part in range(parts):
        load(part).wait()

        def pair(number, carry):
            entry = part * step + 2 * number
            rows = picked[pl.ds(pl.multiple_of(4 * entry, 8), 8), :].astype(BF16)
            first = dot_nt(rows, tile_buffer[entry])
            second = dot_nt(rows, tile_buffer[entry + 1])
            at = entry_block[0, entry]
            summed[at, pl.ds(0, 4), :] += first[0:4]
            at = entry_block[0, entry + 1]
            summed[at, pl.ds(4, 4), :] += second[4:8]
            return carry

        lax.fori_loop(0, step // 2, pair, 0, unroll=8)

    speed = column_of(rate, 0, fields.shape[0])
    share = column_of(level_weight, 0, fields.shape[0])
    force_out[...] = force_part[...]
    padded[pl.ds(0, 8), :] = jnp.zeros((8, LANES), F32)
    padded[pl.ds(8 + blocks, 8), :] = jnp.zeros((8, LANES), F32)
    beside_extra = []
    for side, block, target in ((0, 0, 0), (1, blocks - 1, 2)):
        halo = arrivals[side, pl.ds(FIELD_HI, 8), :] + arrivals[side, pl.ds(FIELD_LO, 8), :]
        halo_old = arrivals[side, pl.ds(OLD_HI, 1), :] + arrivals[side, pl.ds(OLD_LO, 1), :]
        total = edges[0, pl.ds(block, 1), :] + edges[1, pl.ds(block, 1), :] + edges[2, pl.ds(block, 1), :]
        extra = jnp.zeros((8, LANES), F32)
        extra_old = jnp.zeros((8, LANES), F32)
        for link in range(3):
            place = wide(window[link, pl.ds(block, 1), :])
            index = lax.bitwise_and(place, LANES - 1)
            weight = jnp.where(
                lax.shift_right_logical(place, 7) == target, wide(edges[link, pl.ds(block, 1), :]), 0.0
            )
            extra = extra + weight * gather_lanes(halo, index)
            extra_old = extra_old + weight * gather_lanes(wide(halo_old), index)
        change = speed * extra / wide(total)
        ends_out[:, pl.ds(side * LANES, LANES)] = fresh_ends[:, pl.ds(side * LANES, LANES)] + change
        force_out[pl.ds(block, 1), :] += jnp.sum(change * share, axis=0, keepdims=True)
        beside_extra.append(extra_old[0:1])

    force = force_out[...]
    for channel in range(4):
        value = summed[:, channel, :] + summed[:, channel + 4, :]
        force = force + flux_weight[0, channel] * value
    force_out[...] = force
    total = diagonal[...] + edges[0] + edges[1] + edges[2]
    smooth_out[...] = beside_old[...]
    smooth_out[pl.ds(0, 1), :] += beside_extra[0]
    smooth_out[pl.ds(blocks - 1, 1), :] += beside_extra[1]
    previous = old[...]
    smooth = previous + RELAXATION * (force - (total * previous - smooth_out[...])) / total
    smooth_out[...] = smooth
    padded[pl.ds(8, blocks), :] = smooth
    residual = force - total * smooth + neighbour_sum(padded, edges, window, blocks)

    inner, whole = prefix(residual)
    prefixed[...] = inner
    totals[...] = whole
    rows, lanes = ends_row[...], ends_lane[...]
    count = rows.shape[0]
    run = jnp.zeros((count, LANES), F32)
    ends = jnp.zeros((count, LANES), F32)
    for block in range(blocks):
        value = gather_lanes(wide(prefixed[pl.ds(block, 1), :], count), lanes) + run
        ends = jnp.where(rows == block, value, ends)
        run = run + wide(totals[pl.ds(block, 1), :], count)
    ends = jnp.where(rows == blocks, run, ends)
    own_source = ends - previous_one(ends)

    lane = lax.broadcasted_iota(I32, (1, LANES), 1)
    rim_rows, rim_counts = [], []
    for side in range(2):
        inside = padded[pl.ds(8 if side == 0 else 7 + blocks, 1), :]
        value = jnp.zeros((1, LANES), F32)
        for link in range(3):
            place = lane + arrivals[side, pl.ds(OFFSET + link, 1), :].astype(I32)
            index = lax.bitwise_and(place, LANES - 1)
            reached = (place >= LANES) if side == 0 else (place < 0)
            weight = arrivals[side, pl.ds(EDGE_HI + link, 1), :] + arrivals[side, pl.ds(EDGE_LO + link, 1), :]
            value = value + jnp.where(
                wide(reached.astype(I32)) > 0,
                wide(weight) * gather_lanes(wide(inside), wide(index)),
                0.0,
            )[0:1]
        rim_rows.append(value)
        owners = arrivals[side, pl.ds(OWNER, 1), :].astype(I32)
        below = jnp.where(
            lax.broadcasted_iota(I32, (LANES, LANES), 0) >= owners, 1.0, 0.0
        ).astype(BF16)
        rim_counts.append(dot_nt(jnp.ones((8, LANES), BF16), below))
    rim_inner, rim_whole = prefix(jnp.concatenate([wide(r) for r in rim_rows], axis=0))
    rim_source = []
    for side in range(2):
        place = rim_counts[side].astype(I32)
        index = lax.bitwise_and(place, LANES - 1)
        value = gather_lanes(rim_inner[8 * side : 8 * side + 8], index)
        value = jnp.where(place >= LANES, rim_whole[8 * side : 8 * side + 8], value)
        shifted = pltpu.roll(value, 1, axis=1)
        first = lax.broadcasted_iota(I32, (8, LANES), 1) == 0
        rim_source.append((value - jnp.where(first, 0.0, shifted))[0:1])

    frows = own_source.shape[0]
    source_out[...] = jnp.zeros((FRAME, LANES), F32)
    source_out[pl.ds(OWN, frows), :] = own_source
    source_out[pl.ds(OWN - 1, 1), :] = rim_source[0]
    source_out[pl.ds(OWN + frows, 1), :] = rim_source[1]
    reach = LANES // 8
    frame[...] = jnp.zeros(frame.shape, F32)
    frame[pl.ds(6 * FRAME, FRAME), :] = jnp.ones((FRAME, LANES), F32)
    frame[pl.ds(7 * FRAME, FRAME), :] = jnp.full((FRAME, LANES), 127.0, F32)
    bottoms = 16
    for row in range(frows):
        part = pl.ds(row * LANES, LANES)
        offsets = (ctable[:, part] - (reach + row * LANES) - lane).astype(F32)
        weights = cedge[:, part]
        for link in range(3):
            frame[pl.ds(link * FRAME + OWN + row, 1), :] = offsets[link : link + 1]
            frame[pl.ds((3 + link) * FRAME + OWN + row, 1), :] = weights[link : link + 1]
    frame[pl.ds(6 * FRAME + OWN, frows), :] = cdiag[...]
    frame[pl.ds(7 * FRAME + OWN, frows), :] = (cowner[...] + bottoms).astype(F32)
    for side in range(2):
        for row in range(2):
            at = (OWN - 2 + row) if side == 0 else (OWN + frows + row)
            for link in range(3):
                put = 3 * row + link
                frame[pl.ds(link * FRAME + at, 1), :] = arrivals[side, pl.ds(COFFSET + put, 1), :]
                frame[pl.ds((3 + link) * FRAME + at, 1), :] = (
                    arrivals[side, pl.ds(CEDGE_HI + put, 1), :] + arrivals[side, pl.ds(CEDGE_LO + put, 1), :]
                )
            frame[pl.ds(6 * FRAME + at, 1), :] = (
                arrivals[side, pl.ds(CDIAG_HI + row, 1), :] + arrivals[side, pl.ds(CDIAG_LO + row, 1), :]
            )
            frame[pl.ds(7 * FRAME + at, 1), :] = arrivals[side, pl.ds(COWNER + row, 1), :] + (
                2.0 * bottoms * side
            )
    for link in range(3):
        frame[pl.ds(6 * FRAME, FRAME), :] += frame[pl.ds((3 + link) * FRAME, FRAME), :]
    source = source_out[...]
    first = RELAXATION * source / frame[pl.ds(6 * FRAME, FRAME), :]
    residual = (1.0 - RELAXATION) * source + first_level_sum(first, frame)
    codes = frame[pl.ds(7 * FRAME, FRAME), :].astype(I32)
    pieces = split3(residual)
    left_side, right_side = [], []
    bins = lax.broadcasted_iota(I32, (LANES, LANES), 0)
    for row in range(OWN - 2, OWN + frows + 2):
        left_side.append(jnp.concatenate([p[row : row + 1] for p in pieces], axis=0))
        right_side.append(
            jnp.where(bins == codes[row : row + 1], 1.0, 0.0).astype(BF16)
        )
    bottom = dot_nt(jnp.concatenate(left_side, axis=1), jnp.concatenate(right_side, axis=1))
    bottom = bottom[0:1] + bottom[1:2] + bottom[2:3]
    bottom = jnp.where(lane < 3 * bottoms, bottom, 0.0)

    to_left = jnp.concatenate(
        [bottom, padded[pl.ds(8, 1), :], own_source[0:2], rim_source[0], jnp.zeros((3, LANES), F32)], axis=0
    )
    to_right = jnp.concatenate(
        [bottom, padded[pl.ds(7 + blocks, 1), :], own_source[frows - 2 : frows], rim_source[1], jnp.zeros((3, LANES), F32)],
        axis=0,
    )
    for other in range(message.shape[0]):
        message[other] = to_right
    message[lax.rem(tile + tile_count - 1, tile_count)] = to_left


def prepare_kernel(
    fresh, ends_new, summed, near1, far1, cinverse, fresh_out, received, weights, sem, extended
):
    del fresh
    tile = lax.axis_index("tile")
    even = lax.rem(tile, 2) == 0
    cells = fresh_out.shape[1]
    copies = [
        pltpu.make_async_copy(
            ends_new.at[:, pl.ds(side * LANES, LANES)],
            fresh_out.at[:, pl.ds(side * (cells - LANES), LANES)],
            sem.at[side],
        )
        for side in range(2)
    ]
    for copy in copies:
        copy.start()
    blocks = summed.shape[0]
    for block in range(blocks):
        received[:, pl.ds(block * LANES, LANES)] = summed[block, pl.ds(0, 4), :] + summed[block, pl.ds(4, 4), :]
    bottoms, size = cinverse.shape
    halves = size // LANES
    near = near1[pl.ds(INVERSE, 32 * halves), :].astype(F32)
    far = far1[pl.ds(INVERSE, 32 * halves), :].astype(F32)
    left = jnp.where(even, far, near)
    right = jnp.where(even, near, far)
    for half in range(halves):
        part = pl.ds(half * LANES, LANES)
        for at, block in ((0, left), (2, right)):
            extended[pl.ds(at * bottoms, bottoms), part] = (
                block[16 * half : 16 * half + 16]
                + block[16 * (halves + half) : 16 * (halves + half) + 16]
            )
        extended[pl.ds(bottoms, bottoms), part] = cinverse[:, part]
    table = extended[...]
    lane = lax.broadcasted_iota(I32, (3 * bottoms, LANES), 1)
    for other in range(weights.shape[0]):
        shift = (size - (other - 1) * bottoms) % size
        turned = pltpu.roll(table, shift, axis=1) if shift else table
        weights[other] = jnp.where(lane < 3 * bottoms, turned[:, :LANES], 0.0)
    for copy in copies:
        copy.wait()


def backward_kernel(
    frame_rows, arrived, weights, source, frame, force, smooth, edges, window, diagonal, owner, near1, far1,
    height, frame_source, padded, third_rows,
):
    tile = lax.axis_index("tile")
    tile_count = lax.axis_size("tile")
    even = lax.rem(tile, 2) == 0
    blocks = force.shape[0]
    left = arrived[lax.rem(tile + tile_count - 1, tile_count)]
    right = arrived[lax.rem(tile + 1, tile_count)]
    count = weights.shape[1]
    partial = jnp.zeros((count, LANES), F32)
    for other in range(weights.shape[0]):
        partial = partial + weights[other] * wide(arrived[other, pl.ds(0, 1), :], count)
    partial = jnp.concatenate([partial, jnp.zeros((LANES - count, LANES), F32)], axis=0)
    ones = jnp.ones((8, LANES), BF16)
    pieces = split3(partial)
    bottom = dot_nt(ones, pieces[0]) + dot_nt(ones, pieces[1]) + dot_nt(ones, pieces[2])

    frows = frame_rows
    frame_source[...] = source[...]
    frame_source[pl.ds(OWN - 2, 2), :] += left[2:4]
    frame_source[pl.ds(OWN, 1), :] += left[4:5]
    frame_source[pl.ds(OWN + frows - 1, 1), :] += right[4:5]
    frame_source[pl.ds(OWN + frows, 2), :] += right[2:4]
    total_source = frame_source[...]
    total = frame[pl.ds(6 * FRAME, FRAME), :]
    codes = frame[pl.ds(7 * FRAME, FRAME), :].astype(I32)
    second = RELAXATION * total_source / total + gather_lanes(wide(bottom[0:1], FRAME), codes)
    third = second + RELAXATION * (
        total_source - total * second + first_level_sum(second, frame)
    ) / total
    third_rows[...] = third

    owners = owner[...]
    index = lax.bitwise_and(owners, LANES - 1)
    which = lax.shift_right_logical(owners, 7)
    corrected = jnp.zeros((blocks, LANES), F32)
    for row in range(frows):
        corrected = jnp.where(
            which == row, gather_lanes(wide(third_rows[pl.ds(OWN + row, 1), :], blocks), index), corrected
        )
    corrected = smooth[...] + corrected
    padded[pl.ds(8, blocks), :] = corrected
    near = near1[pl.ds(16, 16), :].astype(F32)
    far = far1[pl.ds(16, 16), :].astype(F32)
    left_owner = jnp.where(even, far, near)[OWNER - 16 : OWNER - 15].astype(I32)
    right_owner = jnp.where(even, near, far)[OWNER - 16 : OWNER - 15].astype(I32)
    left_rim = left[1:2] + gather_lanes(wide(third_rows[pl.ds(OWN - 1, 1), :]), wide(left_owner))[0:1]
    right_rim = right[1:2] + gather_lanes(wide(third_rows[pl.ds(OWN + frows, 1), :]), wide(right_owner))[0:1]
    padded[pl.ds(7, 1), :] = left_rim
    padded[pl.ds(8 + blocks, 1), :] = right_rim
    fine_total = diagonal[...] + edges[0] + edges[1] + edges[2]
    beside = neighbour_sum(padded, edges, window, blocks)
    height[...] = corrected + RELAXATION * (force[...] - (fine_total * corrected - beside)) / fine_total


def struct(shape, dtype=F32):
    return jax.ShapeDtypeStruct(shape, dtype)


VMEM = pl.BlockSpec(memory_space=pltpu.VMEM)
SMEM = pl.BlockSpec(memory_space=pltpu.SMEM)
ANY = pl.BlockSpec(memory_space=pl.ANY)
PARAMS = pltpu.CompilerParams(vmem_limit_bytes=48 * 1024 * 1024)


def pair_up(count, distance):
    period = 2 * distance
    result = []
    for start in (0, distance):
        pairs = []
        for i in range(count):
            if (i - start) % period < distance:
                pairs += [(i, (i + distance) % count), ((i + distance) % count, i)]
        result.append(pairs)
    return result


def per_device(
    fields, level_rate, edge_weight, fine_diagonal, fine_table, old_height, level_weight,
    flux_weight, fine_owner, coarse_table, coarse_edge, coarse_diagonal, coarse_owner,
    coarse_inverse, surface_out, send_blocks, entry_slot, entry_block, remap_tiles,
):
    tile_count = lax.axis_size("tile")
    cells = fields.shape[2]
    blocks = cells // LANES
    firsts = coarse_diagonal.shape[1]
    frows = firsts // LANES
    entries = entry_slot.shape[2]
    channels = surface_out.shape[1]
    slots = send_blocks.shape[2]
    each = slots // 5
    halves = coarse_inverse.shape[2] // LANES
    bottoms = coarse_inverse.shape[1]
    base = pick_base(halves)
    swap = [(0, 1), (1, 0)]
    surface = lax.ppermute(surface_out[0], "comp", swap)
    sends = lax.ppermute(send_blocks[0], "comp", swap)
    old = old_height.reshape(blocks, LANES)
    owner = fine_owner.reshape(blocks, LANES)
    diagonal = fine_diagonal.reshape(blocks, LANES)
    cdiag = coarse_diagonal.reshape(frows, LANES)
    cowner = coarse_owner.reshape(frows, LANES)

    near1, far1, near2, far2, here = pl.pallas_call(
        pack_kernel,
        out_shape=[
            struct((base + 4 * each, LANES), BF16),
            struct((base + 4 * each, LANES), BF16),
            struct((4 * each, LANES), BF16),
            struct((4 * each, LANES), BF16),
            struct((4 * each, LANES), BF16),
        ],
        in_specs=[VMEM] * 12,
        out_specs=[VMEM] * 5,
        scratch_shapes=[
            pltpu.VMEM((channels * blocks, LANES), F32),
            pltpu.VMEM((base, LANES), F32),
            pltpu.VMEM((base, LANES), F32),
        ],
        compiler_params=PARAMS,
        name="pack",
    )(
        surface, sends, fields[0], old, edge_weight[0], fine_table[0], owner,
        coarse_table[0], coarse_edge[0], cdiag, cowner, coarse_inverse[0],
    )
    one_a, one_b = pair_up(tile_count, 1)
    two_a, two_b = pair_up(tile_count, 2)
    far1 = lax.ppermute(far1, "tile", one_b)
    far2 = lax.ppermute(far2, "tile", two_b)
    near1 = lax.ppermute(near1, "tile", one_a)
    near2 = lax.ppermute(near2, "tile", two_a)

    fresh, force_part, beside_old, edges, window, ends_row, ends_lane = pl.pallas_call(
        stencil_kernel,
        out_shape=[
            struct((fields.shape[1], cells)),
            struct((blocks, LANES)),
            struct((blocks, LANES)),
            struct((3, blocks, LANES)),
            struct((3, blocks, LANES), I32),
            struct((frows, LANES), I32),
            struct((frows, LANES), I32),
        ],
        in_specs=[SMEM, SMEM] + [VMEM] * 5,
        out_specs=[VMEM] * 7,
        scratch_shapes=[pltpu.VMEM((blocks + 16, LANES), F32)],
        compiler_params=PARAMS,
        name="stencil",
    )(level_rate, level_weight, fields[0], edge_weight[0], fine_table[0], old, owner)
    fresh_ends = jnp.concatenate([fresh[:, :LANES], fresh[:, cells - LANES :]], axis=1)

    parts = 5
    summed, force, smooth, source, frame, ends_new, message = pl.pallas_call(
        forward_kernel,
        out_shape=[
            struct((blocks, 8, LANES)),
            struct((blocks, LANES)),
            struct((blocks, LANES)),
            struct((FRAME, LANES)),
            struct((8 * FRAME, LANES)),
            struct((fields.shape[1], 2 * LANES)),
            struct((tile_count, 8, LANES)),
        ],
        in_specs=[SMEM] * 4 + [ANY] + [VMEM] * 20,
        out_specs=[VMEM] * 7,
        scratch_shapes=[
            pltpu.VMEM((entries, LANES, LANES), BF16),
            pltpu.VMEM((4 * entries, LANES), F32),
            pltpu.VMEM((blocks + 16, LANES), F32),
            pltpu.VMEM((blocks, LANES), F32),
            pltpu.VMEM((blocks, LANES), F32),
            pltpu.VMEM((2, base, LANES), F32),
            pltpu.SemaphoreType.DMA((parts,)),
        ],
        compiler_params=PARAMS,
        name="forward",
    )(
        entry_block[0], level_rate, level_weight, flux_weight,
        remap_tiles[0, 0], near1, far1, near2, far2, here, entry_slot[0], fields[0], edges, window,
        old, diagonal, force_part, beside_old, ends_row, ends_lane, fresh_ends,
        coarse_table[0], coarse_edge[0], cdiag, cowner,
    )
    arrived = lax.all_to_all(message, "tile", split_axis=0, concat_axis=0, tiled=True)
    advanced, received, weights = pl.pallas_call(
        prepare_kernel,
        out_shape=[
            struct((fields.shape[1], cells)),
            struct((channels, cells)),
            struct((tile_count, 3 * bottoms, LANES)),
        ],
        in_specs=[ANY] + [VMEM] * 5,
        out_specs=[ANY, VMEM, VMEM],
        scratch_shapes=[
            pltpu.SemaphoreType.DMA((2,)),
            pltpu.VMEM((3 * bottoms, bottoms * tile_count), F32),
        ],
        input_output_aliases={0: 0},
        compiler_params=PARAMS,
        name="prepare",
    )(fresh, ends_new, summed, near1, far1, coarse_inverse[0])
    height = pl.pallas_call(
        functools.partial(backward_kernel, frows),
        out_shape=struct((blocks, LANES)),
        in_specs=[VMEM] * 12,
        out_specs=VMEM,
        scratch_shapes=[
            pltpu.VMEM((FRAME, LANES), F32),
            pltpu.VMEM((blocks + 16, LANES), F32),
            pltpu.VMEM((FRAME, LANES), F32),
        ],
        compiler_params=PARAMS,
        name="backward",
    )(arrived, weights, source, frame, force, smooth, edges, window, diagonal, owner, near1, far1)
    return advanced[None], received[None], height.reshape(1, cells)


def solution(mesh):
    in_specs = (
        P("comp", None, "tile"),
        P("comp", None),
        P("comp", None, "tile"),
        P("comp", "tile"),
        P("comp", None, "tile"),
        P("comp", "tile"),
        P("comp", None),
        P("comp", None),
        P("comp", "tile"),
        P("comp", None, "tile"),
        P("comp", None, "tile"),
        P("comp", "tile"),
        P("comp", "tile"),
        P("comp", "tile", None),
        P("comp", None, "tile"),
        P("comp", "tile", None),
        P("comp", "tile", None),
        P("comp", "tile", None),
        P("comp", "tile", None, None, None),
    )
    out_specs = (P("comp", None, "tile"), P("comp", None, "tile"), P("comp", "tile"))
    return jax.shard_map(
        per_device, mesh=mesh, in_specs=in_specs, out_specs=out_specs, check_vma=False
    )
```

```python
import functools

import jax
import jax.numpy as jnp
from jax import lax
from jax.experimental import pallas as pl
from jax.experimental.pallas import tpu as pltpu
from jax.sharding import PartitionSpec as P

LANES = 128
RELAXATION = 0.8
F32 = jnp.float32
BF16 = jnp.bfloat16
I32 = jnp.int32

FIELD_HI, FIELD_LO = 0, 8
EDGE_HI, EDGE_LO, OLD_HI, OLD_LO = 16, 19, 22, 23
OFFSET, OWNER = 24, 27
CEDGE_HI, CEDGE_LO, CDIAG_HI, CDIAG_LO = 32, 38, 44, 46
COFFSET, COWNER = 48, 54
INVERSE = 56

FRAME, OWN = 32, 8


def gather_lanes(table, index):
    return jnp.take_along_axis(table, index, axis=1)


def wide(row, count=8):
    return jnp.broadcast_to(row, (count, row.shape[1]))


def split3(x):
    high = x.astype(BF16)
    rest = x - high.astype(F32)
    middle = rest.astype(BF16)
    low = (rest - middle.astype(F32)).astype(BF16)
    return high, middle, low


def dot_nt(a, b):
    return lax.dot_general(a, b, (((1,), (1,)), ((), ())), preferred_element_type=F32)


def dot_tn(a, b):
    return lax.dot_general(a, b, (((0,), (0,)), ((), ())), preferred_element_type=F32)


def pick_base(inverse_blocks):
    return -(-(INVERSE + 32 * inverse_blocks) // 16) * 16


def load_kernel(*refs):
    count = (len(refs) - 2) // 2
    sources, targets = refs[:count], refs[count : 2 * count]
    scalars, sems = refs[2 * count :]
    copies = [
        pltpu.make_async_copy(source, target, sems.at[i])
        for i, (source, target) in enumerate(zip(sources, targets))
    ]
    for copy in copies:
        copy.start()
    for copy in copies:
        copy.wait()
    for i, value in enumerate(targets[-3:]):
        width = value.shape[1]
        diagonal = lax.broadcasted_iota(I32, (8, width), 0) == lax.broadcasted_iota(I32, (8, width), 1)
        column = jnp.sum(jnp.where(diagonal, wide(value[...]), 0.0), axis=1, keepdims=True)
        scalars[pl.ds(8 * i, 8), :] = jnp.broadcast_to(column, (8, LANES))


def pack_kernel(
    surface, sends, fields, old, edge, table, owner, ctable, cedge, cdiag, cowner, cinverse,
    near1, far1, near2, far2, here, chunks, left_rows, right_rows,
):
    tile = lax.axis_index("tile")
    even = lax.rem(tile, 2) == 0
    low = lax.rem(tile, 4) < 2
    cells = fields.shape[1]
    blocks = cells // LANES
    frows = ctable.shape[1]
    firsts = frows * LANES
    base = pick_base(cinverse.shape[1] // LANES)
    lane = lax.broadcasted_iota(I32, (1, LANES), 1)

    for rows, at_left in ((right_rows, False), (left_rows, True)):
        start = 0 if at_left else cells - LANES
        part = pl.ds(start, LANES)

        def both(high, low_row, value):
            count = value.shape[0]
            rows[pl.ds(high, count), :] = value
            rows[pl.ds(low_row, count), :] = value - value.astype(BF16).astype(F32)

        def three(ref, row):
            return jnp.concatenate([ref[link, pl.ds(row, 1), :] for link in range(3)], axis=0)

        rows[pl.ds(24, 8), :] = jnp.zeros((8, LANES), F32)
        both(FIELD_HI, FIELD_LO, fields[:, part])
        block = 0 if at_left else blocks - 1
        both(EDGE_HI, EDGE_LO, three(edge, block))
        both(OLD_HI, OLD_LO, old[pl.ds(block, 1), :])
        rows[pl.ds(OFFSET, 3), :] = (three(table, block) - (LANES + start) - lane).astype(F32)
        shift = 0 if at_left else firsts - LANES
        rows[pl.ds(OWNER, 1), :] = (owner[pl.ds(block, 1), :] - shift).astype(F32)
        first = 0 if at_left else frows - 2
        reach = LANES // 8
        for step in range(2):
            both(CEDGE_HI + 3 * step, CEDGE_LO + 3 * step, three(cedge, first + step))
            rows[pl.ds(COFFSET + 3 * step, 3), :] = (
                three(ctable, first + step) - (reach + (first + step) * LANES) - lane
            ).astype(F32)
            both(CDIAG_HI + step, CDIAG_LO + step, cdiag[pl.ds(first + step, 1), :])
            rows[pl.ds(COWNER + step, 1), :] = cowner[pl.ds(first + step, 1), :].astype(F32)
        halves = cinverse.shape[1] // LANES
        for half in range(halves):
            both(
                INVERSE + 16 * half,
                INVERSE + 16 * (halves + half),
                cinverse[:, pl.ds(half * LANES, LANES)],
            )
        end = INVERSE + 32 * halves
        if base > end:
            rows[pl.ds(end, base - end), :] = jnp.zeros((base - end, LANES), F32)

    for block in range(blocks):
        chunks[pl.ds(4 * block, 4), :] = surface[:, pl.ds(block * LANES, LANES)].astype(F32)
    slots = sends.shape[1]
    hot = jnp.where(
        lax.broadcasted_iota(I32, (blocks, slots), 0) == sends[...], 1.0, 0.0
    ).astype(BF16)
    picks = []
    for channel in range(4):
        source = chunks[pl.ds(channel, blocks, stride=4), :].astype(BF16)
        picks.append(dot_tn(hot, source).astype(BF16))
    count = slots // 5

    def chosen(j):
        return jnp.concatenate([p[j * count : (j + 1) * count] for p in picks], axis=0)

    to_right, to_left = chosen(1), chosen(3)
    far_right, far_left = chosen(0), chosen(4)
    here[...] = chosen(2)
    rim_right = right_rows[...].astype(BF16)
    rim_left = left_rows[...].astype(BF16)
    near1[pl.ds(0, base), :] = jnp.where(even, rim_right, rim_left)
    far1[pl.ds(0, base), :] = jnp.where(even, rim_left, rim_right)
    near1[pl.ds(base, 4 * count), :] = jnp.where(even, to_right, to_left)
    far1[pl.ds(base, 4 * count), :] = jnp.where(even, to_left, to_right)
    near2[...] = jnp.where(low, far_right, far_left)
    far2[...] = jnp.where(low, far_left, far_right)


def stencil_kernel(
    here, scalars, fields, edge, table, old, owner, slots, tiles,
    fresh, force, beside_old, window, ends_row, ends_lane, hot, tile_buffer, padded, sem,
):
    del here
    load = pltpu.make_async_copy(tiles, tile_buffer, sem.at[0])
    load.start()
    blocks = old.shape[0]
    levels = fields.shape[0]
    speed = scalars[pl.ds(0, 8), :]
    share = scalars[pl.ds(8, 8), :]
    starts = lax.broadcasted_iota(I32, (blocks, LANES), 0) * LANES
    total = edge[0] + edge[1] + edge[2]
    inverse = 1.0 / total
    for link in range(3):
        window[link] = table[link] - starts
    blank = jnp.zeros((levels, LANES), F32)

    def chunk(block):
        if 0 <= block < blocks:
            return fields[:, pl.ds(block * LANES, LANES)]
        return blank

    before, here, after = blank, chunk(0), chunk(1)
    for block in range(blocks):
        row = slice(block, block + 1)
        beside = jnp.zeros((levels, LANES), F32)
        for link in range(3):
            place = wide(window[link, pl.ds(block, 1), :])
            index = lax.bitwise_and(place, LANES - 1)
            value = jnp.where(
                place < LANES,
                gather_lanes(before, index),
                jnp.where(place < 2 * LANES, gather_lanes(here, index), gather_lanes(after, index)),
            )
            beside = beside + wide(edge[link, pl.ds(block, 1), :]) * value
        result = here + speed * ((beside - wide(total[row]) * here) * wide(inverse[row]))
        fresh[:, pl.ds(block * LANES, LANES)] = result
        force[pl.ds(block, 1), :] = jnp.sum(result * share, axis=0, keepdims=True)
        before, here, after = here, after, chunk(block + 2)

    padded[pl.ds(0, 8), :] = jnp.zeros((8, LANES), F32)
    padded[pl.ds(8 + blocks, 8), :] = jnp.zeros((8, LANES), F32)
    padded[pl.ds(8, blocks), :] = old[...]
    beside_old[...] = neighbour_sum(padded, edge, window, blocks)
    hot[...] = jnp.where(
        lax.broadcasted_iota(I32, hot.shape, 0) == slots[...], 1.0, 0.0
    ).astype(BF16)

    firsts = ends_row.shape[0] * LANES
    ident = lax.broadcasted_iota(I32, ends_row.shape, 0) * LANES + lax.broadcasted_iota(
        I32, ends_row.shape, 1
    )
    count = ends_row.shape[0]
    rows = jnp.zeros(ends_row.shape, I32)
    for block in range(blocks):
        last = jnp.broadcast_to(owner[pl.ds(block, 1), LANES - 1 : LANES], ends_row.shape)
        rows = rows + jnp.where(last <= ident, 1, 0)
    lanes = jnp.zeros(ends_row.shape, I32)
    for bit in (64, 32, 16, 8, 4, 2, 1):
        probe = lanes + (bit - 1)
        value = jnp.full(ends_row.shape, firsts, I32)
        for block in range(blocks):
            value = jnp.where(
                rows == block, gather_lanes(wide(owner[pl.ds(block, 1), :], count), probe), value
            )
        lanes = jnp.where(value <= ident, lanes + bit, lanes)
    ends_row[...] = rows
    ends_lane[...] = lanes
    load.wait()


def neighbour_sum(padded, edges, window, blocks):
    before = padded[pl.ds(7, blocks), :]
    here = padded[pl.ds(8, blocks), :]
    after = padded[pl.ds(9, blocks), :]
    result = jnp.zeros((blocks, LANES), F32)
    for link in range(3):
        place = window[link]
        index = lax.bitwise_and(place, LANES - 1)
        value = jnp.where(
            place < LANES,
            gather_lanes(before, index),
            jnp.where(place < 2 * LANES, gather_lanes(here, index), gather_lanes(after, index)),
        )
        result = result + edges[link] * value
    return result


def first_level_sum(values, frame):
    before = pltpu.roll(values, 1, axis=0)
    after = pltpu.roll(values, FRAME - 1, axis=0)
    lane = lax.broadcasted_iota(I32, (FRAME, LANES), 1)
    result = jnp.zeros((FRAME, LANES), F32)
    for link in range(3):
        place = lane + frame[pl.ds(link * FRAME, FRAME), :].astype(I32)
        index = lax.bitwise_and(place, LANES - 1)
        value = jnp.where(
            place < 0,
            gather_lanes(before, index),
            jnp.where(place >= LANES, gather_lanes(after, index), gather_lanes(values, index)),
        )
        result = result + frame[pl.ds((3 + link) * FRAME, FRAME), :] * value
    return result


def previous_one(values):
    rolled = pltpu.roll(values, 1, axis=1)
    above = pltpu.roll(rolled, 1, axis=0)
    lane = lax.broadcasted_iota(I32, values.shape, 1)
    row = lax.broadcasted_iota(I32, values.shape, 0)
    return jnp.where(lane > 0, rolled, jnp.where(row > 0, above, 0.0))


def triangle():
    return jnp.where(
        lax.broadcasted_iota(I32, (LANES, LANES), 0) < lax.broadcasted_iota(I32, (LANES, LANES), 1),
        1.0,
        0.0,
    ).astype(BF16)


def prefix(values):
    ones = jnp.ones((LANES, LANES), BF16)
    right = jnp.concatenate([triangle(), ones], axis=1)
    count = values.shape[0]
    out = jnp.dot(
        jnp.concatenate(split3(values), axis=0), right, preferred_element_type=F32
    )
    out = out[:count] + out[count : 2 * count] + out[2 * count :]
    return out[:, :LANES], out[:, LANES:]


def forward_kernel(
    entry_block_any, tiles, scalars, near1, far1, near2, far2, here, hot, fields, edges, window, old,
    diagonal, force_part, beside_old, ends_row, ends_lane, fresh, ctable, cedge, cdiag, cowner,
    summed, force_out, smooth_out, source_out, frame, ends_out, message,
    entry_block, picked, padded, prefixed, totals, arrivals, sem,
):
    fetch = pltpu.make_async_copy(entry_block_any, entry_block, sem.at[0])
    fetch.start()
    tile = lax.axis_index("tile")
    tile_count = lax.axis_size("tile")
    even = lax.rem(tile, 2) == 0
    low = lax.rem(tile, 4) < 2
    entries = tiles.shape[0]
    blocks = old.shape[0]

    base = near1.shape[0] - near2.shape[0]
    near, far = near1[...], far1[...]
    from_left = jnp.where(even, far, near)
    from_right = jnp.where(even, near, far)
    two_near, two_far = near2[...], far2[...]
    j0 = jnp.where(low, two_far, two_near)
    j4 = jnp.where(low, two_near, two_far)
    j1, j3, j2 = from_left[base:], from_right[base:], here[...]
    each = j0.shape[0] // 4
    for channel in range(4):
        span = slice(channel * each, (channel + 1) * each)
        source = jnp.concatenate([j[span] for j in (j0, j1, j2, j3, j4)], axis=0)
        picked[pl.ds(channel, entries, stride=4), :] = dot_tn(hot[...], source)

    arrivals[0] = from_left[:base].astype(F32)
    arrivals[1] = from_right[:base].astype(F32)

    summed[...] = jnp.zeros(summed.shape, F32)
    fetch.wait()

    def pair(number, carry):
        entry = 2 * number
        rows = picked[pl.ds(pl.multiple_of(4 * entry, 8), 8), :].astype(BF16)
        first = dot_nt(rows, tiles[entry])
        second = dot_nt(rows, tiles[entry + 1])
        summed[entry_block[0, entry], pl.ds(0, 4), :] += first[0:4]
        summed[entry_block[0, entry + 1], pl.ds(4, 4), :] += second[4:8]
        return carry

    lax.fori_loop(0, entries // 2, pair, 0, unroll=8)

    speed = scalars[pl.ds(0, 8), :]
    share = scalars[pl.ds(8, 8), :]
    force_out[...] = force_part[...]
    padded[pl.ds(0, 8), :] = jnp.zeros((8, LANES), F32)
    padded[pl.ds(8 + blocks, 8), :] = jnp.zeros((8, LANES), F32)
    beside_extra = []
    for side, block, target in ((0, 0, 0), (1, blocks - 1, 2)):
        halo = arrivals[side, pl.ds(FIELD_HI, 8), :] + arrivals[side, pl.ds(FIELD_LO, 8), :]
        halo_old = arrivals[side, pl.ds(OLD_HI, 1), :] + arrivals[side, pl.ds(OLD_LO, 1), :]
        total = edges[0, pl.ds(block, 1), :] + edges[1, pl.ds(block, 1), :] + edges[2, pl.ds(block, 1), :]
        extra = jnp.zeros((8, LANES), F32)
        extra_old = jnp.zeros((8, LANES), F32)
        for link in range(3):
            place = wide(window[link, pl.ds(block, 1), :])
            index = lax.bitwise_and(place, LANES - 1)
            weight = jnp.where(
                lax.shift_right_logical(place, 7) == target, wide(edges[link, pl.ds(block, 1), :]), 0.0
            )
            extra = extra + weight * gather_lanes(halo, index)
            extra_old = extra_old + weight * gather_lanes(wide(halo_old), index)
        change = speed * extra / wide(total)
        ends_out[:, pl.ds(side * LANES, LANES)] = fresh[:, pl.ds(block * LANES, LANES)] + change
        force_out[pl.ds(block, 1), :] += jnp.sum(change * share, axis=0, keepdims=True)
        beside_extra.append(extra_old[0:1])

    force = force_out[...]
    for channel in range(4):
        value = summed[:, channel, :] + summed[:, channel + 4, :]
        force = force + scalars[pl.ds(16 + channel, 1), :] * value
    force_out[...] = force
    total = diagonal[...] + edges[0] + edges[1] + edges[2]
    smooth_out[...] = beside_old[...]
    smooth_out[pl.ds(0, 1), :] += beside_extra[0]
    smooth_out[pl.ds(blocks - 1, 1), :] += beside_extra[1]
    previous = old[...]
    smooth = previous + RELAXATION * (force - (total * previous - smooth_out[...])) / total
    smooth_out[...] = smooth
    padded[pl.ds(8, blocks), :] = smooth
    residual = force - total * smooth + neighbour_sum(padded, edges, window, blocks)

    inner, whole = prefix(residual)
    prefixed[...] = inner
    totals[...] = whole
    rows, lanes = ends_row[...], ends_lane[...]
    count = rows.shape[0]
    run = jnp.zeros((count, LANES), F32)
    ends = jnp.zeros((count, LANES), F32)
    for block in range(blocks):
        value = gather_lanes(wide(prefixed[pl.ds(block, 1), :], count), lanes) + run
        ends = jnp.where(rows == block, value, ends)
        run = run + wide(totals[pl.ds(block, 1), :], count)
    ends = jnp.where(rows == blocks, run, ends)
    own_source = ends - previous_one(ends)

    lane = lax.broadcasted_iota(I32, (1, LANES), 1)
    rim_rows, rim_counts = [], []
    for side in range(2):
        inside = padded[pl.ds(8 if side == 0 else 7 + blocks, 1), :]
        value = jnp.zeros((1, LANES), F32)
        for link in range(3):
            place = lane + arrivals[side, pl.ds(OFFSET + link, 1), :].astype(I32)
            index = lax.bitwise_and(place, LANES - 1)
            reached = (place >= LANES) if side == 0 else (place < 0)
            weight = arrivals[side, pl.ds(EDGE_HI + link, 1), :] + arrivals[side, pl.ds(EDGE_LO + link, 1), :]
            value = value + jnp.where(
                wide(reached.astype(I32)) > 0,
                wide(weight) * gather_lanes(wide(inside), wide(index)),
                0.0,
            )[0:1]
        rim_rows.append(value)
        owners = arrivals[side, pl.ds(OWNER, 1), :].astype(I32)
        below = jnp.where(
            lax.broadcasted_iota(I32, (LANES, LANES), 0) >= owners, 1.0, 0.0
        ).astype(BF16)
        rim_counts.append(dot_nt(jnp.ones((8, LANES), BF16), below))
    rim_inner, rim_whole = prefix(jnp.concatenate([wide(r) for r in rim_rows], axis=0))
    rim_source = []
    for side in range(2):
        place = rim_counts[side].astype(I32)
        index = lax.bitwise_and(place, LANES - 1)
        value = gather_lanes(rim_inner[8 * side : 8 * side + 8], index)
        value = jnp.where(place >= LANES, rim_whole[8 * side : 8 * side + 8], value)
        shifted = pltpu.roll(value, 1, axis=1)
        first = lax.broadcasted_iota(I32, (8, LANES), 1) == 0
        rim_source.append((value - jnp.where(first, 0.0, shifted))[0:1])

    frows = own_source.shape[0]
    source_out[...] = jnp.zeros((FRAME, LANES), F32)
    source_out[pl.ds(OWN, frows), :] = own_source
    source_out[pl.ds(OWN - 1, 1), :] = rim_source[0]
    source_out[pl.ds(OWN + frows, 1), :] = rim_source[1]
    reach = LANES // 8
    frame[...] = jnp.zeros(frame.shape, F32)
    frame[pl.ds(6 * FRAME, FRAME), :] = jnp.ones((FRAME, LANES), F32)
    frame[pl.ds(7 * FRAME, FRAME), :] = jnp.full((FRAME, LANES), 127.0, F32)
    bottoms = 16
    at_cell = lax.broadcasted_iota(I32, (frows, LANES), 0) * LANES + lax.broadcasted_iota(
        I32, (frows, LANES), 1
    )
    for link in range(3):
        frame[pl.ds(link * FRAME + OWN, frows), :] = (ctable[link] - reach - at_cell).astype(F32)
        frame[pl.ds((3 + link) * FRAME + OWN, frows), :] = cedge[link]
    frame[pl.ds(6 * FRAME + OWN, frows), :] = cdiag[...]
    frame[pl.ds(7 * FRAME + OWN, frows), :] = (cowner[...] + bottoms).astype(F32)
    for side in range(2):
        for row in range(2):
            at = (OWN - 2 + row) if side == 0 else (OWN + frows + row)
            for link in range(3):
                put = 3 * row + link
                frame[pl.ds(link * FRAME + at, 1), :] = arrivals[side, pl.ds(COFFSET + put, 1), :]
                frame[pl.ds((3 + link) * FRAME + at, 1), :] = (
                    arrivals[side, pl.ds(CEDGE_HI + put, 1), :] + arrivals[side, pl.ds(CEDGE_LO + put, 1), :]
                )
            frame[pl.ds(6 * FRAME + at, 1), :] = (
                arrivals[side, pl.ds(CDIAG_HI + row, 1), :] + arrivals[side, pl.ds(CDIAG_LO + row, 1), :]
            )
            frame[pl.ds(7 * FRAME + at, 1), :] = arrivals[side, pl.ds(COWNER + row, 1), :] + (
                2.0 * bottoms * side
            )
    for link in range(3):
        frame[pl.ds(6 * FRAME, FRAME), :] += frame[pl.ds((3 + link) * FRAME, FRAME), :]
    source = source_out[...]
    first = RELAXATION * source / frame[pl.ds(6 * FRAME, FRAME), :]
    residual = (1.0 - RELAXATION) * source + first_level_sum(first, frame)
    codes = frame[pl.ds(7 * FRAME, FRAME), :].astype(I32)
    pieces = split3(residual)
    left_side, right_side = [], []
    bins = lax.broadcasted_iota(I32, (LANES, LANES), 0)
    for row in range(OWN - 2, OWN + frows + 2):
        left_side.append(jnp.concatenate([p[row : row + 1] for p in pieces], axis=0))
        right_side.append(
            jnp.where(bins == codes[row : row + 1], 1.0, 0.0).astype(BF16)
        )
    bottom = dot_nt(jnp.concatenate(left_side, axis=1), jnp.concatenate(right_side, axis=1))
    bottom = bottom[0:1] + bottom[1:2] + bottom[2:3]
    bottom = jnp.where(lane < 3 * bottoms, bottom, 0.0)

    to_left = jnp.concatenate(
        [bottom, padded[pl.ds(8, 1), :], own_source[0:2], rim_source[0], jnp.zeros((3, LANES), F32)], axis=0
    )
    to_right = jnp.concatenate(
        [bottom, padded[pl.ds(7 + blocks, 1), :], own_source[frows - 2 : frows], rim_source[1], jnp.zeros((3, LANES), F32)],
        axis=0,
    )
    for other in range(message.shape[0]):
        message[other] = to_right
    message[lax.rem(tile + tile_count - 1, tile_count)] = to_left


def prepare_kernel(
    fresh, ends_new, summed, near1, far1, cinverse, fresh_out, received, weights, sem, extended
):
    tile = lax.axis_index("tile")
    even = lax.rem(tile, 2) == 0
    cells = fresh_out.shape[1]
    copies = [
        pltpu.make_async_copy(
            ends_new.at[:, pl.ds(side * LANES, LANES)],
            fresh_out.at[:, pl.ds(side * (cells - LANES), LANES)],
            sem.at[side],
        )
        for side in range(2)
    ]
    middle = pl.ds(LANES, cells - 2 * LANES)
    copies.append(pltpu.make_async_copy(fresh.at[:, middle], fresh_out.at[:, middle], sem.at[2]))
    for copy in copies:
        copy.start()
    blocks = summed.shape[0]
    for block in range(blocks):
        received[:, pl.ds(block * LANES, LANES)] = summed[block, pl.ds(0, 4), :] + summed[block, pl.ds(4, 4), :]
    bottoms, size = cinverse.shape
    halves = size // LANES
    near = near1[pl.ds(INVERSE, 32 * halves), :].astype(F32)
    far = far1[pl.ds(INVERSE, 32 * halves), :].astype(F32)
    left = jnp.where(even, far, near)
    right = jnp.where(even, near, far)
    for half in range(halves):
        part = pl.ds(half * LANES, LANES)
        for at, block in ((0, left), (2, right)):
            extended[pl.ds(at * bottoms, bottoms), part] = (
                block[16 * half : 16 * half + 16]
                + block[16 * (halves + half) : 16 * (halves + half) + 16]
            )
        extended[pl.ds(bottoms, bottoms), part] = cinverse[:, part]
    table = extended[...]
    lane = lax.broadcasted_iota(I32, (3 * bottoms, LANES), 1)
    for other in range(weights.shape[0]):
        shift = (size - (other - 1) * bottoms) % size
        turned = pltpu.roll(table, shift, axis=1) if shift else table
        weights[other] = jnp.where(lane < 3 * bottoms, turned[:, :LANES], 0.0)
    for copy in copies:
        copy.wait()


def backward_kernel(
    frame_rows, arrived, weights, source, frame, force, smooth, edges, window, diagonal, owner, near1, far1,
    height, frame_source, padded, third_rows,
):
    tile = lax.axis_index("tile")
    tile_count = lax.axis_size("tile")
    even = lax.rem(tile, 2) == 0
    blocks = force.shape[0]
    left = arrived[lax.rem(tile + tile_count - 1, tile_count)]
    right = arrived[lax.rem(tile + 1, tile_count)]
    count = weights.shape[1]
    partial = jnp.zeros((count, LANES), F32)
    for other in range(weights.shape[0]):
        partial = partial + weights[other] * wide(arrived[other, pl.ds(0, 1), :], count)
    partial = jnp.concatenate([partial, jnp.zeros((LANES - count, LANES), F32)], axis=0)
    ones = jnp.ones((8, LANES), BF16)
    pieces = split3(partial)
    bottom = dot_nt(ones, pieces[0]) + dot_nt(ones, pieces[1]) + dot_nt(ones, pieces[2])

    frows = frame_rows
    frame_source[...] = source[...]
    frame_source[pl.ds(OWN - 2, 2), :] += left[2:4]
    frame_source[pl.ds(OWN, 1), :] += left[4:5]
    frame_source[pl.ds(OWN + frows - 1, 1), :] += right[4:5]
    frame_source[pl.ds(OWN + frows, 2), :] += right[2:4]
    total_source = frame_source[...]
    total = frame[pl.ds(6 * FRAME, FRAME), :]
    codes = frame[pl.ds(7 * FRAME, FRAME), :].astype(I32)
    second = RELAXATION * total_source / total + gather_lanes(wide(bottom[0:1], FRAME), codes)
    third = second + RELAXATION * (
        total_source - total * second + first_level_sum(second, frame)
    ) / total
    third_rows[...] = third

    owners = owner[...]
    index = lax.bitwise_and(owners, LANES - 1)
    which = lax.shift_right_logical(owners, 7)
    corrected = jnp.zeros((blocks, LANES), F32)
    for row in range(frows):
        corrected = jnp.where(
            which == row, gather_lanes(wide(third_rows[pl.ds(OWN + row, 1), :], blocks), index), corrected
        )
    corrected = smooth[...] + corrected
    padded[pl.ds(8, blocks), :] = corrected
    near = near1[pl.ds(16, 16), :].astype(F32)
    far = far1[pl.ds(16, 16), :].astype(F32)
    left_owner = jnp.where(even, far, near)[OWNER - 16 : OWNER - 15].astype(I32)
    right_owner = jnp.where(even, near, far)[OWNER - 16 : OWNER - 15].astype(I32)
    left_rim = left[1:2] + gather_lanes(wide(third_rows[pl.ds(OWN - 1, 1), :]), wide(left_owner))[0:1]
    right_rim = right[1:2] + gather_lanes(wide(third_rows[pl.ds(OWN + frows, 1), :]), wide(right_owner))[0:1]
    padded[pl.ds(7, 1), :] = left_rim
    padded[pl.ds(8 + blocks, 1), :] = right_rim
    fine_total = diagonal[...] + edges[0] + edges[1] + edges[2]
    beside = neighbour_sum(padded, edges, window, blocks)
    height[...] = corrected + RELAXATION * (force[...] - (fine_total * corrected - beside)) / fine_total


def in_hbm(array):
    return pltpu.with_memory_space_constraint(array, pltpu.HBM)


def struct(shape, dtype=F32):
    return jax.ShapeDtypeStruct(shape, dtype)


VMEM = pl.BlockSpec(memory_space=pltpu.VMEM)
SMEM = pl.BlockSpec(memory_space=pltpu.SMEM)
ANY = pl.BlockSpec(memory_space=pltpu.HBM)
PARAMS = pltpu.CompilerParams(vmem_limit_bytes=48 * 1024 * 1024)


def pair_up(count, distance):
    period = 2 * distance
    result = []
    for start in (0, distance):
        pairs = []
        for i in range(count):
            if (i - start) % period < distance:
                pairs += [(i, (i + distance) % count), ((i + distance) % count, i)]
        result.append(pairs)
    return result


def per_device(
    fields, level_rate, edge_weight, fine_diagonal, fine_table, old_height, level_weight,
    flux_weight, fine_owner, coarse_table, coarse_edge, coarse_diagonal, coarse_owner,
    coarse_inverse, surface_out, send_blocks, entry_slot, entry_block, remap_tiles,
):
    tile_count = lax.axis_size("tile")
    cells = fields.shape[2]
    blocks = cells // LANES
    firsts = coarse_diagonal.shape[1]
    frows = firsts // LANES
    entries = entry_slot.shape[2]
    channels = surface_out.shape[1]
    slots = send_blocks.shape[2]
    each = slots // 5
    halves = coarse_inverse.shape[2] // LANES
    bottoms = coarse_inverse.shape[1]
    base = pick_base(halves)
    swap = [(0, 1), (1, 0)]
    surface = lax.ppermute(surface_out[0], "comp", swap)
    sends = lax.ppermute(send_blocks[0], "comp", swap)
    raw = (
        fields[0],
        old_height.reshape(blocks, LANES),
        edge_weight[0].reshape(3, blocks, LANES),
        fine_table[0].reshape(3, blocks, LANES),
        fine_owner.reshape(blocks, LANES),
        fine_diagonal.reshape(blocks, LANES),
        coarse_table[0].reshape(3, frows, LANES),
        coarse_edge[0].reshape(3, frows, LANES),
        coarse_diagonal.reshape(frows, LANES),
        coarse_owner.reshape(frows, LANES),
        coarse_inverse[0],
        entry_slot[0],
        level_rate,
        level_weight,
        flux_weight,
    )
    loaded = pl.pallas_call(
        load_kernel,
        out_shape=[struct(x.shape, x.dtype) for x in raw] + [struct((24, LANES))],
        in_specs=[ANY] * len(raw),
        out_specs=[VMEM] * (len(raw) + 1),
        scratch_shapes=[pltpu.SemaphoreType.DMA((len(raw),))],
        compiler_params=PARAMS,
        name="load",
    )(*[in_hbm(x) for x in raw])
    current, old, edges, table, owner, diagonal, ctable, cedge, cdiag, cowner, cinverse, slot = loaded[:12]
    scalars = loaded[-1]

    near1, far1, near2, far2, here = pl.pallas_call(
        pack_kernel,
        out_shape=[
            struct((base + 4 * each, LANES), BF16),
            struct((base + 4 * each, LANES), BF16),
            struct((4 * each, LANES), BF16),
            struct((4 * each, LANES), BF16),
            struct((4 * each, LANES), BF16),
        ],
        in_specs=[VMEM] * 12,
        out_specs=[VMEM] * 5,
        scratch_shapes=[
            pltpu.VMEM((channels * blocks, LANES), F32),
            pltpu.VMEM((base, LANES), F32),
            pltpu.VMEM((base, LANES), F32),
        ],
        compiler_params=PARAMS,
        name="pack",
    )(
        surface, sends, current, old, edges, table, owner, ctable, cedge, cdiag, cowner, cinverse,
    )
    one_a, one_b = pair_up(tile_count, 1)
    two_a, two_b = pair_up(tile_count, 2)
    far1 = lax.ppermute(far1, "tile", one_b)
    far2 = lax.ppermute(far2, "tile", two_b)
    near1 = lax.ppermute(near1, "tile", one_a)
    near2 = lax.ppermute(near2, "tile", two_a)

    fresh, force_part, beside_old, window, ends_row, ends_lane, hot, tiles = pl.pallas_call(
        stencil_kernel,
        out_shape=[
            struct((fields.shape[1], cells)),
            struct((blocks, LANES)),
            struct((blocks, LANES)),
            struct((3, blocks, LANES), I32),
            struct((frows, LANES), I32),
            struct((frows, LANES), I32),
            struct((slots, entries), BF16),
            struct(remap_tiles.shape[2:], BF16),
        ],
        in_specs=[VMEM] * 8 + [ANY],
        out_specs=[VMEM] * 8,
        scratch_shapes=[pltpu.VMEM((blocks + 16, LANES), F32), pltpu.SemaphoreType.DMA((1,))],
        compiler_params=PARAMS,
        name="stencil",
    )(here, scalars, current, edges, table, old, owner, slot, in_hbm(remap_tiles[0, 0]))

    summed, force, smooth, source, frame, ends_new, message = pl.pallas_call(
        forward_kernel,
        out_shape=[
            struct((blocks, 8, LANES)),
            struct((blocks, LANES)),
            struct((blocks, LANES)),
            struct((FRAME, LANES)),
            struct((8 * FRAME, LANES)),
            struct((fields.shape[1], 2 * LANES)),
            struct((tile_count, 8, LANES)),
        ],
        in_specs=[ANY] + [VMEM] * 22,
        out_specs=[VMEM] * 7,
        scratch_shapes=[
            pltpu.SMEM((1, entries), I32),
            pltpu.VMEM((4 * entries, LANES), F32),
            pltpu.VMEM((blocks + 16, LANES), F32),
            pltpu.VMEM((blocks, LANES), F32),
            pltpu.VMEM((blocks, LANES), F32),
            pltpu.VMEM((2, base, LANES), F32),
            pltpu.SemaphoreType.DMA((1,)),
        ],
        compiler_params=PARAMS,
        name="forward",
    )(
        in_hbm(entry_block[0]), tiles, scalars, near1, far1, near2, far2, here, hot, current, edges, window, old,
        diagonal, force_part, beside_old, ends_row, ends_lane, fresh, ctable, cedge, cdiag, cowner,
    )
    arrived = lax.all_to_all(message, "tile", split_axis=0, concat_axis=0, tiled=True)
    advanced, received, weights = pl.pallas_call(
        prepare_kernel,
        out_shape=[
            struct((fields.shape[1], cells)),
            struct((channels, cells)),
            struct((tile_count, 3 * bottoms, LANES)),
        ],
        in_specs=[VMEM] * 6,
        out_specs=[ANY, VMEM, VMEM],
        scratch_shapes=[
            pltpu.SemaphoreType.DMA((3,)),
            pltpu.VMEM((3 * bottoms, bottoms * tile_count), F32),
        ],
        compiler_params=PARAMS,
        name="prepare",
    )(fresh, ends_new, summed, near1, far1, cinverse)
    height = pl.pallas_call(
        functools.partial(backward_kernel, frows),
        out_shape=struct((blocks, LANES)),
        in_specs=[VMEM] * 12,
        out_specs=VMEM,
        scratch_shapes=[
            pltpu.VMEM((FRAME, LANES), F32),
            pltpu.VMEM((blocks + 16, LANES), F32),
            pltpu.VMEM((FRAME, LANES), F32),
        ],
        compiler_params=PARAMS,
        name="backward",
    )(arrived, weights, source, frame, force, smooth, edges, window, diagonal, owner, near1, far1)
    return advanced[None], received[None], height.reshape(1, cells)


def solution(mesh):
    in_specs = (
        P("comp", None, "tile"),
        P("comp", None),
        P("comp", None, "tile"),
        P("comp", "tile"),
        P("comp", None, "tile"),
        P("comp", "tile"),
        P("comp", None),
        P("comp", None),
        P("comp", "tile"),
        P("comp", None, "tile"),
        P("comp", None, "tile"),
        P("comp", "tile"),
        P("comp", "tile"),
        P("comp", "tile", None),
        P("comp", None, "tile"),
        P("comp", "tile", None),
        P("comp", "tile", None),
        P("comp", "tile", None),
        P("comp", "tile", None, None, None),
    )
    out_specs = (P("comp", None, "tile"), P("comp", None, "tile"), P("comp", "tile"))
    return jax.shard_map(
        per_device, mesh=mesh, in_specs=in_specs, out_specs=out_specs, check_vma=False
    )
```

```python
import functools
import math

import jax
import jax.numpy as jnp
from jax import lax
from jax.experimental import pallas as pl
from jax.experimental.pallas import tpu as pltpu
from jax.sharding import PartitionSpec as P

LANES = 128
RELAXATION = 0.8
F32 = jnp.float32
BF16 = jnp.bfloat16
I32 = jnp.int32

FIELD_HI, FIELD_LO = 0, 8
EDGE_HI, EDGE_LO, OLD_HI, OLD_LO = 16, 19, 22, 23
OFFSET, OWNER = 24, 27
CEDGE_HI, CEDGE_LO, CDIAG_HI, CDIAG_LO = 32, 38, 44, 46
COFFSET, COWNER = 48, 54
INVERSE = 56

FRAME, OWN = 32, 8


def gather_lanes(table, index):
    return jnp.take_along_axis(table, index, axis=1)


def wide(row, count=8):
    return jnp.broadcast_to(row, (count, row.shape[1]))


def split3(x):
    high = x.astype(BF16)
    rest = x - high.astype(F32)
    middle = rest.astype(BF16)
    low = (rest - middle.astype(F32)).astype(BF16)
    return high, middle, low


def dot_nt(a, b):
    return lax.dot_general(a, b, (((1,), (1,)), ((), ())), preferred_element_type=F32)


def dot_tn(a, b):
    return lax.dot_general(a, b, (((0,), (0,)), ((), ())), preferred_element_type=F32)


def pick_base(inverse_blocks):
    return -(-(INVERSE + 32 * inverse_blocks) // 16) * 16


def load_kernel(*refs):
    count = (len(refs) - 2) // 2
    sources, kept, scalars = refs[:count], refs[count : 2 * count - 3], refs[2 * count - 3]
    spread, sems = refs[2 * count - 2 : 2 * count + 1], refs[2 * count + 1]
    copies = [
        pltpu.make_async_copy(source, target, sems.at[i])
        for i, (source, target) in enumerate(zip(sources, kept + spread))
    ]
    for copy in copies:
        copy.start()
    for copy in copies:
        copy.wait()
    for i, value in enumerate(spread):
        width = value.shape[1]
        diagonal = lax.broadcasted_iota(I32, (8, width), 0) == lax.broadcasted_iota(I32, (8, width), 1)
        column = jnp.sum(jnp.where(diagonal, wide(value[...]), 0.0), axis=1, keepdims=True)
        scalars[pl.ds(8 * i, 8), :] = jnp.broadcast_to(column, (8, LANES))


def pack_kernel(
    surface, sends, fields, old, edge, table, owner, ctable, cedge, cdiag, cowner, cinverse,
    near1, far1, near2, far2, here, chunks, left_rows, right_rows,
):
    tile = lax.axis_index("tile")
    even = lax.rem(tile, 2) == 0
    low = lax.rem(tile, 4) < 2
    cells = fields.shape[1]
    blocks = cells // LANES
    frows = ctable.shape[1]
    firsts = frows * LANES
    base = pick_base(cinverse.shape[1] // LANES)
    lane = lax.broadcasted_iota(I32, (1, LANES), 1)

    for rows, at_left in ((right_rows, False), (left_rows, True)):
        start = 0 if at_left else cells - LANES
        part = pl.ds(start, LANES)

        def both(high, low_row, value):
            count = value.shape[0]
            rows[pl.ds(high, count), :] = value
            rows[pl.ds(low_row, count), :] = value - value.astype(BF16).astype(F32)

        def three(ref, row):
            return jnp.concatenate([ref[link, pl.ds(row, 1), :] for link in range(3)], axis=0)

        rows[pl.ds(24, 8), :] = jnp.zeros((8, LANES), F32)
        both(FIELD_HI, FIELD_LO, fields[:, part])
        block = 0 if at_left else blocks - 1
        both(EDGE_HI, EDGE_LO, three(edge, block))
        both(OLD_HI, OLD_LO, old[pl.ds(block, 1), :])
        rows[pl.ds(OFFSET, 3), :] = (three(table, block) - (LANES + start) - lane).astype(F32)
        shift = 0 if at_left else firsts - LANES
        rows[pl.ds(OWNER, 1), :] = (owner[pl.ds(block, 1), :] - shift).astype(F32)
        first = 0 if at_left else frows - 2
        reach = LANES // 8
        for step in range(2):
            both(CEDGE_HI + 3 * step, CEDGE_LO + 3 * step, three(cedge, first + step))
            rows[pl.ds(COFFSET + 3 * step, 3), :] = (
                three(ctable, first + step) - (reach + (first + step) * LANES) - lane
            ).astype(F32)
            both(CDIAG_HI + step, CDIAG_LO + step, cdiag[pl.ds(first + step, 1), :])
            rows[pl.ds(COWNER + step, 1), :] = cowner[pl.ds(first + step, 1), :].astype(F32)
        halves = cinverse.shape[1] // LANES
        for half in range(halves):
            both(
                INVERSE + 16 * half,
                INVERSE + 16 * (halves + half),
                cinverse[:, pl.ds(half * LANES, LANES)],
            )
        end = INVERSE + 32 * halves
        if base > end:
            rows[pl.ds(end, base - end), :] = jnp.zeros((base - end, LANES), F32)

    for block in range(blocks):
        chunks[pl.ds(4 * block, 4), :] = surface[:, pl.ds(block * LANES, LANES)].astype(F32)
    slots = sends.shape[1]
    hot = jnp.where(
        lax.broadcasted_iota(I32, (blocks, slots), 0) == sends[...], 1.0, 0.0
    ).astype(BF16)
    picks = []
    for channel in range(4):
        source = chunks[pl.ds(channel, blocks, stride=4), :].astype(BF16)
        picks.append(dot_tn(hot, source).astype(BF16))
    count = slots // 5

    def chosen(j):
        return jnp.concatenate([p[j * count : (j + 1) * count] for p in picks], axis=0)

    to_right, to_left = chosen(1), chosen(3)
    far_right, far_left = chosen(0), chosen(4)
    here[...] = chosen(2)
    rim_right = right_rows[...].astype(BF16)
    rim_left = left_rows[...].astype(BF16)
    near1[pl.ds(0, base), :] = jnp.where(even, rim_right, rim_left)
    far1[pl.ds(0, base), :] = jnp.where(even, rim_left, rim_right)
    near1[pl.ds(base, 4 * count), :] = jnp.where(even, to_right, to_left)
    far1[pl.ds(base, 4 * count), :] = jnp.where(even, to_left, to_right)
    near2[...] = jnp.where(low, far_right, far_left)
    far2[...] = jnp.where(low, far_left, far_right)


def stencil_kernel(
    here, scalars, fields, edge, table, old, owner, slots, entry_block, tiles,
    fresh, force, beside_old, window, ends_row, ends_lane, hot, member, tile_buffer, padded, sems,
):
    del here
    parts = sems.shape[0]
    step = tiles.shape[0] // parts
    loads = [
        pltpu.make_async_copy(
            tiles.at[pl.ds(part * step, step)], tile_buffer.at[pl.ds(part * step, step)], sems.at[part]
        )
        for part in range(parts)
    ]
    for load in loads:
        load.start()
    blocks = old.shape[0]
    levels = fields.shape[0]
    speed = scalars[pl.ds(0, 8), :]
    share = scalars[pl.ds(8, 8), :]
    starts = lax.broadcasted_iota(I32, (blocks, LANES), 0) * LANES
    total = edge[0] + edge[1] + edge[2]
    inverse = 1.0 / total
    for link in range(3):
        window[link] = table[link] - starts
    blank = jnp.zeros((levels, LANES), F32)

    def chunk(block):
        if 0 <= block < blocks:
            return fields[:, pl.ds(block * LANES, LANES)]
        return blank

    before, here, after = blank, chunk(0), chunk(1)
    for block in range(blocks):
        row = slice(block, block + 1)
        beside = jnp.zeros((levels, LANES), F32)
        for link in range(3):
            place = wide(window[link, pl.ds(block, 1), :])
            index = lax.bitwise_and(place, LANES - 1)
            value = jnp.where(
                place < LANES,
                gather_lanes(before, index),
                jnp.where(place < 2 * LANES, gather_lanes(here, index), gather_lanes(after, index)),
            )
            beside = beside + wide(edge[link, pl.ds(block, 1), :]) * value
        result = here + speed * ((beside - wide(total[row]) * here) * wide(inverse[row]))
        fresh[:, pl.ds(block * LANES, LANES)] = result
        force[pl.ds(block, 1), :] = jnp.sum(result * share, axis=0, keepdims=True)
        before, here, after = here, after, chunk(block + 2)

    padded[pl.ds(0, 8), :] = jnp.zeros((8, LANES), F32)
    padded[pl.ds(8 + blocks, 8), :] = jnp.zeros((8, LANES), F32)
    padded[pl.ds(8, blocks), :] = old[...]
    beside_old[...] = neighbour_sum(padded, edge, window, blocks)
    hot[...] = jnp.where(
        lax.broadcasted_iota(I32, hot.shape, 0) == slots[...], 1.0, 0.0
    ).astype(BF16)
    member[...] = jnp.where(
        lax.broadcasted_iota(I32, member.shape, 0) == entry_block[...], 1.0, 0.0
    ).astype(BF16)

    firsts = ends_row.shape[0] * LANES
    ident = lax.broadcasted_iota(I32, ends_row.shape, 0) * LANES + lax.broadcasted_iota(
        I32, ends_row.shape, 1
    )
    count = ends_row.shape[0]
    rows = jnp.zeros(ends_row.shape, I32)
    for block in range(blocks):
        last = jnp.broadcast_to(owner[pl.ds(block, 1), LANES - 1 : LANES], ends_row.shape)
        rows = rows + jnp.where(last <= ident, 1, 0)
    lanes = jnp.zeros(ends_row.shape, I32)
    for bit in (64, 32, 16, 8, 4, 2, 1):
        probe = lanes + (bit - 1)
        value = jnp.full(ends_row.shape, firsts, I32)
        for block in range(blocks):
            value = jnp.where(
                rows == block, gather_lanes(wide(owner[pl.ds(block, 1), :], count), probe), value
            )
        lanes = jnp.where(value <= ident, lanes + bit, lanes)
    ends_row[...] = rows
    ends_lane[...] = lanes
    for load in loads:
        load.wait()


def neighbour_sum(padded, edges, window, blocks):
    before = padded[pl.ds(7, blocks), :]
    here = padded[pl.ds(8, blocks), :]
    after = padded[pl.ds(9, blocks), :]
    result = jnp.zeros((blocks, LANES), F32)
    for link in range(3):
        place = window[link]
        index = lax.bitwise_and(place, LANES - 1)
        value = jnp.where(
            place < LANES,
            gather_lanes(before, index),
            jnp.where(place < 2 * LANES, gather_lanes(here, index), gather_lanes(after, index)),
        )
        result = result + edges[link] * value
    return result


def first_level_sum(values, frame):
    before = pltpu.roll(values, 1, axis=0)
    after = pltpu.roll(values, FRAME - 1, axis=0)
    lane = lax.broadcasted_iota(I32, (FRAME, LANES), 1)
    result = jnp.zeros((FRAME, LANES), F32)
    for link in range(3):
        place = lane + frame[pl.ds(link * FRAME, FRAME), :].astype(I32)
        index = lax.bitwise_and(place, LANES - 1)
        value = jnp.where(
            place < 0,
            gather_lanes(before, index),
            jnp.where(place >= LANES, gather_lanes(after, index), gather_lanes(values, index)),
        )
        result = result + frame[pl.ds((3 + link) * FRAME, FRAME), :] * value
    return result


def previous_one(values):
    rolled = pltpu.roll(values, 1, axis=1)
    above = pltpu.roll(rolled, 1, axis=0)
    lane = lax.broadcasted_iota(I32, values.shape, 1)
    row = lax.broadcasted_iota(I32, values.shape, 0)
    return jnp.where(lane > 0, rolled, jnp.where(row > 0, above, 0.0))


def triangle():
    return jnp.where(
        lax.broadcasted_iota(I32, (LANES, LANES), 0) < lax.broadcasted_iota(I32, (LANES, LANES), 1),
        1.0,
        0.0,
    ).astype(BF16)


def prefix(values):
    ones = jnp.ones((LANES, LANES), BF16)
    right = jnp.concatenate([triangle(), ones], axis=1)
    count = values.shape[0]
    out = jnp.dot(
        jnp.concatenate(split3(values), axis=0), right, preferred_element_type=F32
    )
    out = out[:count] + out[count : 2 * count] + out[2 * count :]
    return out[:, :LANES], out[:, LANES:]


def forward_kernel(
    tiles, scalars, near1, far1, near2, far2, here, hot, member, fields, edges, window, old,
    diagonal, force_part, beside_old, ends_row, ends_lane, fresh, ctable, cedge, cdiag, cowner,
    summed, force_out, smooth_out, source_out, frame, ends_out, message,
    picked, products, padded, prefixed, totals, arrivals,
):
    tile = lax.axis_index("tile")
    tile_count = lax.axis_size("tile")
    even = lax.rem(tile, 2) == 0
    low = lax.rem(tile, 4) < 2
    entries = tiles.shape[0]
    blocks = old.shape[0]

    base = near1.shape[0] - near2.shape[0]
    near, far = near1[...], far1[...]
    from_left = jnp.where(even, far, near)
    from_right = jnp.where(even, near, far)
    two_near, two_far = near2[...], far2[...]
    j0 = jnp.where(low, two_far, two_near)
    j4 = jnp.where(low, two_near, two_far)
    j1, j3, j2 = from_left[base:], from_right[base:], here[...]
    each = j0.shape[0] // 4
    for channel in range(4):
        span = slice(channel * each, (channel + 1) * each)
        source = jnp.concatenate([j[span] for j in (j0, j1, j2, j3, j4)], axis=0)
        picked[pl.ds(channel, entries, stride=4), :] = dot_tn(hot[...], source)

    arrivals[0] = from_left[:base].astype(F32)
    arrivals[1] = from_right[:base].astype(F32)

    upper = lax.rem(lax.broadcasted_iota(I32, (16, LANES), 0), 8) < 4
    for group in range(entries // 4):
        rows = picked[pl.ds(16 * group, 16), :]
        rows = jnp.concatenate([jnp.where(upper, rows, 0.0), jnp.where(upper, 0.0, rows)], axis=1)
        at = 4 * group
        weights = jnp.concatenate(
            [
                jnp.concatenate([tiles[at], tiles[at + 1]], axis=1),
                jnp.concatenate([tiles[at + 2], tiles[at + 3]], axis=1),
            ],
            axis=0,
        )
        product = dot_nt(rows.astype(BF16), weights)
        products[pl.ds(16 * group, 8), :] = product[0:8, :LANES]
        products[pl.ds(16 * group + 8, 8), :] = product[8:16, LANES:]
    spread = []
    for channel in range(4):
        spread.append(jnp.concatenate(split3(products[pl.ds(channel, entries, stride=4), :]), axis=1))
    for channel in range(4):
        value = jnp.dot(member[...], spread[channel], preferred_element_type=F32)
        summed[channel] = value[:, :LANES] + value[:, LANES : 2 * LANES] + value[:, 2 * LANES :]

    speed = scalars[pl.ds(0, 8), :]
    share = scalars[pl.ds(8, 8), :]
    force_out[...] = force_part[...]
    padded[pl.ds(0, 8), :] = jnp.zeros((8, LANES), F32)
    padded[pl.ds(8 + blocks, 8), :] = jnp.zeros((8, LANES), F32)
    beside_extra = []
    for side, block, target in ((0, 0, 0), (1, blocks - 1, 2)):
        halo = arrivals[side, pl.ds(FIELD_HI, 8), :] + arrivals[side, pl.ds(FIELD_LO, 8), :]
        halo_old = arrivals[side, pl.ds(OLD_HI, 1), :] + arrivals[side, pl.ds(OLD_LO, 1), :]
        total = edges[0, pl.ds(block, 1), :] + edges[1, pl.ds(block, 1), :] + edges[2, pl.ds(block, 1), :]
        extra = jnp.zeros((8, LANES), F32)
        extra_old = jnp.zeros((8, LANES), F32)
        for link in range(3):
            place = wide(window[link, pl.ds(block, 1), :])
            index = lax.bitwise_and(place, LANES - 1)
            weight = jnp.where(
                lax.shift_right_logical(place, 7) == target, wide(edges[link, pl.ds(block, 1), :]), 0.0
            )
            extra = extra + weight * gather_lanes(halo, index)
            extra_old = extra_old + weight * gather_lanes(wide(halo_old), index)
        change = speed * extra / wide(total)
        ends_out[:, pl.ds(side * LANES, LANES)] = fresh[:, pl.ds(block * LANES, LANES)] + change
        force_out[pl.ds(block, 1), :] += jnp.sum(change * share, axis=0, keepdims=True)
        beside_extra.append(extra_old[0:1])

    force = force_out[...]
    for channel in range(4):
        force = force + scalars[pl.ds(16 + channel, 1), :] * summed[channel]
    force_out[...] = force
    total = diagonal[...] + edges[0] + edges[1] + edges[2]
    smooth_out[...] = beside_old[...]
    smooth_out[pl.ds(0, 1), :] += beside_extra[0]
    smooth_out[pl.ds(blocks - 1, 1), :] += beside_extra[1]
    previous = old[...]
    smooth = previous + RELAXATION * (force - (total * previous - smooth_out[...])) / total
    smooth_out[...] = smooth
    padded[pl.ds(8, blocks), :] = smooth
    residual = force - total * smooth + neighbour_sum(padded, edges, window, blocks)

    inner, whole = prefix(residual)
    prefixed[...] = inner
    totals[...] = whole
    rows, lanes = ends_row[...], ends_lane[...]
    count = rows.shape[0]
    run = jnp.zeros((count, LANES), F32)
    ends = jnp.zeros((count, LANES), F32)
    for block in range(blocks):
        value = gather_lanes(wide(prefixed[pl.ds(block, 1), :], count), lanes) + run
        ends = jnp.where(rows == block, value, ends)
        run = run + wide(totals[pl.ds(block, 1), :], count)
    ends = jnp.where(rows == blocks, run, ends)
    own_source = ends - previous_one(ends)

    lane = lax.broadcasted_iota(I32, (1, LANES), 1)
    rim_rows, rim_counts = [], []
    for side in range(2):
        inside = padded[pl.ds(8 if side == 0 else 7 + blocks, 1), :]
        value = jnp.zeros((1, LANES), F32)
        for link in range(3):
            place = lane + arrivals[side, pl.ds(OFFSET + link, 1), :].astype(I32)
            index = lax.bitwise_and(place, LANES - 1)
            reached = (place >= LANES) if side == 0 else (place < 0)
            weight = arrivals[side, pl.ds(EDGE_HI + link, 1), :] + arrivals[side, pl.ds(EDGE_LO + link, 1), :]
            value = value + jnp.where(
                wide(reached.astype(I32)) > 0,
                wide(weight) * gather_lanes(wide(inside), wide(index)),
                0.0,
            )[0:1]
        rim_rows.append(value)
        owners = arrivals[side, pl.ds(OWNER, 1), :].astype(I32)
        below = jnp.where(
            lax.broadcasted_iota(I32, (LANES, LANES), 0) >= owners, 1.0, 0.0
        ).astype(BF16)
        rim_counts.append(dot_nt(jnp.ones((8, LANES), BF16), below))
    rim_inner, rim_whole = prefix(jnp.concatenate([wide(r) for r in rim_rows], axis=0))
    rim_source = []
    for side in range(2):
        place = rim_counts[side].astype(I32)
        index = lax.bitwise_and(place, LANES - 1)
        value = gather_lanes(rim_inner[8 * side : 8 * side + 8], index)
        value = jnp.where(place >= LANES, rim_whole[8 * side : 8 * side + 8], value)
        shifted = pltpu.roll(value, 1, axis=1)
        first = lax.broadcasted_iota(I32, (8, LANES), 1) == 0
        rim_source.append((value - jnp.where(first, 0.0, shifted))[0:1])

    frows = own_source.shape[0]
    source_out[...] = jnp.zeros((FRAME, LANES), F32)
    source_out[pl.ds(OWN, frows), :] = own_source
    source_out[pl.ds(OWN - 1, 1), :] = rim_source[0]
    source_out[pl.ds(OWN + frows, 1), :] = rim_source[1]
    reach = LANES // 8
    frame[...] = jnp.zeros(frame.shape, F32)
    frame[pl.ds(6 * FRAME, FRAME), :] = jnp.ones((FRAME, LANES), F32)
    frame[pl.ds(7 * FRAME, FRAME), :] = jnp.full((FRAME, LANES), 127.0, F32)
    bottoms = 16
    at_cell = lax.broadcasted_iota(I32, (frows, LANES), 0) * LANES + lax.broadcasted_iota(
        I32, (frows, LANES), 1
    )
    for link in range(3):
        frame[pl.ds(link * FRAME + OWN, frows), :] = (ctable[link] - reach - at_cell).astype(F32)
        frame[pl.ds((3 + link) * FRAME + OWN, frows), :] = cedge[link]
    frame[pl.ds(6 * FRAME + OWN, frows), :] = cdiag[...]
    frame[pl.ds(7 * FRAME + OWN, frows), :] = (cowner[...] + bottoms).astype(F32)
    for side in range(2):
        for row in range(2):
            at = (OWN - 2 + row) if side == 0 else (OWN + frows + row)
            for link in range(3):
                put = 3 * row + link
                frame[pl.ds(link * FRAME + at, 1), :] = arrivals[side, pl.ds(COFFSET + put, 1), :]
                frame[pl.ds((3 + link) * FRAME + at, 1), :] = (
                    arrivals[side, pl.ds(CEDGE_HI + put, 1), :] + arrivals[side, pl.ds(CEDGE_LO + put, 1), :]
                )
            frame[pl.ds(6 * FRAME + at, 1), :] = (
                arrivals[side, pl.ds(CDIAG_HI + row, 1), :] + arrivals[side, pl.ds(CDIAG_LO + row, 1), :]
            )
            frame[pl.ds(7 * FRAME + at, 1), :] = arrivals[side, pl.ds(COWNER + row, 1), :] + (
                2.0 * bottoms * side
            )
    for link in range(3):
        frame[pl.ds(6 * FRAME, FRAME), :] += frame[pl.ds((3 + link) * FRAME, FRAME), :]
    source = source_out[...]
    first = RELAXATION * source / frame[pl.ds(6 * FRAME, FRAME), :]
    residual = (1.0 - RELAXATION) * source + first_level_sum(first, frame)
    codes = frame[pl.ds(7 * FRAME, FRAME), :].astype(I32)
    pieces = split3(residual)
    left_side, right_side = [], []
    bins = lax.broadcasted_iota(I32, (LANES, LANES), 0)
    for row in range(OWN - 2, OWN + frows + 2):
        left_side.append(jnp.concatenate([p[row : row + 1] for p in pieces], axis=0))
        right_side.append(
            jnp.where(bins == codes[row : row + 1], 1.0, 0.0).astype(BF16)
        )
    bottom = dot_nt(jnp.concatenate(left_side, axis=1), jnp.concatenate(right_side, axis=1))
    bottom = bottom[0:1] + bottom[1:2] + bottom[2:3]
    bottom = jnp.where(lane < 3 * bottoms, bottom, 0.0)

    to_left = jnp.concatenate(
        [bottom, padded[pl.ds(8, 1), :], own_source[0:2], rim_source[0], jnp.zeros((3, LANES), F32)], axis=0
    )
    to_right = jnp.concatenate(
        [bottom, padded[pl.ds(7 + blocks, 1), :], own_source[frows - 2 : frows], rim_source[1], jnp.zeros((3, LANES), F32)],
        axis=0,
    )
    for other in range(message.shape[0]):
        message[other] = to_right
    message[lax.rem(tile + tile_count - 1, tile_count)] = to_left


def prepare_kernel(
    fresh, ends_new, summed, near1, far1, cinverse, fresh_out, received, weights, sem, extended
):
    tile = lax.axis_index("tile")
    even = lax.rem(tile, 2) == 0
    cells = fresh_out.shape[1]
    copies = [
        pltpu.make_async_copy(
            ends_new.at[:, pl.ds(side * LANES, LANES)],
            fresh_out.at[:, pl.ds(side * (cells - LANES), LANES)],
            sem.at[side],
        )
        for side in range(2)
    ]
    middle = pl.ds(LANES, cells - 2 * LANES)
    copies.append(pltpu.make_async_copy(fresh.at[:, middle], fresh_out.at[:, middle], sem.at[2]))
    for copy in copies:
        copy.start()
    channels, blocks = summed.shape[:2]
    for block in range(blocks):
        for channel in range(channels):
            received[pl.ds(channel, 1), pl.ds(block * LANES, LANES)] = summed[channel, pl.ds(block, 1), :]
    bottoms, size = cinverse.shape
    halves = size // LANES
    near = near1[pl.ds(INVERSE, 32 * halves), :].astype(F32)
    far = far1[pl.ds(INVERSE, 32 * halves), :].astype(F32)
    left = jnp.where(even, far, near)
    right = jnp.where(even, near, far)
    for half in range(halves):
        part = pl.ds(half * LANES, LANES)
        for at, block in ((0, left), (2, right)):
            extended[pl.ds(at * bottoms, bottoms), part] = (
                block[16 * half : 16 * half + 16]
                + block[16 * (halves + half) : 16 * (halves + half) + 16]
            )
        extended[pl.ds(bottoms, bottoms), part] = cinverse[:, part]
    table = extended[...]
    lane = lax.broadcasted_iota(I32, (3 * bottoms, LANES), 1)
    for other in range(weights.shape[0]):
        shift = (size - (other - 1) * bottoms) % size
        turned = pltpu.roll(table, shift, axis=1) if shift else table
        weights[other] = jnp.where(lane < 3 * bottoms, turned[:, :LANES], 0.0)
    for copy in copies:
        copy.wait()


def backward_kernel(
    frame_rows, arrived, weights, source, frame, force, smooth, edges, window, diagonal, owner, near1, far1,
    height, frame_source, padded, third_rows,
):
    tile = lax.axis_index("tile")
    tile_count = lax.axis_size("tile")
    even = lax.rem(tile, 2) == 0
    blocks = force.shape[0]
    left = arrived[lax.rem(tile + tile_count - 1, tile_count)]
    right = arrived[lax.rem(tile + 1, tile_count)]
    count = weights.shape[1]
    partial = jnp.zeros((count, LANES), F32)
    for other in range(weights.shape[0]):
        partial = partial + weights[other] * wide(arrived[other, pl.ds(0, 1), :], count)
    partial = jnp.concatenate([partial, jnp.zeros((LANES - count, LANES), F32)], axis=0)
    ones = jnp.ones((8, LANES), BF16)
    pieces = split3(partial)
    bottom = dot_nt(ones, pieces[0]) + dot_nt(ones, pieces[1]) + dot_nt(ones, pieces[2])

    frows = frame_rows
    frame_source[...] = source[...]
    frame_source[pl.ds(OWN - 2, 2), :] += left[2:4]
    frame_source[pl.ds(OWN, 1), :] += left[4:5]
    frame_source[pl.ds(OWN + frows - 1, 1), :] += right[4:5]
    frame_source[pl.ds(OWN + frows, 2), :] += right[2:4]
    total_source = frame_source[...]
    total = frame[pl.ds(6 * FRAME, FRAME), :]
    codes = frame[pl.ds(7 * FRAME, FRAME), :].astype(I32)
    second = RELAXATION * total_source / total + gather_lanes(wide(bottom[0:1], FRAME), codes)
    third = second + RELAXATION * (
        total_source - total * second + first_level_sum(second, frame)
    ) / total
    third_rows[...] = third

    owners = owner[...]
    index = lax.bitwise_and(owners, LANES - 1)
    which = lax.shift_right_logical(owners, 7)
    corrected = jnp.zeros((blocks, LANES), F32)
    for row in range(frows):
        corrected = jnp.where(
            which == row, gather_lanes(wide(third_rows[pl.ds(OWN + row, 1), :], blocks), index), corrected
        )
    corrected = smooth[...] + corrected
    padded[pl.ds(8, blocks), :] = corrected
    near = near1[pl.ds(16, 16), :].astype(F32)
    far = far1[pl.ds(16, 16), :].astype(F32)
    left_owner = jnp.where(even, far, near)[OWNER - 16 : OWNER - 15].astype(I32)
    right_owner = jnp.where(even, near, far)[OWNER - 16 : OWNER - 15].astype(I32)
    left_rim = left[1:2] + gather_lanes(wide(third_rows[pl.ds(OWN - 1, 1), :]), wide(left_owner))[0:1]
    right_rim = right[1:2] + gather_lanes(wide(third_rows[pl.ds(OWN + frows, 1), :]), wide(right_owner))[0:1]
    padded[pl.ds(7, 1), :] = left_rim
    padded[pl.ds(8 + blocks, 1), :] = right_rim
    fine_total = diagonal[...] + edges[0] + edges[1] + edges[2]
    beside = neighbour_sum(padded, edges, window, blocks)
    height[...] = corrected + RELAXATION * (force[...] - (fine_total * corrected - beside)) / fine_total


def in_hbm(array):
    return pltpu.with_memory_space_constraint(array, pltpu.HBM)


def struct(shape, dtype=F32):
    return jax.ShapeDtypeStruct(shape, dtype)


VMEM = pl.BlockSpec(memory_space=pltpu.VMEM)
SMEM = pl.BlockSpec(memory_space=pltpu.SMEM)
ANY = pl.BlockSpec(memory_space=pltpu.HBM)
PARAMS = pltpu.CompilerParams(vmem_limit_bytes=16 * 1024 * 1024)


def pair_up(count, distance):
    period = 2 * distance
    result = []
    for start in (0, distance):
        pairs = []
        for i in range(count):
            if (i - start) % period < distance:
                pairs += [(i, (i + distance) % count), ((i + distance) % count, i)]
        result.append(pairs)
    return result


def per_device(
    fields, level_rate, edge_weight, fine_diagonal, fine_table, old_height, level_weight,
    flux_weight, fine_owner, coarse_table, coarse_edge, coarse_diagonal, coarse_owner,
    coarse_inverse, surface_out, send_blocks, entry_slot, entry_block, remap_tiles,
):
    tile_count = lax.axis_size("tile")
    cells = fields.shape[2]
    blocks = cells // LANES
    firsts = coarse_diagonal.shape[1]
    frows = firsts // LANES
    entries = entry_slot.shape[2]
    channels = surface_out.shape[1]
    slots = send_blocks.shape[2]
    each = slots // 5
    halves = coarse_inverse.shape[2] // LANES
    bottoms = coarse_inverse.shape[1]
    base = pick_base(halves)
    swap = [(0, 1), (1, 0)]
    surface = lax.ppermute(surface_out[0], "comp", swap)
    sends = lax.ppermute(send_blocks[0], "comp", swap)
    raw = (
        fields[0],
        old_height.reshape(blocks, LANES),
        edge_weight[0].reshape(3, blocks, LANES),
        fine_table[0].reshape(3, blocks, LANES),
        fine_owner.reshape(blocks, LANES),
        fine_diagonal.reshape(blocks, LANES),
        coarse_table[0].reshape(3, frows, LANES),
        coarse_edge[0].reshape(3, frows, LANES),
        coarse_diagonal.reshape(frows, LANES),
        coarse_owner.reshape(frows, LANES),
        coarse_inverse[0],
        entry_slot[0],
        entry_block[0],
        level_rate,
        level_weight,
        flux_weight,
    )
    loaded = pl.pallas_call(
        load_kernel,
        out_shape=[struct(x.shape, x.dtype) for x in raw[:-3]] + [struct((24, LANES))],
        in_specs=[ANY] * len(raw),
        out_specs=[VMEM] * (len(raw) - 2),
        scratch_shapes=[pltpu.VMEM(x.shape, x.dtype) for x in raw[-3:]]
        + [pltpu.SemaphoreType.DMA((len(raw),))],
        compiler_params=PARAMS,
        name="load",
    )(*[in_hbm(x) for x in raw])
    (
        current, old, edges, table, owner, diagonal, ctable, cedge, cdiag, cowner, cinverse,
        slot, block, scalars,
    ) = loaded

    near1, far1, near2, far2, here = pl.pallas_call(
        pack_kernel,
        out_shape=[
            struct((base + 4 * each, LANES), BF16),
            struct((base + 4 * each, LANES), BF16),
            struct((4 * each, LANES), BF16),
            struct((4 * each, LANES), BF16),
            struct((4 * each, LANES), BF16),
        ],
        in_specs=[VMEM] * 12,
        out_specs=[VMEM] * 5,
        scratch_shapes=[
            pltpu.VMEM((channels * blocks, LANES), F32),
            pltpu.VMEM((base, LANES), F32),
            pltpu.VMEM((base, LANES), F32),
        ],
        compiler_params=PARAMS,
        name="pack",
    )(
        surface, sends, current, old, edges, table, owner, ctable, cedge, cdiag, cowner, cinverse,
    )
    one_a, one_b = pair_up(tile_count, 1)
    two_a, two_b = pair_up(tile_count, 2)
    far1 = lax.ppermute(far1, "tile", one_b)
    far2 = lax.ppermute(far2, "tile", two_b)
    near1 = lax.ppermute(near1, "tile", one_a)
    near2 = lax.ppermute(near2, "tile", two_a)

    fresh, force_part, beside_old, window, ends_row, ends_lane, hot, member, tiles = pl.pallas_call(
        stencil_kernel,
        out_shape=[
            struct((fields.shape[1], cells)),
            struct((blocks, LANES)),
            struct((blocks, LANES)),
            struct((3, blocks, LANES), I32),
            struct((frows, LANES), I32),
            struct((frows, LANES), I32),
            struct((slots, entries), BF16),
            struct((blocks, entries), BF16),
            pltpu.VMEM(remap_tiles.shape[2:], BF16),
        ],
        in_specs=[VMEM] * 9 + [ANY],
        out_specs=[VMEM] * 9,
        scratch_shapes=[pltpu.VMEM((blocks + 16, LANES), F32), pltpu.SemaphoreType.DMA((math.gcd(entries, 8),))],
        compiler_params=PARAMS,
        name="stencil",
    )(here, scalars, current, edges, table, old, owner, slot, block, in_hbm(remap_tiles[0, 0]))

    summed, force, smooth, source, frame, ends_new, message = pl.pallas_call(
        forward_kernel,
        out_shape=[
            struct((channels, blocks, LANES)),
            struct((blocks, LANES)),
            struct((blocks, LANES)),
            struct((FRAME, LANES)),
            struct((8 * FRAME, LANES)),
            struct((fields.shape[1], 2 * LANES)),
            struct((tile_count, 8, LANES)),
        ],
        in_specs=[VMEM] * 23,
        out_specs=[VMEM] * 7,
        scratch_shapes=[
            pltpu.VMEM((4 * entries, LANES), F32),
            pltpu.VMEM((4 * entries, LANES), F32),
            pltpu.VMEM((blocks + 16, LANES), F32),
            pltpu.VMEM((blocks, LANES), F32),
            pltpu.VMEM((blocks, LANES), F32),
            pltpu.VMEM((2, base, LANES), F32),
        ],
        compiler_params=PARAMS,
        name="forward",
    )(
        tiles, scalars, near1, far1, near2, far2, here, hot, member, current, edges, window, old,
        diagonal, force_part, beside_old, ends_row, ends_lane, fresh, ctable, cedge, cdiag, cowner,
    )
    arrived = lax.all_to_all(message, "tile", split_axis=0, concat_axis=0, tiled=True)
    advanced, received, weights = pl.pallas_call(
        prepare_kernel,
        out_shape=[
            struct((fields.shape[1], cells)),
            struct((channels, cells)),
            struct((tile_count, 3 * bottoms, LANES)),
        ],
        in_specs=[VMEM] * 6,
        out_specs=[ANY, VMEM, VMEM],
        scratch_shapes=[
            pltpu.SemaphoreType.DMA((3,)),
            pltpu.VMEM((3 * bottoms, bottoms * tile_count), F32),
        ],
        compiler_params=PARAMS,
        name="prepare",
    )(fresh, ends_new, summed, near1, far1, cinverse)
    height = pl.pallas_call(
        functools.partial(backward_kernel, frows),
        out_shape=struct((blocks, LANES)),
        in_specs=[VMEM] * 12,
        out_specs=VMEM,
        scratch_shapes=[
            pltpu.VMEM((FRAME, LANES), F32),
            pltpu.VMEM((blocks + 16, LANES), F32),
            pltpu.VMEM((FRAME, LANES), F32),
        ],
        compiler_params=PARAMS,
        name="backward",
    )(arrived, weights, source, frame, force, smooth, edges, window, diagonal, owner, near1, far1)
    return advanced[None], received[None], height.reshape(1, cells)


def solution(mesh):
    in_specs = (
        P("comp", None, "tile"),
        P("comp", None),
        P("comp", None, "tile"),
        P("comp", "tile"),
        P("comp", None, "tile"),
        P("comp", "tile"),
        P("comp", None),
        P("comp", None),
        P("comp", "tile"),
        P("comp", None, "tile"),
        P("comp", None, "tile"),
        P("comp", "tile"),
        P("comp", "tile"),
        P("comp", "tile", None),
        P("comp", None, "tile"),
        P("comp", "tile", None),
        P("comp", "tile", None),
        P("comp", "tile", None),
        P("comp", "tile", None, None, None),
    )
    out_specs = (P("comp", None, "tile"), P("comp", None, "tile"), P("comp", "tile"))
    return jax.shard_map(
        per_device, mesh=mesh, in_specs=in_specs, out_specs=out_specs, check_vma=False
    )
```

```python
import functools
import math

import jax
import jax.numpy as jnp
from jax import lax
from jax.experimental import pallas as pl
from jax.experimental.pallas import tpu as pltpu
from jax.sharding import PartitionSpec as P

LANES = 128
RELAXATION = 0.8
F32 = jnp.float32
BF16 = jnp.bfloat16
I32 = jnp.int32

FIELD_HI, FIELD_LO = 0, 8
EDGE_HI, EDGE_LO, OLD_HI, OLD_LO = 16, 19, 22, 23
OFFSET, OWNER = 24, 27
CEDGE_HI, CEDGE_LO, CDIAG_HI, CDIAG_LO = 32, 38, 44, 46
COFFSET, COWNER = 48, 54
INVERSE = 56

FRAME, OWN = 32, 8


def sides(far, near, even):
    return jnp.where(even, far, near), jnp.where(even, near, far)


def gather_lanes(table, index):
    return jnp.take_along_axis(table, index, axis=1)


def wide(row, count=8):
    return jnp.broadcast_to(row, (count, row.shape[1]))


def split3(x):
    high = x.astype(BF16)
    rest = x - high.astype(F32)
    middle = rest.astype(BF16)
    low = (rest - middle.astype(F32)).astype(BF16)
    return high, middle, low


def dot_nt(a, b):
    return lax.dot_general(a, b, (((1,), (1,)), ((), ())), preferred_element_type=F32)


def dot_tn(a, b):
    return lax.dot_general(a, b, (((0,), (0,)), ((), ())), preferred_element_type=F32)


def pick_base(inverse_blocks):
    return -(-(INVERSE + 32 * inverse_blocks) // 16) * 16


def load_kernel(*refs):
    count = (len(refs) - 2) // 2
    sources, kept, scalars = refs[:count], refs[count : 2 * count - 3], refs[2 * count - 3]
    spread, sems = refs[2 * count - 2 : 2 * count + 1], refs[2 * count + 1]
    copies = [
        pltpu.make_async_copy(source, target, sems.at[i])
        for i, (source, target) in enumerate(zip(sources, kept + spread))
    ]
    for copy in copies:
        copy.start()
    for copy in copies:
        copy.wait()
    for i, value in enumerate(spread):
        width = value.shape[1]
        diagonal = lax.broadcasted_iota(I32, (8, width), 0) == lax.broadcasted_iota(I32, (8, width), 1)
        column = jnp.sum(jnp.where(diagonal, wide(value[...]), 0.0), axis=1, keepdims=True)
        scalars[pl.ds(8 * i, 8), :] = jnp.broadcast_to(column, (8, LANES))


def pack_kernel(
    surface, sends, fields, old, edge, table, owner, ctable, cedge, cdiag, cowner, cinverse,
    to_right2, far, to_left2, near, here, chunks, left_rows, right_rows,
):
    even = lax.rem(lax.axis_index("tile"), 2) == 0
    cells = fields.shape[1]
    blocks = cells // LANES
    frows = ctable.shape[1]
    firsts = frows * LANES
    base = pick_base(cinverse.shape[1] // LANES)
    lane = lax.broadcasted_iota(I32, (1, LANES), 1)

    for rows, at_left in ((right_rows, False), (left_rows, True)):
        start = 0 if at_left else cells - LANES
        part = pl.ds(start, LANES)

        def both(high, low_row, value):
            count = value.shape[0]
            rows[pl.ds(high, count), :] = value
            rows[pl.ds(low_row, count), :] = value - value.astype(BF16).astype(F32)

        def three(ref, row):
            return jnp.concatenate([ref[link, pl.ds(row, 1), :] for link in range(3)], axis=0)

        rows[pl.ds(24, 8), :] = jnp.zeros((8, LANES), F32)
        both(FIELD_HI, FIELD_LO, fields[:, part])
        block = 0 if at_left else blocks - 1
        both(EDGE_HI, EDGE_LO, three(edge, block))
        both(OLD_HI, OLD_LO, old[pl.ds(block, 1), :])
        rows[pl.ds(OFFSET, 3), :] = (three(table, block) - (LANES + start) - lane).astype(F32)
        shift = 0 if at_left else firsts - LANES
        rows[pl.ds(OWNER, 1), :] = (owner[pl.ds(block, 1), :] - shift).astype(F32)
        first = 0 if at_left else frows - 2
        reach = LANES // 8
        for step in range(2):
            both(CEDGE_HI + 3 * step, CEDGE_LO + 3 * step, three(cedge, first + step))
            rows[pl.ds(COFFSET + 3 * step, 3), :] = (
                three(ctable, first + step) - (reach + (first + step) * LANES) - lane
            ).astype(F32)
            both(CDIAG_HI + step, CDIAG_LO + step, cdiag[pl.ds(first + step, 1), :])
            rows[pl.ds(COWNER + step, 1), :] = cowner[pl.ds(first + step, 1), :].astype(F32)
        halves = cinverse.shape[1] // LANES
        for half in range(halves):
            both(
                INVERSE + 16 * half,
                INVERSE + 16 * (halves + half),
                cinverse[:, pl.ds(half * LANES, LANES)],
            )
        end = INVERSE + 32 * halves
        if base > end:
            rows[pl.ds(end, base - end), :] = jnp.zeros((base - end, LANES), F32)

    for block in range(blocks):
        chunks[pl.ds(4 * block, 4), :] = surface[:, pl.ds(block * LANES, LANES)].astype(F32)
    slots = sends.shape[1]
    hot = jnp.where(
        lax.broadcasted_iota(I32, (blocks, slots), 0) == sends[...], 1.0, 0.0
    ).astype(BF16)
    picks = []
    for channel in range(4):
        source = chunks[pl.ds(channel, blocks, stride=4), :].astype(BF16)
        picks.append(dot_tn(hot, source).astype(BF16))
    count = slots // 5

    chosen = [
        jnp.concatenate([p[j * count : (j + 1) * count] for p in picks], axis=0) for j in range(5)
    ]
    here[...] = chosen[2]
    for out, j in ((to_right2, 0), (to_left2, 4)):
        out[pl.ds(0, base), :] = jnp.zeros((base, LANES), BF16)
        out[pl.ds(base, 4 * count), :] = chosen[j]
    right = jnp.concatenate([right_rows[...].astype(BF16), chosen[1]], axis=0)
    left = jnp.concatenate([left_rows[...].astype(BF16), chosen[3]], axis=0)
    far[...] = jnp.where(even, left, right)
    near[...] = jnp.where(even, right, left)


def stencil_kernel(
    here, scalars, fields, edge, table, old, owner, slots, entry_block, tiles,
    fresh, force, beside_old, window, ends_row, ends_lane, hot, member, tile_buffer, padded, sems,
):
    del here
    parts = sems.shape[0]
    step = tiles.shape[0] // parts
    loads = [
        pltpu.make_async_copy(
            tiles.at[pl.ds(part * step, step)], tile_buffer.at[pl.ds(part * step, step)], sems.at[part]
        )
        for part in range(parts)
    ]
    for load in loads:
        load.start()
    blocks = old.shape[0]
    levels = fields.shape[0]
    speed = scalars[pl.ds(0, 8), :]
    share = scalars[pl.ds(8, 8), :]
    starts = lax.broadcasted_iota(I32, (blocks, LANES), 0) * LANES
    total = edge[0] + edge[1] + edge[2]
    inverse = 1.0 / total
    for link in range(3):
        window[link] = table[link] - starts
    blank = jnp.zeros((levels, LANES), F32)

    def chunk(block):
        if 0 <= block < blocks:
            return fields[:, pl.ds(block * LANES, LANES)]
        return blank

    before, here, after = blank, chunk(0), chunk(1)
    for block in range(blocks):
        row = slice(block, block + 1)
        beside = jnp.zeros((levels, LANES), F32)
        for link in range(3):
            place = wide(window[link, pl.ds(block, 1), :])
            index = lax.bitwise_and(place, LANES - 1)
            value = jnp.where(
                place < LANES,
                gather_lanes(before, index),
                jnp.where(place < 2 * LANES, gather_lanes(here, index), gather_lanes(after, index)),
            )
            beside = beside + wide(edge[link, pl.ds(block, 1), :]) * value
        result = here + speed * ((beside - wide(total[row]) * here) * wide(inverse[row]))
        fresh[:, pl.ds(block * LANES, LANES)] = result
        force[pl.ds(block, 1), :] = jnp.sum(result * share, axis=0, keepdims=True)
        before, here, after = here, after, chunk(block + 2)

    padded[pl.ds(0, 8), :] = jnp.zeros((8, LANES), F32)
    padded[pl.ds(8 + blocks, 8), :] = jnp.zeros((8, LANES), F32)
    padded[pl.ds(8, blocks), :] = old[...]
    beside_old[...] = neighbour_sum(padded, edge, window, blocks)
    hot[...] = jnp.where(
        lax.broadcasted_iota(I32, hot.shape, 0) == slots[...], 1.0, 0.0
    ).astype(BF16)
    member[...] = jnp.where(
        lax.broadcasted_iota(I32, member.shape, 0) == entry_block[...], 1.0, 0.0
    ).astype(BF16)

    firsts = ends_row.shape[0] * LANES
    ident = lax.broadcasted_iota(I32, ends_row.shape, 0) * LANES + lax.broadcasted_iota(
        I32, ends_row.shape, 1
    )
    count = ends_row.shape[0]
    rows = jnp.zeros(ends_row.shape, I32)
    for block in range(blocks):
        last = jnp.broadcast_to(owner[pl.ds(block, 1), LANES - 1 : LANES], ends_row.shape)
        rows = rows + jnp.where(last <= ident, 1, 0)
    lanes = jnp.zeros(ends_row.shape, I32)
    for bit in (64, 32, 16, 8, 4, 2, 1):
        probe = lanes + (bit - 1)
        value = jnp.full(ends_row.shape, firsts, I32)
        for block in range(blocks):
            value = jnp.where(
                rows == block, gather_lanes(wide(owner[pl.ds(block, 1), :], count), probe), value
            )
        lanes = jnp.where(value <= ident, lanes + bit, lanes)
    ends_row[...] = rows
    ends_lane[...] = lanes
    for load in loads:
        load.wait()


def neighbour_sum(padded, edges, window, blocks):
    before = padded[pl.ds(7, blocks), :]
    here = padded[pl.ds(8, blocks), :]
    after = padded[pl.ds(9, blocks), :]
    result = jnp.zeros((blocks, LANES), F32)
    for link in range(3):
        place = window[link]
        index = lax.bitwise_and(place, LANES - 1)
        value = jnp.where(
            place < LANES,
            gather_lanes(before, index),
            jnp.where(place < 2 * LANES, gather_lanes(here, index), gather_lanes(after, index)),
        )
        result = result + edges[link] * value
    return result


def first_level_sum(values, frame):
    before = pltpu.roll(values, 1, axis=0)
    after = pltpu.roll(values, FRAME - 1, axis=0)
    lane = lax.broadcasted_iota(I32, (FRAME, LANES), 1)
    result = jnp.zeros((FRAME, LANES), F32)
    for link in range(3):
        place = lane + frame[pl.ds(link * FRAME, FRAME), :].astype(I32)
        index = lax.bitwise_and(place, LANES - 1)
        value = jnp.where(
            place < 0,
            gather_lanes(before, index),
            jnp.where(place >= LANES, gather_lanes(after, index), gather_lanes(values, index)),
        )
        result = result + frame[pl.ds((3 + link) * FRAME, FRAME), :] * value
    return result


def previous_one(values):
    rolled = pltpu.roll(values, 1, axis=1)
    above = pltpu.roll(rolled, 1, axis=0)
    lane = lax.broadcasted_iota(I32, values.shape, 1)
    row = lax.broadcasted_iota(I32, values.shape, 0)
    return jnp.where(lane > 0, rolled, jnp.where(row > 0, above, 0.0))


def triangle():
    return jnp.where(
        lax.broadcasted_iota(I32, (LANES, LANES), 0) < lax.broadcasted_iota(I32, (LANES, LANES), 1),
        1.0,
        0.0,
    ).astype(BF16)


def prefix(values):
    ones = jnp.ones((LANES, LANES), BF16)
    right = jnp.concatenate([triangle(), ones], axis=1)
    count = values.shape[0]
    out = jnp.dot(
        jnp.concatenate(split3(values), axis=0), right, preferred_element_type=F32
    )
    out = out[:count] + out[count : 2 * count] + out[2 * count :]
    return out[:, :LANES], out[:, LANES:]


def forward_kernel(
    tiles, scalars, from_left2, far, from_right2, near, here, hot, member, fields, edges, window, old,
    diagonal, force_part, beside_old, ends_row, ends_lane, fresh, ctable, cedge, cdiag, cowner,
    summed, force_out, smooth_out, source_out, frame, ends_out, message,
    picked, products, padded, prefixed, totals, arrivals,
):
    tile = lax.axis_index("tile")
    tile_count = lax.axis_size("tile")
    entries = tiles.shape[0]
    blocks = old.shape[0]

    even = lax.rem(tile, 2) == 0
    base = far.shape[0] - here.shape[0]
    each = here.shape[0] // 4
    from_left, from_right = sides(far[...], near[...], even)
    sources = (from_left2[base:, :], from_left[base:], here[...], from_right[base:], from_right2[base:, :])
    for channel in range(4):
        source = jnp.concatenate(
            [rows[channel * each : (channel + 1) * each] for rows in sources], axis=0
        )
        picked[pl.ds(channel, entries, stride=4), :] = dot_tn(hot[...], source)

    arrivals[0] = from_left[:base].astype(F32)
    arrivals[1] = from_right[:base].astype(F32)

    upper = lax.rem(lax.broadcasted_iota(I32, (16, LANES), 0), 8) < 4
    for group in range(entries // 4):
        rows = picked[pl.ds(16 * group, 16), :]
        rows = jnp.concatenate([jnp.where(upper, rows, 0.0), jnp.where(upper, 0.0, rows)], axis=1)
        at = 4 * group
        weights = jnp.concatenate(
            [
                jnp.concatenate([tiles[at], tiles[at + 1]], axis=1),
                jnp.concatenate([tiles[at + 2], tiles[at + 3]], axis=1),
            ],
            axis=0,
        )
        product = dot_nt(rows.astype(BF16), weights)
        products[pl.ds(16 * group, 8), :] = product[0:8, :LANES]
        products[pl.ds(16 * group + 8, 8), :] = product[8:16, LANES:]
    spread = []
    for channel in range(4):
        spread.append(jnp.concatenate(split3(products[pl.ds(channel, entries, stride=4), :]), axis=1))
    for channel in range(4):
        value = jnp.dot(member[...], spread[channel], preferred_element_type=F32)
        summed[channel] = value[:, :LANES] + value[:, LANES : 2 * LANES] + value[:, 2 * LANES :]

    speed = scalars[pl.ds(0, 8), :]
    share = scalars[pl.ds(8, 8), :]
    force_out[...] = force_part[...]
    padded[pl.ds(0, 8), :] = jnp.zeros((8, LANES), F32)
    padded[pl.ds(8 + blocks, 8), :] = jnp.zeros((8, LANES), F32)
    beside_extra = []
    for side, block, target in ((0, 0, 0), (1, blocks - 1, 2)):
        halo = arrivals[side, pl.ds(FIELD_HI, 8), :] + arrivals[side, pl.ds(FIELD_LO, 8), :]
        halo_old = arrivals[side, pl.ds(OLD_HI, 1), :] + arrivals[side, pl.ds(OLD_LO, 1), :]
        total = edges[0, pl.ds(block, 1), :] + edges[1, pl.ds(block, 1), :] + edges[2, pl.ds(block, 1), :]
        extra = jnp.zeros((8, LANES), F32)
        extra_old = jnp.zeros((8, LANES), F32)
        for link in range(3):
            place = wide(window[link, pl.ds(block, 1), :])
            index = lax.bitwise_and(place, LANES - 1)
            weight = jnp.where(
                lax.shift_right_logical(place, 7) == target, wide(edges[link, pl.ds(block, 1), :]), 0.0
            )
            extra = extra + weight * gather_lanes(halo, index)
            extra_old = extra_old + weight * gather_lanes(wide(halo_old), index)
        change = speed * extra / wide(total)
        ends_out[:, pl.ds(side * LANES, LANES)] = fresh[:, pl.ds(block * LANES, LANES)] + change
        force_out[pl.ds(block, 1), :] += jnp.sum(change * share, axis=0, keepdims=True)
        beside_extra.append(extra_old[0:1])

    force = force_out[...]
    for channel in range(4):
        force = force + scalars[pl.ds(16 + channel, 1), :] * summed[channel]
    force_out[...] = force
    total = diagonal[...] + edges[0] + edges[1] + edges[2]
    smooth_out[...] = beside_old[...]
    smooth_out[pl.ds(0, 1), :] += beside_extra[0]
    smooth_out[pl.ds(blocks - 1, 1), :] += beside_extra[1]
    previous = old[...]
    smooth = previous + RELAXATION * (force - (total * previous - smooth_out[...])) / total
    smooth_out[...] = smooth
    padded[pl.ds(8, blocks), :] = smooth
    residual = force - total * smooth + neighbour_sum(padded, edges, window, blocks)

    inner, whole = prefix(residual)
    prefixed[...] = inner
    totals[...] = whole
    rows, lanes = ends_row[...], ends_lane[...]
    count = rows.shape[0]
    run = jnp.zeros((count, LANES), F32)
    ends = jnp.zeros((count, LANES), F32)
    for block in range(blocks):
        value = gather_lanes(wide(prefixed[pl.ds(block, 1), :], count), lanes) + run
        ends = jnp.where(rows == block, value, ends)
        run = run + wide(totals[pl.ds(block, 1), :], count)
    ends = jnp.where(rows == blocks, run, ends)
    own_source = ends - previous_one(ends)

    lane = lax.broadcasted_iota(I32, (1, LANES), 1)
    rim_rows, rim_counts = [], []
    for side in range(2):
        inside = padded[pl.ds(8 if side == 0 else 7 + blocks, 1), :]
        value = jnp.zeros((1, LANES), F32)
        for link in range(3):
            place = lane + arrivals[side, pl.ds(OFFSET + link, 1), :].astype(I32)
            index = lax.bitwise_and(place, LANES - 1)
            reached = (place >= LANES) if side == 0 else (place < 0)
            weight = arrivals[side, pl.ds(EDGE_HI + link, 1), :] + arrivals[side, pl.ds(EDGE_LO + link, 1), :]
            value = value + jnp.where(
                wide(reached.astype(I32)) > 0,
                wide(weight) * gather_lanes(wide(inside), wide(index)),
                0.0,
            )[0:1]
        rim_rows.append(value)
        owners = arrivals[side, pl.ds(OWNER, 1), :].astype(I32)
        below = jnp.where(
            lax.broadcasted_iota(I32, (LANES, LANES), 0) >= owners, 1.0, 0.0
        ).astype(BF16)
        rim_counts.append(dot_nt(jnp.ones((8, LANES), BF16), below))
    rim_inner, rim_whole = prefix(jnp.concatenate([wide(r) for r in rim_rows], axis=0))
    rim_source = []
    for side in range(2):
        place = rim_counts[side].astype(I32)
        index = lax.bitwise_and(place, LANES - 1)
        value = gather_lanes(rim_inner[8 * side : 8 * side + 8], index)
        value = jnp.where(place >= LANES, rim_whole[8 * side : 8 * side + 8], value)
        shifted = pltpu.roll(value, 1, axis=1)
        first = lax.broadcasted_iota(I32, (8, LANES), 1) == 0
        rim_source.append((value - jnp.where(first, 0.0, shifted))[0:1])

    frows = own_source.shape[0]
    source_out[...] = jnp.zeros((FRAME, LANES), F32)
    source_out[pl.ds(OWN, frows), :] = own_source
    source_out[pl.ds(OWN - 1, 1), :] = rim_source[0]
    source_out[pl.ds(OWN + frows, 1), :] = rim_source[1]
    reach = LANES // 8
    frame[...] = jnp.zeros(frame.shape, F32)
    frame[pl.ds(6 * FRAME, FRAME), :] = jnp.ones((FRAME, LANES), F32)
    frame[pl.ds(7 * FRAME, FRAME), :] = jnp.full((FRAME, LANES), 127.0, F32)
    bottoms = 16
    at_cell = lax.broadcasted_iota(I32, (frows, LANES), 0) * LANES + lax.broadcasted_iota(
        I32, (frows, LANES), 1
    )
    for link in range(3):
        frame[pl.ds(link * FRAME + OWN, frows), :] = (ctable[link] - reach - at_cell).astype(F32)
        frame[pl.ds((3 + link) * FRAME + OWN, frows), :] = cedge[link]
    frame[pl.ds(6 * FRAME + OWN, frows), :] = cdiag[...]
    frame[pl.ds(7 * FRAME + OWN, frows), :] = (cowner[...] + bottoms).astype(F32)
    for side in range(2):
        for row in range(2):
            at = (OWN - 2 + row) if side == 0 else (OWN + frows + row)
            for link in range(3):
                put = 3 * row + link
                frame[pl.ds(link * FRAME + at, 1), :] = arrivals[side, pl.ds(COFFSET + put, 1), :]
                frame[pl.ds((3 + link) * FRAME + at, 1), :] = (
                    arrivals[side, pl.ds(CEDGE_HI + put, 1), :] + arrivals[side, pl.ds(CEDGE_LO + put, 1), :]
                )
            frame[pl.ds(6 * FRAME + at, 1), :] = (
                arrivals[side, pl.ds(CDIAG_HI + row, 1), :] + arrivals[side, pl.ds(CDIAG_LO + row, 1), :]
            )
            frame[pl.ds(7 * FRAME + at, 1), :] = arrivals[side, pl.ds(COWNER + row, 1), :] + (
                2.0 * bottoms * side
            )
    for link in range(3):
        frame[pl.ds(6 * FRAME, FRAME), :] += frame[pl.ds((3 + link) * FRAME, FRAME), :]
    source = source_out[...]
    first = RELAXATION * source / frame[pl.ds(6 * FRAME, FRAME), :]
    residual = (1.0 - RELAXATION) * source + first_level_sum(first, frame)
    codes = frame[pl.ds(7 * FRAME, FRAME), :].astype(I32)
    pieces = split3(residual)
    left_side, right_side = [], []
    bins = lax.broadcasted_iota(I32, (LANES, LANES), 0)
    for row in range(OWN - 2, OWN + frows + 2):
        left_side.append(jnp.concatenate([p[row : row + 1] for p in pieces], axis=0))
        right_side.append(
            jnp.where(bins == codes[row : row + 1], 1.0, 0.0).astype(BF16)
        )
    bottom = dot_nt(jnp.concatenate(left_side, axis=1), jnp.concatenate(right_side, axis=1))
    bottom = bottom[0:1] + bottom[1:2] + bottom[2:3]
    bottom = jnp.where(lane < 3 * bottoms, bottom, 0.0)

    to_left = jnp.concatenate(
        [bottom, padded[pl.ds(8, 1), :], own_source[0:2], rim_source[0], jnp.zeros((3, LANES), F32)], axis=0
    )
    to_right = jnp.concatenate(
        [bottom, padded[pl.ds(7 + blocks, 1), :], own_source[frows - 2 : frows], rim_source[1], jnp.zeros((3, LANES), F32)],
        axis=0,
    )
    for other in range(message.shape[0]):
        message[other] = to_right
    message[lax.rem(tile + tile_count - 1, tile_count)] = to_left


def prepare_kernel(
    fresh, ends_new, summed, far, near, cinverse, fresh_out, received, weights, sem, extended
):
    even = lax.rem(lax.axis_index("tile"), 2) == 0
    cells = fresh_out.shape[1]
    copies = [
        pltpu.make_async_copy(
            ends_new.at[:, pl.ds(side * LANES, LANES)],
            fresh_out.at[:, pl.ds(side * (cells - LANES), LANES)],
            sem.at[side],
        )
        for side in range(2)
    ]
    middle = pl.ds(LANES, cells - 2 * LANES)
    copies.append(pltpu.make_async_copy(fresh.at[:, middle], fresh_out.at[:, middle], sem.at[2]))
    for copy in copies:
        copy.start()
    channels, blocks = summed.shape[:2]
    for block in range(blocks):
        for channel in range(channels):
            received[pl.ds(channel, 1), pl.ds(block * LANES, LANES)] = summed[channel, pl.ds(block, 1), :]
    bottoms, size = cinverse.shape
    halves = size // LANES
    part = pl.ds(INVERSE, 32 * halves)
    left, right = sides(far[part, :].astype(F32), near[part, :].astype(F32), even)
    for half in range(halves):
        part = pl.ds(half * LANES, LANES)
        for at, block in ((0, left), (2, right)):
            extended[pl.ds(at * bottoms, bottoms), part] = (
                block[16 * half : 16 * half + 16]
                + block[16 * (halves + half) : 16 * (halves + half) + 16]
            )
        extended[pl.ds(bottoms, bottoms), part] = cinverse[:, part]
    table = extended[...]
    lane = lax.broadcasted_iota(I32, (3 * bottoms, LANES), 1)
    for other in range(weights.shape[0]):
        shift = (size - (other - 1) * bottoms) % size
        turned = pltpu.roll(table, shift, axis=1) if shift else table
        weights[other] = jnp.where(lane < 3 * bottoms, turned[:, :LANES], 0.0)
    for copy in copies:
        copy.wait()


def backward_kernel(
    frame_rows, arrived, weights, source, frame, force, smooth, edges, window, diagonal, owner, far, near,
    height, frame_source, padded, third_rows,
):
    tile = lax.axis_index("tile")
    tile_count = lax.axis_size("tile")
    blocks = force.shape[0]
    left = arrived[lax.rem(tile + tile_count - 1, tile_count)]
    right = arrived[lax.rem(tile + 1, tile_count)]
    count = weights.shape[1]
    partial = jnp.zeros((count, LANES), F32)
    for other in range(weights.shape[0]):
        partial = partial + weights[other] * wide(arrived[other, pl.ds(0, 1), :], count)
    partial = jnp.concatenate([partial, jnp.zeros((LANES - count, LANES), F32)], axis=0)
    ones = jnp.ones((8, LANES), BF16)
    pieces = split3(partial)
    bottom = dot_nt(ones, pieces[0]) + dot_nt(ones, pieces[1]) + dot_nt(ones, pieces[2])

    frows = frame_rows
    frame_source[...] = source[...]
    frame_source[pl.ds(OWN - 2, 2), :] += left[2:4]
    frame_source[pl.ds(OWN, 1), :] += left[4:5]
    frame_source[pl.ds(OWN + frows - 1, 1), :] += right[4:5]
    frame_source[pl.ds(OWN + frows, 2), :] += right[2:4]
    total_source = frame_source[...]
    total = frame[pl.ds(6 * FRAME, FRAME), :]
    codes = frame[pl.ds(7 * FRAME, FRAME), :].astype(I32)
    second = RELAXATION * total_source / total + gather_lanes(wide(bottom[0:1], FRAME), codes)
    third = second + RELAXATION * (
        total_source - total * second + first_level_sum(second, frame)
    ) / total
    third_rows[...] = third

    owners = owner[...]
    index = lax.bitwise_and(owners, LANES - 1)
    which = lax.shift_right_logical(owners, 7)
    corrected = jnp.zeros((blocks, LANES), F32)
    for row in range(frows):
        corrected = jnp.where(
            which == row, gather_lanes(wide(third_rows[pl.ds(OWN + row, 1), :], blocks), index), corrected
        )
    corrected = smooth[...] + corrected
    padded[pl.ds(8, blocks), :] = corrected
    part = pl.ds(16, 16)
    even = lax.rem(tile, 2) == 0
    left_owner, right_owner = [
        rows[OWNER - 16 : OWNER - 15].astype(I32)
        for rows in sides(far[part, :].astype(F32), near[part, :].astype(F32), even)
    ]
    left_rim = left[1:2] + gather_lanes(wide(third_rows[pl.ds(OWN - 1, 1), :]), wide(left_owner))[0:1]
    right_rim = right[1:2] + gather_lanes(wide(third_rows[pl.ds(OWN + frows, 1), :]), wide(right_owner))[0:1]
    padded[pl.ds(7, 1), :] = left_rim
    padded[pl.ds(8 + blocks, 1), :] = right_rim
    fine_total = diagonal[...] + edges[0] + edges[1] + edges[2]
    beside = neighbour_sum(padded, edges, window, blocks)
    height[...] = corrected + RELAXATION * (force[...] - (fine_total * corrected - beside)) / fine_total


def in_hbm(array):
    return pltpu.with_memory_space_constraint(array, pltpu.HBM)


def struct(shape, dtype=F32):
    return jax.ShapeDtypeStruct(shape, dtype)


VMEM = pl.BlockSpec(memory_space=pltpu.VMEM)
SMEM = pl.BlockSpec(memory_space=pltpu.SMEM)
ANY = pl.BlockSpec(memory_space=pltpu.HBM)
PARAMS = pltpu.CompilerParams(vmem_limit_bytes=16 * 1024 * 1024)


def per_device(
    fields, level_rate, edge_weight, fine_diagonal, fine_table, old_height, level_weight,
    flux_weight, fine_owner, coarse_table, coarse_edge, coarse_diagonal, coarse_owner,
    coarse_inverse, surface_out, send_blocks, entry_slot, entry_block, remap_tiles,
):
    tile_count = lax.axis_size("tile")
    cells = fields.shape[2]
    blocks = cells // LANES
    firsts = coarse_diagonal.shape[1]
    frows = firsts // LANES
    entries = entry_slot.shape[2]
    channels = surface_out.shape[1]
    slots = send_blocks.shape[2]
    each = slots // 5
    halves = coarse_inverse.shape[2] // LANES
    bottoms = coarse_inverse.shape[1]
    base = pick_base(halves)
    swap = [(0, 1), (1, 0)]
    surface = lax.ppermute(surface_out[0], "comp", swap)
    sends = lax.ppermute(send_blocks[0], "comp", swap)
    raw = (
        fields[0],
        old_height.reshape(blocks, LANES),
        edge_weight[0].reshape(3, blocks, LANES),
        fine_table[0].reshape(3, blocks, LANES),
        fine_owner.reshape(blocks, LANES),
        fine_diagonal.reshape(blocks, LANES),
        coarse_table[0].reshape(3, frows, LANES),
        coarse_edge[0].reshape(3, frows, LANES),
        coarse_diagonal.reshape(frows, LANES),
        coarse_owner.reshape(frows, LANES),
        coarse_inverse[0],
        entry_slot[0],
        entry_block[0],
        level_rate,
        level_weight,
        flux_weight,
    )
    loaded = pl.pallas_call(
        load_kernel,
        out_shape=[struct(x.shape, x.dtype) for x in raw[:-3]] + [struct((24, LANES))],
        in_specs=[ANY] * len(raw),
        out_specs=[VMEM] * (len(raw) - 2),
        scratch_shapes=[pltpu.VMEM(x.shape, x.dtype) for x in raw[-3:]]
        + [pltpu.SemaphoreType.DMA((len(raw),))],
        compiler_params=PARAMS,
        name="load",
    )(*[in_hbm(x) for x in raw])
    (
        current, old, edges, table, owner, diagonal, ctable, cedge, cdiag, cowner, cinverse,
        slot, block, scalars,
    ) = loaded

    pick = struct((4 * each, LANES), BF16)
    both = struct((base + 4 * each, LANES), BF16)
    to_right2, far, to_left2, near, here = pl.pallas_call(
        pack_kernel,
        out_shape=[both, both, both, both, pick],
        in_specs=[VMEM] * 12,
        out_specs=[VMEM] * 5,
        scratch_shapes=[
            pltpu.VMEM((channels * blocks, LANES), F32),
            pltpu.VMEM((base, LANES), F32),
            pltpu.VMEM((base, LANES), F32),
        ],
        compiler_params=PARAMS,
        name="pack",
    )(
        surface, sends, current, old, edges, table, owner, ctable, cedge, cdiag, cowner, cinverse,
    )

    def shifted(array, distance):
        return lax.ppermute(
            array, "tile", [(i, (i + distance) % tile_count) for i in range(tile_count)]
        )

    def swapped(array, start):
        lower = [i for i in range(tile_count) if i % 2 == start]
        pairs = [(i, (i + 1) % tile_count) for i in lower]
        return lax.ppermute(array, "tile", pairs + [(j, i) for i, j in pairs])

    from_left2 = shifted(to_right2, 2)
    far = swapped(far, 1)
    from_right2 = shifted(to_left2, -2)
    near = swapped(near, 0)

    fresh, force_part, beside_old, window, ends_row, ends_lane, hot, member, tiles = pl.pallas_call(
        stencil_kernel,
        out_shape=[
            struct((fields.shape[1], cells)),
            struct((blocks, LANES)),
            struct((blocks, LANES)),
            struct((3, blocks, LANES), I32),
            struct((frows, LANES), I32),
            struct((frows, LANES), I32),
            struct((slots, entries), BF16),
            struct((blocks, entries), BF16),
            pltpu.VMEM(remap_tiles.shape[2:], BF16),
        ],
        in_specs=[VMEM] * 9 + [ANY],
        out_specs=[VMEM] * 9,
        scratch_shapes=[pltpu.VMEM((blocks + 16, LANES), F32), pltpu.SemaphoreType.DMA((math.gcd(entries, 8),))],
        compiler_params=PARAMS,
        name="stencil",
    )(here, scalars, current, edges, table, old, owner, slot, block, in_hbm(remap_tiles[0, 0]))

    summed, force, smooth, source, frame, ends_new, message = pl.pallas_call(
        forward_kernel,
        out_shape=[
            struct((channels, blocks, LANES)),
            struct((blocks, LANES)),
            struct((blocks, LANES)),
            struct((FRAME, LANES)),
            struct((8 * FRAME, LANES)),
            struct((fields.shape[1], 2 * LANES)),
            struct((tile_count, 8, LANES)),
        ],
        in_specs=[VMEM] * 23,
        out_specs=[VMEM] * 7,
        scratch_shapes=[
            pltpu.VMEM((4 * entries, LANES), F32),
            pltpu.VMEM((4 * entries, LANES), F32),
            pltpu.VMEM((blocks + 16, LANES), F32),
            pltpu.VMEM((blocks, LANES), F32),
            pltpu.VMEM((blocks, LANES), F32),
            pltpu.VMEM((2, base, LANES), F32),
        ],
        compiler_params=PARAMS,
        name="forward",
    )(
        tiles, scalars, from_left2, far, from_right2, near, here, hot, member, current, edges, window, old,
        diagonal, force_part, beside_old, ends_row, ends_lane, fresh, ctable, cedge, cdiag, cowner,
    )
    arrived = lax.all_to_all(message, "tile", split_axis=0, concat_axis=0, tiled=True)
    advanced, received, weights = pl.pallas_call(
        prepare_kernel,
        out_shape=[
            struct((fields.shape[1], cells)),
            struct((channels, cells)),
            struct((tile_count, 3 * bottoms, LANES)),
        ],
        in_specs=[VMEM] * 6,
        out_specs=[ANY, VMEM, VMEM],
        scratch_shapes=[
            pltpu.SemaphoreType.DMA((3,)),
            pltpu.VMEM((3 * bottoms, bottoms * tile_count), F32),
        ],
        compiler_params=PARAMS,
        name="prepare",
    )(fresh, ends_new, summed, far, near, cinverse)
    height = pl.pallas_call(
        functools.partial(backward_kernel, frows),
        out_shape=struct((blocks, LANES)),
        in_specs=[VMEM] * 12,
        out_specs=VMEM,
        scratch_shapes=[
            pltpu.VMEM((FRAME, LANES), F32),
            pltpu.VMEM((blocks + 16, LANES), F32),
            pltpu.VMEM((FRAME, LANES), F32),
        ],
        compiler_params=PARAMS,
        name="backward",
    )(arrived, weights, source, frame, force, smooth, edges, window, diagonal, owner, far, near)
    return advanced[None], received[None], height.reshape(1, cells)


def solution(mesh):
    in_specs = (
        P("comp", None, "tile"),
        P("comp", None),
        P("comp", None, "tile"),
        P("comp", "tile"),
        P("comp", None, "tile"),
        P("comp", "tile"),
        P("comp", None),
        P("comp", None),
        P("comp", "tile"),
        P("comp", None, "tile"),
        P("comp", None, "tile"),
        P("comp", "tile"),
        P("comp", "tile"),
        P("comp", "tile", None),
        P("comp", None, "tile"),
        P("comp", "tile", None),
        P("comp", "tile", None),
        P("comp", "tile", None),
        P("comp", "tile", None, None, None),
    )
    out_specs = (P("comp", None, "tile"), P("comp", None, "tile"), P("comp", "tile"))
    return jax.shard_map(
        per_device, mesh=mesh, in_specs=in_specs, out_specs=out_specs, check_vma=False
    )
```

```python
import functools
import math

import jax
import jax.numpy as jnp
from jax import lax
from jax.experimental import pallas as pl
from jax.experimental.pallas import tpu as pltpu
from jax.sharding import PartitionSpec as P

LANES = 128
RELAXATION = 0.8
F32 = jnp.float32
BF16 = jnp.bfloat16
I32 = jnp.int32

FIELD_HI, FIELD_LO = 0, 8
EDGE_HI, EDGE_LO, OLD_HI, OLD_LO = 16, 19, 22, 23
OFFSET, OWNER = 24, 27
CEDGE_HI, CEDGE_LO, CDIAG_HI, CDIAG_LO = 32, 38, 44, 46
COFFSET, COWNER = 48, 54
INVERSE = 56

FRAME, OWN = 32, 8


def sides(far, near, even):
    return jnp.where(even, far, near), jnp.where(even, near, far)


def gather_lanes(table, index):
    return jnp.take_along_axis(table, index, axis=1)


def wide(row, count=8):
    return jnp.broadcast_to(row, (count, row.shape[1]))


def split2(x):
    high = x.astype(BF16)
    return high, (x - high.astype(F32)).astype(BF16)


def dot_nt(a, b):
    return lax.dot_general(a, b, (((1,), (1,)), ((), ())), preferred_element_type=F32)


def dot_tn(a, b):
    return lax.dot_general(a, b, (((0,), (0,)), ((), ())), preferred_element_type=F32)


def pick_base(inverse_blocks):
    return -(-(INVERSE + 32 * inverse_blocks) // 16) * 16


def load_kernel(*refs):
    count = (len(refs) - 2) // 2
    sources, kept, scalars = refs[:count], refs[count : 2 * count - 3], refs[2 * count - 3]
    spread, sems = refs[2 * count - 2 : 2 * count + 1], refs[2 * count + 1]
    copies = [
        pltpu.make_async_copy(source, target, sems.at[i])
        for i, (source, target) in enumerate(zip(sources, kept + spread))
    ]
    for copy in copies:
        copy.start()
    for copy in copies:
        copy.wait()
    for i, value in enumerate(spread):
        width = value.shape[1]
        diagonal = lax.broadcasted_iota(I32, (8, width), 0) == lax.broadcasted_iota(I32, (8, width), 1)
        column = jnp.sum(jnp.where(diagonal, wide(value[...]), 0.0), axis=1, keepdims=True)
        scalars[pl.ds(8 * i, 8), :] = jnp.broadcast_to(column, (8, LANES))


def pack_kernel(
    surface, sends, fields, old, edge, table, owner, ctable, cedge, cdiag, cowner, cinverse,
    to_right2, far, to_left2, near, here, chunks, left_rows, right_rows,
):
    even = lax.rem(lax.axis_index("tile"), 2) == 0
    cells = fields.shape[1]
    blocks = cells // LANES
    frows = ctable.shape[1]
    firsts = frows * LANES
    base = pick_base(cinverse.shape[1] // LANES)
    lane = lax.broadcasted_iota(I32, (1, LANES), 1)

    for rows, at_left in ((right_rows, False), (left_rows, True)):
        start = 0 if at_left else cells - LANES
        part = pl.ds(start, LANES)

        def both(high, low_row, value):
            count = value.shape[0]
            rows[pl.ds(high, count), :] = value
            rows[pl.ds(low_row, count), :] = value - value.astype(BF16).astype(F32)

        def three(ref, row):
            return jnp.concatenate([ref[link, pl.ds(row, 1), :] for link in range(3)], axis=0)

        rows[pl.ds(24, 8), :] = jnp.zeros((8, LANES), F32)
        both(FIELD_HI, FIELD_LO, fields[:, part])
        block = 0 if at_left else blocks - 1
        both(EDGE_HI, EDGE_LO, three(edge, block))
        both(OLD_HI, OLD_LO, old[pl.ds(block, 1), :])
        rows[pl.ds(OFFSET, 3), :] = (three(table, block) - (LANES + start) - lane).astype(F32)
        shift = 0 if at_left else firsts - LANES
        rows[pl.ds(OWNER, 1), :] = (owner[pl.ds(block, 1), :] - shift).astype(F32)
        first = 0 if at_left else frows - 2
        reach = LANES // 8
        for step in range(2):
            both(CEDGE_HI + 3 * step, CEDGE_LO + 3 * step, three(cedge, first + step))
            rows[pl.ds(COFFSET + 3 * step, 3), :] = (
                three(ctable, first + step) - (reach + (first + step) * LANES) - lane
            ).astype(F32)
            both(CDIAG_HI + step, CDIAG_LO + step, cdiag[pl.ds(first + step, 1), :])
            rows[pl.ds(COWNER + step, 1), :] = cowner[pl.ds(first + step, 1), :].astype(F32)
        halves = cinverse.shape[1] // LANES
        for half in range(halves):
            both(
                INVERSE + 16 * half,
                INVERSE + 16 * (halves + half),
                cinverse[:, pl.ds(half * LANES, LANES)],
            )
        end = INVERSE + 32 * halves
        if base > end:
            rows[pl.ds(end, base - end), :] = jnp.zeros((base - end, LANES), F32)

    for block in range(blocks):
        chunks[pl.ds(4 * block, 4), :] = surface[:, pl.ds(block * LANES, LANES)].astype(F32)
    slots = sends.shape[1]
    hot = jnp.where(
        lax.broadcasted_iota(I32, (blocks, slots), 0) == sends[...], 1.0, 0.0
    ).astype(BF16)
    picks = []
    for channel in range(4):
        source = chunks[pl.ds(channel, blocks, stride=4), :].astype(BF16)
        picks.append(dot_tn(hot, source).astype(BF16))
    count = slots // 5

    chosen = [
        jnp.concatenate([p[j * count : (j + 1) * count] for p in picks], axis=0) for j in range(5)
    ]
    here[...] = chosen[2]
    for out, j in ((to_right2, 0), (to_left2, 4)):
        out[pl.ds(0, base), :] = jnp.zeros((base, LANES), BF16)
        out[pl.ds(base, 4 * count), :] = chosen[j]
    right = jnp.concatenate([right_rows[...].astype(BF16), chosen[1]], axis=0)
    left = jnp.concatenate([left_rows[...].astype(BF16), chosen[3]], axis=0)
    far[...] = jnp.where(even, left, right)
    near[...] = jnp.where(even, right, left)


def stencil_kernel(
    here, scalars, fields, edge, table, old, diagonal, owner, slots, entry_block, tiles,
    fresh, force, beside_old, window, ends_row, ends_lane, hot, member, damping, tile_buffer, padded, sems,
):
    del here
    parts = sems.shape[0]
    step = tiles.shape[0] // parts

    def load(part):
        span = pl.ds(part * step, step)
        return pltpu.make_async_copy(tiles.at[span], tile_buffer.at[span], sems.at[part])

    def begin(part, carry):
        load(part).start()
        return carry

    lax.fori_loop(0, parts, begin, 0)
    blocks = old.shape[0]
    levels = fields.shape[0]
    speed = scalars[pl.ds(0, 8), :]
    share = scalars[pl.ds(8, 8), :]
    starts = lax.broadcasted_iota(I32, (blocks, LANES), 0) * LANES
    total = edge[0] + edge[1] + edge[2]
    inverse = 1.0 / total
    fine_total = diagonal[...] + total
    damping[0] = fine_total
    damping[1] = RELAXATION / fine_total
    for link in range(3):
        window[link] = table[link] - starts
    blank = jnp.zeros((levels, LANES), F32)

    def chunk(block):
        if 0 <= block < blocks:
            return fields[:, pl.ds(block * LANES, LANES)]
        return blank

    before, here, after = blank, chunk(0), chunk(1)
    for block in range(blocks):
        row = slice(block, block + 1)
        beside = jnp.zeros((levels, LANES), F32)
        for link in range(3):
            place = wide(window[link, pl.ds(block, 1), :])
            index = lax.bitwise_and(place, LANES - 1)
            value = jnp.where(
                place < LANES,
                gather_lanes(before, index),
                jnp.where(place < 2 * LANES, gather_lanes(here, index), gather_lanes(after, index)),
            )
            beside = beside + wide(edge[link, pl.ds(block, 1), :]) * value
        result = here + speed * ((beside - wide(total[row]) * here) * wide(inverse[row]))
        fresh[:, pl.ds(block * LANES, LANES)] = result
        force[pl.ds(block, 1), :] = jnp.sum(result * share, axis=0, keepdims=True)
        before, here, after = here, after, chunk(block + 2)

    padded[pl.ds(0, 8), :] = jnp.zeros((8, LANES), F32)
    padded[pl.ds(8 + blocks, 8), :] = jnp.zeros((8, LANES), F32)
    padded[pl.ds(8, blocks), :] = old[...]
    beside_old[...] = neighbour_sum(padded, edge, window, blocks)
    names = jnp.where(
        lax.broadcasted_iota(I32, (slots.shape[1], slots.shape[1]), 0) == slots[...], 1.0, 0.0
    )
    hot[...] = jnp.transpose(names).astype(BF16)
    half = entry_block.shape[1] // 2
    for part in range(2):
        member[part] = jnp.where(
            lax.broadcasted_iota(I32, (blocks, half), 0) == entry_block[:, part * half : (part + 1) * half],
            1.0,
            0.0,
        ).astype(BF16)

    firsts = ends_row.shape[0] * LANES
    ident = lax.broadcasted_iota(I32, ends_row.shape, 0) * LANES + lax.broadcasted_iota(
        I32, ends_row.shape, 1
    )
    count = ends_row.shape[0]
    rows = jnp.zeros(ends_row.shape, I32)
    for block in range(blocks):
        last = jnp.broadcast_to(owner[pl.ds(block, 1), LANES - 1 : LANES], ends_row.shape)
        rows = rows + jnp.where(last <= ident, 1, 0)
    lanes = jnp.zeros(ends_row.shape, I32)
    for bit in (64, 32, 16, 8, 4, 2, 1):
        probe = lanes + (bit - 1)
        value = jnp.full(ends_row.shape, firsts, I32)
        for block in range(blocks):
            value = jnp.where(
                rows == block, gather_lanes(wide(owner[pl.ds(block, 1), :], count), probe), value
            )
        lanes = jnp.where(value <= ident, lanes + bit, lanes)
    ends_row[...] = rows
    ends_lane[...] = lanes
    for part in range(parts):
        load(part).wait()


def neighbour_sum(padded, edges, window, blocks):
    before = padded[pl.ds(7, blocks), :]
    here = padded[pl.ds(8, blocks), :]
    after = padded[pl.ds(9, blocks), :]
    result = jnp.zeros((blocks, LANES), F32)
    for link in range(3):
        place = window[link]
        index = lax.bitwise_and(place, LANES - 1)
        value = jnp.where(
            place < LANES,
            gather_lanes(before, index),
            jnp.where(place < 2 * LANES, gather_lanes(here, index), gather_lanes(after, index)),
        )
        result = result + edges[link] * value
    return result


def first_level_sum(values, frame):
    before = pltpu.roll(values, 1, axis=0)
    after = pltpu.roll(values, FRAME - 1, axis=0)
    lane = lax.broadcasted_iota(I32, (FRAME, LANES), 1)
    result = jnp.zeros((FRAME, LANES), F32)
    for link in range(3):
        place = lane + frame[pl.ds(link * FRAME, FRAME), :].astype(I32)
        index = lax.bitwise_and(place, LANES - 1)
        value = jnp.where(
            place < 0,
            gather_lanes(before, index),
            jnp.where(place >= LANES, gather_lanes(after, index), gather_lanes(values, index)),
        )
        result = result + frame[pl.ds((3 + link) * FRAME, FRAME), :] * value
    return result


def previous_one(values):
    rolled = pltpu.roll(values, 1, axis=1)
    above = pltpu.roll(rolled, 1, axis=0)
    lane = lax.broadcasted_iota(I32, values.shape, 1)
    row = lax.broadcasted_iota(I32, values.shape, 0)
    return jnp.where(lane > 0, rolled, jnp.where(row > 0, above, 0.0))


def triangle():
    return jnp.where(
        lax.broadcasted_iota(I32, (LANES, LANES), 0) < lax.broadcasted_iota(I32, (LANES, LANES), 1),
        1.0,
        0.0,
    ).astype(BF16)


def prefix(values):
    ones = jnp.ones((LANES, LANES), BF16)
    right = jnp.concatenate([triangle(), ones], axis=1)
    count = values.shape[0]
    out = jnp.dot(
        jnp.concatenate(split2(values), axis=0), right, preferred_element_type=F32
    )
    out = out[:count] + out[count:]
    return out[:, :LANES], out[:, LANES:]


def rows_before(values):
    sublane = lax.broadcasted_iota(I32, (8, LANES), 0)
    run = jnp.zeros((8, LANES), F32)
    result = []
    for at in range(0, values.shape[0], 8):
        piece = values[at : at + 8]
        total = piece
        for distance in (1, 2, 4):
            total = total + jnp.where(sublane >= distance, pltpu.roll(total, distance, axis=0), 0.0)
        result.append(run + (total - piece))
        run = run + wide(total[7:8])
    return jnp.concatenate(result, axis=0), run


def forward_kernel(
    tiles, scalars, from_left2, far, from_right2, near, here, hot, member, fields, edges, window, old,
    damping, force_part, beside_old, ends_row, ends_lane, fresh, ctable, cedge, cdiag, cowner,
    summed, force_out, smooth_out, source_out, frame, ends_out, message,
    picked, products, padded, prefixed, arrivals,
):
    tile = lax.axis_index("tile")
    tile_count = lax.axis_size("tile")
    entries = tiles.shape[0]
    blocks = old.shape[0]

    even = lax.rem(tile, 2) == 0
    base = far.shape[0] - here.shape[0]
    each = here.shape[0] // 4
    from_left, from_right = sides(far[...], near[...], even)
    sources = (from_left2[base:, :], from_left[base:], here[...], from_right[base:], from_right2[base:, :])
    for channel in range(4):
        source = jnp.concatenate(
            [rows[channel * each : (channel + 1) * each] for rows in sources], axis=0
        )
        picked[pl.ds(channel, entries, stride=4), :] = jnp.dot(hot[...], source, preferred_element_type=F32)

    arrivals[0] = from_left[:base].astype(F32)
    arrivals[1] = from_right[:base].astype(F32)

    upper = lax.rem(lax.broadcasted_iota(I32, (16, LANES), 0), 8) < 4
    for group in range(entries // 4):
        rows = picked[pl.ds(16 * group, 16), :]
        rows = jnp.concatenate([jnp.where(upper, rows, 0.0), jnp.where(upper, 0.0, rows)], axis=1)
        at = 4 * group
        weights = jnp.concatenate(
            [
                jnp.concatenate([tiles[at], tiles[at + 1]], axis=1),
                jnp.concatenate([tiles[at + 2], tiles[at + 3]], axis=1),
            ],
            axis=0,
        )
        product = dot_nt(rows.astype(BF16), weights)
        products[pl.ds(16 * group, 8), :] = product[0:8, :LANES]
        products[pl.ds(16 * group + 8, 8), :] = product[8:16, LANES:]
    half = entries // 2
    for channel in range(4):
        value = jnp.zeros((blocks, 2 * LANES), F32)
        for part in range(2):
            rows = products[pl.ds(4 * half * part + channel, half, stride=4), :]
            value = value + jnp.dot(
                member[part], jnp.concatenate(split2(rows), axis=1), preferred_element_type=F32
            )
        summed[channel] = value[:, :LANES] + value[:, LANES:]

    speed = scalars[pl.ds(0, 8), :]
    share = scalars[pl.ds(8, 8), :]
    force_out[...] = force_part[...]
    padded[pl.ds(0, 8), :] = jnp.zeros((8, LANES), F32)
    padded[pl.ds(8 + blocks, 8), :] = jnp.zeros((8, LANES), F32)
    beside_extra = []
    for side, block, target in ((0, 0, 0), (1, blocks - 1, 2)):
        halo = arrivals[side, pl.ds(FIELD_HI, 8), :] + arrivals[side, pl.ds(FIELD_LO, 8), :]
        halo_old = arrivals[side, pl.ds(OLD_HI, 1), :] + arrivals[side, pl.ds(OLD_LO, 1), :]
        total = edges[0, pl.ds(block, 1), :] + edges[1, pl.ds(block, 1), :] + edges[2, pl.ds(block, 1), :]
        extra = jnp.zeros((8, LANES), F32)
        extra_old = jnp.zeros((8, LANES), F32)
        for link in range(3):
            place = wide(window[link, pl.ds(block, 1), :])
            index = lax.bitwise_and(place, LANES - 1)
            weight = jnp.where(
                lax.shift_right_logical(place, 7) == target, wide(edges[link, pl.ds(block, 1), :]), 0.0
            )
            extra = extra + weight * gather_lanes(halo, index)
            extra_old = extra_old + weight * gather_lanes(wide(halo_old), index)
        change = speed * extra / wide(total)
        ends_out[:, pl.ds(side * LANES, LANES)] = fresh[:, pl.ds(block * LANES, LANES)] + change
        force_out[pl.ds(block, 1), :] += jnp.sum(change * share, axis=0, keepdims=True)
        beside_extra.append(extra_old[0:1])

    force = force_out[...]
    for channel in range(4):
        force = force + scalars[pl.ds(16 + channel, 1), :] * summed[channel]
    force_out[...] = force
    total, damp = damping[0], damping[1]
    smooth_out[...] = beside_old[...]
    smooth_out[pl.ds(0, 1), :] += beside_extra[0]
    smooth_out[pl.ds(blocks - 1, 1), :] += beside_extra[1]
    previous = old[...]
    smooth = previous + damp * (force - (total * previous - smooth_out[...]))
    smooth_out[...] = smooth
    padded[pl.ds(8, blocks), :] = smooth
    residual = force - total * smooth + neighbour_sum(padded, edges, window, blocks)

    inner, whole = prefix(residual)
    before, run = rows_before(whole)
    prefixed[...] = inner + before
    rows, lanes = ends_row[...], ends_lane[...]
    count = rows.shape[0]
    ends = run[:count]
    for block in range(blocks):
        value = gather_lanes(wide(prefixed[pl.ds(block, 1), :], count), lanes)
        ends = jnp.where(rows == block, value, ends)
    own_source = ends - previous_one(ends)

    lane = lax.broadcasted_iota(I32, (1, LANES), 1)
    rim_rows, rim_counts = [], []
    for side in range(2):
        inside = padded[pl.ds(8 if side == 0 else 7 + blocks, 1), :]
        value = jnp.zeros((1, LANES), F32)
        for link in range(3):
            place = lane + arrivals[side, pl.ds(OFFSET + link, 1), :].astype(I32)
            index = lax.bitwise_and(place, LANES - 1)
            reached = (place >= LANES) if side == 0 else (place < 0)
            weight = arrivals[side, pl.ds(EDGE_HI + link, 1), :] + arrivals[side, pl.ds(EDGE_LO + link, 1), :]
            value = value + jnp.where(
                wide(reached.astype(I32)) > 0,
                wide(weight) * gather_lanes(wide(inside), wide(index)),
                0.0,
            )[0:1]
        rim_rows.append(value)
        owners = arrivals[side, pl.ds(OWNER, 1), :].astype(I32)
        below = jnp.where(
            lax.broadcasted_iota(I32, (LANES, LANES), 0) >= owners, 1.0, 0.0
        ).astype(BF16)
        rim_counts.append(dot_nt(jnp.ones((8, LANES), BF16), below))
    rim_inner, rim_whole = prefix(jnp.concatenate([wide(r) for r in rim_rows], axis=0))
    rim_source = []
    for side in range(2):
        place = rim_counts[side].astype(I32)
        index = lax.bitwise_and(place, LANES - 1)
        value = gather_lanes(rim_inner[8 * side : 8 * side + 8], index)
        value = jnp.where(place >= LANES, rim_whole[8 * side : 8 * side + 8], value)
        shifted = pltpu.roll(value, 1, axis=1)
        first = lax.broadcasted_iota(I32, (8, LANES), 1) == 0
        rim_source.append((value - jnp.where(first, 0.0, shifted))[0:1])

    frows = own_source.shape[0]
    source_out[...] = jnp.zeros((FRAME, LANES), F32)
    source_out[pl.ds(OWN, frows), :] = own_source
    source_out[pl.ds(OWN - 1, 1), :] = rim_source[0]
    source_out[pl.ds(OWN + frows, 1), :] = rim_source[1]
    reach = LANES // 8
    frame[...] = jnp.zeros(frame.shape, F32)
    frame[pl.ds(6 * FRAME, FRAME), :] = jnp.ones((FRAME, LANES), F32)
    frame[pl.ds(7 * FRAME, FRAME), :] = jnp.full((FRAME, LANES), 127.0, F32)
    bottoms = 16
    at_cell = lax.broadcasted_iota(I32, (frows, LANES), 0) * LANES + lax.broadcasted_iota(
        I32, (frows, LANES), 1
    )
    for link in range(3):
        frame[pl.ds(link * FRAME + OWN, frows), :] = (ctable[link] - reach - at_cell).astype(F32)
        frame[pl.ds((3 + link) * FRAME + OWN, frows), :] = cedge[link]
    frame[pl.ds(6 * FRAME + OWN, frows), :] = cdiag[...]
    frame[pl.ds(7 * FRAME + OWN, frows), :] = (cowner[...] + bottoms).astype(F32)
    for side in range(2):
        for row in range(2):
            at = (OWN - 2 + row) if side == 0 else (OWN + frows + row)
            for link in range(3):
                put = 3 * row + link
                frame[pl.ds(link * FRAME + at, 1), :] = arrivals[side, pl.ds(COFFSET + put, 1), :]
                frame[pl.ds((3 + link) * FRAME + at, 1), :] = (
                    arrivals[side, pl.ds(CEDGE_HI + put, 1), :] + arrivals[side, pl.ds(CEDGE_LO + put, 1), :]
                )
            frame[pl.ds(6 * FRAME + at, 1), :] = (
                arrivals[side, pl.ds(CDIAG_HI + row, 1), :] + arrivals[side, pl.ds(CDIAG_LO + row, 1), :]
            )
            frame[pl.ds(7 * FRAME + at, 1), :] = arrivals[side, pl.ds(COWNER + row, 1), :] + (
                2.0 * bottoms * side
            )
    for link in range(3):
        frame[pl.ds(6 * FRAME, FRAME), :] += frame[pl.ds((3 + link) * FRAME, FRAME), :]
    source = source_out[...]
    first = (RELAXATION / frame[pl.ds(6 * FRAME, FRAME), :]) * source
    residual = (1.0 - RELAXATION) * source + first_level_sum(first, frame)
    codes = frame[pl.ds(7 * FRAME, FRAME), :].astype(I32)
    pieces = split2(residual)
    left_side, right_side = [], []
    bins = lax.broadcasted_iota(I32, (3 * bottoms, LANES), 0)
    rest = jnp.zeros((LANES - 3 * bottoms, LANES), BF16)
    for row in range(OWN - 2, OWN + frows + 2):
        left_side.append(jnp.concatenate([p[row : row + 1] for p in pieces], axis=0))
        named = jnp.where(bins == codes[row : row + 1], 1.0, 0.0).astype(BF16)
        right_side.append(jnp.concatenate([named, rest], axis=0))
    bottom = dot_nt(jnp.concatenate(left_side, axis=1), jnp.concatenate(right_side, axis=1))
    bottom = bottom[0:1] + bottom[1:2]

    to_left = jnp.concatenate(
        [bottom, padded[pl.ds(8, 1), :], own_source[0:2], rim_source[0], jnp.zeros((3, LANES), F32)], axis=0
    )
    to_right = jnp.concatenate(
        [bottom, padded[pl.ds(7 + blocks, 1), :], own_source[frows - 2 : frows], rim_source[1], jnp.zeros((3, LANES), F32)],
        axis=0,
    )
    for other in range(message.shape[0]):
        message[other] = to_right
    message[lax.rem(tile + tile_count - 1, tile_count)] = to_left


def prepare_kernel(
    fresh, ends_new, summed, far, near, cinverse, fresh_out, received, weights, sem, extended
):
    even = lax.rem(lax.axis_index("tile"), 2) == 0
    cells = fresh_out.shape[1]
    copies = [
        pltpu.make_async_copy(
            ends_new.at[:, pl.ds(side * LANES, LANES)],
            fresh_out.at[:, pl.ds(side * (cells - LANES), LANES)],
            sem.at[side],
        )
        for side in range(2)
    ]
    middle = pl.ds(LANES, cells - 2 * LANES)
    copies.append(pltpu.make_async_copy(fresh.at[:, middle], fresh_out.at[:, middle], sem.at[2]))
    for copy in copies:
        copy.start()
    channels, blocks = summed.shape[:2]
    for block in range(blocks):
        for channel in range(channels):
            received[pl.ds(channel, 1), pl.ds(block * LANES, LANES)] = summed[channel, pl.ds(block, 1), :]
    bottoms, size = cinverse.shape
    halves = size // LANES
    part = pl.ds(INVERSE, 32 * halves)
    left, right = sides(far[part, :].astype(F32), near[part, :].astype(F32), even)
    for half in range(halves):
        part = pl.ds(half * LANES, LANES)
        for at, block in ((0, left), (2, right)):
            extended[pl.ds(at * bottoms, bottoms), part] = (
                block[16 * half : 16 * half + 16]
                + block[16 * (halves + half) : 16 * (halves + half) + 16]
            )
        extended[pl.ds(bottoms, bottoms), part] = cinverse[:, part]
    table = extended[...]
    lane = lax.broadcasted_iota(I32, (3 * bottoms, LANES), 1)
    for other in range(weights.shape[0]):
        shift = (size - (other - 1) * bottoms) % size
        turned = pltpu.roll(table, shift, axis=1) if shift else table
        weights[other] = jnp.where(lane < 3 * bottoms, turned[:, :LANES], 0.0)
    for copy in copies:
        copy.wait()


def backward_kernel(
    frame_rows, arrived, weights, source, frame, force, smooth, edges, window, damping, owner, far, near,
    height, frame_source, padded, third_rows,
):
    tile = lax.axis_index("tile")
    tile_count = lax.axis_size("tile")
    blocks = force.shape[0]
    left = arrived[lax.rem(tile + tile_count - 1, tile_count)]
    right = arrived[lax.rem(tile + 1, tile_count)]
    count = weights.shape[1]
    partial = jnp.zeros((count, LANES), F32)
    for other in range(weights.shape[0]):
        partial = partial + weights[other] * wide(arrived[other, pl.ds(0, 1), :], count)
    partial = jnp.concatenate([partial, jnp.zeros((LANES - count, LANES), F32)], axis=0)
    ones = jnp.ones((8, LANES), BF16)
    bottom = dot_nt(jnp.concatenate([ones, ones], axis=1), jnp.concatenate(split2(partial), axis=1))

    frows = frame_rows
    frame_source[...] = source[...]
    frame_source[pl.ds(OWN - 2, 2), :] += left[2:4]
    frame_source[pl.ds(OWN, 1), :] += left[4:5]
    frame_source[pl.ds(OWN + frows - 1, 1), :] += right[4:5]
    frame_source[pl.ds(OWN + frows, 2), :] += right[2:4]
    total_source = frame_source[...]
    total = frame[pl.ds(6 * FRAME, FRAME), :]
    codes = frame[pl.ds(7 * FRAME, FRAME), :].astype(I32)
    damp = RELAXATION / total
    second = damp * total_source + gather_lanes(wide(bottom[0:1], FRAME), codes)
    third = second + damp * (total_source - total * second + first_level_sum(second, frame))
    third_rows[...] = third

    owners = owner[...]
    index = lax.bitwise_and(owners, LANES - 1)
    which = lax.shift_right_logical(owners, 7)
    corrected = jnp.zeros((blocks, LANES), F32)
    for row in range(frows):
        corrected = jnp.where(
            which == row, gather_lanes(wide(third_rows[pl.ds(OWN + row, 1), :], blocks), index), corrected
        )
    corrected = smooth[...] + corrected
    padded[pl.ds(8, blocks), :] = corrected
    part = pl.ds(16, 16)
    even = lax.rem(tile, 2) == 0
    left_owner, right_owner = [
        rows[OWNER - 16 : OWNER - 15].astype(I32)
        for rows in sides(far[part, :].astype(F32), near[part, :].astype(F32), even)
    ]
    left_rim = left[1:2] + gather_lanes(wide(third_rows[pl.ds(OWN - 1, 1), :]), wide(left_owner))[0:1]
    right_rim = right[1:2] + gather_lanes(wide(third_rows[pl.ds(OWN + frows, 1), :]), wide(right_owner))[0:1]
    padded[pl.ds(7, 1), :] = left_rim
    padded[pl.ds(8 + blocks, 1), :] = right_rim
    beside = neighbour_sum(padded, edges, window, blocks)
    height[...] = corrected + damping[1] * (force[...] - (damping[0] * corrected - beside))


def in_hbm(array):
    return pltpu.with_memory_space_constraint(array, pltpu.HBM)


def struct(shape, dtype=F32):
    return jax.ShapeDtypeStruct(shape, dtype)


VMEM = pl.BlockSpec(memory_space=pltpu.VMEM)
SMEM = pl.BlockSpec(memory_space=pltpu.SMEM)
ANY = pl.BlockSpec(memory_space=pltpu.HBM)
PARAMS = pltpu.CompilerParams(vmem_limit_bytes=16 * 1024 * 1024)


def per_device(
    fields, level_rate, edge_weight, fine_diagonal, fine_table, old_height, level_weight,
    flux_weight, fine_owner, coarse_table, coarse_edge, coarse_diagonal, coarse_owner,
    coarse_inverse, surface_out, send_blocks, entry_slot, entry_block, remap_tiles,
):
    tile_count = lax.axis_size("tile")
    cells = fields.shape[2]
    blocks = cells // LANES
    firsts = coarse_diagonal.shape[1]
    frows = firsts // LANES
    entries = entry_slot.shape[2]
    channels = surface_out.shape[1]
    slots = send_blocks.shape[2]
    each = slots // 5
    halves = coarse_inverse.shape[2] // LANES
    bottoms = coarse_inverse.shape[1]
    base = pick_base(halves)
    swap = [(0, 1), (1, 0)]
    surface = lax.ppermute(surface_out[0], "comp", swap)
    sends = lax.ppermute(send_blocks[0], "comp", swap)
    raw = (
        fields[0],
        old_height.reshape(blocks, LANES),
        edge_weight[0].reshape(3, blocks, LANES),
        fine_table[0].reshape(3, blocks, LANES),
        fine_owner.reshape(blocks, LANES),
        fine_diagonal.reshape(blocks, LANES),
        coarse_table[0].reshape(3, frows, LANES),
        coarse_edge[0].reshape(3, frows, LANES),
        coarse_diagonal.reshape(frows, LANES),
        coarse_owner.reshape(frows, LANES),
        coarse_inverse[0],
        entry_slot[0],
        entry_block[0],
        level_rate,
        level_weight,
        flux_weight,
    )
    loaded = pl.pallas_call(
        load_kernel,
        out_shape=[struct(x.shape, x.dtype) for x in raw[:-3]] + [struct((24, LANES))],
        in_specs=[ANY] * len(raw),
        out_specs=[VMEM] * (len(raw) - 2),
        scratch_shapes=[pltpu.VMEM(x.shape, x.dtype) for x in raw[-3:]]
        + [pltpu.SemaphoreType.DMA((len(raw),))],
        compiler_params=PARAMS,
        name="load",
    )(*[in_hbm(x) for x in raw])
    (
        current, old, edges, table, owner, diagonal, ctable, cedge, cdiag, cowner, cinverse,
        slot, block, scalars,
    ) = loaded

    pick = struct((4 * each, LANES), BF16)
    both = struct((base + 4 * each, LANES), BF16)
    to_right2, far, to_left2, near, here = pl.pallas_call(
        pack_kernel,
        out_shape=[both, both, both, both, pick],
        in_specs=[VMEM] * 12,
        out_specs=[VMEM] * 5,
        scratch_shapes=[
            pltpu.VMEM((channels * blocks, LANES), F32),
            pltpu.VMEM((base, LANES), F32),
            pltpu.VMEM((base, LANES), F32),
        ],
        compiler_params=PARAMS,
        name="pack",
    )(
        surface, sends, current, old, edges, table, owner, ctable, cedge, cdiag, cowner, cinverse,
    )

    def shifted(array, distance):
        return lax.ppermute(
            array, "tile", [(i, (i + distance) % tile_count) for i in range(tile_count)]
        )

    def swapped(array, start):
        lower = [i for i in range(tile_count) if i % 2 == start]
        pairs = [(i, (i + 1) % tile_count) for i in lower]
        return lax.ppermute(array, "tile", pairs + [(j, i) for i, j in pairs])

    from_left2 = shifted(to_right2, 2)
    far = swapped(far, 1)
    from_right2 = shifted(to_left2, -2)
    near = swapped(near, 0)

    fresh, force_part, beside_old, window, ends_row, ends_lane, hot, member, damping, tiles = pl.pallas_call(
        stencil_kernel,
        out_shape=[
            struct((fields.shape[1], cells)),
            struct((blocks, LANES)),
            struct((blocks, LANES)),
            struct((3, blocks, LANES), I32),
            struct((frows, LANES), I32),
            struct((frows, LANES), I32),
            struct((entries, slots), BF16),
            struct((2, blocks, entries // 2), BF16),
            struct((2, blocks, LANES)),
            pltpu.VMEM(remap_tiles.shape[2:], BF16),
        ],
        in_specs=[VMEM] * 10 + [ANY],
        out_specs=[VMEM] * 10,
        scratch_shapes=[pltpu.VMEM((blocks + 16, LANES), F32), pltpu.SemaphoreType.DMA((math.gcd(entries, 8),))],
        compiler_params=PARAMS,
        name="stencil",
    )(here, scalars, current, edges, table, old, diagonal, owner, slot, block, in_hbm(remap_tiles[0, 0]))

    summed, force, smooth, source, frame, ends_new, message = pl.pallas_call(
        forward_kernel,
        out_shape=[
            struct((channels, blocks, LANES)),
            struct((blocks, LANES)),
            struct((blocks, LANES)),
            struct((FRAME, LANES)),
            struct((8 * FRAME, LANES)),
            struct((fields.shape[1], 2 * LANES)),
            struct((tile_count, 8, LANES)),
        ],
        in_specs=[VMEM] * 23,
        out_specs=[VMEM] * 7,
        scratch_shapes=[
            pltpu.VMEM((4 * entries, LANES), F32),
            pltpu.VMEM((4 * entries, LANES), F32),
            pltpu.VMEM((blocks + 16, LANES), F32),
            pltpu.VMEM((blocks, LANES), F32),
            pltpu.VMEM((2, base, LANES), F32),
        ],
        compiler_params=PARAMS,
        name="forward",
    )(
        tiles, scalars, from_left2, far, from_right2, near, here, hot, member, current, edges, window, old,
        damping, force_part, beside_old, ends_row, ends_lane, fresh, ctable, cedge, cdiag, cowner,
    )
    arrived = lax.all_to_all(message, "tile", split_axis=0, concat_axis=0, tiled=True)
    advanced, received, weights = pl.pallas_call(
        prepare_kernel,
        out_shape=[
            struct((fields.shape[1], cells)),
            struct((channels, cells)),
            struct((tile_count, 3 * bottoms, LANES)),
        ],
        in_specs=[VMEM] * 6,
        out_specs=[ANY, VMEM, VMEM],
        scratch_shapes=[
            pltpu.SemaphoreType.DMA((3,)),
            pltpu.VMEM((3 * bottoms, bottoms * tile_count), F32),
        ],
        compiler_params=PARAMS,
        name="prepare",
    )(fresh, ends_new, summed, far, near, cinverse)
    height = pl.pallas_call(
        functools.partial(backward_kernel, frows),
        out_shape=struct((blocks, LANES)),
        in_specs=[VMEM] * 12,
        out_specs=VMEM,
        scratch_shapes=[
            pltpu.VMEM((FRAME, LANES), F32),
            pltpu.VMEM((blocks + 16, LANES), F32),
            pltpu.VMEM((FRAME, LANES), F32),
        ],
        compiler_params=PARAMS,
        name="backward",
    )(arrived, weights, source, frame, force, smooth, edges, window, damping, owner, far, near)
    return advanced[None], received[None], height.reshape(1, cells)


def solution(mesh):
    in_specs = (
        P("comp", None, "tile"),
        P("comp", None),
        P("comp", None, "tile"),
        P("comp", "tile"),
        P("comp", None, "tile"),
        P("comp", "tile"),
        P("comp", None),
        P("comp", None),
        P("comp", "tile"),
        P("comp", None, "tile"),
        P("comp", None, "tile"),
        P("comp", "tile"),
        P("comp", "tile"),
        P("comp", "tile", None),
        P("comp", None, "tile"),
        P("comp", "tile", None),
        P("comp", "tile", None),
        P("comp", "tile", None),
        P("comp", "tile", None, None, None),
    )
    out_specs = (P("comp", None, "tile"), P("comp", None, "tile"), P("comp", "tile"))
    return jax.shard_map(
        per_device, mesh=mesh, in_specs=in_specs, out_specs=out_specs, check_vma=False
    )
```

```python
import functools
import math

import jax
import jax.numpy as jnp
from jax import lax
from jax.experimental import pallas as pl
from jax.experimental.pallas import tpu as pltpu
from jax.sharding import PartitionSpec as P

LANES = 128
RELAXATION = 0.8
F32 = jnp.float32
BF16 = jnp.bfloat16
I32 = jnp.int32

FIELD_HI, FIELD_LO = 0, 8
EDGE_HI, EDGE_LO, OLD_HI, OLD_LO = 16, 19, 22, 23
OFFSET, OWNER = 24, 27
CEDGE_HI, CEDGE_LO, CDIAG_HI, CDIAG_LO = 32, 38, 44, 46
COFFSET, COWNER = 48, 54
INVERSE = 56

FRAME, OWN = 32, 8


def sides(far, near, even):
    return jnp.where(even, far, near), jnp.where(even, near, far)


def gather_lanes(table, index):
    return jnp.take_along_axis(table, index, axis=1)


def wide(row, count=8):
    return jnp.broadcast_to(row, (count, row.shape[1]))


def split2(x):
    high = x.astype(BF16)
    return high, (x - high.astype(F32)).astype(BF16)


def dot_nt(a, b):
    return lax.dot_general(a, b, (((1,), (1,)), ((), ())), preferred_element_type=F32)


def dot_tn(a, b):
    return lax.dot_general(a, b, (((0,), (0,)), ((), ())), preferred_element_type=F32)


def pick_base(inverse_blocks):
    return -(-(INVERSE + 32 * inverse_blocks) // 16) * 16


def load_kernel(*refs):
    count = (len(refs) - 2) // 2
    sources, kept, scalars = refs[:count], refs[count : 2 * count - 3], refs[2 * count - 3]
    spread, sems = refs[2 * count - 2 : 2 * count + 1], refs[2 * count + 1]
    copies = [
        pltpu.make_async_copy(source, target, sems.at[i])
        for i, (source, target) in enumerate(zip(sources, kept + spread))
    ]
    for copy in copies:
        copy.start()
    for copy in copies:
        copy.wait()
    for i, value in enumerate(spread):
        width = value.shape[1]
        diagonal = lax.broadcasted_iota(I32, (8, width), 0) == lax.broadcasted_iota(I32, (8, width), 1)
        column = jnp.sum(jnp.where(diagonal, wide(value[...]), 0.0), axis=1, keepdims=True)
        scalars[pl.ds(8 * i, 8), :] = jnp.broadcast_to(column, (8, LANES))


def pack_kernel(
    surface, sends, fields, old, edge, table, owner, ctable, cedge, cdiag, cowner, cinverse,
    to_right2, far, to_left2, near, here, chunks, left_rows, right_rows,
):
    even = lax.rem(lax.axis_index("tile"), 2) == 0
    cells = fields.shape[1]
    blocks = cells // LANES
    frows = ctable.shape[1]
    firsts = frows * LANES
    base = pick_base(cinverse.shape[1] // LANES)
    lane = lax.broadcasted_iota(I32, (1, LANES), 1)

    for rows, at_left in ((right_rows, False), (left_rows, True)):
        start = 0 if at_left else cells - LANES
        part = pl.ds(start, LANES)

        def both(high, low_row, value):
            count = value.shape[0]
            rows[pl.ds(high, count), :] = value
            rows[pl.ds(low_row, count), :] = value - value.astype(BF16).astype(F32)

        def three(ref, row):
            return jnp.concatenate([ref[link, pl.ds(row, 1), :] for link in range(3)], axis=0)

        rows[pl.ds(24, 8), :] = jnp.zeros((8, LANES), F32)
        both(FIELD_HI, FIELD_LO, fields[:, part])
        block = 0 if at_left else blocks - 1
        both(EDGE_HI, EDGE_LO, three(edge, block))
        both(OLD_HI, OLD_LO, old[pl.ds(block, 1), :])
        rows[pl.ds(OFFSET, 3), :] = (three(table, block) - (LANES + start) - lane).astype(F32)
        shift = 0 if at_left else firsts - LANES
        rows[pl.ds(OWNER, 1), :] = (owner[pl.ds(block, 1), :] - shift).astype(F32)
        first = 0 if at_left else frows - 2
        reach = LANES // 8
        for step in range(2):
            both(CEDGE_HI + 3 * step, CEDGE_LO + 3 * step, three(cedge, first + step))
            rows[pl.ds(COFFSET + 3 * step, 3), :] = (
                three(ctable, first + step) - (reach + (first + step) * LANES) - lane
            ).astype(F32)
            both(CDIAG_HI + step, CDIAG_LO + step, cdiag[pl.ds(first + step, 1), :])
            rows[pl.ds(COWNER + step, 1), :] = cowner[pl.ds(first + step, 1), :].astype(F32)
        halves = cinverse.shape[1] // LANES
        for half in range(halves):
            both(
                INVERSE + 16 * half,
                INVERSE + 16 * (halves + half),
                cinverse[:, pl.ds(half * LANES, LANES)],
            )
        end = INVERSE + 32 * halves
        if base > end:
            rows[pl.ds(end, base - end), :] = jnp.zeros((base - end, LANES), F32)

    for block in range(blocks):
        chunks[pl.ds(4 * block, 4), :] = surface[:, pl.ds(block * LANES, LANES)].astype(F32)
    slots = sends.shape[1]
    hot = jnp.where(
        lax.broadcasted_iota(I32, (blocks, slots), 0) == sends[...], 1.0, 0.0
    ).astype(BF16)
    picks = []
    for channel in range(4):
        source = chunks[pl.ds(channel, blocks, stride=4), :].astype(BF16)
        picks.append(dot_tn(hot, source).astype(BF16))
    count = slots // 5

    chosen = [
        jnp.concatenate([p[j * count : (j + 1) * count] for p in picks], axis=0) for j in range(5)
    ]
    here[...] = chosen[2]
    for out, j in ((to_right2, 0), (to_left2, 4)):
        out[pl.ds(0, base), :] = jnp.zeros((base, LANES), BF16)
        out[pl.ds(base, 4 * count), :] = chosen[j]
    right = jnp.concatenate([right_rows[...].astype(BF16), chosen[1]], axis=0)
    left = jnp.concatenate([left_rows[...].astype(BF16), chosen[3]], axis=0)
    far[...] = jnp.where(even, left, right)
    near[...] = jnp.where(even, right, left)


def stencil_kernel(
    here, scalars, fields, edge, table, old, diagonal, owner, slots, entry_block, tiles,
    fresh, force, beside_old, window, ends_row, ends_lane, hot, member, damping, tile_buffer, padded, sems,
):
    del here
    parts = sems.shape[0]
    step = tiles.shape[0] // parts

    def load(part):
        span = pl.ds(part * step, step)
        return pltpu.make_async_copy(tiles.at[span], tile_buffer.at[span], sems.at[part])

    def begin(part, carry):
        load(part).start()
        return carry

    lax.fori_loop(0, parts, begin, 0)
    blocks = old.shape[0]
    levels = fields.shape[0]
    speed = scalars[pl.ds(0, 8), :]
    share = scalars[pl.ds(8, 8), :]
    starts = lax.broadcasted_iota(I32, (blocks, LANES), 0) * LANES
    total = edge[0] + edge[1] + edge[2]
    inverse = 1.0 / total
    fine_total = diagonal[...] + total
    damping[0] = fine_total
    damping[1] = RELAXATION / fine_total
    for link in range(3):
        window[link] = table[link] - starts
    blank = jnp.zeros((levels, LANES), F32)

    def chunk(block):
        if 0 <= block < blocks:
            return fields[:, pl.ds(block * LANES, LANES)]
        return blank

    before, here, after = blank, chunk(0), chunk(1)
    for block in range(blocks):
        row = slice(block, block + 1)
        beside = jnp.zeros((levels, LANES), F32)
        for link in range(3):
            place = wide(window[link, pl.ds(block, 1), :])
            index = lax.bitwise_and(place, LANES - 1)
            value = jnp.where(
                place < LANES,
                gather_lanes(before, index),
                jnp.where(place < 2 * LANES, gather_lanes(here, index), gather_lanes(after, index)),
            )
            beside = beside + wide(edge[link, pl.ds(block, 1), :]) * value
        result = here + speed * ((beside - wide(total[row]) * here) * wide(inverse[row]))
        fresh[:, pl.ds(block * LANES, LANES)] = result
        force[pl.ds(block, 1), :] = jnp.sum(result * share, axis=0, keepdims=True)
        before, here, after = here, after, chunk(block + 2)

    padded[pl.ds(0, 8), :] = jnp.zeros((8, LANES), F32)
    padded[pl.ds(8 + blocks, 8), :] = jnp.zeros((8, LANES), F32)
    padded[pl.ds(8, blocks), :] = old[...]
    beside_old[...] = neighbour_sum(padded, edge, window, blocks)
    names = jnp.where(
        lax.broadcasted_iota(I32, (slots.shape[1], slots.shape[1]), 0) == slots[...], 1.0, 0.0
    )
    hot[...] = jnp.transpose(names).astype(BF16)
    half = entry_block.shape[1] // 2
    for part in range(2):
        member[part] = jnp.where(
            lax.broadcasted_iota(I32, (blocks, half), 0) == entry_block[:, part * half : (part + 1) * half],
            1.0,
            0.0,
        ).astype(BF16)

    firsts = ends_row.shape[0] * LANES
    ident = lax.broadcasted_iota(I32, ends_row.shape, 0) * LANES + lax.broadcasted_iota(
        I32, ends_row.shape, 1
    )
    count = ends_row.shape[0]
    rows = jnp.zeros(ends_row.shape, I32)
    for block in range(blocks):
        last = jnp.broadcast_to(owner[pl.ds(block, 1), LANES - 1 : LANES], ends_row.shape)
        rows = rows + jnp.where(last <= ident, 1, 0)
    lanes = jnp.zeros(ends_row.shape, I32)
    for bit in (64, 32, 16, 8, 4, 2, 1):
        probe = lanes + (bit - 1)
        value = jnp.full(ends_row.shape, firsts, I32)
        for block in range(blocks):
            value = jnp.where(
                rows == block, gather_lanes(wide(owner[pl.ds(block, 1), :], count), probe), value
            )
        lanes = jnp.where(value <= ident, lanes + bit, lanes)
    ends_row[...] = rows
    ends_lane[...] = lanes
    for part in range(parts):
        load(part).wait()


def neighbour_sum(padded, edges, window, blocks):
    before = padded[pl.ds(7, blocks), :]
    here = padded[pl.ds(8, blocks), :]
    after = padded[pl.ds(9, blocks), :]
    result = jnp.zeros((blocks, LANES), F32)
    for link in range(3):
        place = window[link]
        index = lax.bitwise_and(place, LANES - 1)
        value = jnp.where(
            place < LANES,
            gather_lanes(before, index),
            jnp.where(place < 2 * LANES, gather_lanes(here, index), gather_lanes(after, index)),
        )
        result = result + edges[link] * value
    return result


def first_level_sum(values, frame):
    before = pltpu.roll(values, 1, axis=0)
    after = pltpu.roll(values, FRAME - 1, axis=0)
    lane = lax.broadcasted_iota(I32, (FRAME, LANES), 1)
    result = jnp.zeros((FRAME, LANES), F32)
    for link in range(3):
        place = lane + frame[pl.ds(link * FRAME, FRAME), :].astype(I32)
        index = lax.bitwise_and(place, LANES - 1)
        value = jnp.where(
            place < 0,
            gather_lanes(before, index),
            jnp.where(place >= LANES, gather_lanes(after, index), gather_lanes(values, index)),
        )
        result = result + frame[pl.ds((3 + link) * FRAME, FRAME), :] * value
    return result


def previous_one(values):
    rolled = pltpu.roll(values, 1, axis=1)
    above = pltpu.roll(rolled, 1, axis=0)
    lane = lax.broadcasted_iota(I32, values.shape, 1)
    row = lax.broadcasted_iota(I32, values.shape, 0)
    return jnp.where(lane > 0, rolled, jnp.where(row > 0, above, 0.0))


def triangle():
    return jnp.where(
        lax.broadcasted_iota(I32, (LANES, LANES), 0) < lax.broadcasted_iota(I32, (LANES, LANES), 1),
        1.0,
        0.0,
    ).astype(BF16)


def prefix(values):
    ones = jnp.ones((LANES, LANES), BF16)
    right = jnp.concatenate([triangle(), ones], axis=1)
    count = values.shape[0]
    out = jnp.dot(
        jnp.concatenate(split2(values), axis=0), right, preferred_element_type=F32
    )
    out = out[:count] + out[count:]
    return out[:, :LANES], out[:, LANES:]


def rows_before(values):
    sublane = lax.broadcasted_iota(I32, (8, LANES), 0)
    run = jnp.zeros((8, LANES), F32)
    result = []
    for at in range(0, values.shape[0], 8):
        piece = values[at : at + 8]
        total = piece
        for distance in (1, 2, 4):
            total = total + jnp.where(sublane >= distance, pltpu.roll(total, distance, axis=0), 0.0)
        result.append(run + (total - piece))
        run = run + wide(total[7:8])
    return jnp.concatenate(result, axis=0), run


def forward_kernel(
    tiles, scalars, from_left2, far, from_right2, near, here, hot, member, fields, edges, window, old,
    damping, force_part, beside_old, ends_row, ends_lane, fresh, ctable, cedge, cdiag, cowner, cinverse,
    force_out, smooth_out, source_out, frame, weights_out, fresh_out, received_out, message_out,
    picked, products, padded, prefixed, arrivals, extended, ends, received, message, sems,
):
    cells = fresh.shape[1]
    middle = pl.ds(LANES, cells - 2 * LANES)
    copies = [pltpu.make_async_copy(fresh.at[:, middle], fresh_out.at[:, middle], sems.at[0])]
    for side in range(2):
        copies.append(
            pltpu.make_async_copy(
                ends.at[side], fresh_out.at[:, pl.ds(side * (cells - LANES), LANES)], sems.at[1 + side]
            )
        )
    copies.append(pltpu.make_async_copy(received, received_out, sems.at[3]))
    copies.append(pltpu.make_async_copy(message, message_out, sems.at[4]))

    def begin(which):
        def body(_, carry):
            for copy in which:
                copy.start()
            return carry

        lax.fori_loop(0, 1 + lax.axis_index("tile") // lax.axis_size("tile"), body, 0)

    begin(copies[:1])
    tile = lax.axis_index("tile")
    tile_count = lax.axis_size("tile")
    entries = tiles.shape[0]
    blocks = old.shape[0]

    even = lax.rem(tile, 2) == 0
    base = far.shape[0] - here.shape[0]
    each = here.shape[0] // 4
    from_left, from_right = sides(far[...], near[...], even)
    sources = (from_left2[base:, :], from_left[base:], here[...], from_right[base:], from_right2[base:, :])
    for channel in range(4):
        source = jnp.concatenate(
            [rows[channel * each : (channel + 1) * each] for rows in sources], axis=0
        )
        picked[pl.ds(channel, entries, stride=4), :] = jnp.dot(hot[...], source, preferred_element_type=F32)

    arrivals[0] = from_left[:base].astype(F32)
    arrivals[1] = from_right[:base].astype(F32)

    upper = lax.rem(lax.broadcasted_iota(I32, (16, LANES), 0), 8) < 4
    for group in range(entries // 4):
        rows = picked[pl.ds(16 * group, 16), :]
        rows = jnp.concatenate([jnp.where(upper, rows, 0.0), jnp.where(upper, 0.0, rows)], axis=1)
        at = 4 * group
        weights = jnp.concatenate(
            [
                jnp.concatenate([tiles[at], tiles[at + 1]], axis=1),
                jnp.concatenate([tiles[at + 2], tiles[at + 3]], axis=1),
            ],
            axis=0,
        )
        product = dot_nt(rows.astype(BF16), weights)
        products[pl.ds(16 * group, 8), :] = product[0:8, :LANES]
        products[pl.ds(16 * group + 8, 8), :] = product[8:16, LANES:]
    speed = scalars[pl.ds(0, 8), :]
    share = scalars[pl.ds(8, 8), :]
    force_out[...] = force_part[...]
    padded[pl.ds(0, 8), :] = jnp.zeros((8, LANES), F32)
    padded[pl.ds(8 + blocks, 8), :] = jnp.zeros((8, LANES), F32)
    beside_extra = []
    for side, block, target in ((0, 0, 0), (1, blocks - 1, 2)):
        halo = arrivals[side, pl.ds(FIELD_HI, 8), :] + arrivals[side, pl.ds(FIELD_LO, 8), :]
        halo_old = arrivals[side, pl.ds(OLD_HI, 1), :] + arrivals[side, pl.ds(OLD_LO, 1), :]
        total = edges[0, pl.ds(block, 1), :] + edges[1, pl.ds(block, 1), :] + edges[2, pl.ds(block, 1), :]
        extra = jnp.zeros((8, LANES), F32)
        extra_old = jnp.zeros((8, LANES), F32)
        for link in range(3):
            place = wide(window[link, pl.ds(block, 1), :])
            index = lax.bitwise_and(place, LANES - 1)
            weight = jnp.where(
                lax.shift_right_logical(place, 7) == target, wide(edges[link, pl.ds(block, 1), :]), 0.0
            )
            extra = extra + weight * gather_lanes(halo, index)
            extra_old = extra_old + weight * gather_lanes(wide(halo_old), index)
        change = speed * extra / wide(total)
        ends[side] = fresh[:, pl.ds(block * LANES, LANES)] + change
        force_out[pl.ds(block, 1), :] += jnp.sum(change * share, axis=0, keepdims=True)
        beside_extra.append(extra_old[0:1])

    inverse_windows(arrivals.at[0], cinverse, arrivals.at[1], extended, weights_out)

    force = force_out[...]
    half = entries // 2
    for channel in range(4):
        value = jnp.zeros((blocks, 2 * LANES), F32)
        for part in range(2):
            rows = products[pl.ds(4 * half * part + channel, half, stride=4), :]
            value = value + jnp.dot(
                member[part], jnp.concatenate(split2(rows), axis=1), preferred_element_type=F32
            )
        value = value[:, :LANES] + value[:, LANES:]
        for block in range(blocks):
            received[pl.ds(channel, 1), pl.ds(block * LANES, LANES)] = value[block : block + 1]
        force = force + scalars[pl.ds(16 + channel, 1), :] * value

    force_out[...] = force
    begin(copies[1:4])
    total, damp = damping[0], damping[1]
    smooth_out[...] = beside_old[...]
    smooth_out[pl.ds(0, 1), :] += beside_extra[0]
    smooth_out[pl.ds(blocks - 1, 1), :] += beside_extra[1]
    previous = old[...]
    smooth = previous + damp * (force - (total * previous - smooth_out[...]))
    smooth_out[...] = smooth
    padded[pl.ds(8, blocks), :] = smooth
    residual = force - total * smooth + neighbour_sum(padded, edges, window, blocks)

    inner, whole = prefix(residual)
    before, run = rows_before(whole)
    prefixed[...] = inner + before
    rows, lanes = ends_row[...], ends_lane[...]
    count = rows.shape[0]
    marks = run[:count]
    for block in range(blocks):
        value = gather_lanes(wide(prefixed[pl.ds(block, 1), :], count), lanes)
        marks = jnp.where(rows == block, value, marks)
    own_source = marks - previous_one(marks)

    lane = lax.broadcasted_iota(I32, (1, LANES), 1)
    rim_rows, rim_counts = [], []
    for side in range(2):
        inside = padded[pl.ds(8 if side == 0 else 7 + blocks, 1), :]
        value = jnp.zeros((1, LANES), F32)
        for link in range(3):
            place = lane + arrivals[side, pl.ds(OFFSET + link, 1), :].astype(I32)
            index = lax.bitwise_and(place, LANES - 1)
            reached = (place >= LANES) if side == 0 else (place < 0)
            weight = arrivals[side, pl.ds(EDGE_HI + link, 1), :] + arrivals[side, pl.ds(EDGE_LO + link, 1), :]
            value = value + jnp.where(
                wide(reached.astype(I32)) > 0,
                wide(weight) * gather_lanes(wide(inside), wide(index)),
                0.0,
            )[0:1]
        rim_rows.append(value)
        owners = arrivals[side, pl.ds(OWNER, 1), :].astype(I32)
        below = jnp.where(
            lax.broadcasted_iota(I32, (LANES, LANES), 0) >= owners, 1.0, 0.0
        ).astype(BF16)
        rim_counts.append(dot_nt(jnp.ones((8, LANES), BF16), below))
    rim_inner, rim_whole = prefix(jnp.concatenate([wide(r) for r in rim_rows], axis=0))
    rim_source = []
    for side in range(2):
        place = rim_counts[side].astype(I32)
        index = lax.bitwise_and(place, LANES - 1)
        value = gather_lanes(rim_inner[8 * side : 8 * side + 8], index)
        value = jnp.where(place >= LANES, rim_whole[8 * side : 8 * side + 8], value)
        shifted = pltpu.roll(value, 1, axis=1)
        first = lax.broadcasted_iota(I32, (8, LANES), 1) == 0
        rim_source.append((value - jnp.where(first, 0.0, shifted))[0:1])

    frows = own_source.shape[0]
    source_out[...] = jnp.zeros((FRAME, LANES), F32)
    source_out[pl.ds(OWN, frows), :] = own_source
    source_out[pl.ds(OWN - 1, 1), :] = rim_source[0]
    source_out[pl.ds(OWN + frows, 1), :] = rim_source[1]
    reach = LANES // 8
    frame[...] = jnp.zeros(frame.shape, F32)
    frame[pl.ds(6 * FRAME, FRAME), :] = jnp.ones((FRAME, LANES), F32)
    frame[pl.ds(7 * FRAME, FRAME), :] = jnp.full((FRAME, LANES), 127.0, F32)
    bottoms = 16
    at_cell = lax.broadcasted_iota(I32, (frows, LANES), 0) * LANES + lax.broadcasted_iota(
        I32, (frows, LANES), 1
    )
    for link in range(3):
        frame[pl.ds(link * FRAME + OWN, frows), :] = (ctable[link] - reach - at_cell).astype(F32)
        frame[pl.ds((3 + link) * FRAME + OWN, frows), :] = cedge[link]
    frame[pl.ds(6 * FRAME + OWN, frows), :] = cdiag[...]
    frame[pl.ds(7 * FRAME + OWN, frows), :] = (cowner[...] + bottoms).astype(F32)
    for side in range(2):
        for row in range(2):
            at = (OWN - 2 + row) if side == 0 else (OWN + frows + row)
            for link in range(3):
                put = 3 * row + link
                frame[pl.ds(link * FRAME + at, 1), :] = arrivals[side, pl.ds(COFFSET + put, 1), :]
                frame[pl.ds((3 + link) * FRAME + at, 1), :] = (
                    arrivals[side, pl.ds(CEDGE_HI + put, 1), :] + arrivals[side, pl.ds(CEDGE_LO + put, 1), :]
                )
            frame[pl.ds(6 * FRAME + at, 1), :] = (
                arrivals[side, pl.ds(CDIAG_HI + row, 1), :] + arrivals[side, pl.ds(CDIAG_LO + row, 1), :]
            )
            frame[pl.ds(7 * FRAME + at, 1), :] = arrivals[side, pl.ds(COWNER + row, 1), :] + (
                2.0 * bottoms * side
            )
    for link in range(3):
        frame[pl.ds(6 * FRAME, FRAME), :] += frame[pl.ds((3 + link) * FRAME, FRAME), :]
    source = source_out[...]
    first = (RELAXATION / frame[pl.ds(6 * FRAME, FRAME), :]) * source
    residual = (1.0 - RELAXATION) * source + first_level_sum(first, frame)
    codes = frame[pl.ds(7 * FRAME, FRAME), :].astype(I32)
    pieces = split2(residual)
    left_side, right_side = [], []
    bins = lax.broadcasted_iota(I32, (3 * bottoms, LANES), 0)
    rest = jnp.zeros((LANES - 3 * bottoms, LANES), BF16)
    for row in range(OWN - 2, OWN + frows + 2):
        left_side.append(jnp.concatenate([p[row : row + 1] for p in pieces], axis=0))
        named = jnp.where(bins == codes[row : row + 1], 1.0, 0.0).astype(BF16)
        right_side.append(jnp.concatenate([named, rest], axis=0))
    bottom = dot_nt(jnp.concatenate(left_side, axis=1), jnp.concatenate(right_side, axis=1))
    bottom = bottom[0:1] + bottom[1:2]

    to_left = jnp.concatenate(
        [bottom, padded[pl.ds(8, 1), :], own_source[0:2], rim_source[0], jnp.zeros((3, LANES), F32)], axis=0
    )
    to_right = jnp.concatenate(
        [bottom, padded[pl.ds(7 + blocks, 1), :], own_source[frows - 2 : frows], rim_source[1], jnp.zeros((3, LANES), F32)],
        axis=0,
    )
    for other in range(message.shape[0]):
        message[other] = to_right
    message[lax.rem(tile + tile_count - 1, tile_count)] = to_left
    copies[4].start()
    for copy in copies:
        copy.wait()


def inverse_windows(left, own, right, extended, weights):
    bottoms, size = own.shape
    halves = size // LANES
    for half in range(halves):
        part = pl.ds(half * LANES, LANES)
        for at, block in ((0, left), (2, right)):
            high, low = INVERSE + 16 * half, INVERSE + 16 * (halves + half)
            extended[pl.ds(at * bottoms, bottoms), part] = (
                block[pl.ds(high, bottoms), :] + block[pl.ds(low, bottoms), :]
            )
        extended[pl.ds(bottoms, bottoms), part] = own[:, part]
    table = extended[...]
    lane = lax.broadcasted_iota(I32, (3 * bottoms, LANES), 1)
    for other in range(weights.shape[0]):
        shift = (size - (other - 1) * bottoms) % size
        turned = pltpu.roll(table, shift, axis=1) if shift else table
        weights[other] = jnp.where(lane < 3 * bottoms, turned[:, :LANES], 0.0)


def backward_kernel(
    frame_rows, arrived, weights, source, frame, force, smooth, edges, window, damping, owner, far, near,
    height, frame_source, padded, third_rows,
):
    tile = lax.axis_index("tile")
    tile_count = lax.axis_size("tile")
    blocks = force.shape[0]
    left = arrived[lax.rem(tile + tile_count - 1, tile_count)]
    right = arrived[lax.rem(tile + 1, tile_count)]
    count = weights.shape[1]
    partial = jnp.zeros((count, LANES), F32)
    for other in range(weights.shape[0]):
        partial = partial + weights[other] * wide(arrived[other, pl.ds(0, 1), :], count)
    partial = jnp.concatenate([partial, jnp.zeros((LANES - count, LANES), F32)], axis=0)
    ones = jnp.ones((8, LANES), BF16)
    bottom = dot_nt(jnp.concatenate([ones, ones], axis=1), jnp.concatenate(split2(partial), axis=1))

    frows = frame_rows
    frame_source[...] = source[...]
    frame_source[pl.ds(OWN - 2, 2), :] += left[2:4]
    frame_source[pl.ds(OWN, 1), :] += left[4:5]
    frame_source[pl.ds(OWN + frows - 1, 1), :] += right[4:5]
    frame_source[pl.ds(OWN + frows, 2), :] += right[2:4]
    total_source = frame_source[...]
    total = frame[pl.ds(6 * FRAME, FRAME), :]
    codes = frame[pl.ds(7 * FRAME, FRAME), :].astype(I32)
    damp = RELAXATION / total
    second = damp * total_source + gather_lanes(wide(bottom[0:1], FRAME), codes)
    third = second + damp * (total_source - total * second + first_level_sum(second, frame))
    third_rows[...] = third

    owners = owner[...]
    index = lax.bitwise_and(owners, LANES - 1)
    which = lax.shift_right_logical(owners, 7)
    corrected = jnp.zeros((blocks, LANES), F32)
    for row in range(frows):
        corrected = jnp.where(
            which == row, gather_lanes(wide(third_rows[pl.ds(OWN + row, 1), :], blocks), index), corrected
        )
    corrected = smooth[...] + corrected
    padded[pl.ds(8, blocks), :] = corrected
    part = pl.ds(16, 16)
    even = lax.rem(tile, 2) == 0
    left_owner, right_owner = [
        rows[OWNER - 16 : OWNER - 15].astype(I32)
        for rows in sides(far[part, :].astype(F32), near[part, :].astype(F32), even)
    ]
    left_rim = left[1:2] + gather_lanes(wide(third_rows[pl.ds(OWN - 1, 1), :]), wide(left_owner))[0:1]
    right_rim = right[1:2] + gather_lanes(wide(third_rows[pl.ds(OWN + frows, 1), :]), wide(right_owner))[0:1]
    padded[pl.ds(7, 1), :] = left_rim
    padded[pl.ds(8 + blocks, 1), :] = right_rim
    beside = neighbour_sum(padded, edges, window, blocks)
    height[...] = corrected + damping[1] * (force[...] - (damping[0] * corrected - beside))


def in_hbm(array):
    return pltpu.with_memory_space_constraint(array, pltpu.HBM)


def struct(shape, dtype=F32):
    return jax.ShapeDtypeStruct(shape, dtype)


VMEM = pl.BlockSpec(memory_space=pltpu.VMEM)
SMEM = pl.BlockSpec(memory_space=pltpu.SMEM)
ANY = pl.BlockSpec(memory_space=pltpu.HBM)
PARAMS = pltpu.CompilerParams(vmem_limit_bytes=16 * 1024 * 1024)


def per_device(
    fields, level_rate, edge_weight, fine_diagonal, fine_table, old_height, level_weight,
    flux_weight, fine_owner, coarse_table, coarse_edge, coarse_diagonal, coarse_owner,
    coarse_inverse, surface_out, send_blocks, entry_slot, entry_block, remap_tiles,
):
    tile_count = lax.axis_size("tile")
    cells = fields.shape[2]
    blocks = cells // LANES
    firsts = coarse_diagonal.shape[1]
    frows = firsts // LANES
    entries = entry_slot.shape[2]
    channels = surface_out.shape[1]
    slots = send_blocks.shape[2]
    each = slots // 5
    halves = coarse_inverse.shape[2] // LANES
    bottoms = coarse_inverse.shape[1]
    base = pick_base(halves)
    swap = [(0, 1), (1, 0)]
    surface = lax.ppermute(surface_out[0], "comp", swap)
    sends = lax.ppermute(send_blocks[0], "comp", swap)
    raw = (
        fields[0],
        old_height.reshape(blocks, LANES),
        edge_weight[0].reshape(3, blocks, LANES),
        fine_table[0].reshape(3, blocks, LANES),
        fine_owner.reshape(blocks, LANES),
        fine_diagonal.reshape(blocks, LANES),
        coarse_table[0].reshape(3, frows, LANES),
        coarse_edge[0].reshape(3, frows, LANES),
        coarse_diagonal.reshape(frows, LANES),
        coarse_owner.reshape(frows, LANES),
        coarse_inverse[0],
        entry_slot[0],
        entry_block[0],
        level_rate,
        level_weight,
        flux_weight,
    )
    loaded = pl.pallas_call(
        load_kernel,
        out_shape=[struct(x.shape, x.dtype) for x in raw[:-3]] + [struct((24, LANES))],
        in_specs=[ANY] * len(raw),
        out_specs=[VMEM] * (len(raw) - 2),
        scratch_shapes=[pltpu.VMEM(x.shape, x.dtype) for x in raw[-3:]]
        + [pltpu.SemaphoreType.DMA((len(raw),))],
        compiler_params=PARAMS,
        name="load",
    )(*[in_hbm(x) for x in raw])
    (
        current, old, edges, table, owner, diagonal, ctable, cedge, cdiag, cowner, cinverse,
        slot, block, scalars,
    ) = loaded

    pick = struct((4 * each, LANES), BF16)
    both = struct((base + 4 * each, LANES), BF16)
    to_right2, far, to_left2, near, here = pl.pallas_call(
        pack_kernel,
        out_shape=[both, both, both, both, pick],
        in_specs=[VMEM] * 12,
        out_specs=[VMEM] * 5,
        scratch_shapes=[
            pltpu.VMEM((channels * blocks, LANES), F32),
            pltpu.VMEM((base, LANES), F32),
            pltpu.VMEM((base, LANES), F32),
        ],
        compiler_params=PARAMS,
        name="pack",
    )(
        surface, sends, current, old, edges, table, owner, ctable, cedge, cdiag, cowner, cinverse,
    )

    def shifted(array, distance):
        return lax.ppermute(
            array, "tile", [(i, (i + distance) % tile_count) for i in range(tile_count)]
        )

    def swapped(array, start):
        lower = [i for i in range(tile_count) if i % 2 == start]
        pairs = [(i, (i + 1) % tile_count) for i in lower]
        return lax.ppermute(array, "tile", pairs + [(j, i) for i, j in pairs])

    from_left2 = shifted(to_right2, 2)
    far = swapped(far, 1)
    from_right2 = shifted(to_left2, -2)
    near = swapped(near, 0)

    fresh, force_part, beside_old, window, ends_row, ends_lane, hot, member, damping, tiles = pl.pallas_call(
        stencil_kernel,
        out_shape=[
            struct((fields.shape[1], cells)),
            struct((blocks, LANES)),
            struct((blocks, LANES)),
            struct((3, blocks, LANES), I32),
            struct((frows, LANES), I32),
            struct((frows, LANES), I32),
            struct((entries, slots), BF16),
            struct((2, blocks, entries // 2), BF16),
            struct((2, blocks, LANES)),
            pltpu.VMEM(remap_tiles.shape[2:], BF16),
        ],
        in_specs=[VMEM] * 10 + [ANY],
        out_specs=[VMEM] * 10,
        scratch_shapes=[pltpu.VMEM((blocks + 16, LANES), F32), pltpu.SemaphoreType.DMA((math.gcd(entries, 8),))],
        compiler_params=PARAMS,
        name="stencil",
    )(here, scalars, current, edges, table, old, diagonal, owner, slot, block, in_hbm(remap_tiles[0, 0]))

    force, smooth, source, frame, weights, advanced, received, message = pl.pallas_call(
        forward_kernel,
        out_shape=[
            struct((blocks, LANES)),
            struct((blocks, LANES)),
            struct((FRAME, LANES)),
            struct((8 * FRAME, LANES)),
            struct((tile_count, 3 * bottoms, LANES)),
            struct((fields.shape[1], cells)),
            struct((channels, cells)),
            struct((tile_count, 8, LANES)),
        ],
        in_specs=[VMEM] * 24,
        out_specs=[VMEM] * 5 + [ANY] * 3,
        scratch_shapes=[
            pltpu.VMEM((4 * entries, LANES), F32),
            pltpu.VMEM((4 * entries, LANES), F32),
            pltpu.VMEM((blocks + 16, LANES), F32),
            pltpu.VMEM((blocks, LANES), F32),
            pltpu.VMEM((2, base, LANES), F32),
            pltpu.VMEM((3 * bottoms, bottoms * tile_count), F32),
            pltpu.VMEM((2, fields.shape[1], LANES), F32),
            pltpu.VMEM((channels, cells), F32),
            pltpu.VMEM((tile_count, 8, LANES), F32),
            pltpu.SemaphoreType.DMA((5,)),
        ],
        compiler_params=PARAMS,
        name="forward",
    )(
        tiles, scalars, from_left2, far, from_right2, near, here, hot, member, current, edges, window, old,
        damping, force_part, beside_old, ends_row, ends_lane, fresh, ctable, cedge, cdiag, cowner, cinverse,
    )
    arrived = lax.all_to_all(message, "tile", split_axis=0, concat_axis=0, tiled=True)
    height = pl.pallas_call(
        functools.partial(backward_kernel, frows),
        out_shape=struct((blocks, LANES)),
        in_specs=[VMEM] * 12,
        out_specs=VMEM,
        scratch_shapes=[
            pltpu.VMEM((FRAME, LANES), F32),
            pltpu.VMEM((blocks + 16, LANES), F32),
            pltpu.VMEM((FRAME, LANES), F32),
        ],
        compiler_params=PARAMS,
        name="backward",
    )(arrived, weights, source, frame, force, smooth, edges, window, damping, owner, far, near)
    return advanced[None], received[None], height.reshape(1, cells)


def solution(mesh):
    in_specs = (
        P("comp", None, "tile"),
        P("comp", None),
        P("comp", None, "tile"),
        P("comp", "tile"),
        P("comp", None, "tile"),
        P("comp", "tile"),
        P("comp", None),
        P("comp", None),
        P("comp", "tile"),
        P("comp", None, "tile"),
        P("comp", None, "tile"),
        P("comp", "tile"),
        P("comp", "tile"),
        P("comp", "tile", None),
        P("comp", None, "tile"),
        P("comp", "tile", None),
        P("comp", "tile", None),
        P("comp", "tile", None),
        P("comp", "tile", None, None, None),
    )
    out_specs = (P("comp", None, "tile"), P("comp", None, "tile"), P("comp", "tile"))
    return jax.shard_map(
        per_device, mesh=mesh, in_specs=in_specs, out_specs=out_specs, check_vma=False
    )
```

```python
import functools
import math

import jax
import jax.numpy as jnp
from jax import lax
from jax.experimental import pallas as pl
from jax.experimental.pallas import tpu as pltpu
from jax.sharding import PartitionSpec as P

LANES = 128
RELAXATION = 0.8
F32 = jnp.float32
BF16 = jnp.bfloat16
I32 = jnp.int32

FIELD_HI, FIELD_LO = 0, 8
EDGE_HI, EDGE_LO, OLD_HI, OLD_LO = 16, 19, 22, 23
OFFSET, OWNER = 24, 27
CEDGE_HI, CEDGE_LO, CDIAG_HI, CDIAG_LO = 32, 38, 44, 46
COFFSET, COWNER = 48, 54
INVERSE = 56

FRAME, OWN = 32, 8

MIDDLE = 32


def sides(far, near, even):
    return jnp.where(even, far, near), jnp.where(even, near, far)


def gather_lanes(table, index):
    return jnp.take_along_axis(table, index, axis=1)


def wide(row, count=8):
    return jnp.broadcast_to(row, (count, row.shape[1]))


def split2(x):
    high = x.astype(BF16)
    return high, (x - high.astype(F32)).astype(BF16)


def dot_nt(a, b):
    return lax.dot_general(a, b, (((1,), (1,)), ((), ())), preferred_element_type=F32)


def dot_tn(a, b):
    return lax.dot_general(a, b, (((0,), (0,)), ((), ())), preferred_element_type=F32)


def pick_base(inverse_blocks):
    return -(-(INVERSE + 32 * inverse_blocks) // 16) * 16


def load_kernel(*refs):
    count = len(refs) // 2
    copies = [
        pltpu.make_async_copy(source, target, refs[-1].at[i])
        for i, (source, target) in enumerate(zip(refs[:count], refs[count : 2 * count]))
    ]
    for copy in copies:
        copy.start()
    for copy in copies:
        copy.wait()


def pack_kernel(
    surface, sends, fields, old, edge, table, owner, ctable, cedge, cdiag, cowner, cinverse,
    to_right2, far, to_left2, near, here, chunks, left_rows, right_rows,
):
    even = lax.rem(lax.axis_index("tile"), 2) == 0
    cells = fields.shape[1]
    blocks = cells // LANES
    frows = ctable.shape[1]
    firsts = frows * LANES
    base = pick_base(cinverse.shape[1] // LANES)
    lane = lax.broadcasted_iota(I32, (1, LANES), 1)

    for rows, at_left in ((right_rows, False), (left_rows, True)):
        start = 0 if at_left else cells - LANES
        part = pl.ds(start, LANES)

        def both(high, low_row, value):
            count = value.shape[0]
            rows[pl.ds(high, count), :] = value
            rows[pl.ds(low_row, count), :] = value - value.astype(BF16).astype(F32)

        def three(ref, row):
            return jnp.concatenate([ref[link, pl.ds(row, 1), :] for link in range(3)], axis=0)

        rows[pl.ds(24, 8), :] = jnp.zeros((8, LANES), F32)
        both(FIELD_HI, FIELD_LO, fields[:, part])
        block = 0 if at_left else blocks - 1
        both(EDGE_HI, EDGE_LO, three(edge, block))
        both(OLD_HI, OLD_LO, old[pl.ds(block, 1), :])
        rows[pl.ds(OFFSET, 3), :] = (three(table, block) - (LANES + start) - lane).astype(F32)
        shift = 0 if at_left else firsts - LANES
        rows[pl.ds(OWNER, 1), :] = (owner[pl.ds(block, 1), :] - shift).astype(F32)
        first = 0 if at_left else frows - 2
        reach = LANES // 8
        for step in range(2):
            both(CEDGE_HI + 3 * step, CEDGE_LO + 3 * step, three(cedge, first + step))
            rows[pl.ds(COFFSET + 3 * step, 3), :] = (
                three(ctable, first + step) - (reach + (first + step) * LANES) - lane
            ).astype(F32)
            both(CDIAG_HI + step, CDIAG_LO + step, cdiag[pl.ds(first + step, 1), :])
            rows[pl.ds(COWNER + step, 1), :] = cowner[pl.ds(first + step, 1), :].astype(F32)
        halves = cinverse.shape[1] // LANES
        for half in range(halves):
            both(
                INVERSE + 16 * half,
                INVERSE + 16 * (halves + half),
                cinverse[:, pl.ds(half * LANES, LANES)],
            )
        end = INVERSE + 32 * halves
        if base > end:
            rows[pl.ds(end, base - end), :] = jnp.zeros((base - end, LANES), F32)

    for block in range(blocks):
        chunks[pl.ds(4 * block, 4), :] = surface[:, pl.ds(block * LANES, LANES)].astype(F32)
    slots = sends.shape[1]
    hot = jnp.where(
        lax.broadcasted_iota(I32, (blocks, slots), 0) == sends[...], 1.0, 0.0
    ).astype(BF16)
    picks = []
    for channel in range(4):
        source = chunks[pl.ds(channel, blocks, stride=4), :].astype(BF16)
        picks.append(dot_tn(hot, source).astype(BF16))
    count = slots // 5

    chosen = [
        jnp.concatenate([p[j * count : (j + 1) * count] for p in picks], axis=0) for j in range(5)
    ]
    here[...] = chosen[2]
    for out, j in ((to_right2, 0), (to_left2, 4)):
        out[pl.ds(0, base), :] = jnp.zeros((base, LANES), BF16)
        out[pl.ds(base, 4 * count), :] = chosen[j]
    right = jnp.concatenate([right_rows[...].astype(BF16), chosen[1]], axis=0)
    left = jnp.concatenate([left_rows[...].astype(BF16), chosen[3]], axis=0)
    far[...] = jnp.where(even, left, right)
    near[...] = jnp.where(even, right, left)


def stencil_kernel(
    here, fields, edge, table, old, owner, tiles, rate, level_weight, flux_weight, diagonal_in, slots_in, block_in,
    fresh, force, beside_old, window, ends_row, ends_lane, hot, member, damping, scalars, tile_buffer,
    padded, rate_row, level_row, flux_row, diagonal, slots, entry_block, small_sems, sems,
):
    del here
    small = [
        pltpu.make_async_copy(source, target, small_sems.at[i])
        for i, (source, target) in enumerate(
            (
                (rate, rate_row), (level_weight, level_row), (flux_weight, flux_row),
                (diagonal_in, diagonal), (slots_in, slots), (block_in, entry_block),
            )
        )
    ]
    parts = sems.shape[0]
    step = tiles.shape[0] // parts

    def load(part):
        span = pl.ds(part * step, step)
        return pltpu.make_async_copy(tiles.at[span], tile_buffer.at[span], sems.at[part])

    def begin(part, carry):
        if part is None:
            for copy in small:
                copy.start()
        else:
            load(part).start()
        return carry

    once = 1 + lax.axis_index("tile") // lax.axis_size("tile")
    lax.fori_loop(0, once, lambda _, carry: begin(None, carry), 0)
    lax.fori_loop(0, parts, begin, 0)
    blocks = old.shape[0]
    levels = fields.shape[0]
    firsts = ends_row.shape[0] * LANES
    ident = lax.broadcasted_iota(I32, ends_row.shape, 0) * LANES + lax.broadcasted_iota(
        I32, ends_row.shape, 1
    )
    count = ends_row.shape[0]
    rows = jnp.zeros(ends_row.shape, I32)
    for block in range(blocks):
        last = jnp.broadcast_to(owner[pl.ds(block, 1), LANES - 1 : LANES], ends_row.shape)
        rows = rows + jnp.where(last <= ident, 1, 0)
    lanes = jnp.zeros(ends_row.shape, I32)
    for bit in (64, 32, 16, 8, 4, 2, 1):
        probe = lanes + (bit - 1)
        value = jnp.full(ends_row.shape, firsts, I32)
        for block in range(blocks):
            value = jnp.where(
                rows == block, gather_lanes(wide(owner[pl.ds(block, 1), :], count), probe), value
            )
        lanes = jnp.where(value <= ident, lanes + bit, lanes)
    ends_row[...] = rows
    ends_lane[...] = lanes
    for copy in small:
        copy.wait()
    for i, value in enumerate((rate_row, level_row, flux_row)):
        width = value.shape[1]
        same = lax.broadcasted_iota(I32, (8, width), 0) == lax.broadcasted_iota(I32, (8, width), 1)
        column = jnp.sum(jnp.where(same, wide(value[...]), 0.0), axis=1, keepdims=True)
        scalars[pl.ds(8 * i, 8), :] = jnp.broadcast_to(column, (8, LANES))
    speed = scalars[pl.ds(0, 8), :]
    share = scalars[pl.ds(8, 8), :]
    starts = lax.broadcasted_iota(I32, (blocks, LANES), 0) * LANES
    total = edge[0] + edge[1] + edge[2]
    inverse = 1.0 / total
    fine_total = diagonal[...] + total
    damping[0] = fine_total
    damping[1] = RELAXATION / fine_total
    for link in range(3):
        window[link] = table[link] - starts
    blank = jnp.zeros((levels, LANES), F32)

    def chunk(block):
        if 0 <= block < blocks:
            return fields[:, pl.ds(block * LANES, LANES)]
        return blank

    before, here, after = blank, chunk(0), chunk(1)
    for block in range(blocks):
        row = slice(block, block + 1)
        beside = jnp.zeros((levels, LANES), F32)
        for link in range(3):
            place = wide(window[link, pl.ds(block, 1), :])
            index = lax.bitwise_and(place, LANES - 1)
            value = jnp.where(
                place < LANES,
                gather_lanes(before, index),
                jnp.where(place < 2 * LANES, gather_lanes(here, index), gather_lanes(after, index)),
            )
            beside = beside + wide(edge[link, pl.ds(block, 1), :]) * value
        result = here + speed * ((beside - wide(total[row]) * here) * wide(inverse[row]))
        fresh[:, pl.ds(block * LANES, LANES)] = result
        force[pl.ds(block, 1), :] = jnp.sum(result * share, axis=0, keepdims=True)
        before, here, after = here, after, chunk(block + 2)

    padded[pl.ds(0, 8), :] = jnp.zeros((8, LANES), F32)
    padded[pl.ds(8 + blocks, 8), :] = jnp.zeros((8, LANES), F32)
    padded[pl.ds(8, blocks), :] = old[...]
    beside_old[...] = neighbour_sum(padded, edge, window, blocks)
    names = jnp.where(
        lax.broadcasted_iota(I32, (slots.shape[1], slots.shape[1]), 0) == slots[...], 1.0, 0.0
    )
    hot[...] = jnp.transpose(names).astype(BF16)
    half = entry_block.shape[1] // 2
    for part in range(2):
        member[part] = jnp.where(
            lax.broadcasted_iota(I32, (blocks, half), 0) == entry_block[:, part * half : (part + 1) * half],
            1.0,
            0.0,
        ).astype(BF16)

    for part in range(parts):
        load(part).wait()


def neighbour_sum(padded, edges, window, blocks):
    before = padded[pl.ds(7, blocks), :]
    here = padded[pl.ds(8, blocks), :]
    after = padded[pl.ds(9, blocks), :]
    result = jnp.zeros((blocks, LANES), F32)
    for link in range(3):
        place = window[link]
        index = lax.bitwise_and(place, LANES - 1)
        value = jnp.where(
            place < LANES,
            gather_lanes(before, index),
            jnp.where(place < 2 * LANES, gather_lanes(here, index), gather_lanes(after, index)),
        )
        result = result + edges[link] * value
    return result


def first_level_sum(values, frame):
    before = pltpu.roll(values, 1, axis=0)
    after = pltpu.roll(values, FRAME - 1, axis=0)
    lane = lax.broadcasted_iota(I32, (FRAME, LANES), 1)
    result = jnp.zeros((FRAME, LANES), F32)
    for link in range(3):
        place = lane + frame[pl.ds(link * FRAME, FRAME), :].astype(I32)
        index = lax.bitwise_and(place, LANES - 1)
        value = jnp.where(
            place < 0,
            gather_lanes(before, index),
            jnp.where(place >= LANES, gather_lanes(after, index), gather_lanes(values, index)),
        )
        result = result + frame[pl.ds((3 + link) * FRAME, FRAME), :] * value
    return result


def previous_one(values):
    rolled = pltpu.roll(values, 1, axis=1)
    above = pltpu.roll(rolled, 1, axis=0)
    lane = lax.broadcasted_iota(I32, values.shape, 1)
    row = lax.broadcasted_iota(I32, values.shape, 0)
    return jnp.where(lane > 0, rolled, jnp.where(row > 0, above, 0.0))


def triangle():
    return jnp.where(
        lax.broadcasted_iota(I32, (LANES, LANES), 0) < lax.broadcasted_iota(I32, (LANES, LANES), 1),
        1.0,
        0.0,
    ).astype(BF16)


def prefix(values):
    ones = jnp.ones((LANES, LANES), BF16)
    right = jnp.concatenate([triangle(), ones], axis=1)
    count = values.shape[0]
    out = jnp.dot(
        jnp.concatenate(split2(values), axis=0), right, preferred_element_type=F32
    )
    out = out[:count] + out[count:]
    return out[:, :LANES], out[:, LANES:]


def rows_before(values):
    sublane = lax.broadcasted_iota(I32, (8, LANES), 0)
    run = jnp.zeros((8, LANES), F32)
    result = []
    for at in range(0, values.shape[0], 8):
        piece = values[at : at + 8]
        total = piece
        for distance in (1, 2, 4):
            total = total + jnp.where(sublane >= distance, pltpu.roll(total, distance, axis=0), 0.0)
        result.append(run + (total - piece))
        run = run + wide(total[7:8])
    return jnp.concatenate(result, axis=0), run


def forward_kernel(
    tiles, scalars, from_left2, far, from_right2, near, here, hot, member, fields, edges, window, old,
    damping, force_part, beside_old, ends_row, ends_lane, fresh, ctable, cedge, cdiag, cowner, cinverse,
    force_out, smooth_out, source_out, frame, weights_out, fresh_out, received_out, message_out,
    picked, products, padded, prefixed, arrivals, extended, ends, received, message, sems,
):
    cells = fresh.shape[1]
    middle = pl.ds(LANES, cells - 2 * LANES)
    copies = [pltpu.make_async_copy(fresh.at[:, middle], fresh_out.at[:, middle], sems.at[0])]
    for side in range(2):
        copies.append(
            pltpu.make_async_copy(
                ends.at[side], fresh_out.at[:, pl.ds(side * (cells - LANES), LANES)], sems.at[1 + side]
            )
        )
    copies.append(pltpu.make_async_copy(received, received_out, sems.at[3]))
    copies.append(pltpu.make_async_copy(message, message_out, sems.at[4]))

    def begin(which):
        def body(_, carry):
            for copy in which:
                copy.start()
            return carry

        lax.fori_loop(0, 1 + lax.axis_index("tile") // lax.axis_size("tile"), body, 0)

    begin(copies[:1])
    tile = lax.axis_index("tile")
    tile_count = lax.axis_size("tile")
    entries = tiles.shape[0]
    blocks = old.shape[0]

    even = lax.rem(tile, 2) == 0
    base = far.shape[0] - here.shape[0]
    each = here.shape[0] // 4
    from_left, from_right = sides(far[...], near[...], even)
    sources = (from_left2[base:, :], from_left[base:], here[...], from_right[base:], from_right2[base:, :])
    for channel in range(4):
        source = jnp.concatenate(
            [rows[channel * each : (channel + 1) * each] for rows in sources], axis=0
        )
        picked[pl.ds(channel, entries, stride=4), :] = jnp.dot(hot[...], source, preferred_element_type=F32)

    arrivals[0] = from_left[:base].astype(F32)
    arrivals[1] = from_right[:base].astype(F32)

    upper = lax.rem(lax.broadcasted_iota(I32, (16, LANES), 0), 8) < 4
    for group in range(entries // 4):
        rows = picked[pl.ds(16 * group, 16), :]
        rows = jnp.concatenate([jnp.where(upper, rows, 0.0), jnp.where(upper, 0.0, rows)], axis=1)
        at = 4 * group
        weights = jnp.concatenate(
            [
                jnp.concatenate([tiles[at], tiles[at + 1]], axis=1),
                jnp.concatenate([tiles[at + 2], tiles[at + 3]], axis=1),
            ],
            axis=0,
        )
        product = dot_nt(rows.astype(BF16), weights)
        products[pl.ds(16 * group, 8), :] = product[0:8, :LANES]
        products[pl.ds(16 * group + 8, 8), :] = product[8:16, LANES:]
    speed = scalars[pl.ds(0, 8), :]
    share = scalars[pl.ds(8, 8), :]
    force_out[...] = force_part[...]
    padded[pl.ds(0, 8), :] = jnp.zeros((8, LANES), F32)
    padded[pl.ds(8 + blocks, 8), :] = jnp.zeros((8, LANES), F32)
    beside_extra = []
    for side, block, target in ((0, 0, 0), (1, blocks - 1, 2)):
        halo = arrivals[side, pl.ds(FIELD_HI, 8), :] + arrivals[side, pl.ds(FIELD_LO, 8), :]
        halo_old = arrivals[side, pl.ds(OLD_HI, 1), :] + arrivals[side, pl.ds(OLD_LO, 1), :]
        total = edges[0, pl.ds(block, 1), :] + edges[1, pl.ds(block, 1), :] + edges[2, pl.ds(block, 1), :]
        extra = jnp.zeros((8, LANES), F32)
        extra_old = jnp.zeros((8, LANES), F32)
        for link in range(3):
            place = wide(window[link, pl.ds(block, 1), :])
            index = lax.bitwise_and(place, LANES - 1)
            weight = jnp.where(
                lax.shift_right_logical(place, 7) == target, wide(edges[link, pl.ds(block, 1), :]), 0.0
            )
            extra = extra + weight * gather_lanes(halo, index)
            extra_old = extra_old + weight * gather_lanes(wide(halo_old), index)
        change = speed * extra / wide(total)
        ends[side] = fresh[:, pl.ds(block * LANES, LANES)] + change
        force_out[pl.ds(block, 1), :] += jnp.sum(change * share, axis=0, keepdims=True)
        beside_extra.append(extra_old[0:1])

    inverse_windows(arrivals.at[0], cinverse, arrivals.at[1], extended, weights_out)

    force = force_out[...]
    half = entries // 2
    for channel in range(4):
        value = jnp.zeros((blocks, 2 * LANES), F32)
        for part in range(2):
            rows = products[pl.ds(4 * half * part + channel, half, stride=4), :]
            value = value + jnp.dot(
                member[part], jnp.concatenate(split2(rows), axis=1), preferred_element_type=F32
            )
        value = value[:, :LANES] + value[:, LANES:]
        for block in range(blocks):
            received[pl.ds(channel, 1), pl.ds(block * LANES, LANES)] = value[block : block + 1]
        force = force + scalars[pl.ds(16 + channel, 1), :] * value

    force_out[...] = force
    begin(copies[1:4])
    total, damp = damping[0], damping[1]
    smooth_out[...] = beside_old[...]
    smooth_out[pl.ds(0, 1), :] += beside_extra[0]
    smooth_out[pl.ds(blocks - 1, 1), :] += beside_extra[1]
    previous = old[...]
    smooth = previous + damp * (force - (total * previous - smooth_out[...]))
    smooth_out[...] = smooth
    padded[pl.ds(8, blocks), :] = smooth
    residual = force - total * smooth + neighbour_sum(padded, edges, window, blocks)

    inner, whole = prefix(residual)
    before, run = rows_before(whole)
    prefixed[...] = inner + before
    rows, lanes = ends_row[...], ends_lane[...]
    count = rows.shape[0]
    marks = run[:count]
    for block in range(blocks):
        value = gather_lanes(wide(prefixed[pl.ds(block, 1), :], count), lanes)
        marks = jnp.where(rows == block, value, marks)
    own_source = marks - previous_one(marks)

    lane = lax.broadcasted_iota(I32, (1, LANES), 1)
    rim_rows, rim_counts = [], []
    for side in range(2):
        inside = padded[pl.ds(8 if side == 0 else 7 + blocks, 1), :]
        value = jnp.zeros((1, LANES), F32)
        for link in range(3):
            place = lane + arrivals[side, pl.ds(OFFSET + link, 1), :].astype(I32)
            index = lax.bitwise_and(place, LANES - 1)
            reached = (place >= LANES) if side == 0 else (place < 0)
            weight = arrivals[side, pl.ds(EDGE_HI + link, 1), :] + arrivals[side, pl.ds(EDGE_LO + link, 1), :]
            value = value + jnp.where(
                wide(reached.astype(I32)) > 0,
                wide(weight) * gather_lanes(wide(inside), wide(index)),
                0.0,
            )[0:1]
        rim_rows.append(value)
        owners = arrivals[side, pl.ds(OWNER, 1), :].astype(I32)
        below = jnp.where(
            lax.broadcasted_iota(I32, (LANES, LANES), 0) >= owners, 1.0, 0.0
        ).astype(BF16)
        rim_counts.append(dot_nt(jnp.ones((8, LANES), BF16), below))
    rim_inner, rim_whole = prefix(jnp.concatenate([wide(r) for r in rim_rows], axis=0))
    rim_source = []
    for side in range(2):
        place = rim_counts[side].astype(I32)
        index = lax.bitwise_and(place, LANES - 1)
        value = gather_lanes(rim_inner[8 * side : 8 * side + 8], index)
        value = jnp.where(place >= LANES, rim_whole[8 * side : 8 * side + 8], value)
        shifted = pltpu.roll(value, 1, axis=1)
        first = lax.broadcasted_iota(I32, (8, LANES), 1) == 0
        rim_source.append((value - jnp.where(first, 0.0, shifted))[0:1])

    frows = own_source.shape[0]
    source_out[...] = jnp.zeros((FRAME, LANES), F32)
    source_out[pl.ds(OWN, frows), :] = own_source
    source_out[pl.ds(OWN - 1, 1), :] = rim_source[0]
    source_out[pl.ds(OWN + frows, 1), :] = rim_source[1]
    reach = LANES // 8
    frame[...] = jnp.zeros(frame.shape, F32)
    frame[pl.ds(6 * FRAME, FRAME), :] = jnp.ones((FRAME, LANES), F32)
    frame[pl.ds(7 * FRAME, FRAME), :] = jnp.full((FRAME, LANES), 127.0, F32)
    bottoms = 16
    at_cell = lax.broadcasted_iota(I32, (frows, LANES), 0) * LANES + lax.broadcasted_iota(
        I32, (frows, LANES), 1
    )
    for link in range(3):
        frame[pl.ds(link * FRAME + OWN, frows), :] = (ctable[link] - reach - at_cell).astype(F32)
        frame[pl.ds((3 + link) * FRAME + OWN, frows), :] = cedge[link]
    frame[pl.ds(6 * FRAME + OWN, frows), :] = cdiag[...]
    frame[pl.ds(7 * FRAME + OWN, frows), :] = (cowner[...] + bottoms).astype(F32)
    for side in range(2):
        for row in range(2):
            at = (OWN - 2 + row) if side == 0 else (OWN + frows + row)
            for link in range(3):
                put = 3 * row + link
                frame[pl.ds(link * FRAME + at, 1), :] = arrivals[side, pl.ds(COFFSET + put, 1), :]
                frame[pl.ds((3 + link) * FRAME + at, 1), :] = (
                    arrivals[side, pl.ds(CEDGE_HI + put, 1), :] + arrivals[side, pl.ds(CEDGE_LO + put, 1), :]
                )
            frame[pl.ds(6 * FRAME + at, 1), :] = (
                arrivals[side, pl.ds(CDIAG_HI + row, 1), :] + arrivals[side, pl.ds(CDIAG_LO + row, 1), :]
            )
            frame[pl.ds(7 * FRAME + at, 1), :] = arrivals[side, pl.ds(COWNER + row, 1), :] + (
                2.0 * bottoms * side
            )
    for link in range(3):
        frame[pl.ds(6 * FRAME, FRAME), :] += frame[pl.ds((3 + link) * FRAME, FRAME), :]
    source = source_out[...]
    first = (RELAXATION / frame[pl.ds(6 * FRAME, FRAME), :]) * source
    residual = (1.0 - RELAXATION) * source + first_level_sum(first, frame)
    codes = frame[pl.ds(7 * FRAME, FRAME), :].astype(I32)
    pieces = split2(residual)
    left_side, right_side = [], []
    bins = lax.broadcasted_iota(I32, (3 * bottoms, LANES), 0)
    rest = [jnp.zeros((rows, LANES), BF16) for rows in (MIDDLE, LANES - MIDDLE - 3 * bottoms)]
    for row in range(OWN - 2, OWN + frows + 2):
        left_side.append(jnp.concatenate([p[row : row + 1] for p in pieces], axis=0))
        named = jnp.where(bins == codes[row : row + 1], 1.0, 0.0).astype(BF16)
        right_side.append(jnp.concatenate([rest[0], named, rest[1]], axis=0))
    bottom = dot_nt(jnp.concatenate(left_side, axis=1), jnp.concatenate(right_side, axis=1))
    bottom = bottom[0:1] + bottom[1:2]

    reach = LANES // 8
    to_left = jnp.concatenate(
        [
            jnp.where(lane < reach, own_source[1:2], bottom),
            padded[pl.ds(8, 1), :],
            own_source[0:1],
            rim_source[0],
        ],
        axis=0,
    )
    to_right = jnp.concatenate(
        [
            jnp.where(lane >= LANES - reach, own_source[frows - 2 : frows - 1], bottom),
            padded[pl.ds(7 + blocks, 1), :],
            own_source[frows - 1 : frows],
            rim_source[1],
        ],
        axis=0,
    )
    for other in range(message.shape[0]):
        message[other] = to_right
    message[lax.rem(tile + tile_count - 1, tile_count)] = to_left
    copies[4].start()
    for copy in copies:
        copy.wait()


def inverse_windows(left, own, right, extended, weights):
    bottoms, size = own.shape
    halves = size // LANES
    for half in range(halves):
        part = pl.ds(half * LANES, LANES)
        for at, block in ((0, left), (2, right)):
            high, low = INVERSE + 16 * half, INVERSE + 16 * (halves + half)
            extended[pl.ds(at * bottoms, bottoms), part] = (
                block[pl.ds(high, bottoms), :] + block[pl.ds(low, bottoms), :]
            )
        extended[pl.ds(bottoms, bottoms), part] = own[:, part]
    table = extended[...]
    lane = lax.broadcasted_iota(I32, (3 * bottoms, LANES), 1)
    for other in range(weights.shape[0]):
        shift = (size + MIDDLE - (other - 1) * bottoms) % size
        turned = pltpu.roll(table, shift, axis=1) if shift else table
        weights[other] = jnp.where(
            lane >= MIDDLE, jnp.where(lane < MIDDLE + 3 * bottoms, turned[:, :LANES], 0.0), 0.0
        )


def backward_kernel(
    frame_rows, arrived, weights, source, frame, force, smooth, edges, window, damping, owner, far, near,
    height, frame_source, padded, third_rows,
):
    tile = lax.axis_index("tile")
    tile_count = lax.axis_size("tile")
    blocks = force.shape[0]
    left = arrived[lax.rem(tile + tile_count - 1, tile_count)]
    right = arrived[lax.rem(tile + 1, tile_count)]
    count = weights.shape[1]
    partial = jnp.zeros((count, LANES), F32)
    for other in range(weights.shape[0]):
        partial = partial + weights[other] * wide(arrived[other, pl.ds(0, 1), :], count)
    partial = jnp.concatenate([partial, jnp.zeros((LANES - count, LANES), F32)], axis=0)
    ones = jnp.ones((8, LANES), BF16)
    bottom = dot_nt(jnp.concatenate([ones, ones], axis=1), jnp.concatenate(split2(partial), axis=1))

    frows = frame_rows
    frame_source[...] = source[...]
    lane = lax.broadcasted_iota(I32, (1, LANES), 1)
    reach = LANES // 8
    frame_source[pl.ds(OWN - 2, 1), :] += jnp.where(lane >= LANES - reach, left[0:1], 0.0)
    frame_source[pl.ds(OWN - 1, 1), :] += left[2:3]
    frame_source[pl.ds(OWN, 1), :] += left[3:4]
    frame_source[pl.ds(OWN + frows - 1, 1), :] += right[3:4]
    frame_source[pl.ds(OWN + frows, 1), :] += right[2:3]
    frame_source[pl.ds(OWN + frows + 1, 1), :] += jnp.where(lane < reach, right[0:1], 0.0)
    total_source = frame_source[...]
    total = frame[pl.ds(6 * FRAME, FRAME), :]
    codes = frame[pl.ds(7 * FRAME, FRAME), :].astype(I32)
    damp = RELAXATION / total
    second = damp * total_source + gather_lanes(wide(bottom[0:1], FRAME), codes)
    third = second + damp * (total_source - total * second + first_level_sum(second, frame))
    third_rows[...] = third

    owners = owner[...]
    index = lax.bitwise_and(owners, LANES - 1)
    which = lax.shift_right_logical(owners, 7)
    corrected = jnp.zeros((blocks, LANES), F32)
    for row in range(frows):
        corrected = jnp.where(
            which == row, gather_lanes(wide(third_rows[pl.ds(OWN + row, 1), :], blocks), index), corrected
        )
    corrected = smooth[...] + corrected
    padded[pl.ds(8, blocks), :] = corrected
    part = pl.ds(16, 16)
    even = lax.rem(tile, 2) == 0
    left_owner, right_owner = [
        rows[OWNER - 16 : OWNER - 15].astype(I32)
        for rows in sides(far[part, :].astype(F32), near[part, :].astype(F32), even)
    ]
    left_rim = left[1:2] + gather_lanes(wide(third_rows[pl.ds(OWN - 1, 1), :]), wide(left_owner))[0:1]
    right_rim = right[1:2] + gather_lanes(wide(third_rows[pl.ds(OWN + frows, 1), :]), wide(right_owner))[0:1]
    padded[pl.ds(7, 1), :] = left_rim
    padded[pl.ds(8 + blocks, 1), :] = right_rim
    beside = neighbour_sum(padded, edges, window, blocks)
    height[...] = corrected + damping[1] * (force[...] - (damping[0] * corrected - beside))


def in_hbm(array):
    return pltpu.with_memory_space_constraint(array, pltpu.HBM)


def struct(shape, dtype=F32):
    return jax.ShapeDtypeStruct(shape, dtype)


VMEM = pl.BlockSpec(memory_space=pltpu.VMEM)
SMEM = pl.BlockSpec(memory_space=pltpu.SMEM)
ANY = pl.BlockSpec(memory_space=pltpu.HBM)
PARAMS = pltpu.CompilerParams(vmem_limit_bytes=16 * 1024 * 1024)


def per_device(
    fields, level_rate, edge_weight, fine_diagonal, fine_table, old_height, level_weight,
    flux_weight, fine_owner, coarse_table, coarse_edge, coarse_diagonal, coarse_owner,
    coarse_inverse, surface_out, send_blocks, entry_slot, entry_block, remap_tiles,
):
    tile_count = lax.axis_size("tile")
    cells = fields.shape[2]
    blocks = cells // LANES
    firsts = coarse_diagonal.shape[1]
    frows = firsts // LANES
    entries = entry_slot.shape[2]
    channels = surface_out.shape[1]
    slots = send_blocks.shape[2]
    each = slots // 5
    halves = coarse_inverse.shape[2] // LANES
    bottoms = coarse_inverse.shape[1]
    base = pick_base(halves)
    swap = [(0, 1), (1, 0)]
    surface = lax.ppermute(surface_out[0], "comp", swap)
    sends = lax.ppermute(send_blocks[0], "comp", swap)
    raw = (
        fields[0],
        old_height.reshape(blocks, LANES),
        edge_weight[0].reshape(3, blocks, LANES),
        fine_table[0].reshape(3, blocks, LANES),
        fine_owner.reshape(blocks, LANES),
        coarse_table[0].reshape(3, frows, LANES),
        coarse_edge[0].reshape(3, frows, LANES),
        coarse_diagonal.reshape(frows, LANES),
        coarse_owner.reshape(frows, LANES),
        coarse_inverse[0],
    )
    current, old, edges, table, owner, ctable, cedge, cdiag, cowner, cinverse = pl.pallas_call(
        load_kernel,
        out_shape=[struct(x.shape, x.dtype) for x in raw],
        in_specs=[ANY] * len(raw),
        out_specs=[VMEM] * len(raw),
        scratch_shapes=[pltpu.SemaphoreType.DMA((len(raw),))],
        compiler_params=PARAMS,
        name="load",
    )(*[in_hbm(x) for x in raw])

    pick = struct((4 * each, LANES), BF16)
    both = struct((base + 4 * each, LANES), BF16)
    to_right2, far, to_left2, near, here = pl.pallas_call(
        pack_kernel,
        out_shape=[both, both, both, both, pick],
        in_specs=[VMEM] * 12,
        out_specs=[VMEM] * 5,
        scratch_shapes=[
            pltpu.VMEM((channels * blocks, LANES), F32),
            pltpu.VMEM((base, LANES), F32),
            pltpu.VMEM((base, LANES), F32),
        ],
        compiler_params=PARAMS,
        name="pack",
    )(
        surface, sends, current, old, edges, table, owner, ctable, cedge, cdiag, cowner, cinverse,
    )

    def shifted(array, distance):
        return lax.ppermute(
            array, "tile", [(i, (i + distance) % tile_count) for i in range(tile_count)]
        )

    def swapped(array, start):
        lower = [i for i in range(tile_count) if i % 2 == start]
        pairs = [(i, (i + 1) % tile_count) for i in lower]
        return lax.ppermute(array, "tile", pairs + [(j, i) for i, j in pairs])

    from_left2 = shifted(to_right2, 2)
    far = swapped(far, 1)
    from_right2 = shifted(to_left2, -2)
    near = swapped(near, 0)

    late = (
        level_rate, level_weight, flux_weight, fine_diagonal.reshape(blocks, LANES), entry_slot[0], entry_block[0]
    )
    fresh, force_part, beside_old, window, ends_row, ends_lane, hot, member, damping, scalars, tiles = pl.pallas_call(
        stencil_kernel,
        out_shape=[
            struct((fields.shape[1], cells)),
            struct((blocks, LANES)),
            struct((blocks, LANES)),
            struct((3, blocks, LANES), I32),
            struct((frows, LANES), I32),
            struct((frows, LANES), I32),
            struct((entries, slots), BF16),
            struct((2, blocks, entries // 2), BF16),
            struct((2, blocks, LANES)),
            struct((24, LANES)),
            pltpu.VMEM(remap_tiles.shape[2:], BF16),
        ],
        in_specs=[VMEM] * 6 + [ANY] * 7,
        out_specs=[VMEM] * 11,
        scratch_shapes=[pltpu.VMEM((blocks + 16, LANES), F32)]
        + [pltpu.VMEM(x.shape, x.dtype) for x in late]
        + [pltpu.SemaphoreType.DMA((len(late),)), pltpu.SemaphoreType.DMA((math.gcd(entries, 8),))],
        compiler_params=PARAMS,
        name="stencil",
    )(here, current, edges, table, old, owner, *[in_hbm(x) for x in (remap_tiles[0, 0],) + late])

    force, smooth, source, frame, weights, advanced, received, message = pl.pallas_call(
        forward_kernel,
        out_shape=[
            struct((blocks, LANES)),
            struct((blocks, LANES)),
            struct((FRAME, LANES)),
            struct((8 * FRAME, LANES)),
            struct((tile_count, 3 * bottoms, LANES)),
            struct((fields.shape[1], cells)),
            struct((channels, cells)),
            struct((tile_count, 4, LANES)),
        ],
        in_specs=[VMEM] * 24,
        out_specs=[VMEM] * 5 + [ANY] * 3,
        scratch_shapes=[
            pltpu.VMEM((4 * entries, LANES), F32),
            pltpu.VMEM((4 * entries, LANES), F32),
            pltpu.VMEM((blocks + 16, LANES), F32),
            pltpu.VMEM((blocks, LANES), F32),
            pltpu.VMEM((2, base, LANES), F32),
            pltpu.VMEM((3 * bottoms, bottoms * tile_count), F32),
            pltpu.VMEM((2, fields.shape[1], LANES), F32),
            pltpu.VMEM((channels, cells), F32),
            pltpu.VMEM((tile_count, 4, LANES), F32),
            pltpu.SemaphoreType.DMA((5,)),
        ],
        compiler_params=PARAMS,
        name="forward",
    )(
        tiles, scalars, from_left2, far, from_right2, near, here, hot, member, current, edges, window, old,
        damping, force_part, beside_old, ends_row, ends_lane, fresh, ctable, cedge, cdiag, cowner, cinverse,
    )
    arrived = lax.all_to_all(message, "tile", split_axis=0, concat_axis=0, tiled=True)
    height = pl.pallas_call(
        functools.partial(backward_kernel, frows),
        out_shape=struct((blocks, LANES)),
        in_specs=[VMEM] * 12,
        out_specs=VMEM,
        scratch_shapes=[
            pltpu.VMEM((FRAME, LANES), F32),
            pltpu.VMEM((blocks + 16, LANES), F32),
            pltpu.VMEM((FRAME, LANES), F32),
        ],
        compiler_params=PARAMS,
        name="backward",
    )(arrived, weights, source, frame, force, smooth, edges, window, damping, owner, far, near)
    return advanced[None], received[None], height.reshape(1, cells)


def solution(mesh):
    in_specs = (
        P("comp", None, "tile"),
        P("comp", None),
        P("comp", None, "tile"),
        P("comp", "tile"),
        P("comp", None, "tile"),
        P("comp", "tile"),
        P("comp", None),
        P("comp", None),
        P("comp", "tile"),
        P("comp", None, "tile"),
        P("comp", None, "tile"),
        P("comp", "tile"),
        P("comp", "tile"),
        P("comp", "tile", None),
        P("comp", None, "tile"),
        P("comp", "tile", None),
        P("comp", "tile", None),
        P("comp", "tile", None),
        P("comp", "tile", None, None, None),
    )
    out_specs = (P("comp", None, "tile"), P("comp", None, "tile"), P("comp", "tile"))
    return jax.shard_map(
        per_device, mesh=mesh, in_specs=in_specs, out_specs=out_specs, check_vma=False
    )
```

```python
import functools
import math

import jax
import jax.numpy as jnp
from jax import lax
from jax.experimental import pallas as pl
from jax.experimental.pallas import tpu as pltpu
from jax.sharding import PartitionSpec as P

LANES = 128
RELAXATION = 0.8
F32 = jnp.float32
BF16 = jnp.bfloat16
I32 = jnp.int32

FIELD_HI, FIELD_LO = 0, 8
EDGE_HI, EDGE_LO, OLD_HI, OLD_LO = 16, 19, 22, 23
OFFSET, OWNER = 24, 27
CEDGE_HI, CEDGE_LO, CDIAG_HI, CDIAG_LO = 32, 38, 44, 46
COFFSET, COWNER = 48, 54
INVERSE = 56

FRAME, OWN = 32, 8

MIDDLE = 32


PLANS = {
    16: (
        (1, 1, 1, 1, 1, 2, 2, -1, 2, 2, -1, 2, 2, 2, -2, 1),
        (-1, 2, 2, -2, -2, 1, -1, 2, -1, 1, -2, 1, 1, -2, 2, -1),
        (-2, -2, -2, -1, -1, -1, 1, -2, -2, -1, 1, -2, -2, -1, -1, 2),
        (2, -1, -1, 2, 2, -2, -2, 1, 1, -2, 2, -1, -1, 1, 1, -2),
    ),
}
DISTANCES = (-1, 1, -2, 2)


def exchange_plan(count):
    if count in PLANS:
        return PLANS[count]
    near = [1 if i % 2 == 0 else -1 for i in range(count)]
    return ([2] * count, [-d for d in near], [-2] * count, near)


def lookup(tile, values):
    result = jnp.int32(values[0])
    for i, value in enumerate(values):
        result = jnp.where(tile == i, jnp.int32(value), result)
    return result


def arrived_by(tile, plan, distance):
    count = len(plan[0])
    found = []
    for i in range(count):
        sender = (i - distance) % count
        found.append([op[sender] for op in plan].index(distance))
    return lookup(tile, found)


def chosen_rows(which, refs, rows):
    value = refs[0][rows, :]
    for i, ref in enumerate(refs[1:]):
        value = jnp.where(which == i + 1, ref[rows, :], value)
    return value


def gather_lanes(table, index):
    return jnp.take_along_axis(table, index, axis=1)


def wide(row, count=8):
    return jnp.broadcast_to(row, (count, row.shape[1]))


def split2(x):
    high = x.astype(BF16)
    return high, (x - high.astype(F32)).astype(BF16)


def dot_nt(a, b):
    return lax.dot_general(a, b, (((1,), (1,)), ((), ())), preferred_element_type=F32)


def dot_tn(a, b):
    return lax.dot_general(a, b, (((0,), (0,)), ((), ())), preferred_element_type=F32)


def pick_base(inverse_blocks):
    return -(-(INVERSE + 32 * inverse_blocks) // 16) * 16


def load_kernel(*refs):
    count = len(refs) // 2
    copies = [
        pltpu.make_async_copy(source, target, refs[-1].at[i])
        for i, (source, target) in enumerate(zip(refs[:count], refs[count : 2 * count]))
    ]
    for copy in copies:
        copy.start()
    for copy in copies:
        copy.wait()


def pack_kernel(
    plan, surface, sends, fields, old, edge, table, owner, ctable, cedge, cdiag, cowner, cinverse,
    out0, out1, out2, out3, here, chunks, left_rows, right_rows, packed,
):
    tile = lax.axis_index("tile")
    cells = fields.shape[1]
    blocks = cells // LANES
    frows = ctable.shape[1]
    firsts = frows * LANES
    base = pick_base(cinverse.shape[1] // LANES)
    lane = lax.broadcasted_iota(I32, (1, LANES), 1)

    for rows, at_left in ((right_rows, False), (left_rows, True)):
        start = 0 if at_left else cells - LANES
        part = pl.ds(start, LANES)

        def both(high, low_row, value):
            count = value.shape[0]
            rows[pl.ds(high, count), :] = value
            rows[pl.ds(low_row, count), :] = value - value.astype(BF16).astype(F32)

        def three(ref, row):
            return jnp.concatenate([ref[link, pl.ds(row, 1), :] for link in range(3)], axis=0)

        rows[pl.ds(24, 8), :] = jnp.zeros((8, LANES), F32)
        both(FIELD_HI, FIELD_LO, fields[:, part])
        block = 0 if at_left else blocks - 1
        both(EDGE_HI, EDGE_LO, three(edge, block))
        both(OLD_HI, OLD_LO, old[pl.ds(block, 1), :])
        rows[pl.ds(OFFSET, 3), :] = (three(table, block) - (LANES + start) - lane).astype(F32)
        shift = 0 if at_left else firsts - LANES
        rows[pl.ds(OWNER, 1), :] = (owner[pl.ds(block, 1), :] - shift).astype(F32)
        first = 0 if at_left else frows - 2
        reach = LANES // 8
        for step in range(2):
            both(CEDGE_HI + 3 * step, CEDGE_LO + 3 * step, three(cedge, first + step))
            rows[pl.ds(COFFSET + 3 * step, 3), :] = (
                three(ctable, first + step) - (reach + (first + step) * LANES) - lane
            ).astype(F32)
            both(CDIAG_HI + step, CDIAG_LO + step, cdiag[pl.ds(first + step, 1), :])
            rows[pl.ds(COWNER + step, 1), :] = cowner[pl.ds(first + step, 1), :].astype(F32)
        halves = cinverse.shape[1] // LANES
        for half in range(halves):
            both(
                INVERSE + 16 * half,
                INVERSE + 16 * (halves + half),
                cinverse[:, pl.ds(half * LANES, LANES)],
            )
        end = INVERSE + 32 * halves
        if base > end:
            rows[pl.ds(end, base - end), :] = jnp.zeros((base - end, LANES), F32)

    for block in range(blocks):
        chunks[pl.ds(4 * block, 4), :] = surface[:, pl.ds(block * LANES, LANES)].astype(F32)
    slots = sends.shape[1]
    hot = jnp.where(
        lax.broadcasted_iota(I32, (blocks, slots), 0) == sends[...], 1.0, 0.0
    ).astype(BF16)
    picks = []
    for channel in range(4):
        source = chunks[pl.ds(channel, blocks, stride=4), :].astype(BF16)
        picks.append(dot_tn(hot, source).astype(BF16))
    count = slots // 5

    chosen = [
        jnp.concatenate([p[j * count : (j + 1) * count] for p in picks], axis=0) for j in range(5)
    ]
    here[...] = chosen[2]
    rims = {-1: left_rows[...].astype(BF16), 1: right_rows[...].astype(BF16)}
    for at, distance in enumerate(DISTANCES):
        packed[at, pl.ds(0, base), :] = rims.get(distance, jnp.zeros((base, LANES), BF16))
        packed[at, pl.ds(base, 4 * count), :] = chosen[2 - distance]
    for out, op in zip((out0, out1, out2, out3), plan):
        out[...] = packed[lookup(tile, [DISTANCES.index(distance) for distance in op])]


def stencil_kernel(
    here, fields, edge, table, old, owner, tiles, rate, level_weight, flux_weight, diagonal_in, slots_in, block_in,
    fresh, force, beside_old, window, ends_row, ends_lane, hot, member, damping, scalars, tile_buffer,
    padded, rate_row, level_row, flux_row, diagonal, slots, entry_block, small_sems, sems,
):
    del here
    small = [
        pltpu.make_async_copy(source, target, small_sems.at[i])
        for i, (source, target) in enumerate(
            (
                (rate, rate_row), (level_weight, level_row), (flux_weight, flux_row),
                (diagonal_in, diagonal), (slots_in, slots), (block_in, entry_block),
            )
        )
    ]
    parts = sems.shape[0]
    step = tiles.shape[0] // parts

    def load(part):
        span = pl.ds(part * step, step)
        return pltpu.make_async_copy(tiles.at[span], tile_buffer.at[span], sems.at[part])

    def begin(part, carry):
        if part is None:
            for copy in small:
                copy.start()
        else:
            load(part).start()
        return carry

    once = 1 + lax.axis_index("tile") // lax.axis_size("tile")
    lax.fori_loop(0, once, lambda _, carry: begin(None, carry), 0)
    lax.fori_loop(0, parts, begin, 0)
    blocks = old.shape[0]
    levels = fields.shape[0]
    firsts = ends_row.shape[0] * LANES
    ident = lax.broadcasted_iota(I32, ends_row.shape, 0) * LANES + lax.broadcasted_iota(
        I32, ends_row.shape, 1
    )
    count = ends_row.shape[0]
    rows = jnp.zeros(ends_row.shape, I32)
    for block in range(blocks):
        last = jnp.broadcast_to(owner[pl.ds(block, 1), LANES - 1 : LANES], ends_row.shape)
        rows = rows + jnp.where(last <= ident, 1, 0)
    lanes = jnp.zeros(ends_row.shape, I32)
    for bit in (64, 32, 16, 8, 4, 2, 1):
        probe = lanes + (bit - 1)
        value = jnp.full(ends_row.shape, firsts, I32)
        for block in range(blocks):
            value = jnp.where(
                rows == block, gather_lanes(wide(owner[pl.ds(block, 1), :], count), probe), value
            )
        lanes = jnp.where(value <= ident, lanes + bit, lanes)
    ends_row[...] = rows
    ends_lane[...] = lanes
    for copy in small:
        copy.wait()
    for i, value in enumerate((rate_row, level_row, flux_row)):
        width = value.shape[1]
        same = lax.broadcasted_iota(I32, (8, width), 0) == lax.broadcasted_iota(I32, (8, width), 1)
        column = jnp.sum(jnp.where(same, wide(value[...]), 0.0), axis=1, keepdims=True)
        scalars[pl.ds(8 * i, 8), :] = jnp.broadcast_to(column, (8, LANES))
    speed = scalars[pl.ds(0, 8), :]
    share = scalars[pl.ds(8, 8), :]
    starts = lax.broadcasted_iota(I32, (blocks, LANES), 0) * LANES
    total = edge[0] + edge[1] + edge[2]
    inverse = 1.0 / total
    fine_total = diagonal[...] + total
    damping[0] = fine_total
    damping[1] = RELAXATION / fine_total
    for link in range(3):
        window[link] = table[link] - starts
    blank = jnp.zeros((levels, LANES), F32)

    def chunk(block):
        if 0 <= block < blocks:
            return fields[:, pl.ds(block * LANES, LANES)]
        return blank

    before, here, after = blank, chunk(0), chunk(1)
    for block in range(blocks):
        row = slice(block, block + 1)
        beside = jnp.zeros((levels, LANES), F32)
        for link in range(3):
            place = wide(window[link, pl.ds(block, 1), :])
            index = lax.bitwise_and(place, LANES - 1)
            value = jnp.where(
                place < LANES,
                gather_lanes(before, index),
                jnp.where(place < 2 * LANES, gather_lanes(here, index), gather_lanes(after, index)),
            )
            beside = beside + wide(edge[link, pl.ds(block, 1), :]) * value
        result = here + speed * ((beside - wide(total[row]) * here) * wide(inverse[row]))
        fresh[:, pl.ds(block * LANES, LANES)] = result
        force[pl.ds(block, 1), :] = jnp.sum(result * share, axis=0, keepdims=True)
        before, here, after = here, after, chunk(block + 2)

    padded[pl.ds(0, 8), :] = jnp.zeros((8, LANES), F32)
    padded[pl.ds(8 + blocks, 8), :] = jnp.zeros((8, LANES), F32)
    padded[pl.ds(8, blocks), :] = old[...]
    beside_old[...] = neighbour_sum(padded, edge, window, blocks)
    names = jnp.where(
        lax.broadcasted_iota(I32, (slots.shape[1], slots.shape[1]), 0) == slots[...], 1.0, 0.0
    )
    hot[...] = jnp.transpose(names).astype(BF16)
    half = entry_block.shape[1] // 2
    for part in range(2):
        member[part] = jnp.where(
            lax.broadcasted_iota(I32, (blocks, half), 0) == entry_block[:, part * half : (part + 1) * half],
            1.0,
            0.0,
        ).astype(BF16)

    for part in range(parts):
        load(part).wait()


def neighbour_sum(padded, edges, window, blocks):
    before = padded[pl.ds(7, blocks), :]
    here = padded[pl.ds(8, blocks), :]
    after = padded[pl.ds(9, blocks), :]
    result = jnp.zeros((blocks, LANES), F32)
    for link in range(3):
        place = window[link]
        index = lax.bitwise_and(place, LANES - 1)
        value = jnp.where(
            place < LANES,
            gather_lanes(before, index),
            jnp.where(place < 2 * LANES, gather_lanes(here, index), gather_lanes(after, index)),
        )
        result = result + edges[link] * value
    return result


def first_level_sum(values, frame):
    before = pltpu.roll(values, 1, axis=0)
    after = pltpu.roll(values, FRAME - 1, axis=0)
    lane = lax.broadcasted_iota(I32, (FRAME, LANES), 1)
    result = jnp.zeros((FRAME, LANES), F32)
    for link in range(3):
        place = lane + frame[pl.ds(link * FRAME, FRAME), :].astype(I32)
        index = lax.bitwise_and(place, LANES - 1)
        value = jnp.where(
            place < 0,
            gather_lanes(before, index),
            jnp.where(place >= LANES, gather_lanes(after, index), gather_lanes(values, index)),
        )
        result = result + frame[pl.ds((3 + link) * FRAME, FRAME), :] * value
    return result


def previous_one(values):
    rolled = pltpu.roll(values, 1, axis=1)
    above = pltpu.roll(rolled, 1, axis=0)
    lane = lax.broadcasted_iota(I32, values.shape, 1)
    row = lax.broadcasted_iota(I32, values.shape, 0)
    return jnp.where(lane > 0, rolled, jnp.where(row > 0, above, 0.0))


def triangle():
    return jnp.where(
        lax.broadcasted_iota(I32, (LANES, LANES), 0) < lax.broadcasted_iota(I32, (LANES, LANES), 1),
        1.0,
        0.0,
    ).astype(BF16)


def prefix(values):
    ones = jnp.ones((LANES, LANES), BF16)
    right = jnp.concatenate([triangle(), ones], axis=1)
    count = values.shape[0]
    out = jnp.dot(
        jnp.concatenate(split2(values), axis=0), right, preferred_element_type=F32
    )
    out = out[:count] + out[count:]
    return out[:, :LANES], out[:, LANES:]


def rows_before(values):
    sublane = lax.broadcasted_iota(I32, (8, LANES), 0)
    run = jnp.zeros((8, LANES), F32)
    result = []
    for at in range(0, values.shape[0], 8):
        piece = values[at : at + 8]
        total = piece
        for distance in (1, 2, 4):
            total = total + jnp.where(sublane >= distance, pltpu.roll(total, distance, axis=0), 0.0)
        result.append(run + (total - piece))
        run = run + wide(total[7:8])
    return jnp.concatenate(result, axis=0), run


def forward_kernel(
    plan, tiles, scalars, message0, message1, message2, message3, here, hot, member, fields, edges, window, old,
    damping, force_part, beside_old, ends_row, ends_lane, fresh, ctable, cedge, cdiag, cowner, cinverse,
    force_out, smooth_out, source_out, frame, weights_out, rim_owner, fresh_out, received_out, message_out,
    picked, products, padded, prefixed, arrivals, extended, ends, received, message, sems,
):
    cells = fresh.shape[1]
    middle = pl.ds(LANES, cells - 2 * LANES)
    copies = [pltpu.make_async_copy(fresh.at[:, middle], fresh_out.at[:, middle], sems.at[0])]
    for side in range(2):
        copies.append(
            pltpu.make_async_copy(
                ends.at[side], fresh_out.at[:, pl.ds(side * (cells - LANES), LANES)], sems.at[1 + side]
            )
        )
    copies.append(pltpu.make_async_copy(received, received_out, sems.at[3]))
    copies.append(pltpu.make_async_copy(message, message_out, sems.at[4]))

    def begin(which):
        def body(_, carry):
            for copy in which:
                copy.start()
            return carry

        lax.fori_loop(0, 1 + lax.axis_index("tile") // lax.axis_size("tile"), body, 0)

    begin(copies[:1])
    tile = lax.axis_index("tile")
    tile_count = lax.axis_size("tile")
    entries = tiles.shape[0]
    blocks = old.shape[0]

    messages = (message0, message1, message2, message3)
    base = message0.shape[0] - here.shape[0]
    each = here.shape[0] // 4
    found = {distance: arrived_by(tile, plan, distance) for distance in DISTANCES}
    sources = [
        chosen_rows(found[distance], messages, pl.ds(base, 4 * each)) if distance else here[...]
        for distance in (2, 1, 0, -1, -2)
    ]
    for channel in range(4):
        source = jnp.concatenate(
            [rows[channel * each : (channel + 1) * each] for rows in sources], axis=0
        )
        picked[pl.ds(channel, entries, stride=4), :] = jnp.dot(hot[...], source, preferred_element_type=F32)

    for side, distance in enumerate((1, -1)):
        arrivals[side] = chosen_rows(found[distance], messages, pl.ds(0, base)).astype(F32)
        rim_owner[side] = wide(arrivals[side, pl.ds(OWNER, 1), :]).astype(I32)

    upper = lax.rem(lax.broadcasted_iota(I32, (16, LANES), 0), 8) < 4
    for group in range(entries // 4):
        rows = picked[pl.ds(16 * group, 16), :]
        rows = jnp.concatenate([jnp.where(upper, rows, 0.0), jnp.where(upper, 0.0, rows)], axis=1)
        at = 4 * group
        weights = jnp.concatenate(
            [
                jnp.concatenate([tiles[at], tiles[at + 1]], axis=1),
                jnp.concatenate([tiles[at + 2], tiles[at + 3]], axis=1),
            ],
            axis=0,
        )
        product = dot_nt(rows.astype(BF16), weights)
        products[pl.ds(16 * group, 8), :] = product[0:8, :LANES]
        products[pl.ds(16 * group + 8, 8), :] = product[8:16, LANES:]
    speed = scalars[pl.ds(0, 8), :]
    share = scalars[pl.ds(8, 8), :]
    force_out[...] = force_part[...]
    padded[pl.ds(0, 8), :] = jnp.zeros((8, LANES), F32)
    padded[pl.ds(8 + blocks, 8), :] = jnp.zeros((8, LANES), F32)
    beside_extra = []
    for side, block, target in ((0, 0, 0), (1, blocks - 1, 2)):
        halo = arrivals[side, pl.ds(FIELD_HI, 8), :] + arrivals[side, pl.ds(FIELD_LO, 8), :]
        halo_old = arrivals[side, pl.ds(OLD_HI, 1), :] + arrivals[side, pl.ds(OLD_LO, 1), :]
        total = edges[0, pl.ds(block, 1), :] + edges[1, pl.ds(block, 1), :] + edges[2, pl.ds(block, 1), :]
        extra = jnp.zeros((8, LANES), F32)
        extra_old = jnp.zeros((8, LANES), F32)
        for link in range(3):
            place = wide(window[link, pl.ds(block, 1), :])
            index = lax.bitwise_and(place, LANES - 1)
            weight = jnp.where(
                lax.shift_right_logical(place, 7) == target, wide(edges[link, pl.ds(block, 1), :]), 0.0
            )
            extra = extra + weight * gather_lanes(halo, index)
            extra_old = extra_old + weight * gather_lanes(wide(halo_old), index)
        change = speed * extra / wide(total)
        ends[side] = fresh[:, pl.ds(block * LANES, LANES)] + change
        force_out[pl.ds(block, 1), :] += jnp.sum(change * share, axis=0, keepdims=True)
        beside_extra.append(extra_old[0:1])

    inverse_windows(arrivals.at[0], cinverse, arrivals.at[1], extended, weights_out)

    force = force_out[...]
    half = entries // 2
    for channel in range(4):
        value = jnp.zeros((blocks, 2 * LANES), F32)
        for part in range(2):
            rows = products[pl.ds(4 * half * part + channel, half, stride=4), :]
            value = value + jnp.dot(
                member[part], jnp.concatenate(split2(rows), axis=1), preferred_element_type=F32
            )
        value = value[:, :LANES] + value[:, LANES:]
        for block in range(blocks):
            received[pl.ds(channel, 1), pl.ds(block * LANES, LANES)] = value[block : block + 1]
        force = force + scalars[pl.ds(16 + channel, 1), :] * value

    force_out[...] = force
    begin(copies[1:4])
    total, damp = damping[0], damping[1]
    smooth_out[...] = beside_old[...]
    smooth_out[pl.ds(0, 1), :] += beside_extra[0]
    smooth_out[pl.ds(blocks - 1, 1), :] += beside_extra[1]
    previous = old[...]
    smooth = previous + damp * (force - (total * previous - smooth_out[...]))
    smooth_out[...] = smooth
    padded[pl.ds(8, blocks), :] = smooth
    residual = force - total * smooth + neighbour_sum(padded, edges, window, blocks)

    inner, whole = prefix(residual)
    before, run = rows_before(whole)
    prefixed[...] = inner + before
    rows, lanes = ends_row[...], ends_lane[...]
    count = rows.shape[0]
    marks = run[:count]
    for block in range(blocks):
        value = gather_lanes(wide(prefixed[pl.ds(block, 1), :], count), lanes)
        marks = jnp.where(rows == block, value, marks)
    own_source = marks - previous_one(marks)

    lane = lax.broadcasted_iota(I32, (1, LANES), 1)
    rim_rows, rim_counts = [], []
    for side in range(2):
        inside = padded[pl.ds(8 if side == 0 else 7 + blocks, 1), :]
        value = jnp.zeros((1, LANES), F32)
        for link in range(3):
            place = lane + arrivals[side, pl.ds(OFFSET + link, 1), :].astype(I32)
            index = lax.bitwise_and(place, LANES - 1)
            reached = (place >= LANES) if side == 0 else (place < 0)
            weight = arrivals[side, pl.ds(EDGE_HI + link, 1), :] + arrivals[side, pl.ds(EDGE_LO + link, 1), :]
            value = value + jnp.where(
                wide(reached.astype(I32)) > 0,
                wide(weight) * gather_lanes(wide(inside), wide(index)),
                0.0,
            )[0:1]
        rim_rows.append(value)
        owners = arrivals[side, pl.ds(OWNER, 1), :].astype(I32)
        below = jnp.where(
            lax.broadcasted_iota(I32, (LANES, LANES), 0) >= owners, 1.0, 0.0
        ).astype(BF16)
        rim_counts.append(dot_nt(jnp.ones((8, LANES), BF16), below))
    rim_inner, rim_whole = prefix(jnp.concatenate([wide(r) for r in rim_rows], axis=0))
    rim_source = []
    for side in range(2):
        place = rim_counts[side].astype(I32)
        index = lax.bitwise_and(place, LANES - 1)
        value = gather_lanes(rim_inner[8 * side : 8 * side + 8], index)
        value = jnp.where(place >= LANES, rim_whole[8 * side : 8 * side + 8], value)
        shifted = pltpu.roll(value, 1, axis=1)
        first = lax.broadcasted_iota(I32, (8, LANES), 1) == 0
        rim_source.append((value - jnp.where(first, 0.0, shifted))[0:1])

    frows = own_source.shape[0]
    source_out[...] = jnp.zeros((FRAME, LANES), F32)
    source_out[pl.ds(OWN, frows), :] = own_source
    source_out[pl.ds(OWN - 1, 1), :] = rim_source[0]
    source_out[pl.ds(OWN + frows, 1), :] = rim_source[1]
    reach = LANES // 8
    frame[...] = jnp.zeros(frame.shape, F32)
    frame[pl.ds(6 * FRAME, FRAME), :] = jnp.ones((FRAME, LANES), F32)
    frame[pl.ds(7 * FRAME, FRAME), :] = jnp.full((FRAME, LANES), 127.0, F32)
    bottoms = 16
    at_cell = lax.broadcasted_iota(I32, (frows, LANES), 0) * LANES + lax.broadcasted_iota(
        I32, (frows, LANES), 1
    )
    for link in range(3):
        frame[pl.ds(link * FRAME + OWN, frows), :] = (ctable[link] - reach - at_cell).astype(F32)
        frame[pl.ds((3 + link) * FRAME + OWN, frows), :] = cedge[link]
    frame[pl.ds(6 * FRAME + OWN, frows), :] = cdiag[...]
    frame[pl.ds(7 * FRAME + OWN, frows), :] = (cowner[...] + bottoms).astype(F32)
    for side in range(2):
        for row in range(2):
            at = (OWN - 2 + row) if side == 0 else (OWN + frows + row)
            for link in range(3):
                put = 3 * row + link
                frame[pl.ds(link * FRAME + at, 1), :] = arrivals[side, pl.ds(COFFSET + put, 1), :]
                frame[pl.ds((3 + link) * FRAME + at, 1), :] = (
                    arrivals[side, pl.ds(CEDGE_HI + put, 1), :] + arrivals[side, pl.ds(CEDGE_LO + put, 1), :]
                )
            frame[pl.ds(6 * FRAME + at, 1), :] = (
                arrivals[side, pl.ds(CDIAG_HI + row, 1), :] + arrivals[side, pl.ds(CDIAG_LO + row, 1), :]
            )
            frame[pl.ds(7 * FRAME + at, 1), :] = arrivals[side, pl.ds(COWNER + row, 1), :] + (
                2.0 * bottoms * side
            )
    for link in range(3):
        frame[pl.ds(6 * FRAME, FRAME), :] += frame[pl.ds((3 + link) * FRAME, FRAME), :]
    source = source_out[...]
    first = (RELAXATION / frame[pl.ds(6 * FRAME, FRAME), :]) * source
    residual = (1.0 - RELAXATION) * source + first_level_sum(first, frame)
    codes = frame[pl.ds(7 * FRAME, FRAME), :].astype(I32)
    pieces = split2(residual)
    left_side, right_side = [], []
    bins = lax.broadcasted_iota(I32, (3 * bottoms, LANES), 0)
    rest = [jnp.zeros((rows, LANES), BF16) for rows in (MIDDLE, LANES - MIDDLE - 3 * bottoms)]
    for row in range(OWN - 2, OWN + frows + 2):
        left_side.append(jnp.concatenate([p[row : row + 1] for p in pieces], axis=0))
        named = jnp.where(bins == codes[row : row + 1], 1.0, 0.0).astype(BF16)
        right_side.append(jnp.concatenate([rest[0], named, rest[1]], axis=0))
    bottom = dot_nt(jnp.concatenate(left_side, axis=1), jnp.concatenate(right_side, axis=1))
    bottom = bottom[0:1] + bottom[1:2]

    reach = LANES // 8
    to_left = jnp.concatenate(
        [
            jnp.where(lane < reach, own_source[1:2], bottom),
            padded[pl.ds(8, 1), :],
            own_source[0:1],
            rim_source[0],
        ],
        axis=0,
    )
    to_right = jnp.concatenate(
        [
            jnp.where(lane >= LANES - reach, own_source[frows - 2 : frows - 1], bottom),
            padded[pl.ds(7 + blocks, 1), :],
            own_source[frows - 1 : frows],
            rim_source[1],
        ],
        axis=0,
    )
    for other in range(message.shape[0]):
        message[other] = to_right
    message[lax.rem(tile + tile_count - 1, tile_count)] = to_left
    copies[4].start()
    for copy in copies:
        copy.wait()


def inverse_windows(left, own, right, extended, weights):
    bottoms, size = own.shape
    halves = size // LANES
    for half in range(halves):
        part = pl.ds(half * LANES, LANES)
        for at, block in ((0, left), (2, right)):
            high, low = INVERSE + 16 * half, INVERSE + 16 * (halves + half)
            extended[pl.ds(at * bottoms, bottoms), part] = (
                block[pl.ds(high, bottoms), :] + block[pl.ds(low, bottoms), :]
            )
        extended[pl.ds(bottoms, bottoms), part] = own[:, part]
    table = extended[...]
    lane = lax.broadcasted_iota(I32, (3 * bottoms, LANES), 1)
    for other in range(weights.shape[0]):
        shift = (size + MIDDLE - (other - 1) * bottoms) % size
        turned = pltpu.roll(table, shift, axis=1) if shift else table
        weights[other] = jnp.where(
            lane >= MIDDLE, jnp.where(lane < MIDDLE + 3 * bottoms, turned[:, :LANES], 0.0), 0.0
        )


def backward_kernel(
    frame_rows, arrived, weights, source, frame, force, smooth, edges, window, damping, owner, rim_owner,
    height, frame_source, padded, third_rows,
):
    tile = lax.axis_index("tile")
    tile_count = lax.axis_size("tile")
    blocks = force.shape[0]
    left = arrived[lax.rem(tile + tile_count - 1, tile_count)]
    right = arrived[lax.rem(tile + 1, tile_count)]
    count = weights.shape[1]
    partial = jnp.zeros((count, LANES), F32)
    for other in range(weights.shape[0]):
        partial = partial + weights[other] * wide(arrived[other, pl.ds(0, 1), :], count)
    partial = jnp.concatenate([partial, jnp.zeros((LANES - count, LANES), F32)], axis=0)
    ones = jnp.ones((8, LANES), BF16)
    bottom = dot_nt(jnp.concatenate([ones, ones], axis=1), jnp.concatenate(split2(partial), axis=1))

    frows = frame_rows
    frame_source[...] = source[...]
    lane = lax.broadcasted_iota(I32, (1, LANES), 1)
    reach = LANES // 8
    frame_source[pl.ds(OWN - 2, 1), :] += jnp.where(lane >= LANES - reach, left[0:1], 0.0)
    frame_source[pl.ds(OWN - 1, 1), :] += left[2:3]
    frame_source[pl.ds(OWN, 1), :] += left[3:4]
    frame_source[pl.ds(OWN + frows - 1, 1), :] += right[3:4]
    frame_source[pl.ds(OWN + frows, 1), :] += right[2:3]
    frame_source[pl.ds(OWN + frows + 1, 1), :] += jnp.where(lane < reach, right[0:1], 0.0)
    total_source = frame_source[...]
    total = frame[pl.ds(6 * FRAME, FRAME), :]
    codes = frame[pl.ds(7 * FRAME, FRAME), :].astype(I32)
    damp = RELAXATION / total
    second = damp * total_source + gather_lanes(wide(bottom[0:1], FRAME), codes)
    third = second + damp * (total_source - total * second + first_level_sum(second, frame))
    third_rows[...] = third

    owners = owner[...]
    index = lax.bitwise_and(owners, LANES - 1)
    which = lax.shift_right_logical(owners, 7)
    corrected = jnp.zeros((blocks, LANES), F32)
    for row in range(frows):
        corrected = jnp.where(
            which == row, gather_lanes(wide(third_rows[pl.ds(OWN + row, 1), :], blocks), index), corrected
        )
    corrected = smooth[...] + corrected
    padded[pl.ds(8, blocks), :] = corrected
    left_rim = left[1:2] + gather_lanes(wide(third_rows[pl.ds(OWN - 1, 1), :]), rim_owner[0])[0:1]
    right_rim = right[1:2] + gather_lanes(wide(third_rows[pl.ds(OWN + frows, 1), :]), rim_owner[1])[0:1]
    padded[pl.ds(7, 1), :] = left_rim
    padded[pl.ds(8 + blocks, 1), :] = right_rim
    beside = neighbour_sum(padded, edges, window, blocks)
    height[...] = corrected + damping[1] * (force[...] - (damping[0] * corrected - beside))


def in_hbm(array):
    return pltpu.with_memory_space_constraint(array, pltpu.HBM)


def struct(shape, dtype=F32):
    return jax.ShapeDtypeStruct(shape, dtype)


VMEM = pl.BlockSpec(memory_space=pltpu.VMEM)
SMEM = pl.BlockSpec(memory_space=pltpu.SMEM)
ANY = pl.BlockSpec(memory_space=pltpu.HBM)
PARAMS = pltpu.CompilerParams(vmem_limit_bytes=16 * 1024 * 1024)


def per_device(
    fields, level_rate, edge_weight, fine_diagonal, fine_table, old_height, level_weight,
    flux_weight, fine_owner, coarse_table, coarse_edge, coarse_diagonal, coarse_owner,
    coarse_inverse, surface_out, send_blocks, entry_slot, entry_block, remap_tiles,
):
    tile_count = lax.axis_size("tile")
    cells = fields.shape[2]
    blocks = cells // LANES
    firsts = coarse_diagonal.shape[1]
    frows = firsts // LANES
    entries = entry_slot.shape[2]
    channels = surface_out.shape[1]
    slots = send_blocks.shape[2]
    each = slots // 5
    halves = coarse_inverse.shape[2] // LANES
    bottoms = coarse_inverse.shape[1]
    base = pick_base(halves)
    swap = [(0, 1), (1, 0)]
    surface = lax.ppermute(surface_out[0], "comp", swap)
    sends = lax.ppermute(send_blocks[0], "comp", swap)
    raw = (
        fields[0],
        old_height.reshape(blocks, LANES),
        edge_weight[0].reshape(3, blocks, LANES),
        fine_table[0].reshape(3, blocks, LANES),
        fine_owner.reshape(blocks, LANES),
        coarse_table[0].reshape(3, frows, LANES),
        coarse_edge[0].reshape(3, frows, LANES),
        coarse_diagonal.reshape(frows, LANES),
        coarse_owner.reshape(frows, LANES),
        coarse_inverse[0],
    )
    current, old, edges, table, owner, ctable, cedge, cdiag, cowner, cinverse = pl.pallas_call(
        load_kernel,
        out_shape=[struct(x.shape, x.dtype) for x in raw],
        in_specs=[ANY] * len(raw),
        out_specs=[VMEM] * len(raw),
        scratch_shapes=[pltpu.SemaphoreType.DMA((len(raw),))],
        compiler_params=PARAMS,
        name="load",
    )(*[in_hbm(x) for x in raw])

    pick = struct((4 * each, LANES), BF16)
    both = struct((base + 4 * each, LANES), BF16)
    plan = exchange_plan(tile_count)
    *messages, here = pl.pallas_call(
        functools.partial(pack_kernel, plan),
        out_shape=[both, both, both, both, pick],
        in_specs=[VMEM] * 12,
        out_specs=[VMEM] * 5,
        scratch_shapes=[
            pltpu.VMEM((channels * blocks, LANES), F32),
            pltpu.VMEM((base, LANES), F32),
            pltpu.VMEM((base, LANES), F32),
            pltpu.VMEM((4, base + 4 * each, LANES), BF16),
        ],
        compiler_params=PARAMS,
        name="pack",
    )(
        surface, sends, current, old, edges, table, owner, ctable, cedge, cdiag, cowner, cinverse,
    )

    messages = [
        lax.ppermute(message, "tile", [(i, (i + op[i]) % tile_count) for i in range(tile_count)])
        for message, op in zip(messages, plan)
    ]

    late = (
        level_rate, level_weight, flux_weight, fine_diagonal.reshape(blocks, LANES), entry_slot[0], entry_block[0]
    )
    fresh, force_part, beside_old, window, ends_row, ends_lane, hot, member, damping, scalars, tiles = pl.pallas_call(
        stencil_kernel,
        out_shape=[
            struct((fields.shape[1], cells)),
            struct((blocks, LANES)),
            struct((blocks, LANES)),
            struct((3, blocks, LANES), I32),
            struct((frows, LANES), I32),
            struct((frows, LANES), I32),
            struct((entries, slots), BF16),
            struct((2, blocks, entries // 2), BF16),
            struct((2, blocks, LANES)),
            struct((24, LANES)),
            pltpu.VMEM(remap_tiles.shape[2:], BF16),
        ],
        in_specs=[VMEM] * 6 + [ANY] * 7,
        out_specs=[VMEM] * 11,
        scratch_shapes=[pltpu.VMEM((blocks + 16, LANES), F32)]
        + [pltpu.VMEM(x.shape, x.dtype) for x in late]
        + [pltpu.SemaphoreType.DMA((len(late),)), pltpu.SemaphoreType.DMA((math.gcd(entries, 8),))],
        compiler_params=PARAMS,
        name="stencil",
    )(here, current, edges, table, old, owner, *[in_hbm(x) for x in (remap_tiles[0, 0],) + late])

    force, smooth, source, frame, weights, rim_owner, advanced, received, message = pl.pallas_call(
        functools.partial(forward_kernel, plan),
        out_shape=[
            struct((blocks, LANES)),
            struct((blocks, LANES)),
            struct((FRAME, LANES)),
            struct((8 * FRAME, LANES)),
            struct((tile_count, 3 * bottoms, LANES)),
            struct((2, 8, LANES), I32),
            struct((fields.shape[1], cells)),
            struct((channels, cells)),
            struct((tile_count, 4, LANES)),
        ],
        in_specs=[VMEM] * 24,
        out_specs=[VMEM] * 6 + [ANY] * 3,
        scratch_shapes=[
            pltpu.VMEM((4 * entries, LANES), F32),
            pltpu.VMEM((4 * entries, LANES), F32),
            pltpu.VMEM((blocks + 16, LANES), F32),
            pltpu.VMEM((blocks, LANES), F32),
            pltpu.VMEM((2, base, LANES), F32),
            pltpu.VMEM((3 * bottoms, bottoms * tile_count), F32),
            pltpu.VMEM((2, fields.shape[1], LANES), F32),
            pltpu.VMEM((channels, cells), F32),
            pltpu.VMEM((tile_count, 4, LANES), F32),
            pltpu.SemaphoreType.DMA((5,)),
        ],
        compiler_params=PARAMS,
        name="forward",
    )(
        tiles, scalars, *messages, here, hot, member, current, edges, window, old,
        damping, force_part, beside_old, ends_row, ends_lane, fresh, ctable, cedge, cdiag, cowner, cinverse,
    )
    arrived = lax.all_to_all(message, "tile", split_axis=0, concat_axis=0, tiled=True)
    height = pl.pallas_call(
        functools.partial(backward_kernel, frows),
        out_shape=struct((blocks, LANES)),
        in_specs=[VMEM] * 11,
        out_specs=VMEM,
        scratch_shapes=[
            pltpu.VMEM((FRAME, LANES), F32),
            pltpu.VMEM((blocks + 16, LANES), F32),
            pltpu.VMEM((FRAME, LANES), F32),
        ],
        compiler_params=PARAMS,
        name="backward",
    )(arrived, weights, source, frame, force, smooth, edges, window, damping, owner, rim_owner)
    return advanced[None], received[None], height.reshape(1, cells)


def solution(mesh):
    in_specs = (
        P("comp", None, "tile"),
        P("comp", None),
        P("comp", None, "tile"),
        P("comp", "tile"),
        P("comp", None, "tile"),
        P("comp", "tile"),
        P("comp", None),
        P("comp", None),
        P("comp", "tile"),
        P("comp", None, "tile"),
        P("comp", None, "tile"),
        P("comp", "tile"),
        P("comp", "tile"),
        P("comp", "tile", None),
        P("comp", None, "tile"),
        P("comp", "tile", None),
        P("comp", "tile", None),
        P("comp", "tile", None),
        P("comp", "tile", None, None, None),
    )
    out_specs = (P("comp", None, "tile"), P("comp", None, "tile"), P("comp", "tile"))
    return jax.shard_map(
        per_device, mesh=mesh, in_specs=in_specs, out_specs=out_specs, check_vma=False
    )
```

```python
import functools
import math

import jax
import jax.numpy as jnp
from jax import lax
from jax.experimental import pallas as pl
from jax.experimental.pallas import tpu as pltpu
from jax.sharding import PartitionSpec as P

LANES = 128
RELAXATION = 0.8
F32 = jnp.float32
BF16 = jnp.bfloat16
I32 = jnp.int32

FIELD_HI, FIELD_LO = 0, 8
EDGE_HI, EDGE_LO, OLD_HI, OLD_LO = 16, 19, 22, 23
OFFSET, OWNER = 24, 27
CEDGE_HI, CEDGE_LO, CDIAG_HI, CDIAG_LO = 32, 38, 44, 46
COFFSET, COWNER = 48, 54
INVERSE = 56

FRAME, OWN = 32, 8

MIDDLE = 32


PLANS = {
    16: (
        (1, 1, 1, 1, 1, 2, 2, -1, 2, 2, -1, 2, 2, 2, -2, 1),
        (-1, 2, 2, -2, -2, 1, -1, 2, -1, 1, -2, 1, 1, -2, 2, -1),
        (-2, -2, -2, -1, -1, -1, 1, -2, -2, -1, 1, -2, -2, -1, -1, 2),
        (2, -1, -1, 2, 2, -2, -2, 1, 1, -2, 2, -1, -1, 1, 1, -2),
    ),
}
DISTANCES = (-1, 1, -2, 2)


def exchange_plan(count):
    if count in PLANS:
        return PLANS[count]
    near = [1 if i % 2 == 0 else -1 for i in range(count)]
    return ([2] * count, [-d for d in near], [-2] * count, near)


def lookup(tile, values):
    result = jnp.int32(values[0])
    for i, value in enumerate(values):
        result = jnp.where(tile == i, jnp.int32(value), result)
    return result


def arrived_by(tile, plan, distance):
    count = len(plan[0])
    found = []
    for i in range(count):
        sender = (i - distance) % count
        found.append([op[sender] for op in plan].index(distance))
    return lookup(tile, found)


def chosen_rows(which, refs, rows):
    value = refs[0][rows, :]
    for i, ref in enumerate(refs[1:]):
        value = jnp.where(which == i + 1, ref[rows, :], value)
    return value


def gather_lanes(table, index):
    return jnp.take_along_axis(table, index, axis=1)


def wide(row, count=8):
    return jnp.broadcast_to(row, (count, row.shape[1]))


def split2(x):
    high = x.astype(BF16)
    return high, (x - high.astype(F32)).astype(BF16)


def dot_nt(a, b):
    return lax.dot_general(a, b, (((1,), (1,)), ((), ())), preferred_element_type=F32)


def dot_tn(a, b):
    return lax.dot_general(a, b, (((0,), (0,)), ((), ())), preferred_element_type=F32)


def pick_base(inverse_blocks):
    return -(-(INVERSE + 32 * inverse_blocks) // 16) * 16


def load_kernel(*refs):
    count = len(refs) // 2
    copies = [
        pltpu.make_async_copy(source, target, refs[-1].at[i])
        for i, (source, target) in enumerate(zip(refs[:count], refs[count : 2 * count]))
    ]
    for copy in copies:
        copy.start()
    for copy in copies:
        copy.wait()


def pack_kernel(
    plan, surface, sends, fields, old, edge, table, owner, ctable, cedge, cdiag, cowner, cinverse,
    out0, out1, out2, out3, here, chunks, left_rows, right_rows, packed,
):
    tile = lax.axis_index("tile")
    cells = fields.shape[1]
    blocks = cells // LANES
    frows = ctable.shape[1]
    firsts = frows * LANES
    base = pick_base(cinverse.shape[1] // LANES)
    lane = lax.broadcasted_iota(I32, (1, LANES), 1)

    for rows, at_left in ((right_rows, False), (left_rows, True)):
        start = 0 if at_left else cells - LANES
        part = pl.ds(start, LANES)

        def both(high, low_row, value):
            count = value.shape[0]
            rows[pl.ds(high, count), :] = value
            rows[pl.ds(low_row, count), :] = value - value.astype(BF16).astype(F32)

        def three(ref, row):
            return jnp.concatenate([ref[link, pl.ds(row, 1), :] for link in range(3)], axis=0)

        rows[pl.ds(24, 8), :] = jnp.zeros((8, LANES), F32)
        both(FIELD_HI, FIELD_LO, fields[:, part])
        block = 0 if at_left else blocks - 1
        both(EDGE_HI, EDGE_LO, three(edge, block))
        both(OLD_HI, OLD_LO, old[pl.ds(block, 1), :])
        rows[pl.ds(OFFSET, 3), :] = (three(table, block) - (LANES + start) - lane).astype(F32)
        shift = 0 if at_left else firsts - LANES
        rows[pl.ds(OWNER, 1), :] = (owner[pl.ds(block, 1), :] - shift).astype(F32)
        first = 0 if at_left else frows - 2
        reach = LANES // 8
        for step in range(2):
            both(CEDGE_HI + 3 * step, CEDGE_LO + 3 * step, three(cedge, first + step))
            rows[pl.ds(COFFSET + 3 * step, 3), :] = (
                three(ctable, first + step) - (reach + (first + step) * LANES) - lane
            ).astype(F32)
            both(CDIAG_HI + step, CDIAG_LO + step, cdiag[pl.ds(first + step, 1), :])
            rows[pl.ds(COWNER + step, 1), :] = cowner[pl.ds(first + step, 1), :].astype(F32)
        halves = cinverse.shape[1] // LANES
        for half in range(halves):
            both(
                INVERSE + 16 * half,
                INVERSE + 16 * (halves + half),
                cinverse[:, pl.ds(half * LANES, LANES)],
            )
        end = INVERSE + 32 * halves
        if base > end:
            rows[pl.ds(end, base - end), :] = jnp.zeros((base - end, LANES), F32)

    for block in range(blocks):
        chunks[pl.ds(4 * block, 4), :] = surface[:, pl.ds(block * LANES, LANES)].astype(F32)
    slots = sends.shape[1]
    hot = jnp.where(
        lax.broadcasted_iota(I32, (blocks, slots), 0) == sends[...], 1.0, 0.0
    ).astype(BF16)
    picks = []
    for channel in range(4):
        source = chunks[pl.ds(channel, blocks, stride=4), :].astype(BF16)
        picks.append(dot_tn(hot, source).astype(BF16))
    count = slots // 5

    chosen = [
        jnp.concatenate([p[j * count : (j + 1) * count] for p in picks], axis=0) for j in range(5)
    ]
    here[...] = chosen[2]
    rims = {-1: left_rows[...].astype(BF16), 1: right_rows[...].astype(BF16)}
    for at, distance in enumerate(DISTANCES):
        packed[at, pl.ds(0, base), :] = rims.get(distance, jnp.zeros((base, LANES), BF16))
        packed[at, pl.ds(base, 4 * count), :] = chosen[2 - distance]
    for out, op in zip((out0, out1, out2, out3), plan):
        out[...] = packed[lookup(tile, [DISTANCES.index(distance) for distance in op])]


def stencil_kernel(
    here, fields, edge, table, old, owner, tiles, rate, level_weight, flux_weight, diagonal_in, slots_in, block_in,
    fresh, force, beside_old, window, ends_row, ends_lane, hot, member, damping, scalars, tile_buffer,
    padded, rate_row, level_row, flux_row, diagonal, slots, entry_block, small_sems, sems,
):
    del here
    small = [
        pltpu.make_async_copy(source, target, small_sems.at[i])
        for i, (source, target) in enumerate(
            (
                (rate, rate_row), (level_weight, level_row), (flux_weight, flux_row),
                (diagonal_in, diagonal), (slots_in, slots), (block_in, entry_block),
            )
        )
    ]
    parts = sems.shape[0]
    step = tiles.shape[0] // parts

    def load(part):
        span = pl.ds(part * step, step)
        return pltpu.make_async_copy(tiles.at[span], tile_buffer.at[span], sems.at[part])

    def begin(part, carry):
        if part is None:
            for copy in small:
                copy.start()
        else:
            load(part).start()
        return carry

    once = 1 + lax.axis_index("tile") // lax.axis_size("tile")
    lax.fori_loop(0, once, lambda _, carry: begin(None, carry), 0)
    lax.fori_loop(0, parts, begin, 0)
    blocks = old.shape[0]
    levels = fields.shape[0]
    firsts = ends_row.shape[0] * LANES
    ident = lax.broadcasted_iota(I32, ends_row.shape, 0) * LANES + lax.broadcasted_iota(
        I32, ends_row.shape, 1
    )
    count = ends_row.shape[0]
    rows = jnp.zeros(ends_row.shape, I32)
    for block in range(blocks):
        last = jnp.broadcast_to(owner[pl.ds(block, 1), LANES - 1 : LANES], ends_row.shape)
        rows = rows + jnp.where(last <= ident, 1, 0)
    lanes = jnp.zeros(ends_row.shape, I32)
    for bit in (64, 32, 16, 8, 4, 2, 1):
        probe = lanes + (bit - 1)
        value = jnp.full(ends_row.shape, firsts, I32)
        for block in range(blocks):
            value = jnp.where(
                rows == block, gather_lanes(wide(owner[pl.ds(block, 1), :], count), probe), value
            )
        lanes = jnp.where(value <= ident, lanes + bit, lanes)
    ends_row[...] = rows
    ends_lane[...] = lanes
    for copy in small:
        copy.wait()
    for i, value in enumerate((rate_row, level_row, flux_row)):
        width = value.shape[1]
        same = lax.broadcasted_iota(I32, (8, width), 0) == lax.broadcasted_iota(I32, (8, width), 1)
        column = jnp.sum(jnp.where(same, wide(value[...]), 0.0), axis=1, keepdims=True)
        scalars[pl.ds(8 * i, 8), :] = jnp.broadcast_to(column, (8, LANES))
    speed = scalars[pl.ds(0, 8), :]
    share = scalars[pl.ds(8, 8), :]
    starts = lax.broadcasted_iota(I32, (blocks, LANES), 0) * LANES
    total = edge[0] + edge[1] + edge[2]
    inverse = 1.0 / total
    fine_total = diagonal[...] + total
    damping[0] = fine_total
    damping[1] = RELAXATION / fine_total
    for link in range(3):
        window[link] = table[link] - starts
    blank = jnp.zeros((levels, LANES), F32)

    def chunk(block):
        if 0 <= block < blocks:
            return fields[:, pl.ds(block * LANES, LANES)]
        return blank

    before, here, after = blank, chunk(0), chunk(1)
    for block in range(blocks):
        row = slice(block, block + 1)
        beside = jnp.zeros((levels, LANES), F32)
        for link in range(3):
            place = wide(window[link, pl.ds(block, 1), :])
            index = lax.bitwise_and(place, LANES - 1)
            value = jnp.where(
                place < LANES,
                gather_lanes(before, index),
                jnp.where(place < 2 * LANES, gather_lanes(here, index), gather_lanes(after, index)),
            )
            beside = beside + wide(edge[link, pl.ds(block, 1), :]) * value
        result = here + speed * ((beside - wide(total[row]) * here) * wide(inverse[row]))
        fresh[:, pl.ds(block * LANES, LANES)] = result
        force[pl.ds(block, 1), :] = jnp.sum(result * share, axis=0, keepdims=True)
        before, here, after = here, after, chunk(block + 2)

    padded[pl.ds(0, 8), :] = jnp.zeros((8, LANES), F32)
    padded[pl.ds(8 + blocks, 8), :] = jnp.zeros((8, LANES), F32)
    padded[pl.ds(8, blocks), :] = old[...]
    beside_old[...] = neighbour_sum(padded, edge, window, blocks)
    names = jnp.where(
        lax.broadcasted_iota(I32, (slots.shape[1], slots.shape[1]), 0) == slots[...], 1.0, 0.0
    )
    hot[...] = jnp.transpose(names).astype(BF16)
    half = entry_block.shape[1] // 2
    for part in range(2):
        member[part] = jnp.where(
            lax.broadcasted_iota(I32, (blocks, half), 0) == entry_block[:, part * half : (part + 1) * half],
            1.0,
            0.0,
        ).astype(BF16)

    for part in range(parts):
        load(part).wait()


def neighbour_sum(padded, edges, window, blocks):
    before = padded[pl.ds(7, blocks), :]
    here = padded[pl.ds(8, blocks), :]
    after = padded[pl.ds(9, blocks), :]
    result = jnp.zeros((blocks, LANES), F32)
    for link in range(3):
        place = window[link]
        index = lax.bitwise_and(place, LANES - 1)
        value = jnp.where(
            place < LANES,
            gather_lanes(before, index),
            jnp.where(place < 2 * LANES, gather_lanes(here, index), gather_lanes(after, index)),
        )
        result = result + edges[link] * value
    return result


def first_level_sum(values, frame):
    before = pltpu.roll(values, 1, axis=0)
    after = pltpu.roll(values, FRAME - 1, axis=0)
    lane = lax.broadcasted_iota(I32, (FRAME, LANES), 1)
    result = jnp.zeros((FRAME, LANES), F32)
    for link in range(3):
        place = lane + frame[pl.ds(link * FRAME, FRAME), :].astype(I32)
        index = lax.bitwise_and(place, LANES - 1)
        value = jnp.where(
            place < 0,
            gather_lanes(before, index),
            jnp.where(place >= LANES, gather_lanes(after, index), gather_lanes(values, index)),
        )
        result = result + frame[pl.ds((3 + link) * FRAME, FRAME), :] * value
    return result


def previous_one(values):
    rolled = pltpu.roll(values, 1, axis=1)
    above = pltpu.roll(rolled, 1, axis=0)
    lane = lax.broadcasted_iota(I32, values.shape, 1)
    row = lax.broadcasted_iota(I32, values.shape, 0)
    return jnp.where(lane > 0, rolled, jnp.where(row > 0, above, 0.0))


def triangle():
    return jnp.where(
        lax.broadcasted_iota(I32, (LANES, LANES), 0) < lax.broadcasted_iota(I32, (LANES, LANES), 1),
        1.0,
        0.0,
    ).astype(BF16)


def prefix(values):
    ones = jnp.ones((LANES, LANES), BF16)
    right = jnp.concatenate([triangle(), ones], axis=1)
    count = values.shape[0]
    out = jnp.dot(
        jnp.concatenate(split2(values), axis=0), right, preferred_element_type=F32
    )
    out = out[:count] + out[count:]
    return out[:, :LANES], out[:, LANES:]


def rows_before(values):
    sublane = lax.broadcasted_iota(I32, (8, LANES), 0)
    run = jnp.zeros((8, LANES), F32)
    result = []
    for at in range(0, values.shape[0], 8):
        piece = values[at : at + 8]
        total = piece
        for distance in (1, 2, 4):
            total = total + jnp.where(sublane >= distance, pltpu.roll(total, distance, axis=0), 0.0)
        result.append(run + (total - piece))
        run = run + wide(total[7:8])
    return jnp.concatenate(result, axis=0), run


def forward_kernel(
    plan, tiles, scalars, message0, message1, message2, message3, here, hot, member, fields, edges, window, old,
    damping, force_part, beside_old, ends_row, ends_lane, fresh, ctable, cedge, cdiag, cowner, cinverse,
    force_out, smooth_out, source_out, frame, weights_out, rim_owner, fresh_out, received_out, message_out,
    picked, products, padded, prefixed, arrivals, extended, ends, received, message, sems,
):
    cells = fresh.shape[1]
    middle = pl.ds(LANES, cells - 2 * LANES)
    copies = [pltpu.make_async_copy(fresh.at[:, middle], fresh_out.at[:, middle], sems.at[0])]
    for side in range(2):
        copies.append(
            pltpu.make_async_copy(
                ends.at[side], fresh_out.at[:, pl.ds(side * (cells - LANES), LANES)], sems.at[1 + side]
            )
        )
    copies.append(pltpu.make_async_copy(received, received_out, sems.at[3]))
    copies.append(pltpu.make_async_copy(message, message_out, sems.at[4]))

    def begin(which):
        def body(_, carry):
            for copy in which:
                copy.start()
            return carry

        lax.fori_loop(0, 1 + lax.axis_index("tile") // lax.axis_size("tile"), body, 0)

    begin(copies[:1])
    tile = lax.axis_index("tile")
    tile_count = lax.axis_size("tile")
    entries = tiles.shape[0]
    blocks = old.shape[0]

    messages = (message0, message1, message2, message3)
    base = message0.shape[0] - here.shape[0]
    each = here.shape[0] // 4
    found = {distance: arrived_by(tile, plan, distance) for distance in DISTANCES}
    sources = [
        chosen_rows(found[distance], messages, pl.ds(base, 4 * each)) if distance else here[...]
        for distance in (2, 1, 0, -1, -2)
    ]
    for channel in range(4):
        source = jnp.concatenate(
            [rows[channel * each : (channel + 1) * each] for rows in sources], axis=0
        )
        picked[pl.ds(channel, entries, stride=4), :] = jnp.dot(hot[...], source, preferred_element_type=F32)

    for side, distance in enumerate((1, -1)):
        arrivals[side] = chosen_rows(found[distance], messages, pl.ds(0, base)).astype(F32)
        rim_owner[side] = wide(arrivals[side, pl.ds(OWNER, 1), :]).astype(I32)

    upper = lax.rem(lax.broadcasted_iota(I32, (16, LANES), 0), 8) < 4
    for group in range(entries // 4):
        rows = picked[pl.ds(16 * group, 16), :]
        rows = jnp.concatenate([jnp.where(upper, rows, 0.0), jnp.where(upper, 0.0, rows)], axis=1)
        at = 4 * group
        weights = jnp.concatenate(
            [
                jnp.concatenate([tiles[at], tiles[at + 1]], axis=1),
                jnp.concatenate([tiles[at + 2], tiles[at + 3]], axis=1),
            ],
            axis=0,
        )
        product = dot_nt(rows.astype(BF16), weights)
        products[pl.ds(16 * group, 8), :] = product[0:8, :LANES]
        products[pl.ds(16 * group + 8, 8), :] = product[8:16, LANES:]
    speed = scalars[pl.ds(0, 8), :]
    share = scalars[pl.ds(8, 8), :]
    force_out[...] = force_part[...]
    padded[pl.ds(0, 8), :] = jnp.zeros((8, LANES), F32)
    padded[pl.ds(8 + blocks, 8), :] = jnp.zeros((8, LANES), F32)
    beside_extra = []
    for side, block, target in ((0, 0, 0), (1, blocks - 1, 2)):
        halo = arrivals[side, pl.ds(FIELD_HI, 8), :] + arrivals[side, pl.ds(FIELD_LO, 8), :]
        halo_old = arrivals[side, pl.ds(OLD_HI, 1), :] + arrivals[side, pl.ds(OLD_LO, 1), :]
        total = edges[0, pl.ds(block, 1), :] + edges[1, pl.ds(block, 1), :] + edges[2, pl.ds(block, 1), :]
        extra = jnp.zeros((8, LANES), F32)
        extra_old = jnp.zeros((8, LANES), F32)
        for link in range(3):
            place = wide(window[link, pl.ds(block, 1), :])
            index = lax.bitwise_and(place, LANES - 1)
            weight = jnp.where(
                lax.shift_right_logical(place, 7) == target, wide(edges[link, pl.ds(block, 1), :]), 0.0
            )
            extra = extra + weight * gather_lanes(halo, index)
            extra_old = extra_old + weight * gather_lanes(wide(halo_old), index)
        change = speed * extra / wide(total)
        ends[side] = fresh[:, pl.ds(block * LANES, LANES)] + change
        force_out[pl.ds(block, 1), :] += jnp.sum(change * share, axis=0, keepdims=True)
        beside_extra.append(extra_old[0:1])

    inverse_windows(arrivals.at[0], cinverse, arrivals.at[1], extended, weights_out)

    force = force_out[...]
    half = entries // 2
    for channel in range(4):
        value = jnp.zeros((blocks, 2 * LANES), F32)
        for part in range(2):
            rows = products[pl.ds(4 * half * part + channel, half, stride=4), :]
            value = value + jnp.dot(
                member[part], jnp.concatenate(split2(rows), axis=1), preferred_element_type=F32
            )
        value = value[:, :LANES] + value[:, LANES:]
        for block in range(blocks):
            received[pl.ds(channel, 1), pl.ds(block * LANES, LANES)] = value[block : block + 1]
        force = force + scalars[pl.ds(16 + channel, 1), :] * value

    force_out[...] = force
    begin(copies[1:4])
    total, damp = damping[0], damping[1]
    smooth_out[...] = beside_old[...]
    smooth_out[pl.ds(0, 1), :] += beside_extra[0]
    smooth_out[pl.ds(blocks - 1, 1), :] += beside_extra[1]
    previous = old[...]
    smooth = previous + damp * (force - (total * previous - smooth_out[...]))
    smooth_out[...] = smooth
    padded[pl.ds(8, blocks), :] = smooth
    residual = force - total * smooth + neighbour_sum(padded, edges, window, blocks)

    inner, whole = prefix(residual)
    before, run = rows_before(whole)
    prefixed[...] = inner + before
    rows, lanes = ends_row[...], ends_lane[...]
    count = rows.shape[0]
    marks = run[:count]
    for block in range(blocks):
        value = gather_lanes(wide(prefixed[pl.ds(block, 1), :], count), lanes)
        marks = jnp.where(rows == block, value, marks)
    own_source = marks - previous_one(marks)

    lane = lax.broadcasted_iota(I32, (1, LANES), 1)
    rim_rows, rim_counts = [], []
    for side in range(2):
        inside = padded[pl.ds(8 if side == 0 else 7 + blocks, 1), :]
        value = jnp.zeros((1, LANES), F32)
        for link in range(3):
            place = lane + arrivals[side, pl.ds(OFFSET + link, 1), :].astype(I32)
            index = lax.bitwise_and(place, LANES - 1)
            reached = (place >= LANES) if side == 0 else (place < 0)
            weight = arrivals[side, pl.ds(EDGE_HI + link, 1), :] + arrivals[side, pl.ds(EDGE_LO + link, 1), :]
            value = value + jnp.where(
                wide(reached.astype(I32)) > 0,
                wide(weight) * gather_lanes(wide(inside), wide(index)),
                0.0,
            )[0:1]
        rim_rows.append(value)
        owners = arrivals[side, pl.ds(OWNER, 1), :].astype(I32)
        below = jnp.where(
            lax.broadcasted_iota(I32, (LANES, LANES), 0) >= owners, 1.0, 0.0
        ).astype(BF16)
        rim_counts.append(dot_nt(jnp.ones((8, LANES), BF16), below))
    rim_inner, rim_whole = prefix(jnp.concatenate([wide(r) for r in rim_rows], axis=0))
    rim_source = []
    for side in range(2):
        place = rim_counts[side].astype(I32)
        index = lax.bitwise_and(place, LANES - 1)
        value = gather_lanes(rim_inner[8 * side : 8 * side + 8], index)
        value = jnp.where(place >= LANES, rim_whole[8 * side : 8 * side + 8], value)
        shifted = pltpu.roll(value, 1, axis=1)
        first = lax.broadcasted_iota(I32, (8, LANES), 1) == 0
        rim_source.append((value - jnp.where(first, 0.0, shifted))[0:1])

    frows = own_source.shape[0]
    source_out[...] = jnp.zeros((FRAME, LANES), F32)
    source_out[pl.ds(OWN, frows), :] = own_source
    source_out[pl.ds(OWN - 1, 1), :] = rim_source[0]
    source_out[pl.ds(OWN + frows, 1), :] = rim_source[1]
    reach = LANES // 8
    frame[...] = jnp.zeros(frame.shape, F32)
    frame[pl.ds(6 * FRAME, FRAME), :] = jnp.ones((FRAME, LANES), F32)
    frame[pl.ds(7 * FRAME, FRAME), :] = jnp.full((FRAME, LANES), 127.0, F32)
    bottoms = 16
    at_cell = lax.broadcasted_iota(I32, (frows, LANES), 0) * LANES + lax.broadcasted_iota(
        I32, (frows, LANES), 1
    )
    for link in range(3):
        frame[pl.ds(link * FRAME + OWN, frows), :] = (ctable[link] - reach - at_cell).astype(F32)
        frame[pl.ds((3 + link) * FRAME + OWN, frows), :] = cedge[link]
    frame[pl.ds(6 * FRAME + OWN, frows), :] = cdiag[...]
    frame[pl.ds(7 * FRAME + OWN, frows), :] = (cowner[...] + bottoms).astype(F32)
    for side in range(2):
        for row in range(2):
            at = (OWN - 2 + row) if side == 0 else (OWN + frows + row)
            for link in range(3):
                put = 3 * row + link
                frame[pl.ds(link * FRAME + at, 1), :] = arrivals[side, pl.ds(COFFSET + put, 1), :]
                frame[pl.ds((3 + link) * FRAME + at, 1), :] = (
                    arrivals[side, pl.ds(CEDGE_HI + put, 1), :] + arrivals[side, pl.ds(CEDGE_LO + put, 1), :]
                )
            frame[pl.ds(6 * FRAME + at, 1), :] = (
                arrivals[side, pl.ds(CDIAG_HI + row, 1), :] + arrivals[side, pl.ds(CDIAG_LO + row, 1), :]
            )
            frame[pl.ds(7 * FRAME + at, 1), :] = arrivals[side, pl.ds(COWNER + row, 1), :] + (
                2.0 * bottoms * side
            )
    for link in range(3):
        frame[pl.ds(6 * FRAME, FRAME), :] += frame[pl.ds((3 + link) * FRAME, FRAME), :]
    source = source_out[...]
    first = (RELAXATION / frame[pl.ds(6 * FRAME, FRAME), :]) * source
    residual = (1.0 - RELAXATION) * source + first_level_sum(first, frame)
    codes = frame[pl.ds(7 * FRAME, FRAME), :].astype(I32)
    pieces = split2(residual)
    left_side, right_side = [], []
    bins = lax.broadcasted_iota(I32, (3 * bottoms, LANES), 0)
    rest = [jnp.zeros((rows, LANES), BF16) for rows in (MIDDLE, LANES - MIDDLE - 3 * bottoms)]
    for row in range(OWN - 2, OWN + frows + 2):
        left_side.append(jnp.concatenate([p[row : row + 1] for p in pieces], axis=0))
        named = jnp.where(bins == codes[row : row + 1], 1.0, 0.0).astype(BF16)
        right_side.append(jnp.concatenate([rest[0], named, rest[1]], axis=0))
    bottom = dot_nt(jnp.concatenate(left_side, axis=1), jnp.concatenate(right_side, axis=1))
    bottom = bottom[0:1] + bottom[1:2]

    reach = LANES // 8
    to_left = jnp.concatenate(
        [
            jnp.where(lane < reach, own_source[1:2], bottom),
            padded[pl.ds(8, 1), :],
            own_source[0:1],
            rim_source[0],
        ],
        axis=0,
    )
    to_right = jnp.concatenate(
        [
            jnp.where(lane >= LANES - reach, own_source[frows - 2 : frows - 1], bottom),
            padded[pl.ds(7 + blocks, 1), :],
            own_source[frows - 1 : frows],
            rim_source[1],
        ],
        axis=0,
    )
    for other in range(message.shape[0]):
        message[other] = to_right
    for group in range(2):
        message[group * tile_count + lax.rem(tile + tile_count - 1, tile_count)] = to_left
    copies[4].start()
    for copy in copies:
        copy.wait()


def inverse_windows(left, own, right, extended, weights):
    bottoms, size = own.shape
    halves = size // LANES
    for half in range(halves):
        part = pl.ds(half * LANES, LANES)
        for at, block in ((0, left), (2, right)):
            high, low = INVERSE + 16 * half, INVERSE + 16 * (halves + half)
            extended[pl.ds(at * bottoms, bottoms), part] = (
                block[pl.ds(high, bottoms), :] + block[pl.ds(low, bottoms), :]
            )
        extended[pl.ds(bottoms, bottoms), part] = own[:, part]
    table = extended[...]
    lane = lax.broadcasted_iota(I32, (3 * bottoms, LANES), 1)
    for other in range(weights.shape[0]):
        shift = (size + MIDDLE - (other - 1) * bottoms) % size
        turned = pltpu.roll(table, shift, axis=1) if shift else table
        weights[other] = jnp.where(
            lane >= MIDDLE, jnp.where(lane < MIDDLE + 3 * bottoms, turned[:, :LANES], 0.0), 0.0
        )


def backward_kernel(
    frame_rows, arrived, weights, source, frame, force, smooth, edges, window, damping, owner, rim_owner,
    height, frame_source, padded, third_rows,
):
    tile = lax.axis_index("tile")
    tile_count = lax.axis_size("tile")
    blocks = force.shape[0]
    arrived = arrived.at[pl.ds(lax.axis_index("comp") * tile_count, tile_count)]
    left = arrived[lax.rem(tile + tile_count - 1, tile_count)]
    right = arrived[lax.rem(tile + 1, tile_count)]
    count = weights.shape[1]
    partial = jnp.zeros((count, LANES), F32)
    for other in range(weights.shape[0]):
        partial = partial + weights[other] * wide(arrived[other, pl.ds(0, 1), :], count)
    partial = jnp.concatenate([partial, jnp.zeros((LANES - count, LANES), F32)], axis=0)
    ones = jnp.ones((8, LANES), BF16)
    bottom = dot_nt(jnp.concatenate([ones, ones], axis=1), jnp.concatenate(split2(partial), axis=1))

    frows = frame_rows
    frame_source[...] = source[...]
    lane = lax.broadcasted_iota(I32, (1, LANES), 1)
    reach = LANES // 8
    frame_source[pl.ds(OWN - 2, 1), :] += jnp.where(lane >= LANES - reach, left[0:1], 0.0)
    frame_source[pl.ds(OWN - 1, 1), :] += left[2:3]
    frame_source[pl.ds(OWN, 1), :] += left[3:4]
    frame_source[pl.ds(OWN + frows - 1, 1), :] += right[3:4]
    frame_source[pl.ds(OWN + frows, 1), :] += right[2:3]
    frame_source[pl.ds(OWN + frows + 1, 1), :] += jnp.where(lane < reach, right[0:1], 0.0)
    total_source = frame_source[...]
    total = frame[pl.ds(6 * FRAME, FRAME), :]
    codes = frame[pl.ds(7 * FRAME, FRAME), :].astype(I32)
    damp = RELAXATION / total
    second = damp * total_source + gather_lanes(wide(bottom[0:1], FRAME), codes)
    third = second + damp * (total_source - total * second + first_level_sum(second, frame))
    third_rows[...] = third

    owners = owner[...]
    index = lax.bitwise_and(owners, LANES - 1)
    which = lax.shift_right_logical(owners, 7)
    corrected = jnp.zeros((blocks, LANES), F32)
    for row in range(frows):
        corrected = jnp.where(
            which == row, gather_lanes(wide(third_rows[pl.ds(OWN + row, 1), :], blocks), index), corrected
        )
    corrected = smooth[...] + corrected
    padded[pl.ds(8, blocks), :] = corrected
    left_rim = left[1:2] + gather_lanes(wide(third_rows[pl.ds(OWN - 1, 1), :]), rim_owner[0])[0:1]
    right_rim = right[1:2] + gather_lanes(wide(third_rows[pl.ds(OWN + frows, 1), :]), rim_owner[1])[0:1]
    padded[pl.ds(7, 1), :] = left_rim
    padded[pl.ds(8 + blocks, 1), :] = right_rim
    beside = neighbour_sum(padded, edges, window, blocks)
    height[...] = corrected + damping[1] * (force[...] - (damping[0] * corrected - beside))


def in_hbm(array):
    return pltpu.with_memory_space_constraint(array, pltpu.HBM)


def struct(shape, dtype=F32):
    return jax.ShapeDtypeStruct(shape, dtype)


VMEM = pl.BlockSpec(memory_space=pltpu.VMEM)
SMEM = pl.BlockSpec(memory_space=pltpu.SMEM)
ANY = pl.BlockSpec(memory_space=pltpu.HBM)
PARAMS = pltpu.CompilerParams(vmem_limit_bytes=16 * 1024 * 1024)


def per_device(
    fields, level_rate, edge_weight, fine_diagonal, fine_table, old_height, level_weight,
    flux_weight, fine_owner, coarse_table, coarse_edge, coarse_diagonal, coarse_owner,
    coarse_inverse, surface_out, send_blocks, entry_slot, entry_block, remap_tiles,
):
    tile_count = lax.axis_size("tile")
    cells = fields.shape[2]
    blocks = cells // LANES
    firsts = coarse_diagonal.shape[1]
    frows = firsts // LANES
    entries = entry_slot.shape[2]
    channels = surface_out.shape[1]
    slots = send_blocks.shape[2]
    each = slots // 5
    halves = coarse_inverse.shape[2] // LANES
    bottoms = coarse_inverse.shape[1]
    base = pick_base(halves)
    swap = [(0, 1), (1, 0)]
    surface = lax.ppermute(surface_out[0], "comp", swap)
    sends = lax.ppermute(send_blocks[0], "comp", swap)
    raw = (
        fields[0],
        old_height.reshape(blocks, LANES),
        edge_weight[0].reshape(3, blocks, LANES),
        fine_table[0].reshape(3, blocks, LANES),
        fine_owner.reshape(blocks, LANES),
        coarse_table[0].reshape(3, frows, LANES),
        coarse_edge[0].reshape(3, frows, LANES),
        coarse_diagonal.reshape(frows, LANES),
        coarse_owner.reshape(frows, LANES),
        coarse_inverse[0],
    )
    current, old, edges, table, owner, ctable, cedge, cdiag, cowner, cinverse = pl.pallas_call(
        load_kernel,
        out_shape=[struct(x.shape, x.dtype) for x in raw],
        in_specs=[ANY] * len(raw),
        out_specs=[VMEM] * len(raw),
        scratch_shapes=[pltpu.SemaphoreType.DMA((len(raw),))],
        compiler_params=PARAMS,
        name="load",
    )(*[in_hbm(x) for x in raw])

    pick = struct((4 * each, LANES), BF16)
    both = struct((base + 4 * each, LANES), BF16)
    plan = exchange_plan(tile_count)
    *messages, here = pl.pallas_call(
        functools.partial(pack_kernel, plan),
        out_shape=[both, both, both, both, pick],
        in_specs=[VMEM] * 12,
        out_specs=[VMEM] * 5,
        scratch_shapes=[
            pltpu.VMEM((channels * blocks, LANES), F32),
            pltpu.VMEM((base, LANES), F32),
            pltpu.VMEM((base, LANES), F32),
            pltpu.VMEM((4, base + 4 * each, LANES), BF16),
        ],
        compiler_params=PARAMS,
        name="pack",
    )(
        surface, sends, current, old, edges, table, owner, ctable, cedge, cdiag, cowner, cinverse,
    )

    messages = [
        lax.ppermute(message, "tile", [(i, (i + op[i]) % tile_count) for i in range(tile_count)])
        for message, op in zip(messages, plan)
    ]

    late = (
        level_rate, level_weight, flux_weight, fine_diagonal.reshape(blocks, LANES), entry_slot[0], entry_block[0]
    )
    fresh, force_part, beside_old, window, ends_row, ends_lane, hot, member, damping, scalars, tiles = pl.pallas_call(
        stencil_kernel,
        out_shape=[
            struct((fields.shape[1], cells)),
            struct((blocks, LANES)),
            struct((blocks, LANES)),
            struct((3, blocks, LANES), I32),
            struct((frows, LANES), I32),
            struct((frows, LANES), I32),
            struct((entries, slots), BF16),
            struct((2, blocks, entries // 2), BF16),
            struct((2, blocks, LANES)),
            struct((24, LANES)),
            pltpu.VMEM(remap_tiles.shape[2:], BF16),
        ],
        in_specs=[VMEM] * 6 + [ANY] * 7,
        out_specs=[VMEM] * 11,
        scratch_shapes=[pltpu.VMEM((blocks + 16, LANES), F32)]
        + [pltpu.VMEM(x.shape, x.dtype) for x in late]
        + [pltpu.SemaphoreType.DMA((len(late),)), pltpu.SemaphoreType.DMA((math.gcd(entries, 8),))],
        compiler_params=PARAMS,
        name="stencil",
    )(here, current, edges, table, old, owner, *[in_hbm(x) for x in (remap_tiles[0, 0],) + late])

    force, smooth, source, frame, weights, rim_owner, advanced, received, message = pl.pallas_call(
        functools.partial(forward_kernel, plan),
        out_shape=[
            struct((blocks, LANES)),
            struct((blocks, LANES)),
            struct((FRAME, LANES)),
            struct((8 * FRAME, LANES)),
            struct((tile_count, 3 * bottoms, LANES)),
            struct((2, 8, LANES), I32),
            struct((fields.shape[1], cells)),
            struct((channels, cells)),
            struct((2 * tile_count, 4, LANES)),
        ],
        in_specs=[VMEM] * 24,
        out_specs=[VMEM] * 6 + [ANY] * 3,
        scratch_shapes=[
            pltpu.VMEM((4 * entries, LANES), F32),
            pltpu.VMEM((4 * entries, LANES), F32),
            pltpu.VMEM((blocks + 16, LANES), F32),
            pltpu.VMEM((blocks, LANES), F32),
            pltpu.VMEM((2, base, LANES), F32),
            pltpu.VMEM((3 * bottoms, bottoms * tile_count), F32),
            pltpu.VMEM((2, fields.shape[1], LANES), F32),
            pltpu.VMEM((channels, cells), F32),
            pltpu.VMEM((2 * tile_count, 4, LANES), F32),
            pltpu.SemaphoreType.DMA((5,)),
        ],
        compiler_params=PARAMS,
        name="forward",
    )(
        tiles, scalars, *messages, here, hot, member, current, edges, window, old,
        damping, force_part, beside_old, ends_row, ends_lane, fresh, ctable, cedge, cdiag, cowner, cinverse,
    )
    arrived = lax.all_to_all(message, ("comp", "tile"), split_axis=0, concat_axis=0, tiled=True)
    height = pl.pallas_call(
        functools.partial(backward_kernel, frows),
        out_shape=struct((blocks, LANES)),
        in_specs=[VMEM] * 11,
        out_specs=VMEM,
        scratch_shapes=[
            pltpu.VMEM((FRAME, LANES), F32),
            pltpu.VMEM((blocks + 16, LANES), F32),
            pltpu.VMEM((FRAME, LANES), F32),
        ],
        compiler_params=PARAMS,
        name="backward",
    )(arrived, weights, source, frame, force, smooth, edges, window, damping, owner, rim_owner)
    return advanced[None], received[None], height.reshape(1, cells)


def solution(mesh):
    in_specs = (
        P("comp", None, "tile"),
        P("comp", None),
        P("comp", None, "tile"),
        P("comp", "tile"),
        P("comp", None, "tile"),
        P("comp", "tile"),
        P("comp", None),
        P("comp", None),
        P("comp", "tile"),
        P("comp", None, "tile"),
        P("comp", None, "tile"),
        P("comp", "tile"),
        P("comp", "tile"),
        P("comp", "tile", None),
        P("comp", None, "tile"),
        P("comp", "tile", None),
        P("comp", "tile", None),
        P("comp", "tile", None),
        P("comp", "tile", None, None, None),
    )
    out_specs = (P("comp", None, "tile"), P("comp", None, "tile"), P("comp", "tile"))
    return jax.shard_map(
        per_device, mesh=mesh, in_specs=in_specs, out_specs=out_specs, check_vma=False
    )
```

```python
import functools
import math

import jax
import jax.numpy as jnp
from jax import lax
from jax.experimental import pallas as pl
from jax.experimental.pallas import tpu as pltpu
from jax.sharding import PartitionSpec as P

LANES = 128
RELAXATION = 0.8
F32 = jnp.float32
BF16 = jnp.bfloat16
I32 = jnp.int32

FIELD_HI, FIELD_LO = 0, 8
EDGE_HI, EDGE_LO, OLD_HI, OLD_LO = 16, 19, 22, 23
OFFSET, OWNER = 24, 27
CEDGE_HI, CEDGE_LO, CDIAG_HI, CDIAG_LO = 32, 38, 44, 46
COFFSET, COWNER = 48, 54
INVERSE = 56

FRAME, OWN = 32, 8

MIDDLE = 32


PLANS = {
    16: (
        (1, 1, 1, 1, 1, 2, 2, -1, 2, 2, -1, 2, 2, 2, -2, 1),
        (-1, 2, 2, -2, -2, 1, -1, 2, -1, 1, -2, 1, 1, -2, 2, -1),
        (-2, -2, -2, -1, -1, -1, 1, -2, -2, -1, 1, -2, -2, -1, -1, 2),
        (2, -1, -1, 2, 2, -2, -2, 1, 1, -2, 2, -1, -1, 1, 1, -2),
    ),
}
DISTANCES = (-1, 1, -2, 2)


def exchange_plan(count):
    if count in PLANS:
        return PLANS[count]
    near = [1 if i % 2 == 0 else -1 for i in range(count)]
    return ([2] * count, [-d for d in near], [-2] * count, near)


def lookup(tile, values):
    result = jnp.int32(values[0])
    for i, value in enumerate(values):
        result = jnp.where(tile == i, jnp.int32(value), result)
    return result


def arrived_by(tile, plan, distance):
    count = len(plan[0])
    found = []
    for i in range(count):
        sender = (i - distance) % count
        found.append([op[sender] for op in plan].index(distance))
    return lookup(tile, found)


def chosen_rows(which, refs, rows):
    value = refs[0][rows, :]
    for i, ref in enumerate(refs[1:]):
        value = jnp.where(which == i + 1, ref[rows, :], value)
    return value


def gather_lanes(table, index):
    return jnp.take_along_axis(table, index, axis=1)


def wide(row, count=8):
    return jnp.broadcast_to(row, (count, row.shape[1]))


def split2(x):
    high = x.astype(BF16)
    return high, (x - high.astype(F32)).astype(BF16)


def dot_nt(a, b):
    return lax.dot_general(a, b, (((1,), (1,)), ((), ())), preferred_element_type=F32)


def dot_tn(a, b):
    return lax.dot_general(a, b, (((0,), (0,)), ((), ())), preferred_element_type=F32)


def pick_base(bottoms, size):
    return -(-(INVERSE + 2 * bottoms * (size // LANES)) // 16) * 16


def load_kernel(*refs):
    count = len(refs) // 2
    copies = [
        pltpu.make_async_copy(source, target, refs[-1].at[i])
        for i, (source, target) in enumerate(zip(refs[:count], refs[count : 2 * count]))
    ]
    for copy in copies:
        copy.start()
    for copy in copies:
        copy.wait()


def pack_kernel(
    plan, surface, sends, fields, old, edge, table, owner, ctable, cedge, cdiag, cowner, cinverse,
    out0, out1, out2, out3, here, chunks, left_rows, right_rows, packed,
):
    tile = lax.axis_index("tile")
    cells = fields.shape[1]
    blocks = cells // LANES
    frows = ctable.shape[1]
    firsts = frows * LANES
    bottoms = cinverse.shape[0]
    base = pick_base(*cinverse.shape)
    lane = lax.broadcasted_iota(I32, (1, LANES), 1)

    for rows, at_left in ((right_rows, False), (left_rows, True)):
        start = 0 if at_left else cells - LANES
        part = pl.ds(start, LANES)

        def both(high, low_row, value):
            count = value.shape[0]
            rows[pl.ds(high, count), :] = value
            rows[pl.ds(low_row, count), :] = value - value.astype(BF16).astype(F32)

        def three(ref, row):
            return jnp.concatenate([ref[link, pl.ds(row, 1), :] for link in range(3)], axis=0)

        rows[pl.ds(24, 8), :] = jnp.zeros((8, LANES), F32)
        both(FIELD_HI, FIELD_LO, fields[:, part])
        block = 0 if at_left else blocks - 1
        both(EDGE_HI, EDGE_LO, three(edge, block))
        both(OLD_HI, OLD_LO, old[pl.ds(block, 1), :])
        rows[pl.ds(OFFSET, 3), :] = (three(table, block) - (LANES + start) - lane).astype(F32)
        shift = 0 if at_left else firsts - LANES
        rows[pl.ds(OWNER, 1), :] = (owner[pl.ds(block, 1), :] - shift).astype(F32)
        first = 0 if at_left else frows - 2
        reach = LANES // 8
        for step in range(2):
            both(CEDGE_HI + 3 * step, CEDGE_LO + 3 * step, three(cedge, first + step))
            rows[pl.ds(COFFSET + 3 * step, 3), :] = (
                three(ctable, first + step) - (reach + (first + step) * LANES) - lane
            ).astype(F32)
            both(CDIAG_HI + step, CDIAG_LO + step, cdiag[pl.ds(first + step, 1), :])
            rows[pl.ds(COWNER + step, 1), :] = cowner[pl.ds(first + step, 1), :].astype(F32)
        halves = cinverse.shape[1] // LANES
        for half in range(halves):
            both(
                INVERSE + bottoms * half,
                INVERSE + bottoms * (halves + half),
                cinverse[:, pl.ds(half * LANES, LANES)],
            )
        end = INVERSE + 2 * bottoms * halves
        if base > end:
            rows[pl.ds(end, base - end), :] = jnp.zeros((base - end, LANES), F32)

    for block in range(blocks):
        chunks[pl.ds(4 * block, 4), :] = surface[:, pl.ds(block * LANES, LANES)].astype(F32)
    slots = sends.shape[1]
    hot = jnp.where(
        lax.broadcasted_iota(I32, (blocks, slots), 0) == sends[...], 1.0, 0.0
    ).astype(BF16)
    picks = []
    for channel in range(4):
        source = chunks[pl.ds(channel, blocks, stride=4), :].astype(BF16)
        picks.append(dot_tn(hot, source).astype(BF16))
    count = slots // 5

    chosen = [
        jnp.concatenate([p[j * count : (j + 1) * count] for p in picks], axis=0) for j in range(5)
    ]
    here[...] = chosen[2]
    rims = {-1: left_rows[...].astype(BF16), 1: right_rows[...].astype(BF16)}
    for at, distance in enumerate(DISTANCES):
        packed[at, pl.ds(0, base), :] = rims.get(distance, jnp.zeros((base, LANES), BF16))
        packed[at, pl.ds(base, 4 * count), :] = chosen[2 - distance]
    for out, op in zip((out0, out1, out2, out3), plan):
        out[...] = packed[lookup(tile, [DISTANCES.index(distance) for distance in op])]


def stencil_kernel(
    here, fields, edge, table, old, owner, tiles, rate, level_weight, flux_weight, diagonal_in, slots_in, block_in,
    fresh, force, beside_old, window, ends_row, ends_lane, hot, member, damping, scalars, tile_buffer,
    padded, rate_row, level_row, flux_row, diagonal, slots, entry_block, small_sems, sems,
):
    del here
    small = [
        pltpu.make_async_copy(source, target, small_sems.at[i])
        for i, (source, target) in enumerate(
            (
                (rate, rate_row), (level_weight, level_row), (flux_weight, flux_row),
                (diagonal_in, diagonal), (slots_in, slots), (block_in, entry_block),
            )
        )
    ]
    parts = sems.shape[0]
    step = tiles.shape[0] // parts

    def load(part):
        span = pl.ds(part * step, step)
        return pltpu.make_async_copy(tiles.at[span], tile_buffer.at[span], sems.at[part])

    def begin(part, carry):
        if part is None:
            for copy in small:
                copy.start()
        else:
            load(part).start()
        return carry

    once = 1 + lax.axis_index("tile") // lax.axis_size("tile")
    lax.fori_loop(0, once, lambda _, carry: begin(None, carry), 0)
    lax.fori_loop(0, parts, begin, 0)
    blocks = old.shape[0]
    levels = fields.shape[0]
    firsts = ends_row.shape[0] * LANES
    ident = lax.broadcasted_iota(I32, ends_row.shape, 0) * LANES + lax.broadcasted_iota(
        I32, ends_row.shape, 1
    )
    count = ends_row.shape[0]
    rows = jnp.zeros(ends_row.shape, I32)
    for block in range(blocks):
        last = jnp.broadcast_to(owner[pl.ds(block, 1), LANES - 1 : LANES], ends_row.shape)
        rows = rows + jnp.where(last <= ident, 1, 0)
    lanes = jnp.zeros(ends_row.shape, I32)
    for bit in (64, 32, 16, 8, 4, 2, 1):
        probe = lanes + (bit - 1)
        value = jnp.full(ends_row.shape, firsts, I32)
        for block in range(blocks):
            value = jnp.where(
                rows == block, gather_lanes(wide(owner[pl.ds(block, 1), :], count), probe), value
            )
        lanes = jnp.where(value <= ident, lanes + bit, lanes)
    ends_row[...] = rows
    ends_lane[...] = lanes
    for copy in small:
        copy.wait()
    for i, value in enumerate((rate_row, level_row, flux_row)):
        width = value.shape[1]
        same = lax.broadcasted_iota(I32, (8, width), 0) == lax.broadcasted_iota(I32, (8, width), 1)
        column = jnp.sum(jnp.where(same, wide(value[...]), 0.0), axis=1, keepdims=True)
        scalars[pl.ds(8 * i, 8), :] = jnp.broadcast_to(column, (8, LANES))
    speed = scalars[pl.ds(0, 8), :]
    share = scalars[pl.ds(8, 8), :]
    starts = lax.broadcasted_iota(I32, (blocks, LANES), 0) * LANES
    total = edge[0] + edge[1] + edge[2]
    inverse = 1.0 / total
    fine_total = diagonal[...] + total
    damping[0] = fine_total
    damping[1] = RELAXATION / fine_total
    for link in range(3):
        window[link] = table[link] - starts
    blank = jnp.zeros((levels, LANES), F32)

    def chunk(block):
        if 0 <= block < blocks:
            return fields[:, pl.ds(block * LANES, LANES)]
        return blank

    before, here, after = blank, chunk(0), chunk(1)
    for block in range(blocks):
        row = slice(block, block + 1)
        beside = jnp.zeros((levels, LANES), F32)
        for link in range(3):
            place = wide(window[link, pl.ds(block, 1), :])
            index = lax.bitwise_and(place, LANES - 1)
            value = jnp.where(
                place < LANES,
                gather_lanes(before, index),
                jnp.where(place < 2 * LANES, gather_lanes(here, index), gather_lanes(after, index)),
            )
            beside = beside + wide(edge[link, pl.ds(block, 1), :]) * value
        result = here + speed * ((beside - wide(total[row]) * here) * wide(inverse[row]))
        fresh[:, pl.ds(block * LANES, LANES)] = result
        force[pl.ds(block, 1), :] = jnp.sum(result * share, axis=0, keepdims=True)
        before, here, after = here, after, chunk(block + 2)

    padded[pl.ds(0, 8), :] = jnp.zeros((8, LANES), F32)
    padded[pl.ds(8 + blocks, 8), :] = jnp.zeros((8, LANES), F32)
    padded[pl.ds(8, blocks), :] = old[...]
    beside_old[...] = neighbour_sum(padded, edge, window, blocks)
    names = jnp.where(
        lax.broadcasted_iota(I32, (slots.shape[1], slots.shape[1]), 0) == slots[...], 1.0, 0.0
    )
    hot[...] = jnp.transpose(names).astype(BF16)
    half = entry_block.shape[1] // 2
    for part in range(2):
        member[part] = jnp.where(
            lax.broadcasted_iota(I32, (blocks, half), 0) == entry_block[:, part * half : (part + 1) * half],
            1.0,
            0.0,
        ).astype(BF16)

    for part in range(parts):
        load(part).wait()


def neighbour_sum(padded, edges, window, blocks):
    before = padded[pl.ds(7, blocks), :]
    here = padded[pl.ds(8, blocks), :]
    after = padded[pl.ds(9, blocks), :]
    result = jnp.zeros((blocks, LANES), F32)
    for link in range(3):
        place = window[link]
        index = lax.bitwise_and(place, LANES - 1)
        value = jnp.where(
            place < LANES,
            gather_lanes(before, index),
            jnp.where(place < 2 * LANES, gather_lanes(here, index), gather_lanes(after, index)),
        )
        result = result + edges[link] * value
    return result


def first_level_sum(values, frame):
    before = pltpu.roll(values, 1, axis=0)
    after = pltpu.roll(values, FRAME - 1, axis=0)
    lane = lax.broadcasted_iota(I32, (FRAME, LANES), 1)
    result = jnp.zeros((FRAME, LANES), F32)
    for link in range(3):
        place = lane + frame[pl.ds(link * FRAME, FRAME), :].astype(I32)
        index = lax.bitwise_and(place, LANES - 1)
        value = jnp.where(
            place < 0,
            gather_lanes(before, index),
            jnp.where(place >= LANES, gather_lanes(after, index), gather_lanes(values, index)),
        )
        result = result + frame[pl.ds((3 + link) * FRAME, FRAME), :] * value
    return result


def previous_one(values):
    rolled = pltpu.roll(values, 1, axis=1)
    above = pltpu.roll(rolled, 1, axis=0)
    lane = lax.broadcasted_iota(I32, values.shape, 1)
    row = lax.broadcasted_iota(I32, values.shape, 0)
    return jnp.where(lane > 0, rolled, jnp.where(row > 0, above, 0.0))


def triangle():
    return jnp.where(
        lax.broadcasted_iota(I32, (LANES, LANES), 0) < lax.broadcasted_iota(I32, (LANES, LANES), 1),
        1.0,
        0.0,
    ).astype(BF16)


def prefix(values):
    ones = jnp.ones((LANES, LANES), BF16)
    right = jnp.concatenate([triangle(), ones], axis=1)
    count = values.shape[0]
    out = jnp.dot(
        jnp.concatenate(split2(values), axis=0), right, preferred_element_type=F32
    )
    out = out[:count] + out[count:]
    return out[:, :LANES], out[:, LANES:]


def rows_before(values):
    sublane = lax.broadcasted_iota(I32, (8, LANES), 0)
    run = jnp.zeros((8, LANES), F32)
    result = []
    for at in range(0, values.shape[0], 8):
        piece = values[at : at + 8]
        total = piece
        for distance in (1, 2, 4):
            total = total + jnp.where(sublane >= distance, pltpu.roll(total, distance, axis=0), 0.0)
        result.append(run + (total - piece))
        run = run + wide(total[7:8])
    return jnp.concatenate(result, axis=0), run


def forward_kernel(
    plan, tiles, scalars, message0, message1, message2, message3, here, hot, member, fields, edges, window, old,
    damping, force_part, beside_old, ends_row, ends_lane, fresh, ctable, cedge, cdiag, cowner, cinverse,
    force_out, smooth_out, source_out, frame, weights_out, rim_owner, fresh_out, received_out, message_out,
    picked, products, padded, prefixed, arrivals, extended, ends, received, message, sems,
):
    cells = fresh.shape[1]
    middle = pl.ds(LANES, cells - 2 * LANES)
    copies = [pltpu.make_async_copy(fresh.at[:, middle], fresh_out.at[:, middle], sems.at[0])]
    for side in range(2):
        copies.append(
            pltpu.make_async_copy(
                ends.at[side], fresh_out.at[:, pl.ds(side * (cells - LANES), LANES)], sems.at[1 + side]
            )
        )
    copies.append(pltpu.make_async_copy(received, received_out, sems.at[3]))
    copies.append(pltpu.make_async_copy(message, message_out, sems.at[4]))

    def begin(which):
        def body(_, carry):
            for copy in which:
                copy.start()
            return carry

        lax.fori_loop(0, 1 + lax.axis_index("tile") // lax.axis_size("tile"), body, 0)

    begin(copies[:1])
    tile = lax.axis_index("tile")
    tile_count = lax.axis_size("tile")
    entries = tiles.shape[0]
    blocks = old.shape[0]

    messages = (message0, message1, message2, message3)
    base = message0.shape[0] - here.shape[0]
    each = here.shape[0] // 4
    found = {distance: arrived_by(tile, plan, distance) for distance in DISTANCES}
    sources = [
        chosen_rows(found[distance], messages, pl.ds(base, 4 * each)) if distance else here[...]
        for distance in (2, 1, 0, -1, -2)
    ]
    for channel in range(4):
        source = jnp.concatenate(
            [rows[channel * each : (channel + 1) * each] for rows in sources], axis=0
        )
        picked[pl.ds(channel, entries, stride=4), :] = jnp.dot(hot[...], source, preferred_element_type=F32)

    for side, distance in enumerate((1, -1)):
        arrivals[side] = chosen_rows(found[distance], messages, pl.ds(0, base)).astype(F32)
        rim_owner[side] = wide(arrivals[side, pl.ds(OWNER, 1), :]).astype(I32)

    upper = lax.rem(lax.broadcasted_iota(I32, (16, LANES), 0), 8) < 4
    for group in range(entries // 4):
        rows = picked[pl.ds(16 * group, 16), :]
        rows = jnp.concatenate([jnp.where(upper, rows, 0.0), jnp.where(upper, 0.0, rows)], axis=1)
        at = 4 * group
        weights = jnp.concatenate(
            [
                jnp.concatenate([tiles[at], tiles[at + 1]], axis=1),
                jnp.concatenate([tiles[at + 2], tiles[at + 3]], axis=1),
            ],
            axis=0,
        )
        product = dot_nt(rows.astype(BF16), weights)
        products[pl.ds(16 * group, 8), :] = product[0:8, :LANES]
        products[pl.ds(16 * group + 8, 8), :] = product[8:16, LANES:]
    speed = scalars[pl.ds(0, 8), :]
    share = scalars[pl.ds(8, 8), :]
    force_out[...] = force_part[...]
    padded[pl.ds(0, 8), :] = jnp.zeros((8, LANES), F32)
    padded[pl.ds(8 + blocks, 8), :] = jnp.zeros((8, LANES), F32)
    beside_extra = []
    for side, block, target in ((0, 0, 0), (1, blocks - 1, 2)):
        halo = arrivals[side, pl.ds(FIELD_HI, 8), :] + arrivals[side, pl.ds(FIELD_LO, 8), :]
        halo_old = arrivals[side, pl.ds(OLD_HI, 1), :] + arrivals[side, pl.ds(OLD_LO, 1), :]
        total = edges[0, pl.ds(block, 1), :] + edges[1, pl.ds(block, 1), :] + edges[2, pl.ds(block, 1), :]
        extra = jnp.zeros((8, LANES), F32)
        extra_old = jnp.zeros((8, LANES), F32)
        for link in range(3):
            place = wide(window[link, pl.ds(block, 1), :])
            index = lax.bitwise_and(place, LANES - 1)
            weight = jnp.where(
                lax.shift_right_logical(place, 7) == target, wide(edges[link, pl.ds(block, 1), :]), 0.0
            )
            extra = extra + weight * gather_lanes(halo, index)
            extra_old = extra_old + weight * gather_lanes(wide(halo_old), index)
        change = speed * extra / wide(total)
        ends[side] = fresh[:, pl.ds(block * LANES, LANES)] + change
        force_out[pl.ds(block, 1), :] += jnp.sum(change * share, axis=0, keepdims=True)
        beside_extra.append(extra_old[0:1])

    inverse_windows(arrivals.at[0], cinverse, arrivals.at[1], extended, weights_out)

    force = force_out[...]
    half = entries // 2
    for channel in range(4):
        value = jnp.zeros((blocks, 2 * LANES), F32)
        for part in range(2):
            rows = products[pl.ds(4 * half * part + channel, half, stride=4), :]
            value = value + jnp.dot(
                member[part], jnp.concatenate(split2(rows), axis=1), preferred_element_type=F32
            )
        value = value[:, :LANES] + value[:, LANES:]
        for block in range(blocks):
            received[pl.ds(channel, 1), pl.ds(block * LANES, LANES)] = value[block : block + 1]
        force = force + scalars[pl.ds(16 + channel, 1), :] * value

    force_out[...] = force
    begin(copies[1:4])
    total, damp = damping[0], damping[1]
    smooth_out[...] = beside_old[...]
    smooth_out[pl.ds(0, 1), :] += beside_extra[0]
    smooth_out[pl.ds(blocks - 1, 1), :] += beside_extra[1]
    previous = old[...]
    smooth = previous + damp * (force - (total * previous - smooth_out[...]))
    smooth_out[...] = smooth
    padded[pl.ds(8, blocks), :] = smooth
    residual = force - total * smooth + neighbour_sum(padded, edges, window, blocks)

    inner, whole = prefix(residual)
    before, run = rows_before(whole)
    prefixed[...] = inner + before
    rows, lanes = ends_row[...], ends_lane[...]
    count = rows.shape[0]
    marks = run[:count]
    for block in range(blocks):
        value = gather_lanes(wide(prefixed[pl.ds(block, 1), :], count), lanes)
        marks = jnp.where(rows == block, value, marks)
    own_source = marks - previous_one(marks)

    lane = lax.broadcasted_iota(I32, (1, LANES), 1)
    rim_rows, rim_counts = [], []
    for side in range(2):
        inside = padded[pl.ds(8 if side == 0 else 7 + blocks, 1), :]
        value = jnp.zeros((1, LANES), F32)
        for link in range(3):
            place = lane + arrivals[side, pl.ds(OFFSET + link, 1), :].astype(I32)
            index = lax.bitwise_and(place, LANES - 1)
            reached = (place >= LANES) if side == 0 else (place < 0)
            weight = arrivals[side, pl.ds(EDGE_HI + link, 1), :] + arrivals[side, pl.ds(EDGE_LO + link, 1), :]
            value = value + jnp.where(
                wide(reached.astype(I32)) > 0,
                wide(weight) * gather_lanes(wide(inside), wide(index)),
                0.0,
            )[0:1]
        rim_rows.append(value)
        owners = arrivals[side, pl.ds(OWNER, 1), :].astype(I32)
        below = jnp.where(
            lax.broadcasted_iota(I32, (LANES, LANES), 0) >= owners, 1.0, 0.0
        ).astype(BF16)
        rim_counts.append(dot_nt(jnp.ones((8, LANES), BF16), below))
    rim_inner, rim_whole = prefix(jnp.concatenate([wide(r) for r in rim_rows], axis=0))
    rim_source = []
    for side in range(2):
        place = rim_counts[side].astype(I32)
        index = lax.bitwise_and(place, LANES - 1)
        value = gather_lanes(rim_inner[8 * side : 8 * side + 8], index)
        value = jnp.where(place >= LANES, rim_whole[8 * side : 8 * side + 8], value)
        shifted = pltpu.roll(value, 1, axis=1)
        first = lax.broadcasted_iota(I32, (8, LANES), 1) == 0
        rim_source.append((value - jnp.where(first, 0.0, shifted))[0:1])

    frows = own_source.shape[0]
    source_out[...] = jnp.zeros((FRAME, LANES), F32)
    source_out[pl.ds(OWN, frows), :] = own_source
    source_out[pl.ds(OWN - 1, 1), :] = rim_source[0]
    source_out[pl.ds(OWN + frows, 1), :] = rim_source[1]
    reach = LANES // 8
    frame[...] = jnp.zeros(frame.shape, F32)
    frame[pl.ds(6 * FRAME, FRAME), :] = jnp.ones((FRAME, LANES), F32)
    frame[pl.ds(7 * FRAME, FRAME), :] = jnp.full((FRAME, LANES), 127.0, F32)
    bottoms = cinverse.shape[0]
    at_cell = lax.broadcasted_iota(I32, (frows, LANES), 0) * LANES + lax.broadcasted_iota(
        I32, (frows, LANES), 1
    )
    for link in range(3):
        frame[pl.ds(link * FRAME + OWN, frows), :] = (ctable[link] - reach - at_cell).astype(F32)
        frame[pl.ds((3 + link) * FRAME + OWN, frows), :] = cedge[link]
    frame[pl.ds(6 * FRAME + OWN, frows), :] = cdiag[...]
    frame[pl.ds(7 * FRAME + OWN, frows), :] = (cowner[...] + bottoms).astype(F32)
    for side in range(2):
        for row in range(2):
            at = (OWN - 2 + row) if side == 0 else (OWN + frows + row)
            for link in range(3):
                put = 3 * row + link
                frame[pl.ds(link * FRAME + at, 1), :] = arrivals[side, pl.ds(COFFSET + put, 1), :]
                frame[pl.ds((3 + link) * FRAME + at, 1), :] = (
                    arrivals[side, pl.ds(CEDGE_HI + put, 1), :] + arrivals[side, pl.ds(CEDGE_LO + put, 1), :]
                )
            frame[pl.ds(6 * FRAME + at, 1), :] = (
                arrivals[side, pl.ds(CDIAG_HI + row, 1), :] + arrivals[side, pl.ds(CDIAG_LO + row, 1), :]
            )
            frame[pl.ds(7 * FRAME + at, 1), :] = arrivals[side, pl.ds(COWNER + row, 1), :] + (
                2.0 * bottoms * side
            )
    for link in range(3):
        frame[pl.ds(6 * FRAME, FRAME), :] += frame[pl.ds((3 + link) * FRAME, FRAME), :]
    source = source_out[...]
    first = (RELAXATION / frame[pl.ds(6 * FRAME, FRAME), :]) * source
    residual = (1.0 - RELAXATION) * source + first_level_sum(first, frame)
    codes = frame[pl.ds(7 * FRAME, FRAME), :].astype(I32)
    pieces = split2(residual)
    left_side, right_side = [], []
    bins = lax.broadcasted_iota(I32, (3 * bottoms, LANES), 0)
    rest = [jnp.zeros((rows, LANES), BF16) for rows in (MIDDLE, LANES - MIDDLE - 3 * bottoms)]
    for row in range(OWN - 2, OWN + frows + 2):
        left_side.append(jnp.concatenate([p[row : row + 1] for p in pieces], axis=0))
        named = jnp.where(bins == codes[row : row + 1], 1.0, 0.0).astype(BF16)
        right_side.append(jnp.concatenate([rest[0], named, rest[1]], axis=0))
    bottom = dot_nt(jnp.concatenate(left_side, axis=1), jnp.concatenate(right_side, axis=1))
    bottom = bottom[0:1] + bottom[1:2]

    reach = LANES // 8
    to_left = jnp.concatenate(
        [
            jnp.where(lane < reach, own_source[1:2], bottom),
            padded[pl.ds(8, 1), :],
            own_source[0:1],
            rim_source[0],
        ],
        axis=0,
    )
    to_right = jnp.concatenate(
        [
            jnp.where(lane >= LANES - reach, own_source[frows - 2 : frows - 1], bottom),
            padded[pl.ds(7 + blocks, 1), :],
            own_source[frows - 1 : frows],
            rim_source[1],
        ],
        axis=0,
    )
    for other in range(message.shape[0]):
        message[other] = to_right
    for group in range(2):
        message[group * tile_count + lax.rem(tile + tile_count - 1, tile_count)] = to_left
    copies[4].start()
    for copy in copies:
        copy.wait()


def inverse_windows(left, own, right, extended, weights):
    bottoms, size = own.shape
    halves = size // LANES
    for half in range(halves):
        part = pl.ds(half * LANES, LANES)
        for at, block in ((0, left), (2, right)):
            high, low = INVERSE + bottoms * half, INVERSE + bottoms * (halves + half)
            extended[pl.ds(at * bottoms, bottoms), part] = (
                block[pl.ds(high, bottoms), :] + block[pl.ds(low, bottoms), :]
            )
        extended[pl.ds(bottoms, bottoms), part] = own[:, part]
    table = extended[...]
    lane = lax.broadcasted_iota(I32, (3 * bottoms, LANES), 1)
    for other in range(weights.shape[0]):
        shift = (size + MIDDLE - (other - 1) * bottoms) % size
        turned = pltpu.roll(table, shift, axis=1) if shift else table
        weights[other] = jnp.where(
            lane >= MIDDLE, jnp.where(lane < MIDDLE + 3 * bottoms, turned[:, :LANES], 0.0), 0.0
        )


def backward_kernel(
    frame_rows, arrived, weights, source, frame, force, smooth, edges, window, damping, owner, rim_owner,
    height, frame_source, padded, third_rows,
):
    tile = lax.axis_index("tile")
    tile_count = lax.axis_size("tile")
    blocks = force.shape[0]
    arrived = arrived.at[pl.ds(lax.axis_index("comp") * tile_count, tile_count)]
    left = arrived[lax.rem(tile + tile_count - 1, tile_count)]
    right = arrived[lax.rem(tile + 1, tile_count)]
    count = weights.shape[1]
    sums = [jnp.zeros((count, LANES), F32)] * 4
    for other in range(weights.shape[0]):
        part = weights[other] * wide(arrived[other, pl.ds(0, 1), :], count)
        sums[other % 4] = sums[other % 4] + part
    partial = (sums[0] + sums[1]) + (sums[2] + sums[3])
    partial = jnp.concatenate([partial, jnp.zeros((LANES - count, LANES), F32)], axis=0)
    ones = jnp.ones((8, LANES), BF16)
    bottom = dot_nt(jnp.concatenate([ones, ones], axis=1), jnp.concatenate(split2(partial), axis=1))

    frows = frame_rows
    frame_source[...] = source[...]
    lane = lax.broadcasted_iota(I32, (1, LANES), 1)
    reach = LANES // 8
    frame_source[pl.ds(OWN - 2, 1), :] += jnp.where(lane >= LANES - reach, left[0:1], 0.0)
    frame_source[pl.ds(OWN - 1, 1), :] += left[2:3]
    frame_source[pl.ds(OWN, 1), :] += left[3:4]
    frame_source[pl.ds(OWN + frows - 1, 1), :] += right[3:4]
    frame_source[pl.ds(OWN + frows, 1), :] += right[2:3]
    frame_source[pl.ds(OWN + frows + 1, 1), :] += jnp.where(lane < reach, right[0:1], 0.0)
    total_source = frame_source[...]
    total = frame[pl.ds(6 * FRAME, FRAME), :]
    codes = frame[pl.ds(7 * FRAME, FRAME), :].astype(I32)
    damp = RELAXATION / total
    second = damp * total_source + gather_lanes(wide(bottom[0:1], FRAME), codes)
    third = second + damp * (total_source - total * second + first_level_sum(second, frame))
    third_rows[...] = third

    owners = owner[...]
    index = lax.bitwise_and(owners, LANES - 1)
    which = lax.shift_right_logical(owners, 7)
    corrected = jnp.zeros((blocks, LANES), F32)
    for row in range(frows):
        corrected = jnp.where(
            which == row, gather_lanes(wide(third_rows[pl.ds(OWN + row, 1), :], blocks), index), corrected
        )
    corrected = smooth[...] + corrected
    padded[pl.ds(8, blocks), :] = corrected
    left_rim = left[1:2] + gather_lanes(wide(third_rows[pl.ds(OWN - 1, 1), :]), rim_owner[0])[0:1]
    right_rim = right[1:2] + gather_lanes(wide(third_rows[pl.ds(OWN + frows, 1), :]), rim_owner[1])[0:1]
    padded[pl.ds(7, 1), :] = left_rim
    padded[pl.ds(8 + blocks, 1), :] = right_rim
    beside = neighbour_sum(padded, edges, window, blocks)
    height[...] = corrected + damping[1] * (force[...] - (damping[0] * corrected - beside))


def in_hbm(array):
    return pltpu.with_memory_space_constraint(array, pltpu.HBM)


def struct(shape, dtype=F32):
    return jax.ShapeDtypeStruct(shape, dtype)


VMEM = pl.BlockSpec(memory_space=pltpu.VMEM)
SMEM = pl.BlockSpec(memory_space=pltpu.SMEM)
ANY = pl.BlockSpec(memory_space=pltpu.HBM)
PARAMS = pltpu.CompilerParams(vmem_limit_bytes=16 * 1024 * 1024)


def per_device(
    fields, level_rate, edge_weight, fine_diagonal, fine_table, old_height, level_weight,
    flux_weight, fine_owner, coarse_table, coarse_edge, coarse_diagonal, coarse_owner,
    coarse_inverse, surface_out, send_blocks, entry_slot, entry_block, remap_tiles,
):
    tile_count = lax.axis_size("tile")
    cells = fields.shape[2]
    blocks = cells // LANES
    firsts = coarse_diagonal.shape[1]
    frows = firsts // LANES
    entries = entry_slot.shape[2]
    channels = surface_out.shape[1]
    slots = send_blocks.shape[2]
    each = slots // 5
    bottoms = coarse_inverse.shape[1]
    base = pick_base(*coarse_inverse.shape[1:])
    swap = [(0, 1), (1, 0)]
    surface = lax.ppermute(surface_out[0], "comp", swap)
    sends = lax.ppermute(send_blocks[0], "comp", swap)
    raw = (
        fields[0],
        old_height.reshape(blocks, LANES),
        edge_weight[0].reshape(3, blocks, LANES),
        fine_table[0].reshape(3, blocks, LANES),
        fine_owner.reshape(blocks, LANES),
        coarse_table[0].reshape(3, frows, LANES),
        coarse_edge[0].reshape(3, frows, LANES),
        coarse_diagonal.reshape(frows, LANES),
        coarse_owner.reshape(frows, LANES),
        coarse_inverse[0],
    )
    current, old, edges, table, owner, ctable, cedge, cdiag, cowner, cinverse = pl.pallas_call(
        load_kernel,
        out_shape=[struct(x.shape, x.dtype) for x in raw],
        in_specs=[ANY] * len(raw),
        out_specs=[VMEM] * len(raw),
        scratch_shapes=[pltpu.SemaphoreType.DMA((len(raw),))],
        compiler_params=PARAMS,
        name="load",
    )(*[in_hbm(x) for x in raw])

    pick = struct((4 * each, LANES), BF16)
    both = struct((base + 4 * each, LANES), BF16)
    plan = exchange_plan(tile_count)
    *messages, here = pl.pallas_call(
        functools.partial(pack_kernel, plan),
        out_shape=[both, both, both, both, pick],
        in_specs=[VMEM] * 12,
        out_specs=[VMEM] * 5,
        scratch_shapes=[
            pltpu.VMEM((channels * blocks, LANES), F32),
            pltpu.VMEM((base, LANES), F32),
            pltpu.VMEM((base, LANES), F32),
            pltpu.VMEM((4, base + 4 * each, LANES), BF16),
        ],
        compiler_params=PARAMS,
        name="pack",
    )(
        surface, sends, current, old, edges, table, owner, ctable, cedge, cdiag, cowner, cinverse,
    )

    messages = [
        lax.ppermute(message, "tile", [(i, (i + op[i]) % tile_count) for i in range(tile_count)])
        for message, op in zip(messages, plan)
    ]

    late = (
        level_rate, level_weight, flux_weight, fine_diagonal.reshape(blocks, LANES), entry_slot[0], entry_block[0]
    )
    fresh, force_part, beside_old, window, ends_row, ends_lane, hot, member, damping, scalars, tiles = pl.pallas_call(
        stencil_kernel,
        out_shape=[
            struct((fields.shape[1], cells)),
            struct((blocks, LANES)),
            struct((blocks, LANES)),
            struct((3, blocks, LANES), I32),
            struct((frows, LANES), I32),
            struct((frows, LANES), I32),
            struct((entries, slots), BF16),
            struct((2, blocks, entries // 2), BF16),
            struct((2, blocks, LANES)),
            struct((24, LANES)),
            pltpu.VMEM(remap_tiles.shape[2:], BF16),
        ],
        in_specs=[VMEM] * 6 + [ANY] * 7,
        out_specs=[VMEM] * 11,
        scratch_shapes=[pltpu.VMEM((blocks + 16, LANES), F32)]
        + [pltpu.VMEM(x.shape, x.dtype) for x in late]
        + [pltpu.SemaphoreType.DMA((len(late),)), pltpu.SemaphoreType.DMA((math.gcd(entries, 8),))],
        compiler_params=PARAMS,
        name="stencil",
    )(here, current, edges, table, old, owner, *[in_hbm(x) for x in (remap_tiles[0, 0],) + late])

    force, smooth, source, frame, weights, rim_owner, advanced, received, message = pl.pallas_call(
        functools.partial(forward_kernel, plan),
        out_shape=[
            struct((blocks, LANES)),
            struct((blocks, LANES)),
            struct((FRAME, LANES)),
            struct((8 * FRAME, LANES)),
            struct((tile_count, 3 * bottoms, LANES)),
            struct((2, 8, LANES), I32),
            struct((fields.shape[1], cells)),
            struct((channels, cells)),
            struct((2 * tile_count, 4, LANES)),
        ],
        in_specs=[VMEM] * 24,
        out_specs=[VMEM] * 6 + [ANY] * 3,
        scratch_shapes=[
            pltpu.VMEM((4 * entries, LANES), F32),
            pltpu.VMEM((4 * entries, LANES), F32),
            pltpu.VMEM((blocks + 16, LANES), F32),
            pltpu.VMEM((blocks, LANES), F32),
            pltpu.VMEM((2, base, LANES), F32),
            pltpu.VMEM((3 * bottoms, bottoms * tile_count), F32),
            pltpu.VMEM((2, fields.shape[1], LANES), F32),
            pltpu.VMEM((channels, cells), F32),
            pltpu.VMEM((2 * tile_count, 4, LANES), F32),
            pltpu.SemaphoreType.DMA((5,)),
        ],
        compiler_params=PARAMS,
        name="forward",
    )(
        tiles, scalars, *messages, here, hot, member, current, edges, window, old,
        damping, force_part, beside_old, ends_row, ends_lane, fresh, ctable, cedge, cdiag, cowner, cinverse,
    )
    arrived = lax.all_to_all(message, ("comp", "tile"), split_axis=0, concat_axis=0, tiled=True)
    height = pl.pallas_call(
        functools.partial(backward_kernel, frows),
        out_shape=struct((blocks, LANES)),
        in_specs=[VMEM] * 11,
        out_specs=VMEM,
        scratch_shapes=[
            pltpu.VMEM((FRAME, LANES), F32),
            pltpu.VMEM((blocks + 16, LANES), F32),
            pltpu.VMEM((FRAME, LANES), F32),
        ],
        compiler_params=PARAMS,
        name="backward",
    )(arrived, weights, source, frame, force, smooth, edges, window, damping, owner, rim_owner)
    return advanced[None], received[None], height.reshape(1, cells)


def solution(mesh):
    in_specs = (
        P("comp", None, "tile"),
        P("comp", None),
        P("comp", None, "tile"),
        P("comp", "tile"),
        P("comp", None, "tile"),
        P("comp", "tile"),
        P("comp", None),
        P("comp", None),
        P("comp", "tile"),
        P("comp", None, "tile"),
        P("comp", None, "tile"),
        P("comp", "tile"),
        P("comp", "tile"),
        P("comp", "tile", None),
        P("comp", None, "tile"),
        P("comp", "tile", None),
        P("comp", "tile", None),
        P("comp", "tile", None),
        P("comp", "tile", None, None, None),
    )
    out_specs = (P("comp", None, "tile"), P("comp", None, "tile"), P("comp", "tile"))
    return jax.shard_map(
        per_device, mesh=mesh, in_specs=in_specs, out_specs=out_specs, check_vma=False
    )
```

```python
import functools
import math

import jax
import jax.numpy as jnp
from jax import lax
from jax.experimental import pallas as pl
from jax.experimental.pallas import tpu as pltpu
from jax.sharding import PartitionSpec as P

LANES = 128
RELAXATION = 0.8
F32 = jnp.float32
BF16 = jnp.bfloat16
I32 = jnp.int32

FIELD_HI, FIELD_LO = 0, 8
EDGE_HI, EDGE_LO, OLD_HI, OLD_LO = 16, 19, 22, 23
OFFSET, OWNER = 24, 27
CEDGE_HI, CEDGE_LO, CDIAG_HI, CDIAG_LO = 32, 38, 44, 46
COFFSET, COWNER = 48, 54
INVERSE = 56

FRAME, OWN = 32, 8

MIDDLE = 32


PLANS = {
    16: (
        (1, 1, 1, 1, 1, 2, 2, -1, 2, 2, -1, 2, 2, 2, -2, 1),
        (-1, 2, 2, -2, -2, 1, -1, 2, -1, 1, -2, 1, 1, -2, 2, -1),
        (-2, -2, -2, -1, -1, -1, 1, -2, -2, -1, 1, -2, -2, -1, -1, 2),
        (2, -1, -1, 2, 2, -2, -2, 1, 1, -2, 2, -1, -1, 1, 1, -2),
    ),
}
DISTANCES = (-1, 1, -2, 2)


def exchange_plan(count):
    if count in PLANS:
        return PLANS[count]
    near = [1 if i % 2 == 0 else -1 for i in range(count)]
    return ([2] * count, [-d for d in near], [-2] * count, near)


def lookup(tile, values):
    result = jnp.int32(values[0])
    for i, value in enumerate(values):
        result = jnp.where(tile == i, jnp.int32(value), result)
    return result


def arrived_by(tile, plan, distance):
    count = len(plan[0])
    found = []
    for i in range(count):
        sender = (i - distance) % count
        found.append([op[sender] for op in plan].index(distance))
    return lookup(tile, found)


def chosen_rows(which, refs, rows):
    value = refs[0][rows, :]
    for i, ref in enumerate(refs[1:]):
        value = jnp.where(which == i + 1, ref[rows, :], value)
    return value


def gather_lanes(table, index):
    return jnp.take_along_axis(table, index, axis=1)


def wide(row, count=8):
    return jnp.broadcast_to(row, (count, row.shape[1]))


def split2(x):
    high = x.astype(BF16)
    return high, (x - high.astype(F32)).astype(BF16)


def dot_nt(a, b):
    return lax.dot_general(a, b, (((1,), (1,)), ((), ())), preferred_element_type=F32)


def dot_tn(a, b):
    return lax.dot_general(a, b, (((0,), (0,)), ((), ())), preferred_element_type=F32)


def pick_base(bottoms, size):
    return -(-(INVERSE + 2 * bottoms * (size // LANES)) // 16) * 16


def load_kernel(*refs):
    count = len(refs) // 2
    copies = [
        pltpu.make_async_copy(source, target, refs[-1].at[i])
        for i, (source, target) in enumerate(zip(refs[:count], refs[count : 2 * count]))
    ]
    for copy in copies:
        copy.start()
    for copy in copies:
        copy.wait()


def pack_kernel(
    plan, surface, sends, fields, old, edge, table, owner, ctable, cedge, cdiag, cowner, cinverse,
    out0, out1, out2, out3, here, chunks, left_rows, right_rows, packed,
):
    tile = lax.axis_index("tile")
    cells = fields.shape[1]
    blocks = cells // LANES
    frows = ctable.shape[1]
    firsts = frows * LANES
    bottoms = cinverse.shape[0]
    base = pick_base(*cinverse.shape)
    lane = lax.broadcasted_iota(I32, (1, LANES), 1)

    for rows, at_left in ((right_rows, False), (left_rows, True)):
        start = 0 if at_left else cells - LANES
        part = pl.ds(start, LANES)

        def both(high, low_row, value):
            count = value.shape[0]
            rows[pl.ds(high, count), :] = value
            rows[pl.ds(low_row, count), :] = value - value.astype(BF16).astype(F32)

        def three(ref, row):
            return jnp.concatenate([ref[link, pl.ds(row, 1), :] for link in range(3)], axis=0)

        rows[pl.ds(24, 8), :] = jnp.zeros((8, LANES), F32)
        both(FIELD_HI, FIELD_LO, fields[:, part])
        block = 0 if at_left else blocks - 1
        both(EDGE_HI, EDGE_LO, three(edge, block))
        both(OLD_HI, OLD_LO, old[pl.ds(block, 1), :])
        rows[pl.ds(OFFSET, 3), :] = (three(table, block) - (LANES + start) - lane).astype(F32)
        shift = 0 if at_left else firsts - LANES
        rows[pl.ds(OWNER, 1), :] = (owner[pl.ds(block, 1), :] - shift).astype(F32)
        first = 0 if at_left else frows - 2
        reach = LANES // 8
        for step in range(2):
            both(CEDGE_HI + 3 * step, CEDGE_LO + 3 * step, three(cedge, first + step))
            rows[pl.ds(COFFSET + 3 * step, 3), :] = (
                three(ctable, first + step) - (reach + (first + step) * LANES) - lane
            ).astype(F32)
            both(CDIAG_HI + step, CDIAG_LO + step, cdiag[pl.ds(first + step, 1), :])
            rows[pl.ds(COWNER + step, 1), :] = cowner[pl.ds(first + step, 1), :].astype(F32)
        halves = cinverse.shape[1] // LANES
        for half in range(halves):
            both(
                INVERSE + bottoms * half,
                INVERSE + bottoms * (halves + half),
                cinverse[:, pl.ds(half * LANES, LANES)],
            )
        end = INVERSE + 2 * bottoms * halves
        if base > end:
            rows[pl.ds(end, base - end), :] = jnp.zeros((base - end, LANES), F32)

    for block in range(blocks):
        chunks[pl.ds(4 * block, 4), :] = surface[:, pl.ds(block * LANES, LANES)].astype(F32)
    slots = sends.shape[1]
    hot = jnp.where(
        lax.broadcasted_iota(I32, (blocks, slots), 0) == sends[...], 1.0, 0.0
    ).astype(BF16)
    picks = []
    for channel in range(4):
        source = chunks[pl.ds(channel, blocks, stride=4), :].astype(BF16)
        picks.append(dot_tn(hot, source).astype(BF16))
    count = slots // 5

    chosen = [
        jnp.concatenate([p[j * count : (j + 1) * count] for p in picks], axis=0) for j in range(5)
    ]
    here[...] = chosen[2]
    rims = {-1: left_rows[...].astype(BF16), 1: right_rows[...].astype(BF16)}
    for at, distance in enumerate(DISTANCES):
        packed[at, pl.ds(0, base), :] = rims.get(distance, jnp.zeros((base, LANES), BF16))
        packed[at, pl.ds(base, 4 * count), :] = chosen[2 - distance]
    for out, op in zip((out0, out1, out2, out3), plan):
        out[...] = packed[lookup(tile, [DISTANCES.index(distance) for distance in op])]


def stencil_kernel(
    here, fields, edge, table, old, owner, tiles, rate, level_weight, flux_weight, diagonal_in, slots_in, block_in,
    fresh, force, beside_old, window, ends_row, ends_lane, hot, member, damping, scalars, tile_buffer,
    padded, rate_row, level_row, flux_row, diagonal, slots, entry_block, small_sems, sems,
):
    del here
    small = [
        pltpu.make_async_copy(source, target, small_sems.at[i])
        for i, (source, target) in enumerate(
            (
                (rate, rate_row), (level_weight, level_row), (flux_weight, flux_row),
                (diagonal_in, diagonal), (slots_in, slots), (block_in, entry_block),
            )
        )
    ]
    parts = sems.shape[0]
    step = tiles.shape[0] // parts

    def load(part):
        span = pl.ds(part * step, step)
        return pltpu.make_async_copy(tiles.at[span], tile_buffer.at[span], sems.at[part])

    def begin(part, carry):
        if part is None:
            for copy in small:
                copy.start()
        else:
            load(part).start()
        return carry

    once = 1 + lax.axis_index("tile") // lax.axis_size("tile")
    lax.fori_loop(0, once, lambda _, carry: begin(None, carry), 0)
    lax.fori_loop(0, parts, begin, 0)
    blocks = old.shape[0]
    levels = fields.shape[0]
    firsts = ends_row.shape[0] * LANES
    ident = lax.broadcasted_iota(I32, ends_row.shape, 0) * LANES + lax.broadcasted_iota(
        I32, ends_row.shape, 1
    )
    count = ends_row.shape[0]
    rows = jnp.zeros(ends_row.shape, I32)
    for block in range(blocks):
        last = jnp.broadcast_to(owner[pl.ds(block, 1), LANES - 1 : LANES], ends_row.shape)
        rows = rows + jnp.where(last <= ident, 1, 0)
    lanes = jnp.zeros(ends_row.shape, I32)
    for bit in (64, 32, 16, 8, 4, 2, 1):
        probe = lanes + (bit - 1)
        value = jnp.full(ends_row.shape, firsts, I32)
        for block in range(blocks):
            value = jnp.where(
                rows == block, gather_lanes(wide(owner[pl.ds(block, 1), :], count), probe), value
            )
        lanes = jnp.where(value <= ident, lanes + bit, lanes)
    ends_row[...] = rows
    ends_lane[...] = lanes
    for copy in small:
        copy.wait()
    for i, value in enumerate((rate_row, level_row, flux_row)):
        width = value.shape[1]
        same = lax.broadcasted_iota(I32, (8, width), 0) == lax.broadcasted_iota(I32, (8, width), 1)
        column = jnp.sum(jnp.where(same, wide(value[...]), 0.0), axis=1, keepdims=True)
        scalars[pl.ds(8 * i, 8), :] = jnp.broadcast_to(column, (8, LANES))
    speed = scalars[pl.ds(0, 8), :]
    share = scalars[pl.ds(8, 8), :]
    starts = lax.broadcasted_iota(I32, (blocks, LANES), 0) * LANES
    total = edge[0] + edge[1] + edge[2]
    inverse = 1.0 / total
    fine_total = diagonal[...] + total
    damping[0] = fine_total
    damping[1] = RELAXATION / fine_total
    for link in range(3):
        window[link] = table[link] - starts
    blank = jnp.zeros((levels, LANES), F32)

    def chunk(block):
        if 0 <= block < blocks:
            return fields[:, pl.ds(block * LANES, LANES)]
        return blank

    before, here, after = blank, chunk(0), chunk(1)
    for block in range(blocks):
        row = slice(block, block + 1)
        beside = jnp.zeros((levels, LANES), F32)
        for link in range(3):
            place = wide(window[link, pl.ds(block, 1), :])
            index = lax.bitwise_and(place, LANES - 1)
            value = jnp.where(
                place < LANES,
                gather_lanes(before, index),
                jnp.where(place < 2 * LANES, gather_lanes(here, index), gather_lanes(after, index)),
            )
            beside = beside + wide(edge[link, pl.ds(block, 1), :]) * value
        result = here + speed * ((beside - wide(total[row]) * here) * wide(inverse[row]))
        fresh[:, pl.ds(block * LANES, LANES)] = result
        force[pl.ds(block, 1), :] = jnp.sum(result * share, axis=0, keepdims=True)
        before, here, after = here, after, chunk(block + 2)

    padded[pl.ds(0, 8), :] = jnp.zeros((8, LANES), F32)
    padded[pl.ds(8 + blocks, 8), :] = jnp.zeros((8, LANES), F32)
    padded[pl.ds(8, blocks), :] = old[...]
    beside_old[...] = neighbour_sum(padded, edge, window, blocks)
    names = jnp.where(
        lax.broadcasted_iota(I32, (slots.shape[1], slots.shape[1]), 0) == slots[...], 1.0, 0.0
    )
    hot[...] = jnp.transpose(names).astype(BF16)
    half = entry_block.shape[1] // 2
    for part in range(2):
        member[part] = jnp.where(
            lax.broadcasted_iota(I32, (blocks, half), 0) == entry_block[:, part * half : (part + 1) * half],
            1.0,
            0.0,
        ).astype(BF16)

    for part in range(parts):
        load(part).wait()


def neighbour_sum(padded, edges, window, blocks):
    before = padded[pl.ds(7, blocks), :]
    here = padded[pl.ds(8, blocks), :]
    after = padded[pl.ds(9, blocks), :]
    result = jnp.zeros((blocks, LANES), F32)
    for link in range(3):
        place = window[link]
        index = lax.bitwise_and(place, LANES - 1)
        value = jnp.where(
            place < LANES,
            gather_lanes(before, index),
            jnp.where(place < 2 * LANES, gather_lanes(here, index), gather_lanes(after, index)),
        )
        result = result + edges[link] * value
    return result


def first_level_sum(values, frame):
    before = pltpu.roll(values, 1, axis=0)
    after = pltpu.roll(values, FRAME - 1, axis=0)
    lane = lax.broadcasted_iota(I32, (FRAME, LANES), 1)
    result = jnp.zeros((FRAME, LANES), F32)
    for link in range(3):
        place = lane + frame[pl.ds(link * FRAME, FRAME), :].astype(I32)
        index = lax.bitwise_and(place, LANES - 1)
        value = jnp.where(
            place < 0,
            gather_lanes(before, index),
            jnp.where(place >= LANES, gather_lanes(after, index), gather_lanes(values, index)),
        )
        result = result + frame[pl.ds((3 + link) * FRAME, FRAME), :] * value
    return result


def previous_one(values):
    rolled = pltpu.roll(values, 1, axis=1)
    above = pltpu.roll(rolled, 1, axis=0)
    lane = lax.broadcasted_iota(I32, values.shape, 1)
    row = lax.broadcasted_iota(I32, values.shape, 0)
    return jnp.where(lane > 0, rolled, jnp.where(row > 0, above, 0.0))


def triangle():
    return jnp.where(
        lax.broadcasted_iota(I32, (LANES, LANES), 0) < lax.broadcasted_iota(I32, (LANES, LANES), 1),
        1.0,
        0.0,
    ).astype(BF16)


def prefix(values):
    ones = jnp.ones((LANES, LANES), BF16)
    right = jnp.concatenate([triangle(), ones], axis=1)
    count = values.shape[0]
    out = jnp.dot(
        jnp.concatenate(split2(values), axis=0), right, preferred_element_type=F32
    )
    out = out[:count] + out[count:]
    return out[:, :LANES], out[:, LANES:]


def rows_before(values):
    sublane = lax.broadcasted_iota(I32, (8, LANES), 0)
    run = jnp.zeros((8, LANES), F32)
    result = []
    for at in range(0, values.shape[0], 8):
        piece = values[at : at + 8]
        total = piece
        for distance in (1, 2, 4):
            total = total + jnp.where(sublane >= distance, pltpu.roll(total, distance, axis=0), 0.0)
        result.append(run + (total - piece))
        run = run + wide(total[7:8])
    return jnp.concatenate(result, axis=0), run


def forward_kernel(
    plan, tiles, scalars, message0, message1, message2, message3, here, hot, member, fields, edges, window, old,
    damping, force_part, beside_old, ends_row, ends_lane, fresh, ctable, cedge, cdiag, cowner, cinverse,
    force_out, smooth_out, source_out, frame, weights_out, rim_owner, fresh_out, received_out, message_out,
    picked, products, padded, prefixed, arrivals, extended, ends, received, message, sems,
):
    cells = fresh.shape[1]
    middle = pl.ds(LANES, cells - 2 * LANES)
    copies = [pltpu.make_async_copy(fresh.at[:, middle], fresh_out.at[:, middle], sems.at[0])]
    for side in range(2):
        copies.append(
            pltpu.make_async_copy(
                ends.at[side], fresh_out.at[:, pl.ds(side * (cells - LANES), LANES)], sems.at[1 + side]
            )
        )
    copies.append(pltpu.make_async_copy(received, received_out, sems.at[3]))
    copies.append(pltpu.make_async_copy(message, message_out, sems.at[4]))

    def begin(which):
        def body(_, carry):
            for copy in which:
                copy.start()
            return carry

        lax.fori_loop(0, 1 + lax.axis_index("tile") // lax.axis_size("tile"), body, 0)

    begin(copies[:1])
    tile = lax.axis_index("tile")
    tile_count = lax.axis_size("tile")
    entries = tiles.shape[0]
    blocks = old.shape[0]

    messages = (message0, message1, message2, message3)
    base = message0.shape[0] - here.shape[0]
    each = here.shape[0] // 4
    found = {distance: arrived_by(tile, plan, distance) for distance in DISTANCES}
    sources = [
        chosen_rows(found[distance], messages, pl.ds(base, 4 * each)) if distance else here[...]
        for distance in (2, 1, 0, -1, -2)
    ]
    for channel in range(4):
        source = jnp.concatenate(
            [rows[channel * each : (channel + 1) * each] for rows in sources], axis=0
        )
        picked[pl.ds(channel, entries, stride=4), :] = jnp.dot(hot[...], source, preferred_element_type=F32)

    for side, distance in enumerate((1, -1)):
        arrivals[side] = chosen_rows(found[distance], messages, pl.ds(0, base)).astype(F32)
        rim_owner[side] = wide(arrivals[side, pl.ds(OWNER, 1), :]).astype(I32)

    upper = lax.rem(lax.broadcasted_iota(I32, (16, LANES), 0), 8) < 4
    for group in range(entries // 4):
        rows = picked[pl.ds(16 * group, 16), :]
        rows = jnp.concatenate([jnp.where(upper, rows, 0.0), jnp.where(upper, 0.0, rows)], axis=1)
        at = 4 * group
        weights = jnp.concatenate(
            [
                jnp.concatenate([tiles[at], tiles[at + 1]], axis=1),
                jnp.concatenate([tiles[at + 2], tiles[at + 3]], axis=1),
            ],
            axis=0,
        )
        product = dot_nt(rows.astype(BF16), weights)
        products[pl.ds(16 * group, 8), :] = product[0:8, :LANES]
        products[pl.ds(16 * group + 8, 8), :] = product[8:16, LANES:]
    speed = scalars[pl.ds(0, 8), :]
    share = scalars[pl.ds(8, 8), :]
    force_out[...] = force_part[...]
    padded[pl.ds(0, 8), :] = jnp.zeros((8, LANES), F32)
    padded[pl.ds(8 + blocks, 8), :] = jnp.zeros((8, LANES), F32)
    beside_extra = []
    for side, block, target in ((0, 0, 0), (1, blocks - 1, 2)):
        halo = arrivals[side, pl.ds(FIELD_HI, 8), :] + arrivals[side, pl.ds(FIELD_LO, 8), :]
        halo_old = arrivals[side, pl.ds(OLD_HI, 1), :] + arrivals[side, pl.ds(OLD_LO, 1), :]
        total = edges[0, pl.ds(block, 1), :] + edges[1, pl.ds(block, 1), :] + edges[2, pl.ds(block, 1), :]
        extra = jnp.zeros((8, LANES), F32)
        extra_old = jnp.zeros((8, LANES), F32)
        for link in range(3):
            place = wide(window[link, pl.ds(block, 1), :])
            index = lax.bitwise_and(place, LANES - 1)
            weight = jnp.where(
                lax.shift_right_logical(place, 7) == target, wide(edges[link, pl.ds(block, 1), :]), 0.0
            )
            extra = extra + weight * gather_lanes(halo, index)
            extra_old = extra_old + weight * gather_lanes(wide(halo_old), index)
        change = speed * extra / wide(total)
        ends[side] = fresh[:, pl.ds(block * LANES, LANES)] + change
        force_out[pl.ds(block, 1), :] += jnp.sum(change * share, axis=0, keepdims=True)
        beside_extra.append(extra_old[0:1])

    inverse_windows(arrivals.at[0], cinverse, arrivals.at[1], extended, weights_out)

    force = force_out[...]
    half = entries // 2
    for channel in range(4):
        value = jnp.zeros((blocks, 2 * LANES), F32)
        for part in range(2):
            rows = products[pl.ds(4 * half * part + channel, half, stride=4), :]
            value = value + jnp.dot(
                member[part], jnp.concatenate(split2(rows), axis=1), preferred_element_type=F32
            )
        value = value[:, :LANES] + value[:, LANES:]
        for block in range(blocks):
            received[pl.ds(channel, 1), pl.ds(block * LANES, LANES)] = value[block : block + 1]
        force = force + scalars[pl.ds(16 + channel, 1), :] * value

    force_out[...] = force
    begin(copies[1:4])
    total, damp = damping[0], damping[1]
    smooth_out[...] = beside_old[...]
    smooth_out[pl.ds(0, 1), :] += beside_extra[0]
    smooth_out[pl.ds(blocks - 1, 1), :] += beside_extra[1]
    previous = old[...]
    smooth = previous + damp * (force - (total * previous - smooth_out[...]))
    smooth_out[...] = smooth
    padded[pl.ds(8, blocks), :] = smooth
    residual = force - total * smooth + neighbour_sum(padded, edges, window, blocks)

    inner, whole = prefix(residual)
    before, run = rows_before(whole)
    prefixed[...] = inner + before
    rows, lanes = ends_row[...], ends_lane[...]
    count = rows.shape[0]
    marks = run[:count]
    for block in range(blocks):
        value = gather_lanes(wide(prefixed[pl.ds(block, 1), :], count), lanes)
        marks = jnp.where(rows == block, value, marks)
    own_source = marks - previous_one(marks)

    lane = lax.broadcasted_iota(I32, (1, LANES), 1)
    rim_rows, rim_counts = [], []
    for side in range(2):
        inside = padded[pl.ds(8 if side == 0 else 7 + blocks, 1), :]
        value = jnp.zeros((1, LANES), F32)
        for link in range(3):
            place = lane + arrivals[side, pl.ds(OFFSET + link, 1), :].astype(I32)
            index = lax.bitwise_and(place, LANES - 1)
            reached = (place >= LANES) if side == 0 else (place < 0)
            weight = arrivals[side, pl.ds(EDGE_HI + link, 1), :] + arrivals[side, pl.ds(EDGE_LO + link, 1), :]
            value = value + jnp.where(
                wide(reached.astype(I32)) > 0,
                wide(weight) * gather_lanes(wide(inside), wide(index)),
                0.0,
            )[0:1]
        rim_rows.append(value)
        owners = arrivals[side, pl.ds(OWNER, 1), :].astype(I32)
        below = jnp.where(
            lax.broadcasted_iota(I32, (LANES, LANES), 0) >= owners, 1.0, 0.0
        ).astype(BF16)
        rim_counts.append(dot_nt(jnp.ones((8, LANES), BF16), below))
    rim_inner, rim_whole = prefix(jnp.concatenate([wide(r) for r in rim_rows], axis=0))
    rim_source = []
    for side in range(2):
        place = rim_counts[side].astype(I32)
        index = lax.bitwise_and(place, LANES - 1)
        value = gather_lanes(rim_inner[8 * side : 8 * side + 8], index)
        value = jnp.where(place >= LANES, rim_whole[8 * side : 8 * side + 8], value)
        shifted = pltpu.roll(value, 1, axis=1)
        first = lax.broadcasted_iota(I32, (8, LANES), 1) == 0
        rim_source.append((value - jnp.where(first, 0.0, shifted))[0:1])

    frows = own_source.shape[0]
    source_out[...] = jnp.zeros((FRAME, LANES), F32)
    source_out[pl.ds(OWN, frows), :] = own_source
    source_out[pl.ds(OWN - 1, 1), :] = rim_source[0]
    source_out[pl.ds(OWN + frows, 1), :] = rim_source[1]
    reach = LANES // 8
    frame[...] = jnp.zeros(frame.shape, F32)
    frame[pl.ds(6 * FRAME, FRAME), :] = jnp.ones((FRAME, LANES), F32)
    frame[pl.ds(7 * FRAME, FRAME), :] = jnp.full((FRAME, LANES), 127.0, F32)
    bottoms = cinverse.shape[0]
    at_cell = lax.broadcasted_iota(I32, (frows, LANES), 0) * LANES + lax.broadcasted_iota(
        I32, (frows, LANES), 1
    )
    for link in range(3):
        frame[pl.ds(link * FRAME + OWN, frows), :] = (ctable[link] - reach - at_cell).astype(F32)
        frame[pl.ds((3 + link) * FRAME + OWN, frows), :] = cedge[link]
    frame[pl.ds(6 * FRAME + OWN, frows), :] = cdiag[...]
    frame[pl.ds(7 * FRAME + OWN, frows), :] = (cowner[...] + bottoms).astype(F32)
    for side in range(2):
        for row in range(2):
            at = (OWN - 2 + row) if side == 0 else (OWN + frows + row)
            for link in range(3):
                put = 3 * row + link
                frame[pl.ds(link * FRAME + at, 1), :] = arrivals[side, pl.ds(COFFSET + put, 1), :]
                frame[pl.ds((3 + link) * FRAME + at, 1), :] = (
                    arrivals[side, pl.ds(CEDGE_HI + put, 1), :] + arrivals[side, pl.ds(CEDGE_LO + put, 1), :]
                )
            frame[pl.ds(6 * FRAME + at, 1), :] = (
                arrivals[side, pl.ds(CDIAG_HI + row, 1), :] + arrivals[side, pl.ds(CDIAG_LO + row, 1), :]
            )
            frame[pl.ds(7 * FRAME + at, 1), :] = arrivals[side, pl.ds(COWNER + row, 1), :] + (
                2.0 * bottoms * side
            )
    for link in range(3):
        frame[pl.ds(6 * FRAME, FRAME), :] += frame[pl.ds((3 + link) * FRAME, FRAME), :]
    source = source_out[...]
    damp_first = RELAXATION / frame[pl.ds(6 * FRAME, FRAME), :]
    frame[pl.ds(8 * FRAME, FRAME), :] = damp_first
    first = damp_first * source
    residual = (1.0 - RELAXATION) * source + first_level_sum(first, frame)
    codes = frame[pl.ds(7 * FRAME, FRAME), :].astype(I32)
    pieces = split2(residual)
    left_side, right_side = [], []
    bins = lax.broadcasted_iota(I32, (3 * bottoms, LANES), 0)
    rest = [jnp.zeros((rows, LANES), BF16) for rows in (MIDDLE, LANES - MIDDLE - 3 * bottoms)]
    for row in range(OWN - 2, OWN + frows + 2):
        left_side.append(jnp.concatenate([p[row : row + 1] for p in pieces], axis=0))
        named = jnp.where(bins == codes[row : row + 1], 1.0, 0.0).astype(BF16)
        right_side.append(jnp.concatenate([rest[0], named, rest[1]], axis=0))
    bottom = dot_nt(jnp.concatenate(left_side, axis=1), jnp.concatenate(right_side, axis=1))
    bottom = bottom[0:1] + bottom[1:2]

    reach = LANES // 8
    to_left = jnp.concatenate(
        [
            jnp.where(lane < reach, own_source[1:2], bottom),
            padded[pl.ds(8, 1), :],
            own_source[0:1],
            rim_source[0],
        ],
        axis=0,
    )
    to_right = jnp.concatenate(
        [
            jnp.where(lane >= LANES - reach, own_source[frows - 2 : frows - 1], bottom),
            padded[pl.ds(7 + blocks, 1), :],
            own_source[frows - 1 : frows],
            rim_source[1],
        ],
        axis=0,
    )
    for other in range(message.shape[0]):
        message[other] = to_right
    for group in range(2):
        message[group * tile_count + lax.rem(tile + tile_count - 1, tile_count)] = to_left
    copies[4].start()
    for copy in copies:
        copy.wait()


def inverse_windows(left, own, right, extended, weights):
    bottoms, size = own.shape
    halves = size // LANES
    for half in range(halves):
        part = pl.ds(half * LANES, LANES)
        for at, block in ((0, left), (2, right)):
            high, low = INVERSE + bottoms * half, INVERSE + bottoms * (halves + half)
            extended[pl.ds(at * bottoms, bottoms), part] = (
                block[pl.ds(high, bottoms), :] + block[pl.ds(low, bottoms), :]
            )
        extended[pl.ds(bottoms, bottoms), part] = own[:, part]
    table = extended[...]
    lane = lax.broadcasted_iota(I32, (3 * bottoms, LANES), 1)
    for other in range(weights.shape[0]):
        shift = (size + MIDDLE - (other - 1) * bottoms) % size
        turned = pltpu.roll(table, shift, axis=1) if shift else table
        weights[other] = jnp.where(
            lane >= MIDDLE, jnp.where(lane < MIDDLE + 3 * bottoms, turned[:, :LANES], 0.0), 0.0
        )


def backward_kernel(
    frame_rows, arrived, weights, source, frame, force, smooth, edges, window, damping, owner, rim_owner,
    height, frame_source, padded, third_rows,
):
    tile = lax.axis_index("tile")
    tile_count = lax.axis_size("tile")
    blocks = force.shape[0]
    arrived = arrived.at[pl.ds(lax.axis_index("comp") * tile_count, tile_count)]
    left = arrived[lax.rem(tile + tile_count - 1, tile_count)]
    right = arrived[lax.rem(tile + 1, tile_count)]
    count = weights.shape[1]
    sums = [jnp.zeros((count, LANES), F32)] * 4
    for other in range(weights.shape[0]):
        part = weights[other] * wide(arrived[other, pl.ds(0, 1), :], count)
        sums[other % 4] = sums[other % 4] + part
    partial = (sums[0] + sums[1]) + (sums[2] + sums[3])
    partial = jnp.concatenate([partial, jnp.zeros((LANES - count, LANES), F32)], axis=0)
    ones = jnp.ones((8, LANES), BF16)
    bottom = dot_nt(jnp.concatenate([ones, ones], axis=1), jnp.concatenate(split2(partial), axis=1))

    frows = frame_rows
    frame_source[...] = source[...]
    lane = lax.broadcasted_iota(I32, (1, LANES), 1)
    reach = LANES // 8
    frame_source[pl.ds(OWN - 2, 1), :] += jnp.where(lane >= LANES - reach, left[0:1], 0.0)
    frame_source[pl.ds(OWN - 1, 1), :] += left[2:3]
    frame_source[pl.ds(OWN, 1), :] += left[3:4]
    frame_source[pl.ds(OWN + frows - 1, 1), :] += right[3:4]
    frame_source[pl.ds(OWN + frows, 1), :] += right[2:3]
    frame_source[pl.ds(OWN + frows + 1, 1), :] += jnp.where(lane < reach, right[0:1], 0.0)
    total_source = frame_source[...]
    total = frame[pl.ds(6 * FRAME, FRAME), :]
    codes = frame[pl.ds(7 * FRAME, FRAME), :].astype(I32)
    damp = frame[pl.ds(8 * FRAME, FRAME), :]
    second = damp * total_source + gather_lanes(wide(bottom[0:1], FRAME), codes)
    third = second + damp * (total_source - total * second + first_level_sum(second, frame))
    third_rows[...] = third

    owners = owner[...]
    index = lax.bitwise_and(owners, LANES - 1)
    which = lax.shift_right_logical(owners, 7)
    corrected = jnp.zeros((blocks, LANES), F32)
    for row in range(frows):
        corrected = jnp.where(
            which == row, gather_lanes(wide(third_rows[pl.ds(OWN + row, 1), :], blocks), index), corrected
        )
    corrected = smooth[...] + corrected
    padded[pl.ds(8, blocks), :] = corrected
    left_rim = left[1:2] + gather_lanes(wide(third_rows[pl.ds(OWN - 1, 1), :]), rim_owner[0])[0:1]
    right_rim = right[1:2] + gather_lanes(wide(third_rows[pl.ds(OWN + frows, 1), :]), rim_owner[1])[0:1]
    padded[pl.ds(7, 1), :] = left_rim
    padded[pl.ds(8 + blocks, 1), :] = right_rim
    beside = neighbour_sum(padded, edges, window, blocks)
    height[...] = corrected + damping[1] * (force[...] - (damping[0] * corrected - beside))


def in_hbm(array):
    return pltpu.with_memory_space_constraint(array, pltpu.HBM)


def struct(shape, dtype=F32):
    return jax.ShapeDtypeStruct(shape, dtype)


VMEM = pl.BlockSpec(memory_space=pltpu.VMEM)
SMEM = pl.BlockSpec(memory_space=pltpu.SMEM)
ANY = pl.BlockSpec(memory_space=pltpu.HBM)
PARAMS = pltpu.CompilerParams(vmem_limit_bytes=16 * 1024 * 1024)


def per_device(
    fields, level_rate, edge_weight, fine_diagonal, fine_table, old_height, level_weight,
    flux_weight, fine_owner, coarse_table, coarse_edge, coarse_diagonal, coarse_owner,
    coarse_inverse, surface_out, send_blocks, entry_slot, entry_block, remap_tiles,
):
    tile_count = lax.axis_size("tile")
    cells = fields.shape[2]
    blocks = cells // LANES
    firsts = coarse_diagonal.shape[1]
    frows = firsts // LANES
    entries = entry_slot.shape[2]
    channels = surface_out.shape[1]
    slots = send_blocks.shape[2]
    each = slots // 5
    bottoms = coarse_inverse.shape[1]
    base = pick_base(*coarse_inverse.shape[1:])
    swap = [(0, 1), (1, 0)]
    surface = lax.ppermute(surface_out[0], "comp", swap)
    sends = lax.ppermute(send_blocks[0], "comp", swap)
    raw = (
        fields[0],
        old_height.reshape(blocks, LANES),
        edge_weight[0].reshape(3, blocks, LANES),
        fine_table[0].reshape(3, blocks, LANES),
        fine_owner.reshape(blocks, LANES),
        coarse_table[0].reshape(3, frows, LANES),
        coarse_edge[0].reshape(3, frows, LANES),
        coarse_diagonal.reshape(frows, LANES),
        coarse_owner.reshape(frows, LANES),
        coarse_inverse[0],
    )
    current, old, edges, table, owner, ctable, cedge, cdiag, cowner, cinverse = pl.pallas_call(
        load_kernel,
        out_shape=[struct(x.shape, x.dtype) for x in raw],
        in_specs=[ANY] * len(raw),
        out_specs=[VMEM] * len(raw),
        scratch_shapes=[pltpu.SemaphoreType.DMA((len(raw),))],
        compiler_params=PARAMS,
        name="load",
    )(*[in_hbm(x) for x in raw])

    pick = struct((4 * each, LANES), BF16)
    both = struct((base + 4 * each, LANES), BF16)
    plan = exchange_plan(tile_count)
    *messages, here = pl.pallas_call(
        functools.partial(pack_kernel, plan),
        out_shape=[both, both, both, both, pick],
        in_specs=[VMEM] * 12,
        out_specs=[VMEM] * 5,
        scratch_shapes=[
            pltpu.VMEM((channels * blocks, LANES), F32),
            pltpu.VMEM((base, LANES), F32),
            pltpu.VMEM((base, LANES), F32),
            pltpu.VMEM((4, base + 4 * each, LANES), BF16),
        ],
        compiler_params=PARAMS,
        name="pack",
    )(
        surface, sends, current, old, edges, table, owner, ctable, cedge, cdiag, cowner, cinverse,
    )

    messages = [
        lax.ppermute(message, "tile", [(i, (i + op[i]) % tile_count) for i in range(tile_count)])
        for message, op in zip(messages, plan)
    ]

    late = (
        level_rate, level_weight, flux_weight, fine_diagonal.reshape(blocks, LANES), entry_slot[0], entry_block[0]
    )
    fresh, force_part, beside_old, window, ends_row, ends_lane, hot, member, damping, scalars, tiles = pl.pallas_call(
        stencil_kernel,
        out_shape=[
            struct((fields.shape[1], cells)),
            struct((blocks, LANES)),
            struct((blocks, LANES)),
            struct((3, blocks, LANES), I32),
            struct((frows, LANES), I32),
            struct((frows, LANES), I32),
            struct((entries, slots), BF16),
            struct((2, blocks, entries // 2), BF16),
            struct((2, blocks, LANES)),
            struct((24, LANES)),
            pltpu.VMEM(remap_tiles.shape[2:], BF16),
        ],
        in_specs=[VMEM] * 6 + [ANY] * 7,
        out_specs=[VMEM] * 11,
        scratch_shapes=[pltpu.VMEM((blocks + 16, LANES), F32)]
        + [pltpu.VMEM(x.shape, x.dtype) for x in late]
        + [pltpu.SemaphoreType.DMA((len(late),)), pltpu.SemaphoreType.DMA((math.gcd(entries, 8),))],
        compiler_params=PARAMS,
        name="stencil",
    )(here, current, edges, table, old, owner, *[in_hbm(x) for x in (remap_tiles[0, 0],) + late])

    force, smooth, source, frame, weights, rim_owner, advanced, received, message = pl.pallas_call(
        functools.partial(forward_kernel, plan),
        out_shape=[
            struct((blocks, LANES)),
            struct((blocks, LANES)),
            struct((FRAME, LANES)),
            struct((9 * FRAME, LANES)),
            struct((tile_count, 3 * bottoms, LANES)),
            struct((2, 8, LANES), I32),
            struct((fields.shape[1], cells)),
            struct((channels, cells)),
            struct((2 * tile_count, 4, LANES)),
        ],
        in_specs=[VMEM] * 24,
        out_specs=[VMEM] * 6 + [ANY] * 3,
        scratch_shapes=[
            pltpu.VMEM((4 * entries, LANES), F32),
            pltpu.VMEM((4 * entries, LANES), F32),
            pltpu.VMEM((blocks + 16, LANES), F32),
            pltpu.VMEM((blocks, LANES), F32),
            pltpu.VMEM((2, base, LANES), F32),
            pltpu.VMEM((3 * bottoms, bottoms * tile_count), F32),
            pltpu.VMEM((2, fields.shape[1], LANES), F32),
            pltpu.VMEM((channels, cells), F32),
            pltpu.VMEM((2 * tile_count, 4, LANES), F32),
            pltpu.SemaphoreType.DMA((5,)),
        ],
        compiler_params=PARAMS,
        name="forward",
    )(
        tiles, scalars, *messages, here, hot, member, current, edges, window, old,
        damping, force_part, beside_old, ends_row, ends_lane, fresh, ctable, cedge, cdiag, cowner, cinverse,
    )
    arrived = lax.all_to_all(message, ("comp", "tile"), split_axis=0, concat_axis=0, tiled=True)
    height = pl.pallas_call(
        functools.partial(backward_kernel, frows),
        out_shape=struct((blocks, LANES)),
        in_specs=[VMEM] * 11,
        out_specs=VMEM,
        scratch_shapes=[
            pltpu.VMEM((FRAME, LANES), F32),
            pltpu.VMEM((blocks + 16, LANES), F32),
            pltpu.VMEM((FRAME, LANES), F32),
        ],
        compiler_params=PARAMS,
        name="backward",
    )(arrived, weights, source, frame, force, smooth, edges, window, damping, owner, rim_owner)
    return advanced[None], received[None], height.reshape(1, cells)


def solution(mesh):
    in_specs = (
        P("comp", None, "tile"),
        P("comp", None),
        P("comp", None, "tile"),
        P("comp", "tile"),
        P("comp", None, "tile"),
        P("comp", "tile"),
        P("comp", None),
        P("comp", None),
        P("comp", "tile"),
        P("comp", None, "tile"),
        P("comp", None, "tile"),
        P("comp", "tile"),
        P("comp", "tile"),
        P("comp", "tile", None),
        P("comp", None, "tile"),
        P("comp", "tile", None),
        P("comp", "tile", None),
        P("comp", "tile", None),
        P("comp", "tile", None, None, None),
    )
    out_specs = (P("comp", None, "tile"), P("comp", None, "tile"), P("comp", "tile"))
    return jax.shard_map(
        per_device, mesh=mesh, in_specs=in_specs, out_specs=out_specs, check_vma=False
    )
```
